32 devices in a mesh: stream: 2 (over x), batch: 8 (over z, y), mp: 2 (over core).
Axes of the slice: x: 2, y: 2, z: 4, core: 2. Of those that a mesh axis runs over, the one named last changes fastest.
Arguments:
- tokens: bfloat16 [2, 8, 512, 768], P('stream', 'batch', 'mp'), may hold values from -6 to 6
- segments: int32 [8, 512], P('batch'), may hold values from 0 to 7, never falling along the last dimension, each value on 1 to 128 neighbouring positions
- top_mask: int32 [8, 16, 8, 512], P(None, 'mp', 'batch'), may hold values 0 or 1
- positive: int32 [8, 16], P(None, 'mp'), may hold values from 0 to 63
- w_query: bfloat16 [2, 768, 768], P(None, None, 'mp'), may hold values from -0.02734375 to 0.02734375
- w_kv: bfloat16 [2, 2, 768, 768], P(None, None, None, 'mp'), may hold values from -0.21875 to 0.21875
- w_out: bfloat16 [2, 768, 768], P(None, None, 'mp'), may hold values from -1.75 to 1.75
- w_in: bfloat16 [2, 2, 768, 3072], P(None, None, None, 'mp'), may hold values from -0.21875 to 0.21875
- w_down: bfloat16 [2, 768, 3072], P(None, None, 'mp'), may hold values from -0.15625 to 0.15625
- gains: float32 [5, 768], replicated, may hold values from 0.5 to 1.5
- rel_bias: float32 [32, 12], P(None, 'mp'), may hold values from -4 to 4
- w_proj: bfloat16 [768, 128], replicated, may hold values from -0.21875 to 0.21875
Outputs:
- vectors: bfloat16 [2, 8, 512, 128], P('stream', 'batch', 'mp')
- query_loss: float32 [8, 16], P('batch', 'mp')
- grad_tokens: float32 [2, 8, 512, 768], P('stream', 'batch', 'mp')
- grad_query: float32 [2, 768, 768], P(None, 'batch', 'mp')
- grad_kv: float32 [2, 2, 768, 768], P(None, None, 'batch', 'mp')
- grad_out: float32 [2, 768, 768], P(None, 'batch', 'mp')
- grad_in: float32 [2, 2, 768, 3072], P(None, None, 'batch', 'mp')
- grad_down: float32 [2, 768, 3072], P(None, 'batch', 'mp')
- grad_gains: float32 [5, 768], P(None, 'batch')
- grad_bias: float32 [32, 12], P(None, 'mp')
- grad_proj: float32 [768, 128], P('batch')
The draws below stay inside these ranges and needn't reach their ends.
Inputs may be any that keep to these rules, and one draw needn't show every extreme that they name: `segments`: in each row the ids rise from 0 to 7 in runs, each document 1 to 128 positions long, one exactly 128.
All inputs are finite; a program needn't handle non-finite values. No bound on the sum of `top_mask` on one device may be relied on, other than what follows from the above.
Results may differ from the reference program's by a relative error of at most 0.033.
Values may be sent and summed in bfloat16 or wider, within the bound.
A program may use at most 256 MiB of HBM per device.

```python
import math
import jax
import jax.numpy as jnp
import numpy as np
from jax import lax

D = 768
H = 12
DH = 64
FF = 3072
P_SIZE = 128
BUCKETS = 32
LAYERS = 2
SEQ = 512
QLEN = 32
DOCS_ROW = 8
DOC_MOST = 128
ROWS = 8
QPR = 16
INNER = 768
NDOCS = 64


def set_ends(entries, stream_key, smallest, high):
    longest = entries.shape.index(max(entries.shape))
    spots = []
    for shift in (0, 1):
        where = [jax.random.randint(jax.random.fold_in(stream_key, axis), (), 0, length) for axis, length in enumerate(entries.shape)]
        where[longest] = (where[longest] + shift) % entries.shape[longest]
        spots.append(tuple(where))
    return entries.at[spots[0]].set(smallest).at[spots[1]].set(high)


def steps_of(rng, dims, split, low, high):
    loudness = 1.0
    for dim, blocks in split:
        draws = jax.random.uniform(jax.random.fold_in(jax.random.fold_in(rng, 6), dim), (blocks,), jnp.float32, low / len(split), high / len(split))
        loudness = loudness * jnp.repeat(jnp.exp(draws), dims[dim] // blocks).reshape((-1,) + (1,) * (len(dims) - 1 - dim))
    return loudness


def profile(number_of, total, reach, slope):
    weights = [(1 << 20) // math.isqrt(rank ** slope) + 1 for rank in range(2, number_of + 1)]
    surplus, holding = total - reach - (number_of - 1), [1] * (number_of - 1)
    while surplus > 0:
        candidates = [i for i in range(number_of - 1) if holding[i] < reach]
        whole, remaining = sum([weights[i] for i in candidates]), surplus
        for i in candidates:
            more = min(reach - holding[i], max(1, remaining * weights[i] // whole), surplus)
            holding[i] = holding[i] + more
            surplus = surplus - more
    return np.array([reach] + holding)


def ragged_sizes(rng, count, total, reach, slope):
    if count == 2:
        one = jax.random.randint(rng, (), max(1, total - reach), min(reach, total - 1) + 1)
        return jnp.stack([one, total - one])
    tallies = jnp.asarray(profile(count, total, reach, slope), jnp.int32)
    twos = (count - 1) // 2
    giver, receiver = tallies[1:1 + 2 * twos:2], tallies[2:2 + 2 * twos:2]
    room = jnp.minimum(giver - 1, reach - receiver)
    moved = jax.random.randint(jax.random.fold_in(rng, 1), (twos,), 0, 1 << 20) % (room + 1)
    tallies = tallies.at[1:1 + 2 * twos:2].set(giver - moved).at[2:2 + 2 * twos:2].set(receiver + moved)
    return tallies[jax.random.permutation(jax.random.fold_in(rng, 2), count)]


def centred(own_key, dims, width, bound, shards=(), kind=jnp.bfloat16):
    values = jax.random.normal(own_key, dims, jnp.float32) * width
    if len(shards) > 0:
        values = steps_of(own_key, dims, shards, -0.22, 0.18) * values
    return jnp.clip(values, min=-bound, max=bound).astype(kind)


def setup_inputs(seed: int = 0) -> dict:
    key_list = jax.random.split(jax.random.key(seed), 13)
    return {
        "tokens": centred(key_list[0], (2, ROWS, SEQ, D), 1.0, 6.0, ((0, 2), (1, 8), (2, 2))),
        "segments": jax.vmap(lambda own: jnp.searchsorted(jnp.cumsum(ragged_sizes(own, DOCS_ROW, SEQ, DOC_MOST, 1)), jnp.arange(SEQ), side="right"))(jax.random.split(key_list[1], ROWS)).reshape((ROWS, SEQ)).astype(jnp.int32),
        "top_mask": set_ends((jax.random.randint(key_list[2], (ROWS, QPR, ROWS, SEQ), 0, 4) < 1).astype(jnp.int32), jax.random.fold_in(key_list[2], 1), 0, 1),
        "positive": set_ends(jax.random.randint(key_list[3], (ROWS, QPR), 0, NDOCS), jax.random.fold_in(key_list[3], 1), 0, NDOCS - 1).astype(jnp.int32),
        "w_query": centred(key_list[4], (LAYERS, D, INNER), (D * DH) ** -0.5, 0.02734375, ((2, 2),)),
        "w_kv": centred(key_list[5], (LAYERS, 2, D, INNER), D ** -0.5, 0.21875, ((3, 2),)),
        "w_out": centred(key_list[6], (LAYERS, D, INNER), (INNER * DOCS_ROW // SEQ) ** -0.5, 1.75, ((2, 2),)),
        "w_in": centred(key_list[7], (LAYERS, 2, D, FF), D ** -0.5, 0.21875, ((3, 2),)),
        "w_down": centred(key_list[8], (LAYERS, D, FF), (FF // 2) ** -0.5, 0.15625, ((2, 2),)),
        "gains": jnp.clip(1.0 + 0.1 * jax.random.normal(key_list[9], (2 * LAYERS + 1, D), jnp.float32), 0.5, 1.5),
        "rel_bias": centred(key_list[10], (BUCKETS, H), 1.0, 4.0, ((1, 2),), jnp.float32),
        "w_proj": centred(key_list[11], (D, P_SIZE), D ** -0.5, 0.21875),
    }


norm_eps = 1e-06
vector_eps = 1e-06
temper = 0.05
logit_scale = 32.0
bucket_edges = (12, 16, 23, 32, 46, 64, 91)
highest = lax.Precision.HIGHEST

@jax.custom_vjp
def low(v):
    return lax.optimization_barrier(v.astype(jnp.bfloat16)).astype(jnp.float32)

@jax.custom_vjp
def low_back(v):
    return v

def low_keep(v):
    return (low(v), None)

def low_pass(kept, grad):
    return (grad,)

def back_keep(v):
    return (v, None)

def back_low(kept, grad):
    return (low(grad),)
low.defvjp(low_keep, low_pass)
low_back.defvjp(back_keep, back_low)

def bucket_grid(length):
    offsets = jnp.arange(2 * length - 1, dtype=jnp.int32) - (length - 1)
    magnitude = jnp.abs(offsets)
    far_bucket = jnp.full(offsets.shape, 8, jnp.int32)
    for threshold in bucket_edges:
        far_bucket = far_bucket + (magnitude >= threshold).astype(jnp.int32)
    bucket = jnp.where(magnitude < 8, magnitude, jnp.minimum(far_bucket, 15))
    bucket = bucket + jnp.where(offsets > 0, 16, 0).astype(jnp.int32)
    places = jnp.arange(length, dtype=jnp.int32)
    return bucket[places[None, :] - places[:, None] + (length - 1)]

def rms_scale(values, gain_row):
    return values * lax.rsqrt(lax.optimization_barrier(jnp.mean(values * values, axis=-1, keepdims=True)) + norm_eps) * gain_row

def encode_and_score(tokens, w_query, w_kv, w_out, w_in, w_down, gains, rel_bias, w_proj, segments, top_mask, positive):
    streams, row_count, length, model_width = tokens.shape
    head_count = rel_bias.shape[1]
    head_size = w_query.shape[2] // head_count
    layers = w_query.shape[0]
    all_rows = streams * row_count
    query_segments = jnp.broadcast_to(jnp.arange(length, dtype=jnp.int32) // QLEN, (row_count, length))
    all_segments = jnp.concatenate([query_segments, segments.astype(jnp.int32)], axis=0)
    same_doc = all_segments[:, :, None] == all_segments[:, None, :]
    bias_grid = jnp.transpose(jnp.take(rel_bias, bucket_grid(length), axis=0), (2, 0, 1))
    hidden_state = tokens.reshape(all_rows, length, model_width)

    def attend_row(inputs):
        queries, keys_row, values_row, same_row = inputs
        scores = low_back(jnp.einsum('she,the->hst', queries, keys_row, precision=highest) + bias_grid)
        scores = jnp.where(same_row[None], scores, -1000000000.0)
        weights_row = low(jax.nn.softmax(scores, axis=-1))
        return jnp.einsum('hst,the->she', weights_row, values_row, precision=highest)
    head_shape = (all_rows, length, head_count, head_size)
    for layer_index in range(layers):
        normed = low(rms_scale(hidden_state, gains[2 * layer_index]))
        queries = low_back(low(jnp.einsum('nsd,di->nsi', normed, w_query[layer_index], precision=highest)))
        key_value = low_back(low(jnp.einsum('nsd,tdi->tnsi', normed, w_kv[layer_index], precision=highest)))
        attended = lax.map(jax.checkpoint(attend_row), (queries.reshape(head_shape), key_value[0].reshape(head_shape), key_value[1].reshape(head_shape), same_doc))
        attended = low_back(low(attended.reshape(all_rows, length, head_count * head_size)))
        hidden_state = hidden_state + low_back(jnp.einsum('nsi,di->nsd', attended, w_out[layer_index], precision=highest))
        normed_ffn = low(rms_scale(hidden_state, gains[2 * layer_index + 1]))
        gate_up = low_back(jnp.einsum('nsd,tdf->tnsf', normed_ffn, w_in[layer_index], precision=highest))
        activated = low(jax.nn.gelu(gate_up[0], approximate=True) * gate_up[1])
        hidden_state = hidden_state + low_back(jnp.einsum('nsf,df->nsd', activated, w_down[layer_index], precision=highest))
    final_in = low(rms_scale(hidden_state, gains[2 * layers]))
    projected = low_back(jnp.einsum('nsd,dp->nsp', final_in, w_proj, precision=highest))
    vectors = low_back(low(projected * lax.rsqrt(lax.optimization_barrier(jnp.sum(projected * projected, axis=-1, keepdims=True)) + vector_eps)))
    vectors = vectors.reshape(streams, row_count, length, -1)
    query_vectors = vectors[0].reshape(row_count, length // QLEN, QLEN, -1)
    doc_vectors = vectors[1].reshape(row_count * length, -1)
    doc_count = row_count * DOCS_ROW
    doc_ids = (segments.astype(jnp.int32) + DOCS_ROW * jnp.arange(row_count, dtype=jnp.int32)[:, None]).reshape(-1)
    doc_onehot = (doc_ids[:, None] == jnp.arange(doc_count, dtype=jnp.int32)[None, :]).astype(jnp.float32)
    mask_rows = top_mask.astype(jnp.float32).reshape(row_count, length // QLEN, row_count * length)

    def score_row(inputs):
        query_block, mask_row = inputs
        similarity = low_back(jnp.einsum('qlp,tp->qlt', query_block, doc_vectors, precision=highest))
        raised = jnp.exp(similarity / temper) * mask_row[:, None, :]
        totals = jnp.einsum('qlt,tn->qln', raised, doc_onehot, precision=highest)
        return logit_scale * lax.optimization_barrier(jnp.mean(temper * jnp.log1p(totals), axis=1))
    logits = lax.map(jax.checkpoint(score_row), (query_vectors, mask_rows))
    is_positive = (jnp.arange(doc_count, dtype=jnp.int32)[None, None, :] == positive.astype(jnp.int32)[:, :, None]).astype(jnp.float32)
    chosen = lax.optimization_barrier(jnp.sum(logits * is_positive, axis=-1))
    losses = jax.nn.logsumexp(logits, axis=-1) - chosen
    return (jnp.sum(losses), (vectors, losses))

def reference(tokens, segments, top_mask, positive, w_query, w_kv, w_out, w_in, w_down, gains, rel_bias, w_proj):
    floats = (tokens.astype(jnp.float32), w_query.astype(jnp.float32), w_kv.astype(jnp.float32), w_out.astype(jnp.float32), w_in.astype(jnp.float32), w_down.astype(jnp.float32), gains.astype(jnp.float32), rel_bias.astype(jnp.float32), w_proj.astype(jnp.float32))

    def objective(tokens_f, query_f, kv_f, out_f, in_f, down_f, gains_f, bias_f, proj_f):
        return encode_and_score(tokens_f, query_f, kv_f, out_f, in_f, down_f, gains_f, bias_f, proj_f, segments, top_mask, positive)
    loss_total, pull_back, outputs = jax.vjp(objective, *floats, has_aux=True)
    gradients = pull_back(jnp.ones_like(loss_total))
    vectors, losses = outputs
    return (vectors.astype(jnp.bfloat16), losses, gradients[0], gradients[1], gradients[2], gradients[3], gradients[4], gradients[5], gradients[6], gradients[7], gradients[8])
```

```python
import functools
import math

import jax
import jax.numpy as jnp
from jax import lax
from jax.experimental import pallas as pl
from jax.experimental.pallas import tpu as pltpu
from jax.sharding import PartitionSpec as P

QLEN = 32
DOCS_ROW = 8
TILE = 128
SPAN = 512


norm_eps = 1e-06
vector_eps = 1e-06
temper = 0.05
logit_scale = 32.0
bucket_edges = (12, 16, 23, 32, 46, 64, 91)
highest = lax.Precision.HIGHEST
bf16 = jnp.bfloat16
f32 = jnp.float32


def dot(a, b):
    return lax.dot_general(a, b, (((1,), (0,)), ((), ())), preferred_element_type=f32)


def dot_nt(a, b):
    return lax.dot_general(a, b, (((1,), (1,)), ((), ())), preferred_element_type=f32)


def dot_tn(a, b):
    return lax.dot_general(a, b, (((0,), (0,)), ((), ())), preferred_element_type=f32)


def offset_buckets():
    index = jnp.arange(SPAN, dtype=jnp.int32)
    offsets = jnp.where(index < SPAN // 2, index, index - SPAN)
    magnitude = jnp.abs(offsets)
    far_bucket = jnp.full(offsets.shape, 8, jnp.int32)
    for threshold in bucket_edges:
        far_bucket = far_bucket + (magnitude >= threshold).astype(jnp.int32)
    bucket = jnp.where(magnitude < 8, magnitude, jnp.minimum(far_bucket, 15))
    return bucket + jnp.where(offsets > 0, 16, 0).astype(jnp.int32)


def window(tile, tiles):
    first, last = max(0, tile - 1), min(tiles, tile + 2)
    shift = first - (tile - 1)
    return pl.ds(first * TILE, (last - first) * TILE), slice(shift * TILE, (shift + last - first) * TILE)


def fill_masks(row_ids, col_ids, mask, tiles):
    for tile in range(tiles):
        rows = pl.ds(tile * TILE, TILE)
        own = col_ids[rows, :]
        for near in range(max(0, tile - 1), min(tiles, tile + 2)):
            other = jnp.broadcast_to(row_ids[0:1, near * TILE : (near + 1) * TILE], (TILE, TILE))
            place = (near - tile + 1) * TILE
            mask[rows, place : place + TILE] = jnp.where(own == other, 0.0, -1e30)


def bias_tile(table, head):
    line = jnp.broadcast_to(table[pl.ds(head, 1), :], (TILE, SPAN))
    return pltpu.roll(line, TILE, axis=1, stride=1, stride_axis=0)[:, : 3 * TILE]


def attend_kernel(table, row_ids, col_ids, q, k, v, o, lse, mask, bias):
    tiles = q.shape[0] // TILE
    fill_masks(row_ids, col_ids, mask, tiles)
    lane = lax.broadcasted_iota(jnp.int32, (TILE, TILE), 1)
    lse[...] = jnp.zeros(lse.shape, f32)

    def pair(p, carry):
        cols = pl.ds(pl.multiple_of(p * TILE, TILE), TILE)
        for half in range(2):
            bias[half] = bias_tile(table, 2 * p + half)
        for tile in range(tiles):
            rows = pl.ds(tile * TILE, TILE)
            keys, frame = window(tile, tiles)
            queries = q[rows, cols]
            near_keys, near_values = k[keys, cols], v[keys, cols]
            outs = []
            kept = lse[rows, :]
            for half in range(2):
                mine = (lane >= 64) if half else (lane < 64)
                s = dot_nt(jnp.where(mine, queries, jnp.zeros_like(queries)), near_keys)
                s = s + bias[half][:, frame] + mask[rows, frame]
                top = jnp.max(s, axis=-1, keepdims=True)
                e = jnp.exp(s - top)
                total = jnp.sum(e, axis=-1, keepdims=True)
                weights = (e * (1.0 / total)).astype(bf16)
                outs.append(dot(weights, near_values))
                kept = jnp.where(lane == 2 * p + half, top + jnp.log(total), kept)
            lse[rows, :] = kept
            o[rows, cols] = jnp.where(lane < 64, outs[0], outs[1]).astype(bf16)
        return carry

    lax.fori_loop(0, q.shape[1] // TILE, pair, 0)


def attend(table, row_ids, col_ids, q, k, v):
    length, width = q.shape
    return pl.pallas_call(
        attend_kernel,
        out_shape=(
            jax.ShapeDtypeStruct((length, width), bf16),
            jax.ShapeDtypeStruct((length, TILE), f32),
        ),
        scratch_shapes=[pltpu.VMEM((length, 3 * TILE), f32), pltpu.VMEM((2, TILE, 3 * TILE), f32)],
        compiler_params=pltpu.CompilerParams(vmem_limit_bytes=32 * 1024 * 1024),
        cost_estimate=pl.CostEstimate(flops=10**9, bytes_accessed=3 * 10**6, transcendentals=10**6),
        name="attend",
    )(table, row_ids, col_ids, q, k, v)


def attend_back_kernel(
    table, row_ids, col_ids, lse, q, k, v, do, dq, dk, dv, sums, mask, bias, grid, dk_sum, dv_sum
):
    tiles = q.shape[0] // TILE
    fill_masks(row_ids, col_ids, mask, tiles)
    lane = lax.broadcasted_iota(jnp.int32, (TILE, TILE), 1)
    row_index = lax.broadcasted_iota(jnp.int32, (TILE, SPAN), 0)
    sums[...] = jnp.zeros(sums.shape, f32)

    def pair(p, carry):
        cols = pl.ds(pl.multiple_of(p * TILE, TILE), TILE)
        for half in range(2):
            bias[half] = bias_tile(table, 2 * p + half)
        grid[...] = jnp.zeros(grid.shape, f32)
        dk_sum[...] = jnp.zeros(dk_sum.shape, f32)
        dv_sum[...] = jnp.zeros(dv_sum.shape, f32)
        for tile in range(tiles):
            rows = pl.ds(tile * TILE, TILE)
            keys, frame = window(tile, tiles)
            queries, grads = q[rows, cols], do[rows, cols]
            near_keys, near_values = k[keys, cols], v[keys, cols]
            kept = lse[rows, :]
            outs = []
            for half in range(2):
                mine = (lane >= 64) if half else (lane < 64)
                own_queries = jnp.where(mine, queries, jnp.zeros_like(queries))
                own_grads = jnp.where(mine, grads, jnp.zeros_like(grads))
                log_total = jnp.sum(
                    jnp.where(lane == 2 * p + half, kept, 0.0), axis=-1, keepdims=True
                )
                s = dot_nt(own_queries, near_keys)
                s = s + bias[half][:, frame] + mask[rows, frame]
                weights = jnp.exp(s - log_total)
                grad_weights = dot_nt(own_grads, near_values)
                mean = jnp.sum(weights * grad_weights, axis=-1, keepdims=True)
                ds = (weights * (grad_weights - mean)).astype(bf16)
                outs.append(dot(ds, near_keys))
                dk_sum[keys, :] += dot_tn(ds, own_queries)
                dv_sum[keys, :] += dot_tn(weights.astype(bf16), own_grads)
                grid[half, :, frame] += ds.astype(f32)
            dq[rows, cols] = jnp.where(lane < 64, outs[0], outs[1]).astype(bf16)
        dk[:, cols] = dk_sum[...].astype(bf16)
        dv[:, cols] = dv_sum[...].astype(bf16)
        for half in range(2):
            turned = pltpu.roll(grid[half], SPAN - TILE, axis=1)
            for bit in range(7):
                moved = pltpu.roll(turned, SPAN - (1 << bit), axis=1)
                turned = jnp.where((row_index >> bit) & 1 == 1, moved, turned)
            sums[pl.ds(2 * p + half, 1), :] = jnp.sum(turned, axis=0, keepdims=True)
        return carry

    lax.fori_loop(0, q.shape[1] // TILE, pair, 0)


def attend_back(table, row_ids, col_ids, lse, q, k, v, do):
    length, width = q.shape
    grad = jax.ShapeDtypeStruct((length, width), bf16)
    return pl.pallas_call(
        attend_back_kernel,
        out_shape=(grad, grad, grad, jax.ShapeDtypeStruct(table.shape, f32)),
        scratch_shapes=[
            pltpu.VMEM((length, 3 * TILE), f32),
            pltpu.VMEM((2, TILE, 3 * TILE), f32),
            pltpu.VMEM((2, TILE, SPAN), f32),
            pltpu.VMEM((length, TILE), f32),
            pltpu.VMEM((length, TILE), f32),
        ],
        compiler_params=pltpu.CompilerParams(vmem_limit_bytes=32 * 1024 * 1024),
        cost_estimate=pl.CostEstimate(flops=25 * 10**8, bytes_accessed=4 * 10**6, transcendentals=10**6),
        name="attend_back",
    )(table, row_ids, col_ids, lse, q, k, v, do)


def rms_scale(values, gain_row):
    return (
        values * lax.rsqrt(jnp.mean(values * values, axis=-1, keepdims=True) + norm_eps) * gain_row
    )


def gated_gelu(gate, up):
    return jax.nn.gelu(gate, approximate=True) * up


def normalize(values):
    return values * lax.rsqrt(jnp.sum(values * values, axis=-1, keepdims=True) + vector_eps)


def swap(value, axis):
    return lax.ppermute(value, axis, [(0, 1), (1, 0)])


def sum_of_two(part, axis):
    mine = lax.optimization_barrier(part.astype(bf16))
    return mine.astype(f32) + swap(mine, axis).astype(f32)


def layer_forward(inputs, table, row_ids, col_ids, weights_layer):
    query_weight, kv_weight, out_weight, in_weight, down_weight, gain_attn, gain_ffn = weights_layer
    normed = rms_scale(inputs, gain_attn).astype(bf16)
    q = dot(normed, query_weight).astype(bf16)
    k = dot(normed, kv_weight[0]).astype(bf16)
    v = dot(normed, kv_weight[1]).astype(bf16)
    attended, lse = attend(table, row_ids, col_ids, q, k, v)
    middle = inputs + sum_of_two(dot_nt(attended, out_weight), "mp")
    ffn_input = rms_scale(middle, gain_ffn).astype(bf16)
    gate, up = dot(ffn_input, in_weight[0]), dot(ffn_input, in_weight[1])
    hidden = gated_gelu(gate, up).astype(bf16)
    output = middle + sum_of_two(dot_nt(hidden, down_weight), "mp")
    return output, (inputs, normed, q, k, v, lse, attended, middle, ffn_input, gate, up, hidden)


def ffn_backward(grad_output, kept, weights_layer):
    middle, ffn_input, gate, up, hidden = kept[7:]
    in_weight, down_weight, gain_ffn = weights_layer[3], weights_layer[4], weights_layer[6]
    grad_branch = grad_output.astype(bf16)
    grad_hidden = dot(grad_branch, down_weight)
    grad_down = dot_tn(grad_branch, hidden).astype(bf16)
    grad_gate, grad_up = jax.vjp(gated_gelu, gate, up)[1](grad_hidden)
    grad_gate, grad_up = grad_gate.astype(bf16), grad_up.astype(bf16)
    grad_in = (dot_tn(ffn_input, grad_gate).astype(bf16), dot_tn(ffn_input, grad_up).astype(bf16))
    grad_input = sum_of_two(dot_nt(grad_gate, in_weight[0]) + dot_nt(grad_up, in_weight[1]), "mp")
    grad_mid_norm, grad_gain = jax.vjp(rms_scale, middle, gain_ffn)[1](grad_input)
    return grad_output + grad_mid_norm, grad_down, grad_in, grad_gain


def attention_backward(grad_middle, table, row_ids, col_ids, kept, weights_layer):
    inputs, normed, q, k, v, lse, attended = kept[:7]
    query_weight, kv_weight, out_weight, gain_attn = (
        weights_layer[0],
        weights_layer[1],
        weights_layer[2],
        weights_layer[5],
    )
    grad_attn = grad_middle.astype(bf16)
    do = dot(grad_attn, out_weight).astype(bf16)
    dq, dk, dv, sums = attend_back(table, row_ids, col_ids, lse, q, k, v, do)
    grads = [dot_tn(grad_attn, attended)] + [dot_tn(normed, part) for part in (dq, dk, dv)]
    grads = jnp.concatenate([part.astype(bf16) for part in grads], axis=1)
    grad_normed = sum_of_two(
        dot_nt(dq, query_weight) + dot_nt(dk, kv_weight[0]) + dot_nt(dv, kv_weight[1]), "mp"
    )
    grad_in_norm, grad_gain = jax.vjp(rms_scale, inputs, gain_attn)[1](grad_normed)
    return grad_middle + grad_in_norm, grads, grad_gain, sums


def pick(value, index, axis):
    return lax.dynamic_index_in_dim(value, index, axis, False)


def paired(sent, kept, axis, pairs):
    return (kept.astype(f32) + lax.ppermute(sent, axis, pairs).astype(f32)).astype(bf16)


def scatter_inner(part):
    inner = lax.axis_index("batch") % 2
    pairs = [(i, i ^ 1) for i in range(lax.axis_size("batch"))]
    return paired(pick(part, 1 - inner, 1), pick(part, inner, 1), "batch", pairs)


def scatter_outer(part):
    count = lax.axis_size("batch") // 2
    outer = lax.axis_index("batch") // 2
    total = pick(part, outer, 0).astype(f32)
    for step in range(1, count):
        pairs = [(i, ((i // 2 + step) % count) * 2 + i % 2) for i in range(2 * count)]
        total = total + lax.ppermute(pick(part, (outer + step) % count, 0), "batch", pairs).astype(f32)
    return lax.optimization_barrier(total.astype(bf16))


def reduce_rows(grad, streams_first):
    batch = lax.axis_size("batch")
    rows, columns = grad.shape[0] // batch, grad.shape[1]
    if batch % 2 or batch > 8:
        part = lax.psum_scatter(grad, "batch", scatter_dimension=0, tiled=True)
        return sum_of_two(part, "stream")
    if not streams_first:
        part = scatter_outer(scatter_inner(grad.reshape(batch // 2, 2, rows, columns)))
        return part.astype(f32) + swap(part, "stream").astype(f32)
    side = lax.axis_index("stream")
    half = columns // 2
    kept = lax.dynamic_slice_in_dim(grad, side * half, half, 1)
    sent = lax.dynamic_slice_in_dim(grad, (1 - side) * half, half, 1)
    part = paired(sent, kept, "stream", [(0, 1), (1, 0)])
    part = scatter_outer(scatter_inner(part.reshape(batch // 2, 2, rows, half)))
    other = swap(part, "stream")
    first = jnp.where(side == 0, part, other)
    last = jnp.where(side == 0, other, part)
    return jnp.concatenate([first, last], axis=1).astype(f32)


def on_device(
    tokens,
    segments,
    top_mask,
    positive,
    w_query,
    w_kv,
    w_out,
    w_in,
    w_down,
    gains,
    rel_bias,
    w_proj,
):
    stream_side = lax.axis_index("stream")
    batch_index = lax.axis_index("batch")
    mp_index = lax.axis_index("mp")
    row = lax.all_gather(tokens[0], "mp", axis=1, tiled=True)
    row_count, length, model_width = row.shape
    share_len = tokens.shape[2]
    hidden_state = row[0].astype(f32)
    head_count = rel_bias.shape[1]
    layers = w_query.shape[0]
    query_segments = jnp.arange(length, dtype=jnp.int32) // QLEN
    row_segments = jnp.where(stream_side == 0, query_segments, segments[0])
    row_ids = jnp.broadcast_to(row_segments[None, :], (8, length))
    col_ids = jnp.broadcast_to(row_segments[:, None], (length, TILE))
    offset_onehot = (
        offset_buckets()[None, :] == jnp.arange(rel_bias.shape[0], dtype=jnp.int32)[:, None]
    ).astype(f32)
    table = jnp.einsum(
        "bh,bk->hk", jnp.pad(rel_bias, ((0, 0), (0, 8 - head_count))), offset_onehot, precision=highest
    )
    layer_weights = []
    kept_layers = []
    for layer_index in range(layers):
        weights_layer = (
            w_query[layer_index],
            w_kv[layer_index],
            w_out[layer_index],
            w_in[layer_index],
            w_down[layer_index],
            gains[2 * layer_index],
            gains[2 * layer_index + 1],
        )
        layer_weights.append(weights_layer)
        hidden_state, kept_state = layer_forward(
            hidden_state, table, row_ids, col_ids, weights_layer
        )
        kept_layers.append(kept_state)
    final_in = rms_scale(hidden_state, gains[2 * layers]).astype(bf16)
    projected = dot(final_in, w_proj)
    unit_vectors, normalize_back = jax.vjp(normalize, projected)
    vectors = unit_vectors.astype(bf16)
    own_vectors = lax.dynamic_slice_in_dim(vectors, mp_index * share_len, share_len, 0)
    sent_half = lax.ppermute(own_vectors, "stream", [(0, 1)])
    gathered = lax.all_gather(sent_half, "batch", axis=0)
    query_rows = gathered.shape[0]
    per_half = share_len // QLEN
    block_rows = math.gcd(query_rows, 8)
    block_count = query_rows // block_rows
    block_slots = block_rows * per_half
    block_tokens = block_slots * QLEN
    doc_tokens = length
    query_blocks = gathered.reshape(block_count, block_tokens, -1)
    mask_cols = jnp.transpose(top_mask.reshape(query_rows * per_half, doc_tokens), (1, 0)).astype(
        f32
    )
    mask_blocks = jnp.transpose(mask_cols.reshape(doc_tokens, block_count, block_slots), (1, 0, 2))
    doc_flat = vectors
    local_docs = DOCS_ROW
    doc_ids = segments.reshape(-1)
    doc_onehot = (jnp.arange(local_docs, dtype=jnp.int32)[:, None] == doc_ids[None, :]).astype(f32)

    def pooled_sums(query_block, mask_block):
        similarity = dot_nt(doc_flat, query_block)
        mask_wide = jnp.broadcast_to(
            mask_block[:, :, None], (doc_tokens, block_slots, QLEN)
        ).reshape(doc_tokens, block_tokens)
        raised = jnp.exp(similarity / temper) * mask_wide
        totals = jnp.einsum("nt,tk->nk", doc_onehot, raised, precision=highest)
        return (raised, totals)

    def block_logits(inputs):
        raised, totals = pooled_sums(inputs[0], inputs[1])
        pooled = jnp.mean(
            (temper * jnp.log1p(totals)).reshape(local_docs, block_slots, QLEN), axis=-1
        )
        return logit_scale * pooled

    logit_blocks = lax.map(block_logits, (query_blocks, mask_blocks))
    logits = jnp.transpose(logit_blocks, (0, 2, 1)).reshape(query_rows, per_half, local_docs)
    global_docs = batch_index * local_docs + jnp.arange(local_docs, dtype=jnp.int32)
    is_positive = (global_docs[None, None, :] == positive[:, :, None]).astype(f32)
    doc_side = stream_side == 1
    stats = jnp.stack([jnp.sum(jnp.exp(logits), axis=-1), jnp.sum(logits * is_positive, axis=-1)])
    stats = lax.psum(jnp.where(doc_side, stats, 0.0), ("stream", "batch"))
    log_total = jnp.log(stats[0])
    losses = log_total - stats[1]
    query_loss = lax.dynamic_slice_in_dim(losses, batch_index * row_count, row_count, 0)
    grad_logits = jnp.exp(logits - log_total[..., None]) - is_positive
    grad_blocks = jnp.transpose(
        grad_logits.reshape(block_count, block_slots, local_docs), (0, 2, 1)
    )

    def block_back(doc_grad, inputs):
        query_block, mask_block, grad_block = inputs
        raised, totals = pooled_sums(query_block, mask_block)
        grad_wide = jnp.broadcast_to(
            grad_block[:, :, None], (local_docs, block_slots, QLEN)
        ).reshape(local_docs, block_tokens)
        factor = grad_wide * (logit_scale / QLEN) / (1.0 + totals)
        spread = jnp.einsum("nt,nk->tk", doc_onehot, factor, precision=highest)
        grad_sims = (raised * spread).astype(bf16)
        grad_block_query = dot_tn(grad_sims, doc_flat)
        doc_grad = doc_grad + dot(grad_sims, query_block)
        return (doc_grad, grad_block_query)

    doc_grad, grad_query_blocks = lax.scan(
        block_back, jnp.zeros(doc_flat.shape, f32), (query_blocks, mask_blocks, grad_blocks)
    )
    summed_query = lax.psum_scatter(
        grad_query_blocks.reshape(query_rows, share_len, -1).astype(bf16),
        "batch",
        scatter_dimension=0,
        tiled=False,
    )
    returned = lax.ppermute(summed_query, "stream", [(1, 0)])
    returned = lax.all_gather(returned, "mp", axis=0, tiled=True)
    grad_vectors = jnp.where(
        stream_side == 0, returned.astype(f32), sum_of_two(doc_grad, "mp").astype(bf16).astype(f32)
    )
    grad_projected = normalize_back(grad_vectors)[0].astype(bf16)
    grad_proj = dot_tn(final_in, grad_projected).astype(bf16)
    grad_final = dot_nt(grad_projected, w_proj)
    grad_state, grad_gain_final = jax.vjp(rms_scale, hidden_state, gains[2 * layers])[1](grad_final)
    gain_grads = [None] * (2 * layers)
    reduced = [None] * layers
    reduced_proj = None
    sums = jnp.zeros(table.shape, f32)
    for layer_index in reversed(range(layers)):
        kept, weights_layer = kept_layers[layer_index], layer_weights[layer_index]
        grad_state, grad_down, grad_in, gain_grads[2 * layer_index + 1] = ffn_backward(
            grad_state, kept, weights_layer
        )
        down = reduce_rows(grad_down, False)
        gate, up = reduce_rows(grad_in[0], True), reduce_rows(grad_in[1], True)
        grad_state, grads, gain_grads[2 * layer_index], part = attention_backward(
            grad_state, table, row_ids, col_ids, kept, weights_layer
        )
        sums = sums + part
        if reduced_proj is None:
            rest = reduce_rows(jnp.concatenate([grads, grad_proj], axis=1), False)
            reduced_proj = rest[:, grads.shape[1] :]
            rest = rest[:, : grads.shape[1]]
        else:
            rest = reduce_rows(grads, False)
        reduced[layer_index] = (down, jnp.stack([gate, up]), jnp.split(rest, 4, axis=1))
    grad_bias_local = jnp.einsum("hk,bk->bh", sums, offset_onehot, precision=highest)[:, :head_count]
    grad_gains = jnp.stack(gain_grads + [grad_gain_final])
    grad_bias, grad_gains = lax.psum((grad_bias_local, grad_gains), ("stream", "batch"))
    rows = model_width // lax.axis_size("batch")
    grad_state = lax.dynamic_slice_in_dim(grad_state, mp_index * share_len, share_len, 0)
    return (
        own_vectors[None, None],
        query_loss,
        grad_state[None, None],
        jnp.stack([member[2][1] for member in reduced]),
        jnp.stack([jnp.stack(member[2][2:]) for member in reduced]),
        jnp.stack([member[2][0] for member in reduced]),
        jnp.stack([member[1] for member in reduced]),
        jnp.stack([member[0] for member in reduced]),
        lax.dynamic_slice_in_dim(grad_gains, batch_index * rows, rows, 1),
        grad_bias,
        reduced_proj,
    )


def solution(mesh):
    placed = (
        P("stream", "batch", "mp", None),
        P("batch", None),
        P(None, "mp", "batch", None),
        P(None, "mp"),
        P(None, None, "mp"),
        P(None, None, None, "mp"),
        P(None, None, "mp"),
        P(None, None, None, "mp"),
        P(None, None, "mp"),
        P(),
        P(None, "mp"),
        P(),
    )
    return jax.shard_map(
        on_device,
        mesh=mesh,
        in_specs=placed,
        out_specs=(
            P("stream", "batch", "mp", None),
            P("batch", "mp"),
            P("stream", "batch", "mp", None),
            P(None, "batch", "mp"),
            P(None, None, "batch", "mp"),
            P(None, "batch", "mp"),
            P(None, None, "batch", "mp"),
            P(None, "batch", "mp"),
            P(None, "batch"),
            P(None, "mp"),
            P("batch", None),
        ),
        check_vma=False,
    )
```

```python
import functools

import jax
import jax.numpy as jnp
from jax import lax
from jax.experimental import pallas as pl
from jax.experimental.pallas import tpu as pltpu
from jax.sharding import PartitionSpec as P

QLEN = 32
DOCS_ROW = 8
TILE = 128
SPAN = 512


norm_eps = 1e-06
vector_eps = 1e-06
temper = 0.05
logit_scale = 32.0
bucket_edges = (12, 16, 23, 32, 46, 64, 91)
highest = lax.Precision.HIGHEST
bf16 = jnp.bfloat16
f32 = jnp.float32


def dot(a, b):
    return lax.dot_general(a, b, (((1,), (0,)), ((), ())), preferred_element_type=f32)


def dot_nt(a, b):
    return lax.dot_general(a, b, (((1,), (1,)), ((), ())), preferred_element_type=f32)


def dot_tn(a, b):
    return lax.dot_general(a, b, (((0,), (0,)), ((), ())), preferred_element_type=f32)


def offset_buckets():
    index = jnp.arange(SPAN, dtype=jnp.int32)
    offsets = jnp.where(index < SPAN // 2, index, index - SPAN)
    magnitude = jnp.abs(offsets)
    far_bucket = jnp.full(offsets.shape, 8, jnp.int32)
    for threshold in bucket_edges:
        far_bucket = far_bucket + (magnitude >= threshold).astype(jnp.int32)
    bucket = jnp.where(magnitude < 8, magnitude, jnp.minimum(far_bucket, 15))
    return bucket + jnp.where(offsets > 0, 16, 0).astype(jnp.int32)


def window(tile, tiles):
    first, last = max(0, tile - 1), min(tiles, tile + 2)
    shift = first - (tile - 1)
    return pl.ds(first * TILE, (last - first) * TILE), slice(shift * TILE, (shift + last - first) * TILE)


def fill_masks(row_ids, col_ids, mask, tiles):
    for tile in range(tiles):
        rows = pl.ds(tile * TILE, TILE)
        own = col_ids[rows, :]
        for near in range(max(0, tile - 1), min(tiles, tile + 2)):
            other = jnp.broadcast_to(row_ids[0:1, near * TILE : (near + 1) * TILE], (TILE, TILE))
            place = (near - tile + 1) * TILE
            mask[rows, place : place + TILE] = jnp.where(own == other, 0.0, -1e30)


def bias_tile(table, head):
    line = jnp.broadcast_to(table[pl.ds(head, 1), :], (TILE, SPAN))
    return pltpu.roll(line, TILE, axis=1, stride=1, stride_axis=0)[:, : 3 * TILE]


def attend_kernel(table, row_ids, col_ids, q, k, v, o, lse, mask, bias):
    tiles = q.shape[0] // TILE
    fill_masks(row_ids, col_ids, mask, tiles)
    lane = lax.broadcasted_iota(jnp.int32, (TILE, TILE), 1)
    lse[...] = jnp.zeros(lse.shape, f32)

    def pair(p, carry):
        cols = pl.ds(pl.multiple_of(p * TILE, TILE), TILE)
        for half in range(2):
            bias[half] = bias_tile(table, 2 * p + half)
        for tile in range(tiles):
            rows = pl.ds(tile * TILE, TILE)
            keys, frame = window(tile, tiles)
            queries = q[rows, cols]
            near_keys, near_values = k[keys, cols], v[keys, cols]
            outs = []
            kept = lse[rows, :]
            for half in range(2):
                mine = (lane >= 64) if half else (lane < 64)
                s = dot_nt(jnp.where(mine, queries, jnp.zeros_like(queries)), near_keys)
                s = s + bias[half][:, frame] + mask[rows, frame]
                top = jnp.max(s, axis=-1, keepdims=True)
                e = jnp.exp(s - top)
                total = jnp.sum(e, axis=-1, keepdims=True)
                weights = (e * (1.0 / total)).astype(bf16)
                outs.append(dot(weights, near_values))
                kept = jnp.where(lane == 2 * p + half, top + jnp.log(total), kept)
            lse[rows, :] = kept
            o[rows, cols] = jnp.where(lane < 64, outs[0], outs[1]).astype(bf16)
        return carry

    lax.fori_loop(0, q.shape[1] // TILE, pair, 0)


def attend(table, row_ids, col_ids, q, k, v):
    length, width = q.shape
    return pl.pallas_call(
        attend_kernel,
        out_shape=(
            jax.ShapeDtypeStruct((length, width), bf16),
            jax.ShapeDtypeStruct((length, TILE), f32),
        ),
        scratch_shapes=[pltpu.VMEM((length, 3 * TILE), f32), pltpu.VMEM((2, TILE, 3 * TILE), f32)],
        compiler_params=pltpu.CompilerParams(vmem_limit_bytes=32 * 1024 * 1024),
        cost_estimate=pl.CostEstimate(flops=10**9, bytes_accessed=3 * 10**6, transcendentals=10**6),
        name="attend",
    )(table, row_ids, col_ids, q, k, v)


def attend_back_kernel(
    table, row_ids, col_ids, lse, q, k, v, do, dq, dk, dv, sums, mask, bias, grid, dk_sum, dv_sum
):
    tiles = q.shape[0] // TILE
    fill_masks(row_ids, col_ids, mask, tiles)
    lane = lax.broadcasted_iota(jnp.int32, (TILE, TILE), 1)
    row_index = lax.broadcasted_iota(jnp.int32, (TILE, SPAN), 0)
    sums[...] = jnp.zeros(sums.shape, f32)

    def pair(p, carry):
        cols = pl.ds(pl.multiple_of(p * TILE, TILE), TILE)
        for half in range(2):
            bias[half] = bias_tile(table, 2 * p + half)
        grid[...] = jnp.zeros(grid.shape, f32)
        dk_sum[...] = jnp.zeros(dk_sum.shape, f32)
        dv_sum[...] = jnp.zeros(dv_sum.shape, f32)
        for tile in range(tiles):
            rows = pl.ds(tile * TILE, TILE)
            keys, frame = window(tile, tiles)
            queries, grads = q[rows, cols], do[rows, cols]
            near_keys, near_values = k[keys, cols], v[keys, cols]
            kept = lse[rows, :]
            outs = []
            for half in range(2):
                mine = (lane >= 64) if half else (lane < 64)
                own_queries = jnp.where(mine, queries, jnp.zeros_like(queries))
                own_grads = jnp.where(mine, grads, jnp.zeros_like(grads))
                log_total = jnp.sum(
                    jnp.where(lane == 2 * p + half, kept, 0.0), axis=-1, keepdims=True
                )
                s = dot_nt(own_queries, near_keys)
                s = s + bias[half][:, frame] + mask[rows, frame]
                weights = jnp.exp(s - log_total)
                grad_weights = dot_nt(own_grads, near_values)
                mean = jnp.sum(weights * grad_weights, axis=-1, keepdims=True)
                ds = (weights * (grad_weights - mean)).astype(bf16)
                outs.append(dot(ds, near_keys))
                dk_sum[keys, :] += dot_tn(ds, own_queries)
                dv_sum[keys, :] += dot_tn(weights.astype(bf16), own_grads)
                grid[half, :, frame] += ds.astype(f32)
            dq[rows, cols] = jnp.where(lane < 64, outs[0], outs[1]).astype(bf16)
        dk[:, cols] = dk_sum[...].astype(bf16)
        dv[:, cols] = dv_sum[...].astype(bf16)
        for half in range(2):
            turned = pltpu.roll(grid[half], SPAN - TILE, axis=1)
            for bit in range(7):
                moved = pltpu.roll(turned, SPAN - (1 << bit), axis=1)
                turned = jnp.where((row_index >> bit) & 1 == 1, moved, turned)
            sums[pl.ds(2 * p + half, 1), :] = jnp.sum(turned, axis=0, keepdims=True)
        return carry

    lax.fori_loop(0, q.shape[1] // TILE, pair, 0)


def attend_back(table, row_ids, col_ids, lse, q, k, v, do):
    length, width = q.shape
    grad = jax.ShapeDtypeStruct((length, width), bf16)
    return pl.pallas_call(
        attend_back_kernel,
        out_shape=(grad, grad, grad, jax.ShapeDtypeStruct(table.shape, f32)),
        scratch_shapes=[
            pltpu.VMEM((length, 3 * TILE), f32),
            pltpu.VMEM((2, TILE, 3 * TILE), f32),
            pltpu.VMEM((2, TILE, SPAN), f32),
            pltpu.VMEM((length, TILE), f32),
            pltpu.VMEM((length, TILE), f32),
        ],
        compiler_params=pltpu.CompilerParams(vmem_limit_bytes=32 * 1024 * 1024),
        cost_estimate=pl.CostEstimate(flops=25 * 10**8, bytes_accessed=4 * 10**6, transcendentals=10**6),
        name="attend_back",
    )(table, row_ids, col_ids, lse, q, k, v, do)


def rms_scale(values, gain_row):
    return (
        values * lax.rsqrt(jnp.mean(values * values, axis=-1, keepdims=True) + norm_eps) * gain_row
    )


def gated_gelu(gate, up):
    return jax.nn.gelu(gate, approximate=True) * up


def normalize(values):
    return values * lax.rsqrt(jnp.sum(values * values, axis=-1, keepdims=True) + vector_eps)


def swap(value, axis):
    return lax.ppermute(value, axis, [(0, 1), (1, 0)])


def sum_of_two(part, axis):
    mine = lax.optimization_barrier(part.astype(bf16))
    return mine.astype(f32) + swap(mine, axis).astype(f32)


def layer_forward(inputs, table, row_ids, col_ids, weights_layer):
    query_weight, kv_weight, out_weight, in_weight, down_weight, gain_attn, gain_ffn = weights_layer
    normed = rms_scale(inputs, gain_attn).astype(bf16)
    q = dot(normed, query_weight).astype(bf16)
    k = dot(normed, kv_weight[0]).astype(bf16)
    v = dot(normed, kv_weight[1]).astype(bf16)
    attended, lse = attend(table, row_ids, col_ids, q, k, v)
    middle = inputs + sum_of_two(dot_nt(attended, out_weight), "mp")
    ffn_input = rms_scale(middle, gain_ffn).astype(bf16)
    gate, up = dot(ffn_input, in_weight[0]), dot(ffn_input, in_weight[1])
    hidden = gated_gelu(gate, up).astype(bf16)
    output = middle + sum_of_two(dot_nt(hidden, down_weight), "mp")
    return output, (inputs, normed, q, k, v, lse, attended, middle, ffn_input, gate, up, hidden)


def ffn_backward(grad_output, kept, weights_layer):
    middle, ffn_input, gate, up, hidden = kept[7:]
    in_weight, down_weight, gain_ffn = weights_layer[3], weights_layer[4], weights_layer[6]
    grad_branch = grad_output.astype(bf16)
    grad_hidden = dot(grad_branch, down_weight)
    grad_down = dot_tn(grad_branch, hidden).astype(bf16)
    grad_gate, grad_up = jax.vjp(gated_gelu, gate, up)[1](grad_hidden)
    grad_gate, grad_up = grad_gate.astype(bf16), grad_up.astype(bf16)
    grad_in = (dot_tn(ffn_input, grad_gate).astype(bf16), dot_tn(ffn_input, grad_up).astype(bf16))
    grad_input = sum_of_two(dot_nt(grad_gate, in_weight[0]) + dot_nt(grad_up, in_weight[1]), "mp")
    grad_mid_norm, grad_gain = jax.vjp(rms_scale, middle, gain_ffn)[1](grad_input)
    return grad_output + grad_mid_norm, grad_down, grad_in, grad_gain


def attention_backward(grad_middle, table, row_ids, col_ids, kept, weights_layer):
    inputs, normed, q, k, v, lse, attended = kept[:7]
    query_weight, kv_weight, out_weight, gain_attn = (
        weights_layer[0],
        weights_layer[1],
        weights_layer[2],
        weights_layer[5],
    )
    grad_attn = grad_middle.astype(bf16)
    do = dot(grad_attn, out_weight).astype(bf16)
    dq, dk, dv, sums = attend_back(table, row_ids, col_ids, lse, q, k, v, do)
    grads = [dot_tn(grad_attn, attended)] + [dot_tn(normed, part) for part in (dq, dk, dv)]
    grads = jnp.concatenate([part.astype(bf16) for part in grads], axis=1)
    grad_normed = sum_of_two(
        dot_nt(dq, query_weight) + dot_nt(dk, kv_weight[0]) + dot_nt(dv, kv_weight[1]), "mp"
    )
    grad_in_norm, grad_gain = jax.vjp(rms_scale, inputs, gain_attn)[1](grad_normed)
    return grad_middle + grad_in_norm, grads, grad_gain, sums


def pick(value, index, axis):
    return lax.dynamic_index_in_dim(value, index, axis, False)


def paired(sent, kept, axis, pairs):
    return (kept.astype(f32) + lax.ppermute(sent, axis, pairs).astype(f32)).astype(bf16)


def scatter_inner(part):
    inner = lax.axis_index("batch") % 2
    pairs = [(i, i ^ 1) for i in range(lax.axis_size("batch"))]
    return paired(pick(part, 1 - inner, 1), pick(part, inner, 1), "batch", pairs)


def scatter_outer(part):
    count = lax.axis_size("batch") // 2
    outer = lax.axis_index("batch") // 2
    total = pick(part, outer, 0).astype(f32)
    for step in range(1, count):
        pairs = [(i, ((i // 2 + step) % count) * 2 + i % 2) for i in range(2 * count)]
        total = total + lax.ppermute(pick(part, (outer + step) % count, 0), "batch", pairs).astype(f32)
    return lax.optimization_barrier(total.astype(bf16))


def reduce_rows(grad, streams_first):
    batch = lax.axis_size("batch")
    rows, columns = grad.shape[0] // batch, grad.shape[1]
    if batch % 2 or batch > 8:
        part = lax.psum_scatter(grad, "batch", scatter_dimension=0, tiled=True)
        return sum_of_two(part, "stream")
    if not streams_first:
        part = scatter_outer(scatter_inner(grad.reshape(batch // 2, 2, rows, columns)))
        return part.astype(f32) + swap(part, "stream").astype(f32)
    side = lax.axis_index("stream")
    half = columns // 2
    kept = lax.dynamic_slice_in_dim(grad, side * half, half, 1)
    sent = lax.dynamic_slice_in_dim(grad, (1 - side) * half, half, 1)
    part = paired(sent, kept, "stream", [(0, 1), (1, 0)])
    part = scatter_outer(scatter_inner(part.reshape(batch // 2, 2, rows, half)))
    other = swap(part, "stream")
    first = jnp.where(side == 0, part, other)
    last = jnp.where(side == 0, other, part)
    return jnp.concatenate([first, last], axis=1).astype(f32)


def mesh_id(stream, batch):
    return {"stream": stream, "batch": batch}


def send(source, target, send_sem, recv_sem, device):
    copy = pltpu.make_async_remote_copy(
        src_ref=source,
        dst_ref=target,
        send_sem=send_sem,
        recv_sem=recv_sem,
        device_id=device,
        device_id_type=pl.DeviceIdType.MESH,
    )
    copy.start()


def await_send(source, send_sem):
    pltpu.make_async_copy(source, source, send_sem).wait()


def split_dot(contract, left, right):
    high = left.astype(bf16)
    low = (left - high.astype(f32)).astype(bf16)
    return contract(high, right) + contract(low, right)


def score_kernel(
    count,
    vectors,
    doc_row,
    top_mask,
    positive,
    grad,
    loss,
    queries,
    docs,
    raised,
    totals,
    logits,
    stats,
    own_loss,
    other_loss,
    sent_grads,
    got_grads,
    doc_sum,
    sent_docs,
    got_docs,
    core_sent,
    core_got,
    query_send,
    query_recv,
    doc_send,
    doc_recv,
    stat_send,
    stat_recv,
    loss_sems,
    grad_send,
    grad_recv,
    back_sems,
    core_sems,
):
    side, batch, half = lax.axis_index("stream"), lax.axis_index("batch"), lax.axis_index("mp")
    length, width = vectors.shape
    quarter = length // 4
    slots = quarter // QLEN
    core = {"mp": 1 - half}
    other = {"stream": 1 - side}
    mine = side * count + batch

    barrier = pltpu.get_barrier_semaphore()

    def greet(step, carry):
        peer = lax.rem(mine + step, 2 * count)
        pl.semaphore_signal(
            barrier,
            inc=1,
            device_id=mesh_id(peer // count, lax.rem(peer, count)),
            device_id_type=pl.DeviceIdType.MESH,
        )
        return carry

    lax.fori_loop(1, 2 * count, greet, 0)
    pl.semaphore_signal(barrier, inc=1, device_id=core, device_id_type=pl.DeviceIdType.MESH)
    pl.semaphore_wait(barrier, 2 * count)

    def query_part(plane):
        return vectors.at[pl.ds(pl.multiple_of(half * (length // 2), QLEN) + plane * quarter, quarter), :]

    @pl.when(side == 0)
    def _():
        def push(step, carry):
            peer = lax.rem(batch + step, count)
            send(query_part(1), queries.at[batch], query_send.at[1, peer], query_recv.at[batch], mesh_id(1, peer))

            @pl.when(step > 0)
            def _():
                send(query_part(0), queries.at[batch], query_send.at[0, peer], query_recv.at[batch], mesh_id(0, peer))

            return carry

        lax.fori_loop(0, count, push, 0)
        queries[batch] = vectors[pl.ds(pl.multiple_of(half * (length // 2), QLEN), quarter), :]

    @pl.when(side == 1)
    def _():
        send(vectors, docs, doc_send, doc_recv, mesh_id(0, batch))
        docs[...] = vectors[...]

    lane = lax.broadcasted_iota(jnp.int32, (width, length), 0)
    onehot = jnp.where(lane == jnp.broadcast_to(doc_row[0:1, :], (width, length)), 1.0, 0.0).astype(bf16)

    @pl.when(side == 0)
    def _():
        pltpu.make_async_copy(docs, docs, doc_recv).wait()

    def await_queries(source):
        @pl.when(jnp.logical_or(side == 1, source != batch))
        def _():
            pltpu.make_async_copy(queries.at[source], queries.at[source], query_recv.at[source]).wait()

    def forward(step, carry):
        source = lax.rem(batch + step, count)
        await_queries(source)
        sims = dot_nt(queries[source], docs[...]) * (1.0 / temper)
        for slot in range(slots):
            chosen = top_mask[pl.ds(source * 2 * slots + side * slots + slot, 1), :].astype(f32)
            part = jnp.exp(sims[slot * QLEN : (slot + 1) * QLEN]) * chosen
            raised[source, slot * QLEN : (slot + 1) * QLEN, :] = part
        summed = split_dot(dot_nt, raised[source], onehot)
        totals[source] = summed
        pooled = jnp.log1p(summed) * (logit_scale * temper / QLEN)
        for slot in range(slots):
            logits[pl.ds(source * slots + slot, 1), :] = jnp.sum(
                pooled[slot * QLEN : (slot + 1) * QLEN], axis=0, keepdims=True
            )
        return carry

    lax.fori_loop(0, count, forward, 0)

    doc = lax.broadcasted_iota(jnp.int32, logits.shape, 1)
    local = doc < DOCS_ROW
    scores = logits[...]
    is_positive = jnp.where(
        jnp.logical_and(local, positive[...] == doc + batch * DOCS_ROW), 1.0, 0.0
    )
    exps = jnp.sum(jnp.where(local, jnp.exp(scores), 0.0), axis=1, keepdims=True)
    hits = jnp.sum(is_positive * scores, axis=1, keepdims=True)
    stats[batch] = jnp.where(doc == 0, exps, jnp.where(doc == 1, hits, 0.0))

    def push_stats(step, carry):
        peer = lax.rem(batch + step, count)
        send(stats.at[batch], stats.at[batch], stat_send.at[peer], stat_recv.at[batch], mesh_id(side, peer))
        return carry

    lax.fori_loop(1, count, push_stats, 0)

    def take_stats(step, carry):
        peer = lax.rem(batch + step, count)
        pltpu.make_async_copy(stats.at[peer], stats.at[peer], stat_recv.at[peer]).wait()
        return carry

    lax.fori_loop(1, count, take_stats, 0)
    summed = lax.fori_loop(1, count, lambda source, total: total + stats[source], stats[0])
    log_total = jnp.log(jnp.sum(jnp.where(doc == 0, summed, 0.0), axis=1, keepdims=True))
    hit_total = jnp.sum(jnp.where(doc == 1, summed, 0.0), axis=1, keepdims=True)
    losses = jnp.broadcast_to(log_total - hit_total, logits.shape)
    sent_grad = jnp.where(local, jnp.exp(scores - log_total), 0.0) - is_positive
    logits[...] = losses
    for slot in range(slots):
        own_loss[pl.ds(slot, 1), :] = logits[pl.ds(batch * slots + slot, 1), :]
    send(own_loss, other_loss, loss_sems.at[0], loss_sems.at[1], other)
    logits[...] = sent_grad
    doc_sum[...] = jnp.zeros(doc_sum.shape, f32)

    def backward(step, carry):
        source = lax.rem(batch + step + 1, count)
        parts = []
        for slot in range(slots):
            line = logits[pl.ds(source * slots + slot, 1), :] * (logit_scale / QLEN)
            parts.append(line / (1.0 + totals[source, slot * QLEN : (slot + 1) * QLEN, :]))
        spread = split_dot(dot, jnp.concatenate(parts, axis=0), onehot)
        ds = (raised[source] * spread).astype(bf16)
        back = dot(ds, docs[...]).astype(bf16)
        doc_sum[...] += dot_tn(ds, queries[source])

        @pl.when(jnp.logical_or(side == 1, source != batch))
        def _():
            sent_grads[source] = back
            send(
                sent_grads.at[source],
                got_grads.at[side, batch],
                grad_send.at[source],
                grad_recv.at[side, batch],
                mesh_id(0, source),
            )

        @pl.when(jnp.logical_and(side == 0, source == batch))
        def _():
            got_grads[0, batch] = back

        return carry

    lax.fori_loop(0, count, backward, 0)

    @pl.when(side == 0)
    def _():
        sent_docs[...] = doc_sum[...].astype(bf16)
        send(sent_docs, got_docs, back_sems.at[0], back_sems.at[1], mesh_id(1, batch))

        def take(step, carry):
            peer = lax.rem(batch + step, count)

            @pl.when(step > 0)
            def _():
                pltpu.make_async_copy(got_grads.at[0, peer], got_grads.at[0, peer], grad_recv.at[0, peer]).wait()

            pltpu.make_async_copy(got_grads.at[1, peer], got_grads.at[1, peer], grad_recv.at[1, peer]).wait()
            return carry

        lax.fori_loop(0, count, take, 0)
        for plane in range(2):
            total = lax.fori_loop(
                1,
                count,
                lambda source, total, plane=plane: total + got_grads[plane, source].astype(f32),
                got_grads[plane, 0].astype(f32),
            )
            core_sent[plane * quarter : (plane + 1) * quarter, :] = total.astype(bf16)
        part = core_sent.at[pl.ds(0, length // 2), :]
        there = core_got.at[pl.ds(0, length // 2), :]
        send(part, there, core_sems.at[0], core_sems.at[1], core)
        pltpu.make_async_copy(there, there, core_sems.at[1]).wait()
        first = pl.multiple_of(half * (length // 2), QLEN)
        grad[pl.ds(first, length // 2), :] = core_sent[pl.ds(0, length // 2), :].astype(f32)
        grad[pl.ds(length // 2 - first, length // 2), :] = core_got[pl.ds(0, length // 2), :].astype(f32)
        await_send(part, core_sems.at[0])
        await_send(sent_docs, back_sems.at[0])

    @pl.when(side == 1)
    def _():
        pltpu.make_async_copy(got_docs, got_docs, back_sems.at[1]).wait()
        core_sent[...] = (doc_sum[...] + got_docs[...].astype(f32)).astype(bf16)
        send(core_sent, core_got, core_sems.at[0], core_sems.at[1], core)
        pltpu.make_async_copy(core_got, core_got, core_sems.at[1]).wait()
        grad[...] = (core_sent[...].astype(f32) + core_got[...].astype(f32)).astype(bf16).astype(f32)
        await_send(core_sent, core_sems.at[0])
        await_send(vectors, doc_send)

    pltpu.make_async_copy(other_loss, other_loss, loss_sems.at[1]).wait()
    lower = jnp.where(side == 0, own_loss[0:slots, :], other_loss[0:slots, :])
    upper = jnp.where(side == 0, other_loss[0:slots, :], own_loss[0:slots, :])
    loss[...] = jnp.concatenate([lower, upper], axis=0)
    await_send(own_loss, loss_sems.at[0])

    def settle(step, carry):
        peer = lax.rem(batch + step, count)

        @pl.when(step > 0)
        def _():
            await_send(stats.at[batch], stat_send.at[peer])

        @pl.when(jnp.logical_or(side == 1, step > 0))
        def _():
            await_send(sent_grads.at[peer], grad_send.at[peer])

        @pl.when(side == 0)
        def _():
            await_send(query_part(1), query_send.at[1, peer])

            @pl.when(step > 0)
            def _():
                await_send(query_part(0), query_send.at[0, peer])

        return carry

    lax.fori_loop(0, count, settle, 0)


def score(vectors, doc_row, top_mask, positive):
    count = lax.axis_size("batch")
    length, width = vectors.shape
    quarter = length // 4
    slots = quarter // QLEN
    dma = pltpu.SemaphoreType.DMA
    return pl.pallas_call(
        functools.partial(score_kernel, count),
        out_shape=(
            jax.ShapeDtypeStruct((length, width), f32),
            jax.ShapeDtypeStruct((2 * slots, width), f32),
        ),
        in_specs=[pl.BlockSpec(memory_space=pltpu.VMEM)] * 4,
        out_specs=(pl.BlockSpec(memory_space=pltpu.VMEM),) * 2,
        scratch_shapes=[
            pltpu.VMEM((count, quarter, width), bf16),
            pltpu.VMEM((length, width), bf16),
            pltpu.VMEM((count, quarter, length), f32),
            pltpu.VMEM((count, quarter, width), f32),
            pltpu.VMEM((count * slots, width), f32),
            pltpu.VMEM((count, count * slots, width), f32),
            pltpu.VMEM((8, width), f32),
            pltpu.VMEM((8, width), f32),
            pltpu.VMEM((count, quarter, width), bf16),
            pltpu.VMEM((2, count, quarter, width), bf16),
            pltpu.VMEM((length, width), f32),
            pltpu.VMEM((length, width), bf16),
            pltpu.VMEM((length, width), bf16),
            pltpu.VMEM((length, width), bf16),
            pltpu.VMEM((length, width), bf16),
            dma((2, count)),
            dma((count,)),
            dma,
            dma,
            dma((count,)),
            dma((count,)),
            dma((2,)),
            dma((count,)),
            dma((2, count)),
            dma((2,)),
            dma((2,)),
        ],
        compiler_params=pltpu.CompilerParams(
            collective_id=0, has_side_effects=True, vmem_limit_bytes=56 * 1024 * 1024
        ),
        cost_estimate=pl.CostEstimate(flops=10**9, bytes_accessed=2 * 10**6, transcendentals=10**6),
        name="score",
    )(vectors, doc_row, top_mask, positive)


def on_device(
    tokens,
    segments,
    top_mask,
    positive,
    w_query,
    w_kv,
    w_out,
    w_in,
    w_down,
    gains,
    rel_bias,
    w_proj,
):
    stream_side = lax.axis_index("stream")
    batch_index = lax.axis_index("batch")
    mp_index = lax.axis_index("mp")
    row = lax.all_gather(tokens[0], "mp", axis=1, tiled=True)
    row_count, length, model_width = row.shape
    share_len = tokens.shape[2]
    hidden_state = row[0].astype(f32)
    head_count = rel_bias.shape[1]
    layers = w_query.shape[0]
    query_segments = jnp.arange(length, dtype=jnp.int32) // QLEN
    row_segments = jnp.where(stream_side == 0, query_segments, segments[0])
    row_ids = jnp.broadcast_to(row_segments[None, :], (8, length))
    col_ids = jnp.broadcast_to(row_segments[:, None], (length, TILE))
    offset_onehot = (
        offset_buckets()[None, :] == jnp.arange(rel_bias.shape[0], dtype=jnp.int32)[:, None]
    ).astype(f32)
    table = jnp.einsum(
        "bh,bk->hk", jnp.pad(rel_bias, ((0, 0), (0, 8 - head_count))), offset_onehot, precision=highest
    )
    layer_weights = []
    kept_layers = []
    for layer_index in range(layers):
        weights_layer = (
            w_query[layer_index],
            w_kv[layer_index],
            w_out[layer_index],
            w_in[layer_index],
            w_down[layer_index],
            gains[2 * layer_index],
            gains[2 * layer_index + 1],
        )
        layer_weights.append(weights_layer)
        hidden_state, kept_state = layer_forward(
            hidden_state, table, row_ids, col_ids, weights_layer
        )
        kept_layers.append(kept_state)
    final_in = rms_scale(hidden_state, gains[2 * layers]).astype(bf16)
    projected = dot(final_in, w_proj)
    unit_vectors, normalize_back = jax.vjp(normalize, projected)
    vectors = unit_vectors.astype(bf16)
    own_vectors = lax.dynamic_slice_in_dim(vectors, mp_index * share_len, share_len, 0)
    query_rows, slot_count = positive.shape
    plane_slots = slot_count // 2
    own_slots = lax.dynamic_slice_in_dim(positive, stream_side * plane_slots, plane_slots, 1)
    grad_vectors, losses = score(
        vectors,
        jnp.broadcast_to(segments, (8, length)),
        top_mask.reshape(query_rows * slot_count, length),
        jnp.broadcast_to(own_slots.reshape(-1, 1), (query_rows * plane_slots, vectors.shape[1])),
    )
    query_loss = losses[:, 0][None]
    grad_projected = normalize_back(grad_vectors)[0].astype(bf16)
    grad_proj = dot_tn(final_in, grad_projected).astype(bf16)
    grad_final = dot_nt(grad_projected, w_proj)
    grad_state, grad_gain_final = jax.vjp(rms_scale, hidden_state, gains[2 * layers])[1](grad_final)
    gain_grads = [None] * (2 * layers)
    reduced = [None] * layers
    reduced_proj = None
    sums = jnp.zeros(table.shape, f32)
    for layer_index in reversed(range(layers)):
        kept, weights_layer = kept_layers[layer_index], layer_weights[layer_index]
        grad_state, grad_down, grad_in, gain_grads[2 * layer_index + 1] = ffn_backward(
            grad_state, kept, weights_layer
        )
        down = reduce_rows(grad_down, False)
        gate, up = reduce_rows(grad_in[0], True), reduce_rows(grad_in[1], True)
        grad_state, grads, gain_grads[2 * layer_index], part = attention_backward(
            grad_state, table, row_ids, col_ids, kept, weights_layer
        )
        sums = sums + part
        if reduced_proj is None:
            rest = reduce_rows(jnp.concatenate([grads, grad_proj], axis=1), False)
            reduced_proj = rest[:, grads.shape[1] :]
            rest = rest[:, : grads.shape[1]]
        else:
            rest = reduce_rows(grads, False)
        reduced[layer_index] = (down, jnp.stack([gate, up]), jnp.split(rest, 4, axis=1))
    grad_bias_local = jnp.einsum("hk,bk->bh", sums, offset_onehot, precision=highest)[:, :head_count]
    grad_gains = jnp.stack(gain_grads + [grad_gain_final])
    grad_bias, grad_gains = lax.psum((grad_bias_local, grad_gains), ("stream", "batch"))
    rows = model_width // lax.axis_size("batch")
    grad_state = lax.dynamic_slice_in_dim(grad_state, mp_index * share_len, share_len, 0)
    return (
        own_vectors[None, None],
        query_loss,
        grad_state[None, None],
        jnp.stack([member[2][1] for member in reduced]),
        jnp.stack([jnp.stack(member[2][2:]) for member in reduced]),
        jnp.stack([member[2][0] for member in reduced]),
        jnp.stack([member[1] for member in reduced]),
        jnp.stack([member[0] for member in reduced]),
        lax.dynamic_slice_in_dim(grad_gains, batch_index * rows, rows, 1),
        grad_bias,
        reduced_proj,
    )


def solution(mesh):
    placed = (
        P("stream", "batch", "mp", None),
        P("batch", None),
        P(None, "mp", "batch", None),
        P(None, "mp"),
        P(None, None, "mp"),
        P(None, None, None, "mp"),
        P(None, None, "mp"),
        P(None, None, None, "mp"),
        P(None, None, "mp"),
        P(),
        P(None, "mp"),
        P(),
    )
    return jax.shard_map(
        on_device,
        mesh=mesh,
        in_specs=placed,
        out_specs=(
            P("stream", "batch", "mp", None),
            P("batch", "mp"),
            P("stream", "batch", "mp", None),
            P(None, "batch", "mp"),
            P(None, None, "batch", "mp"),
            P(None, "batch", "mp"),
            P(None, None, "batch", "mp"),
            P(None, "batch", "mp"),
            P(None, "batch"),
            P(None, "mp"),
            P("batch", None),
        ),
        check_vma=False,
    )
```

```python
import functools

import jax
import jax.numpy as jnp
from jax import lax
from jax.experimental import pallas as pl
from jax.experimental.pallas import tpu as pltpu
from jax.sharding import PartitionSpec as P

QLEN = 32
DOCS_ROW = 8
TILE = 128
SPAN = 512


norm_eps = 1e-06
vector_eps = 1e-06
temper = 0.05
logit_scale = 32.0
bucket_edges = (12, 16, 23, 32, 46, 64, 91)
highest = lax.Precision.HIGHEST
bf16 = jnp.bfloat16
f32 = jnp.float32


def dot(a, b):
    return lax.dot_general(a, b, (((1,), (0,)), ((), ())), preferred_element_type=f32)


def dot_nt(a, b):
    return lax.dot_general(a, b, (((1,), (1,)), ((), ())), preferred_element_type=f32)


def dot_tn(a, b):
    return lax.dot_general(a, b, (((0,), (0,)), ((), ())), preferred_element_type=f32)


def offset_buckets():
    index = jnp.arange(SPAN, dtype=jnp.int32)
    offsets = jnp.where(index < SPAN // 2, index, index - SPAN)
    magnitude = jnp.abs(offsets)
    far_bucket = jnp.full(offsets.shape, 8, jnp.int32)
    for threshold in bucket_edges:
        far_bucket = far_bucket + (magnitude >= threshold).astype(jnp.int32)
    bucket = jnp.where(magnitude < 8, magnitude, jnp.minimum(far_bucket, 15))
    return bucket + jnp.where(offsets > 0, 16, 0).astype(jnp.int32)


def window(tile, tiles):
    first, last = max(0, tile - 1), min(tiles, tile + 2)
    shift = first - (tile - 1)
    return pl.ds(first * TILE, (last - first) * TILE), slice(shift * TILE, (shift + last - first) * TILE)


def fill_masks(row_ids, col_ids, mask, tiles):
    for tile in range(tiles):
        rows = pl.ds(tile * TILE, TILE)
        own = col_ids[rows, :]
        for near in range(max(0, tile - 1), min(tiles, tile + 2)):
            other = jnp.broadcast_to(row_ids[0:1, near * TILE : (near + 1) * TILE], (TILE, TILE))
            place = (near - tile + 1) * TILE
            mask[rows, place : place + TILE] = jnp.where(own == other, 0.0, -1e30)


def bias_tile(table, head):
    line = jnp.broadcast_to(table[pl.ds(head, 1), :], (TILE, SPAN))
    return pltpu.roll(line, TILE, axis=1, stride=1, stride_axis=0)[:, : 3 * TILE]


def attend_kernel(table, row_ids, col_ids, q, k, v, o, lse, mask, bias):
    tiles = q.shape[0] // TILE
    fill_masks(row_ids, col_ids, mask, tiles)
    lane = lax.broadcasted_iota(jnp.int32, (TILE, TILE), 1)
    lse[...] = jnp.zeros(lse.shape, f32)

    def pair(p, carry):
        cols = pl.ds(pl.multiple_of(p * TILE, TILE), TILE)
        for half in range(2):
            bias[half] = bias_tile(table, 2 * p + half)
        for tile in range(tiles):
            rows = pl.ds(tile * TILE, TILE)
            keys, frame = window(tile, tiles)
            queries = q[rows, cols]
            near_keys, near_values = k[keys, cols], v[keys, cols]
            outs = []
            kept = lse[rows, :]
            for half in range(2):
                mine = (lane >= 64) if half else (lane < 64)
                s = dot_nt(jnp.where(mine, queries, jnp.zeros_like(queries)), near_keys)
                s = s + bias[half][:, frame] + mask[rows, frame]
                top = jnp.max(s, axis=-1, keepdims=True)
                e = jnp.exp(s - top)
                total = jnp.sum(e, axis=-1, keepdims=True)
                weights = (e * (1.0 / total)).astype(bf16)
                outs.append(dot(weights, near_values))
                kept = jnp.where(lane == 2 * p + half, top + jnp.log(total), kept)
            lse[rows, :] = kept
            o[rows, cols] = jnp.where(lane < 64, outs[0], outs[1]).astype(bf16)
        return carry

    lax.fori_loop(0, q.shape[1] // TILE, pair, 0)


def attend(table, row_ids, col_ids, q, k, v):
    length, width = q.shape
    return pl.pallas_call(
        attend_kernel,
        out_shape=(
            jax.ShapeDtypeStruct((length, width), bf16),
            jax.ShapeDtypeStruct((length, TILE), f32),
        ),
        scratch_shapes=[pltpu.VMEM((length, 3 * TILE), f32), pltpu.VMEM((2, TILE, 3 * TILE), f32)],
        compiler_params=pltpu.CompilerParams(vmem_limit_bytes=32 * 1024 * 1024),
        cost_estimate=pl.CostEstimate(flops=10**9, bytes_accessed=3 * 10**6, transcendentals=10**6),
        name="attend",
    )(table, row_ids, col_ids, q, k, v)


def attend_back_kernel(
    table, row_ids, col_ids, lse, q, k, v, do, dq, dk, dv, sums, mask, bias, grid, dk_sum, dv_sum
):
    tiles = q.shape[0] // TILE
    fill_masks(row_ids, col_ids, mask, tiles)
    lane = lax.broadcasted_iota(jnp.int32, (TILE, TILE), 1)
    row_index = lax.broadcasted_iota(jnp.int32, (TILE, SPAN), 0)
    sums[...] = jnp.zeros(sums.shape, f32)

    def pair(p, carry):
        cols = pl.ds(pl.multiple_of(p * TILE, TILE), TILE)
        for half in range(2):
            bias[half] = bias_tile(table, 2 * p + half)
        grid[...] = jnp.zeros(grid.shape, f32)
        dk_sum[...] = jnp.zeros(dk_sum.shape, f32)
        dv_sum[...] = jnp.zeros(dv_sum.shape, f32)
        for tile in range(tiles):
            rows = pl.ds(tile * TILE, TILE)
            keys, frame = window(tile, tiles)
            queries, grads = q[rows, cols], do[rows, cols]
            near_keys, near_values = k[keys, cols], v[keys, cols]
            kept = lse[rows, :]
            outs = []
            for half in range(2):
                mine = (lane >= 64) if half else (lane < 64)
                own_queries = jnp.where(mine, queries, jnp.zeros_like(queries))
                own_grads = jnp.where(mine, grads, jnp.zeros_like(grads))
                log_total = jnp.sum(
                    jnp.where(lane == 2 * p + half, kept, 0.0), axis=-1, keepdims=True
                )
                s = dot_nt(own_queries, near_keys)
                s = s + bias[half][:, frame] + mask[rows, frame]
                weights = jnp.exp(s - log_total)
                grad_weights = dot_nt(own_grads, near_values)
                mean = jnp.sum(weights * grad_weights, axis=-1, keepdims=True)
                ds = (weights * (grad_weights - mean)).astype(bf16)
                outs.append(dot(ds, near_keys))
                dk_sum[keys, :] += dot_tn(ds, own_queries)
                dv_sum[keys, :] += dot_tn(weights.astype(bf16), own_grads)
                grid[half, :, frame] += ds.astype(f32)
            dq[rows, cols] = jnp.where(lane < 64, outs[0], outs[1]).astype(bf16)
        dk[:, cols] = dk_sum[...].astype(bf16)
        dv[:, cols] = dv_sum[...].astype(bf16)
        for half in range(2):
            turned = pltpu.roll(grid[half], SPAN - TILE, axis=1)
            for bit in range(7):
                moved = pltpu.roll(turned, SPAN - (1 << bit), axis=1)
                turned = jnp.where((row_index >> bit) & 1 == 1, moved, turned)
            sums[pl.ds(2 * p + half, 1), :] = jnp.sum(turned, axis=0, keepdims=True)
        return carry

    lax.fori_loop(0, q.shape[1] // TILE, pair, 0)


def attend_back(table, row_ids, col_ids, lse, q, k, v, do):
    length, width = q.shape
    grad = jax.ShapeDtypeStruct((length, width), bf16)
    return pl.pallas_call(
        attend_back_kernel,
        out_shape=(grad, grad, grad, jax.ShapeDtypeStruct(table.shape, f32)),
        scratch_shapes=[
            pltpu.VMEM((length, 3 * TILE), f32),
            pltpu.VMEM((2, TILE, 3 * TILE), f32),
            pltpu.VMEM((2, TILE, SPAN), f32),
            pltpu.VMEM((length, TILE), f32),
            pltpu.VMEM((length, TILE), f32),
        ],
        compiler_params=pltpu.CompilerParams(vmem_limit_bytes=32 * 1024 * 1024),
        cost_estimate=pl.CostEstimate(flops=25 * 10**8, bytes_accessed=4 * 10**6, transcendentals=10**6),
        name="attend_back",
    )(table, row_ids, col_ids, lse, q, k, v, do)


def rms_scale(values, gain_row):
    return (
        values * lax.rsqrt(jnp.mean(values * values, axis=-1, keepdims=True) + norm_eps) * gain_row
    )


def gated_gelu(gate, up):
    return jax.nn.gelu(gate, approximate=True) * up


def normalize(values):
    return values * lax.rsqrt(jnp.sum(values * values, axis=-1, keepdims=True) + vector_eps)


def swap(value, axis):
    return lax.ppermute(value, axis, [(0, 1), (1, 0)])


def sum_of_two(part, axis):
    mine = lax.optimization_barrier(part.astype(bf16))
    return mine.astype(f32) + swap(mine, axis).astype(f32)


def layer_forward(inputs, table, row_ids, col_ids, weights_layer):
    query_weight, kv_weight, out_weight, in_weight, down_weight, gain_attn, gain_ffn = weights_layer
    normed = rms_scale(inputs, gain_attn).astype(bf16)
    q = dot(normed, query_weight).astype(bf16)
    k = dot(normed, kv_weight[0]).astype(bf16)
    v = dot(normed, kv_weight[1]).astype(bf16)
    attended, lse = attend(table, row_ids, col_ids, q, k, v)
    middle = inputs + sum_of_two(dot_nt(attended, out_weight), "mp")
    ffn_input = rms_scale(middle, gain_ffn).astype(bf16)
    gate, up = dot(ffn_input, in_weight[0]), dot(ffn_input, in_weight[1])
    hidden = gated_gelu(gate, up).astype(bf16)
    output = middle + sum_of_two(dot_nt(hidden, down_weight), "mp")
    return output, (inputs, normed, q, k, v, lse, attended, middle, ffn_input, gate, up, hidden)


def ffn_backward(grad_output, kept, weights_layer):
    middle, ffn_input, gate, up, hidden = kept[7:]
    in_weight, down_weight, gain_ffn = weights_layer[3], weights_layer[4], weights_layer[6]
    grad_branch = grad_output.astype(bf16)
    grad_hidden = dot(grad_branch, down_weight)
    grad_gate, grad_up = jax.vjp(gated_gelu, gate, up)[1](grad_hidden)
    grad_gate, grad_up = grad_gate.astype(bf16), grad_up.astype(bf16)
    grad_input = sum_of_two(dot_nt(grad_gate, in_weight[0]) + dot_nt(grad_up, in_weight[1]), "mp")
    grad_mid_norm, grad_gain = jax.vjp(rms_scale, middle, gain_ffn)[1](grad_input)
    return grad_output + grad_mid_norm, (grad_branch, ffn_input), (hidden, grad_gate, grad_up), grad_gain


def attention_backward(grad_middle, table, row_ids, col_ids, kept, weights_layer):
    inputs, normed, q, k, v, lse, attended = kept[:7]
    query_weight, kv_weight, out_weight, gain_attn = (
        weights_layer[0],
        weights_layer[1],
        weights_layer[2],
        weights_layer[5],
    )
    grad_attn = grad_middle.astype(bf16)
    do = dot(grad_attn, out_weight).astype(bf16)
    dq, dk, dv, sums = attend_back(table, row_ids, col_ids, lse, q, k, v, do)
    grad_normed = sum_of_two(
        dot_nt(dq, query_weight) + dot_nt(dk, kv_weight[0]) + dot_nt(dv, kv_weight[1]), "mp"
    )
    grad_in_norm, grad_gain = jax.vjp(rms_scale, inputs, gain_attn)[1](grad_normed)
    return grad_middle + grad_in_norm, (grad_attn, normed), (attended, dq, dk, dv), grad_gain, sums


def mesh_id(stream, batch):
    return {"stream": stream, "batch": batch}


def send(source, target, send_sem, recv_sem, device):
    copy = pltpu.make_async_remote_copy(
        src_ref=source,
        dst_ref=target,
        send_sem=send_sem,
        recv_sem=recv_sem,
        device_id=device,
        device_id_type=pl.DeviceIdType.MESH,
    )
    copy.start()


def await_send(source, send_sem):
    pltpu.make_async_copy(source, source, send_sem).wait()


def split_dot(contract, left, right):
    high = left.astype(bf16)
    low = (left - high.astype(f32)).astype(bf16)
    return contract(high, right) + contract(low, right)


def score_kernel(
    count,
    vectors,
    doc_row,
    top_mask,
    positive,
    grad,
    loss,
    queries,
    docs,
    raised,
    totals,
    logits,
    stats,
    own_loss,
    other_loss,
    sent_grads,
    got_grads,
    doc_sum,
    sent_docs,
    got_docs,
    core_sent,
    core_got,
    query_send,
    query_recv,
    doc_send,
    doc_recv,
    stat_send,
    stat_recv,
    loss_sems,
    grad_send,
    grad_recv,
    back_sems,
    core_sems,
):
    side, batch, half = lax.axis_index("stream"), lax.axis_index("batch"), lax.axis_index("mp")
    length, width = vectors.shape
    quarter = length // 4
    slots = quarter // QLEN
    core = {"mp": 1 - half}
    other = {"stream": 1 - side}
    mine = side * count + batch

    barrier = pltpu.get_barrier_semaphore()

    def greet(step, carry):
        peer = lax.rem(mine + step, 2 * count)
        pl.semaphore_signal(
            barrier,
            inc=1,
            device_id=mesh_id(peer // count, lax.rem(peer, count)),
            device_id_type=pl.DeviceIdType.MESH,
        )
        return carry

    lax.fori_loop(1, 2 * count, greet, 0)
    pl.semaphore_signal(barrier, inc=1, device_id=core, device_id_type=pl.DeviceIdType.MESH)
    pl.semaphore_wait(barrier, 2 * count)

    def query_part(plane):
        return vectors.at[pl.ds(pl.multiple_of(half * (length // 2), QLEN) + plane * quarter, quarter), :]

    @pl.when(side == 0)
    def _():
        def push(step, carry):
            peer = lax.rem(batch + step, count)
            send(query_part(1), queries.at[batch], query_send.at[1, peer], query_recv.at[batch], mesh_id(1, peer))

            @pl.when(step > 0)
            def _():
                send(query_part(0), queries.at[batch], query_send.at[0, peer], query_recv.at[batch], mesh_id(0, peer))

            return carry

        lax.fori_loop(0, count, push, 0)
        queries[batch] = vectors[pl.ds(pl.multiple_of(half * (length // 2), QLEN), quarter), :]

    @pl.when(side == 1)
    def _():
        send(vectors, docs, doc_send, doc_recv, mesh_id(0, batch))
        docs[...] = vectors[...]

    lane = lax.broadcasted_iota(jnp.int32, (width, length), 0)
    onehot = jnp.where(lane == jnp.broadcast_to(doc_row[0:1, :], (width, length)), 1.0, 0.0).astype(bf16)

    @pl.when(side == 0)
    def _():
        pltpu.make_async_copy(docs, docs, doc_recv).wait()

    def await_queries(source):
        @pl.when(jnp.logical_or(side == 1, source != batch))
        def _():
            pltpu.make_async_copy(queries.at[source], queries.at[source], query_recv.at[source]).wait()

    def forward(step, carry):
        source = lax.rem(batch + step, count)
        await_queries(source)
        sims = dot_nt(queries[source], docs[...]) * (1.0 / temper)
        for slot in range(slots):
            chosen = top_mask[pl.ds(source * 2 * slots + side * slots + slot, 1), :].astype(f32)
            part = jnp.exp(sims[slot * QLEN : (slot + 1) * QLEN]) * chosen
            raised[source, slot * QLEN : (slot + 1) * QLEN, :] = part
        summed = split_dot(dot_nt, raised[source], onehot)
        totals[source] = summed
        pooled = jnp.log1p(summed) * (logit_scale * temper / QLEN)
        for slot in range(slots):
            logits[pl.ds(source * slots + slot, 1), :] = jnp.sum(
                pooled[slot * QLEN : (slot + 1) * QLEN], axis=0, keepdims=True
            )
        return carry

    lax.fori_loop(0, count, forward, 0)

    doc = lax.broadcasted_iota(jnp.int32, logits.shape, 1)
    local = doc < DOCS_ROW
    scores = logits[...]
    is_positive = jnp.where(
        jnp.logical_and(local, positive[...] == doc + batch * DOCS_ROW), 1.0, 0.0
    )
    exps = jnp.sum(jnp.where(local, jnp.exp(scores), 0.0), axis=1, keepdims=True)
    hits = jnp.sum(is_positive * scores, axis=1, keepdims=True)
    stats[batch] = jnp.where(doc == 0, exps, jnp.where(doc == 1, hits, 0.0))

    def push_stats(step, carry):
        peer = lax.rem(batch + step, count)
        send(stats.at[batch], stats.at[batch], stat_send.at[peer], stat_recv.at[batch], mesh_id(side, peer))
        return carry

    lax.fori_loop(1, count, push_stats, 0)

    def take_stats(step, carry):
        peer = lax.rem(batch + step, count)
        pltpu.make_async_copy(stats.at[peer], stats.at[peer], stat_recv.at[peer]).wait()
        return carry

    lax.fori_loop(1, count, take_stats, 0)
    summed = lax.fori_loop(1, count, lambda source, total: total + stats[source], stats[0])
    log_total = jnp.log(jnp.sum(jnp.where(doc == 0, summed, 0.0), axis=1, keepdims=True))
    hit_total = jnp.sum(jnp.where(doc == 1, summed, 0.0), axis=1, keepdims=True)
    losses = jnp.broadcast_to(log_total - hit_total, logits.shape)
    sent_grad = jnp.where(local, jnp.exp(scores - log_total), 0.0) - is_positive
    logits[...] = losses
    for slot in range(slots):
        own_loss[pl.ds(slot, 1), :] = logits[pl.ds(batch * slots + slot, 1), :]
    send(own_loss, other_loss, loss_sems.at[0], loss_sems.at[1], other)
    logits[...] = sent_grad
    doc_sum[...] = jnp.zeros(doc_sum.shape, f32)

    def backward(step, carry):
        source = lax.rem(batch + step + 1, count)
        parts = []
        for slot in range(slots):
            line = logits[pl.ds(source * slots + slot, 1), :] * (logit_scale / QLEN)
            parts.append(line / (1.0 + totals[source, slot * QLEN : (slot + 1) * QLEN, :]))
        spread = split_dot(dot, jnp.concatenate(parts, axis=0), onehot)
        ds = (raised[source] * spread).astype(bf16)
        back = dot(ds, docs[...]).astype(bf16)
        doc_sum[...] += dot_tn(ds, queries[source])

        @pl.when(jnp.logical_or(side == 1, source != batch))
        def _():
            sent_grads[source] = back
            send(
                sent_grads.at[source],
                got_grads.at[side, batch],
                grad_send.at[source],
                grad_recv.at[side, batch],
                mesh_id(0, source),
            )

        @pl.when(jnp.logical_and(side == 0, source == batch))
        def _():
            got_grads[0, batch] = back

        return carry

    lax.fori_loop(0, count, backward, 0)

    @pl.when(side == 0)
    def _():
        sent_docs[...] = doc_sum[...].astype(bf16)
        send(sent_docs, got_docs, back_sems.at[0], back_sems.at[1], mesh_id(1, batch))

        def take(step, carry):
            peer = lax.rem(batch + step, count)

            @pl.when(step > 0)
            def _():
                pltpu.make_async_copy(got_grads.at[0, peer], got_grads.at[0, peer], grad_recv.at[0, peer]).wait()

            pltpu.make_async_copy(got_grads.at[1, peer], got_grads.at[1, peer], grad_recv.at[1, peer]).wait()
            return carry

        lax.fori_loop(0, count, take, 0)
        for plane in range(2):
            total = lax.fori_loop(
                1,
                count,
                lambda source, total, plane=plane: total + got_grads[plane, source].astype(f32),
                got_grads[plane, 0].astype(f32),
            )
            core_sent[plane * quarter : (plane + 1) * quarter, :] = total.astype(bf16)
        part = core_sent.at[pl.ds(0, length // 2), :]
        there = core_got.at[pl.ds(0, length // 2), :]
        send(part, there, core_sems.at[0], core_sems.at[1], core)
        pltpu.make_async_copy(there, there, core_sems.at[1]).wait()
        first = pl.multiple_of(half * (length // 2), QLEN)
        grad[pl.ds(first, length // 2), :] = core_sent[pl.ds(0, length // 2), :].astype(f32)
        grad[pl.ds(length // 2 - first, length // 2), :] = core_got[pl.ds(0, length // 2), :].astype(f32)
        await_send(part, core_sems.at[0])
        await_send(sent_docs, back_sems.at[0])

    @pl.when(side == 1)
    def _():
        pltpu.make_async_copy(got_docs, got_docs, back_sems.at[1]).wait()
        core_sent[...] = (doc_sum[...] + got_docs[...].astype(f32)).astype(bf16)
        send(core_sent, core_got, core_sems.at[0], core_sems.at[1], core)
        pltpu.make_async_copy(core_got, core_got, core_sems.at[1]).wait()
        grad[...] = (core_sent[...].astype(f32) + core_got[...].astype(f32)).astype(bf16).astype(f32)
        await_send(core_sent, core_sems.at[0])
        await_send(vectors, doc_send)

    pltpu.make_async_copy(other_loss, other_loss, loss_sems.at[1]).wait()
    lower = jnp.where(side == 0, own_loss[0:slots, :], other_loss[0:slots, :])
    upper = jnp.where(side == 0, other_loss[0:slots, :], own_loss[0:slots, :])
    loss[...] = jnp.concatenate([lower, upper], axis=0)
    await_send(own_loss, loss_sems.at[0])

    def settle(step, carry):
        peer = lax.rem(batch + step, count)

        @pl.when(step > 0)
        def _():
            await_send(stats.at[batch], stat_send.at[peer])

        @pl.when(jnp.logical_or(side == 1, step > 0))
        def _():
            await_send(sent_grads.at[peer], grad_send.at[peer])

        @pl.when(side == 0)
        def _():
            await_send(query_part(1), query_send.at[1, peer])

            @pl.when(step > 0)
            def _():
                await_send(query_part(0), query_send.at[0, peer])

        return carry

    lax.fori_loop(0, count, settle, 0)


def score(vectors, doc_row, top_mask, positive):
    count = lax.axis_size("batch")
    length, width = vectors.shape
    quarter = length // 4
    slots = quarter // QLEN
    dma = pltpu.SemaphoreType.DMA
    return pl.pallas_call(
        functools.partial(score_kernel, count),
        out_shape=(
            jax.ShapeDtypeStruct((length, width), f32),
            jax.ShapeDtypeStruct((2 * slots, width), f32),
        ),
        in_specs=[pl.BlockSpec(memory_space=pltpu.VMEM)] * 4,
        out_specs=(pl.BlockSpec(memory_space=pltpu.VMEM),) * 2,
        scratch_shapes=[
            pltpu.VMEM((count, quarter, width), bf16),
            pltpu.VMEM((length, width), bf16),
            pltpu.VMEM((count, quarter, length), f32),
            pltpu.VMEM((count, quarter, width), f32),
            pltpu.VMEM((count * slots, width), f32),
            pltpu.VMEM((count, count * slots, width), f32),
            pltpu.VMEM((8, width), f32),
            pltpu.VMEM((8, width), f32),
            pltpu.VMEM((count, quarter, width), bf16),
            pltpu.VMEM((2, count, quarter, width), bf16),
            pltpu.VMEM((length, width), f32),
            pltpu.VMEM((length, width), bf16),
            pltpu.VMEM((length, width), bf16),
            pltpu.VMEM((length, width), bf16),
            pltpu.VMEM((length, width), bf16),
            dma((2, count)),
            dma((count,)),
            dma,
            dma,
            dma((count,)),
            dma((count,)),
            dma((2,)),
            dma((count,)),
            dma((2, count)),
            dma((2,)),
            dma((2,)),
        ],
        compiler_params=pltpu.CompilerParams(
            collective_id=0, has_side_effects=True, vmem_limit_bytes=56 * 1024 * 1024
        ),
        cost_estimate=pl.CostEstimate(flops=10**9, bytes_accessed=2 * 10**6, transcendentals=10**6),
        name="score",
    )(vectors, doc_row, top_mask, positive)


CHUNK = 384


def block_copy(ref, sem):
    pltpu.make_async_copy(ref, ref, sem).wait()


class Sums:
    def __init__(self, refs, ring):
        self.refs, self.ring = refs, ring
        self.side, batch = lax.axis_index("stream"), lax.axis_index("batch")
        self.inner, self.outer = lax.rem(batch, 2), batch // 2
        self.batch = batch
        self.count = lax.axis_size("batch") // 2

    def stream_peer(self):
        return {"stream": 1 - self.side}

    def inner_peer(self):
        return {"batch": self.batch + 1 - 2 * self.inner}

    def outer_peer(self, step):
        return {"batch": lax.rem(self.outer + step, self.count) * 2 + self.inner}

    def greet(self):
        barrier = pltpu.get_barrier_semaphore()
        peers = [self.stream_peer(), self.inner_peer()]
        peers += [self.outer_peer(step) for step in range(1, self.count)]
        for peer in peers:
            pl.semaphore_signal(barrier, inc=1, device_id=peer, device_id_type=pl.DeviceIdType.MESH)
        pl.semaphore_wait(barrier, len(peers))


class StreamFirst(Sums):
    def half(self, side):
        rows = self.refs["work"].shape[3] // 2
        return pl.ds(pl.multiple_of(side * rows, 16), rows)

    def start(self, n):
        r = self.refs
        work = r["work"].at[n % self.ring]
        send(work.at[:, :, self.half(1 - self.side), :], r["got0"].at[n], r["send"].at[0, n], r["recv"].at[0, n], self.stream_peer())

    def step(self, n, stage):
        r = self.refs
        slot = n % self.ring
        work, own = r["work"].at[slot], self.half(self.side)
        if stage == 1:
            block_copy(r["got0"].at[n], r["recv"].at[0, n])

            def add(index, carry):
                o, i = index // 2, lax.rem(index, 2)
                total = work[o, i, own, :].astype(f32) + r["got0"][n, o, i].astype(f32)
                work[o, i, own, :] = total.astype(bf16)
                return carry

            lax.fori_loop(0, 2 * self.count, add, 0)
            send(work.at[:, 1 - self.inner, own, :], r["got1"].at[n], r["send"].at[1, n], r["recv"].at[1, n], self.inner_peer())
        if stage == 2:
            block_copy(r["got1"].at[n], r["recv"].at[1, n])

            def add(o, carry):
                total = work[o, self.inner, own, :].astype(f32) + r["got1"][n, o].astype(f32)
                work[o, self.inner, own, :] = total.astype(bf16)
                return carry

            lax.fori_loop(0, self.count, add, 0)
            for step in range(1, self.count):
                o = lax.rem(self.outer + step, self.count)
                send(work.at[o, self.inner, own, :], r["got2"].at[n, step - 1], r["send"].at[2, n], r["recv"].at[2, n], self.outer_peer(step))
        if stage == 3:
            block_copy(r["got2"].at[n], r["recv"].at[2, n])
            total = work[self.outer, self.inner, own, :].astype(f32)
            for step in range(1, self.count):
                total = total + r["got2"][n, step - 1].astype(f32)
            r["last"][n] = total.astype(bf16)
            send(r["last"].at[n], r["got3"].at[n], r["send"].at[3, n], r["recv"].at[3, n], self.stream_peer())
            r["out"](n)[own, :] = r["last"][n].astype(f32)
            block_copy(r["got0"].at[n], r["send"].at[0, n])
            block_copy(r["got1"].at[n], r["send"].at[1, n])
            block_copy(r["got2"].at[n], r["send"].at[2, n])
        if stage == 4:
            block_copy(r["got3"].at[n], r["recv"].at[3, n])
            r["out"](n)[self.half(1 - self.side), :] = r["got3"][n].astype(f32)
            block_copy(r["last"].at[n], r["send"].at[3, n])


class BatchFirst(Sums):
    def start(self, n):
        r = self.refs
        work = r["work"].at[n % self.ring]
        send(work.at[:, 1 - self.inner], r["got0"].at[n], r["send"].at[0, n], r["recv"].at[0, n], self.inner_peer())

    def step(self, n, stage):
        r = self.refs
        work = r["work"].at[n % self.ring]
        if stage == 1:
            block_copy(r["got0"].at[n], r["recv"].at[0, n])

            def add(o, carry):
                total = work[o, self.inner].astype(f32) + r["got0"][n, o].astype(f32)
                work[o, self.inner] = total.astype(bf16)
                return carry

            lax.fori_loop(0, self.count, add, 0)
            for step in range(1, self.count):
                o = lax.rem(self.outer + step, self.count)
                send(work.at[o, self.inner], r["got1"].at[n, step - 1], r["send"].at[1, n], r["recv"].at[1, n], self.outer_peer(step))
        if stage == 2:
            block_copy(r["got1"].at[n], r["recv"].at[1, n])
            total = work[self.outer, self.inner].astype(f32)
            for step in range(1, self.count):
                total = total + r["got1"][n, step - 1].astype(f32)
            r["last"][n] = total.astype(bf16)
            send(r["last"].at[n], r["got2"].at[n], r["send"].at[2, n], r["recv"].at[2, n], self.stream_peer())
            block_copy(r["got0"].at[n], r["send"].at[0, n])
            block_copy(r["got1"].at[n], r["send"].at[1, n])
        if stage == 3:
            block_copy(r["got2"].at[n], r["recv"].at[2, n])
            r["out"](n)[...] = r["last"][n].astype(f32) + r["got2"][n].astype(f32)
            block_copy(r["last"].at[n], r["send"].at[2, n])


def blocks_of(layers, wide):
    found = []
    for layer in reversed(range(layers)):
        for left, right, output, index in ((0, 0, 0, ()), (1, 1, 1, (0,)), (1, 2, 1, (1,))):
            found += [(layer, left, right, c * CHUNK, output, index) for c in range(wide // CHUNK)]
        for left, right, output, index in ((2, 3, 2, ()), (3, 4, 3, ()), (3, 5, 4, (0,)), (3, 6, 4, (1,))):
            found.append((layer, left, right, 0, output, index))
    return found


LEFTS, RIGHTS = 4, 7
RING = 6


def sums_kernel(layers, blocks, *refs):
    pairs = layers * (LEFTS + RIGHTS) + 2
    given, refs = refs[:pairs], refs[pairs:]
    little, refs = refs[0], refs[1:]
    outs, refs = refs[:7], refs[7:]
    held, refs = refs[:pairs], refs[pairs:]
    (little_got, little_sems, load_sems, first_work, first_got0, first_got1, first_got2, first_got3, first_last, first_send, first_recv,
     last_work, last_got0, last_got1, last_got2, last_last, last_send, last_recv,
     proj_work, proj_got0, proj_got1, proj_got2, proj_last, proj_send, proj_recv) = refs
    loads = [pltpu.make_async_copy(given[i], held[i], load_sems.at[i]) for i in range(pairs)]
    for load in loads:
        load.start()
    loaded = set()

    def operand(i):
        if i not in loaded:
            loads[i].wait()
            loaded.add(i)
        return held[i]

    def left_of(layer, which):
        return operand(layer * (LEFTS + RIGHTS) + which)

    def right_of(layer, which):
        return operand(layer * (LEFTS + RIGHTS) + LEFTS + which)

    half = len(blocks) // 2
    firsts, lasts = blocks[0::2], blocks[1::2]

    def out_of(blocks):
        def place(n):
            layer, _, _, column, output, index = blocks[n]
            return outs[output].at[(layer,) + index + (slice(None), pl.ds(column, CHUNK))]

        return place

    stream_first = StreamFirst(
        dict(work=first_work, got0=first_got0, got1=first_got1, got2=first_got2, got3=first_got3, last=first_last,
             send=first_send, recv=first_recv, out=out_of(firsts)), RING)
    batch_first = BatchFirst(
        dict(work=last_work, got0=last_got0, got1=last_got1, got2=last_got2, last=last_last,
             send=last_send, recv=last_recv, out=out_of(lasts)), RING)
    projection = BatchFirst(
        dict(work=proj_work, got0=proj_got0, got1=proj_got1, got2=proj_got2, last=proj_last,
             send=proj_send, recv=proj_recv, out=lambda n: outs[5]), 1)
    stream_first.greet()

    def product(left, right, work):
        width = left.shape[1] // 2
        for part in range(2):
            block = dot_tn(left[:, part * width : (part + 1) * width], right).astype(bf16)
            outer = work.shape[0] // 2
            work[part * outer : (part + 1) * outer] = block.reshape((outer,) + work.shape[1:])

    def make(sums, blocks, n):
        layer, left, right, column, _, _ = blocks[n]
        product(
            left_of(layer, left),
            right_of(layer, right)[:, column : column + CHUNK],
            sums.refs["work"].at[n % RING],
        )
        sums.start(n)

    def little_start():
        little_got[0] = little[...]
        send(little_got.at[0], little_got.at[1], little_sems.at[0], little_sems.at[1], stream_first.stream_peer())

    def little_step(stage):
        if stage == 1:
            block_copy(little_got.at[1], little_sems.at[1])
            little_got[2] = little_got[0] + little_got[1]
            send(little_got.at[2], little_got.at[3], little_sems.at[2], little_sems.at[3], stream_first.inner_peer())
        if stage == 2:
            block_copy(little_got.at[3], little_sems.at[3])
            little_got[4] = little_got[2] + little_got[3]
            for step in range(1, stream_first.count):
                send(little_got.at[4], little_got.at[4 + step], little_sems.at[4], little_sems.at[5], stream_first.outer_peer(step))
        if stage == 3:
            parts = little_got.at[pl.ds(5, stream_first.count - 1)]
            block_copy(parts, little_sems.at[5])
            total = None
            for o in range(stream_first.count):
                step = lax.rem(stream_first.outer - o + stream_first.count, stream_first.count)
                term = little_got[4 + step]
                total = term if total is None else total + term
            outs[6][...] = total
            block_copy(little_got.at[0], little_sems.at[0])
            block_copy(little_got.at[2], little_sems.at[2])
            block_copy(parts, little_sems.at[4])

    for t in range(half + 4):
        if t < half:
            make(stream_first, firsts, t)
            make(batch_first, lasts, t)
        if t == half - 4:
            product(operand(pairs - 2), operand(pairs - 1)[...], proj_work.at[0])
            projection.start(0)
            little_start()
        for stage in (1, 2, 3, 4):
            if 0 <= t - stage < half:
                stream_first.step(t - stage, stage)
                if stage < 4:
                    batch_first.step(t - stage, stage)
            if t - stage == half - 4 and stage < 4:
                projection.step(0, stage)
                little_step(stage)


def sum_gradients(kept, final_pair, little):
    layers = len(kept)
    batch = lax.axis_size("batch")
    outer = batch // 2
    model = kept[0][0].shape[1]
    rows = model // batch
    narrow, wide = kept[0][LEFTS + 3].shape[1], kept[0][LEFTS].shape[1]
    width = final_pair[1].shape[1]
    blocks = blocks_of(layers, wide)
    half = len(blocks) // 2
    operands = [value for layer in kept for value in layer] + list(final_pair)
    dma = pltpu.SemaphoreType.DMA
    vmem = pltpu.VMEM
    shape = jax.ShapeDtypeStruct
    rh = rows // 2
    return pl.pallas_call(
        functools.partial(sums_kernel, layers, blocks),
        out_shape=(
            shape((layers, rows, wide), f32),
            shape((layers, 2, rows, wide), f32),
            shape((layers, rows, narrow), f32),
            shape((layers, rows, narrow), f32),
            shape((layers, 2, rows, narrow), f32),
            shape((rows, width), f32),
            shape(little.shape, f32),
        ),
        in_specs=[pl.BlockSpec(memory_space=pl.ANY)] * len(operands) + [pl.BlockSpec(memory_space=vmem)],
        out_specs=(pl.BlockSpec(memory_space=vmem),) * 7,
        scratch_shapes=[vmem(value.shape, bf16) for value in operands]
        + [
            vmem((4 + outer,) + little.shape, f32),
            dma((6,)),
            dma((len(operands),)),
            vmem((RING, outer, 2, rows, CHUNK), bf16),
            vmem((half, outer, 2, rh, CHUNK), bf16),
            vmem((half, outer, rh, CHUNK), bf16),
            vmem((half, outer - 1, rh, CHUNK), bf16),
            vmem((half, rh, CHUNK), bf16),
            vmem((half, rh, CHUNK), bf16),
            dma((4, half)),
            dma((4, half)),
            vmem((RING, outer, 2, rows, CHUNK), bf16),
            vmem((half, outer, rows, CHUNK), bf16),
            vmem((half, outer - 1, rows, CHUNK), bf16),
            vmem((half, rows, CHUNK), bf16),
            vmem((half, rows, CHUNK), bf16),
            dma((3, half)),
            dma((3, half)),
            vmem((1, outer, 2, rows, width), bf16),
            vmem((1, outer, rows, width), bf16),
            vmem((1, outer - 1, rows, width), bf16),
            vmem((1, rows, width), bf16),
            vmem((1, rows, width), bf16),
            dma((3, 1)),
            dma((3, 1)),
        ],
        compiler_params=pltpu.CompilerParams(
            collective_id=1, has_side_effects=True, vmem_limit_bytes=60 * 1024 * 1024
        ),
        cost_estimate=pl.CostEstimate(flops=10**10, bytes_accessed=2 * 10**7, transcendentals=0),
        name="sum_gradients",
    )(*operands, little)


def sum_gradients_plainly(kept, final_pair, little):
    def summed(left, right):
        part = lax.psum_scatter(dot_tn(left, right).astype(bf16), "batch", scatter_dimension=0, tiled=True)
        return sum_of_two(part, "stream")

    found = []
    for e, n2, c, n1, hidden, dg, du, o, dq, dk, dv in kept:
        found.append((
            summed(e, hidden),
            jnp.stack([summed(n2, dg), summed(n2, du)]),
            summed(c, o),
            summed(n1, dq),
            jnp.stack([summed(n1, dk), summed(n1, dv)]),
        ))
    return [jnp.stack(parts) for parts in zip(*found)] + [
        summed(*final_pair),
        lax.psum(little, ("stream", "batch")),
    ]


def on_device(
    tokens,
    segments,
    top_mask,
    positive,
    w_query,
    w_kv,
    w_out,
    w_in,
    w_down,
    gains,
    rel_bias,
    w_proj,
):
    stream_side = lax.axis_index("stream")
    batch_index = lax.axis_index("batch")
    mp_index = lax.axis_index("mp")
    row = lax.all_gather(tokens[0], "mp", axis=1, tiled=True)
    row_count, length, model_width = row.shape
    share_len = tokens.shape[2]
    hidden_state = row[0].astype(f32)
    head_count = rel_bias.shape[1]
    layers = w_query.shape[0]
    query_segments = jnp.arange(length, dtype=jnp.int32) // QLEN
    row_segments = jnp.where(stream_side == 0, query_segments, segments[0])
    row_ids = jnp.broadcast_to(row_segments[None, :], (8, length))
    col_ids = jnp.broadcast_to(row_segments[:, None], (length, TILE))
    offset_onehot = (
        offset_buckets()[None, :] == jnp.arange(rel_bias.shape[0], dtype=jnp.int32)[:, None]
    ).astype(f32)
    table = jnp.einsum(
        "bh,bk->hk", jnp.pad(rel_bias, ((0, 0), (0, 8 - head_count))), offset_onehot, precision=highest
    )
    layer_weights = []
    kept_layers = []
    for layer_index in range(layers):
        weights_layer = (
            w_query[layer_index],
            w_kv[layer_index],
            w_out[layer_index],
            w_in[layer_index],
            w_down[layer_index],
            gains[2 * layer_index],
            gains[2 * layer_index + 1],
        )
        layer_weights.append(weights_layer)
        hidden_state, kept_state = layer_forward(
            hidden_state, table, row_ids, col_ids, weights_layer
        )
        kept_layers.append(kept_state)
    final_in = rms_scale(hidden_state, gains[2 * layers]).astype(bf16)
    projected = dot(final_in, w_proj)
    unit_vectors, normalize_back = jax.vjp(normalize, projected)
    vectors = unit_vectors.astype(bf16)
    own_vectors = lax.dynamic_slice_in_dim(vectors, mp_index * share_len, share_len, 0)
    query_rows, slot_count = positive.shape
    plane_slots = slot_count // 2
    own_slots = lax.dynamic_slice_in_dim(positive, stream_side * plane_slots, plane_slots, 1)
    grad_vectors, losses = score(
        vectors,
        jnp.broadcast_to(segments, (8, length)),
        top_mask.reshape(query_rows * slot_count, length),
        jnp.broadcast_to(own_slots.reshape(-1, 1), (query_rows * plane_slots, vectors.shape[1])),
    )
    query_loss = losses[:, 0][None]
    grad_projected = normalize_back(grad_vectors)[0].astype(bf16)
    grad_final = dot_nt(grad_projected, w_proj)
    grad_state, grad_gain_final = jax.vjp(rms_scale, hidden_state, gains[2 * layers])[1](grad_final)
    gain_grads = [None] * (2 * layers)
    operands = [None] * layers
    sums = jnp.zeros(table.shape, f32)
    for layer_index in reversed(range(layers)):
        kept, weights_layer = kept_layers[layer_index], layer_weights[layer_index]
        grad_state, ffn_lefts, ffn_rights, gain_grads[2 * layer_index + 1] = ffn_backward(
            grad_state, kept, weights_layer
        )
        grad_state, lefts, rights, gain_grads[2 * layer_index], part = attention_backward(
            grad_state, table, row_ids, col_ids, kept, weights_layer
        )
        operands[layer_index] = ffn_lefts + lefts + ffn_rights + rights
        sums = sums + part
    little = jnp.concatenate(
        [jnp.pad(jnp.stack(gain_grads + [grad_gain_final]), ((0, 7 - 2 * layers), (0, 0))), sums], axis=1
    )
    batch = lax.axis_size("batch")
    final_pair = (final_in, grad_projected)
    if batch % 2 == 0 and batch <= 8 and (model_width // batch) % 32 == 0:
        summed = sum_gradients(operands, final_pair, little)
    else:
        summed = sum_gradients_plainly(operands, final_pair, little)
    grad_down, grad_in, grad_out, grad_query, grad_kv, grad_proj, little = summed
    grad_bias = jnp.einsum("hk,bk->bh", little[:, model_width:], offset_onehot, precision=highest)
    rows = model_width // batch
    grad_gains = lax.dynamic_slice(little, (0, batch_index * rows), (2 * layers + 1, rows))
    grad_state = lax.dynamic_slice_in_dim(grad_state, mp_index * share_len, share_len, 0)
    return (
        own_vectors[None, None],
        query_loss,
        grad_state[None, None],
        grad_query,
        grad_kv,
        grad_out,
        grad_in,
        grad_down,
        grad_gains,
        grad_bias[:, :head_count],
        grad_proj,
    )


def solution(mesh):
    placed = (
        P("stream", "batch", "mp", None),
        P("batch", None),
        P(None, "mp", "batch", None),
        P(None, "mp"),
        P(None, None, "mp"),
        P(None, None, None, "mp"),
        P(None, None, "mp"),
        P(None, None, None, "mp"),
        P(None, None, "mp"),
        P(),
        P(None, "mp"),
        P(),
    )
    return jax.shard_map(
        on_device,
        mesh=mesh,
        in_specs=placed,
        out_specs=(
            P("stream", "batch", "mp", None),
            P("batch", "mp"),
            P("stream", "batch", "mp", None),
            P(None, "batch", "mp"),
            P(None, None, "batch", "mp"),
            P(None, "batch", "mp"),
            P(None, None, "batch", "mp"),
            P(None, "batch", "mp"),
            P(None, "batch"),
            P(None, "mp"),
            P("batch", None),
        ),
        check_vma=False,
    )
```

```python
import functools
import math

import jax
import jax.numpy as jnp
from jax import lax
from jax.experimental import pallas as pl
from jax.experimental.pallas import tpu as pltpu
from jax.sharding import PartitionSpec as P

QLEN = 32
DOCS_ROW = 8
TILE = 128
SPAN = 512


norm_eps = 1e-06
vector_eps = 1e-06
temper = 0.05
logit_scale = 32.0
bucket_edges = (12, 16, 23, 32, 46, 64, 91)
highest = lax.Precision.HIGHEST
bf16 = jnp.bfloat16
f32 = jnp.float32


def dot(a, b):
    return lax.dot_general(a, b, (((1,), (0,)), ((), ())), preferred_element_type=f32)


def dot_nt(a, b):
    return lax.dot_general(a, b, (((1,), (1,)), ((), ())), preferred_element_type=f32)


def dot_tn(a, b):
    return lax.dot_general(a, b, (((0,), (0,)), ((), ())), preferred_element_type=f32)


def offset_buckets():
    index = jnp.arange(SPAN, dtype=jnp.int32)
    offsets = jnp.where(index < SPAN // 2, index, index - SPAN)
    magnitude = jnp.abs(offsets)
    far_bucket = jnp.full(offsets.shape, 8, jnp.int32)
    for threshold in bucket_edges:
        far_bucket = far_bucket + (magnitude >= threshold).astype(jnp.int32)
    bucket = jnp.where(magnitude < 8, magnitude, jnp.minimum(far_bucket, 15))
    return bucket + jnp.where(offsets > 0, 16, 0).astype(jnp.int32)


def window(tile, tiles):
    first, last = max(0, tile - 1), min(tiles, tile + 2)
    shift = first - (tile - 1)
    return pl.ds(first * TILE, (last - first) * TILE), slice(shift * TILE, (shift + last - first) * TILE)


def fill_masks(row_ids, col_ids, mask, tiles):
    for tile in range(tiles):
        rows = pl.ds(tile * TILE, TILE)
        own = col_ids[rows, :]
        for near in range(max(0, tile - 1), min(tiles, tile + 2)):
            other = jnp.broadcast_to(row_ids[0:1, near * TILE : (near + 1) * TILE], (TILE, TILE))
            place = (near - tile + 1) * TILE
            mask[rows, place : place + TILE] = jnp.where(own == other, 0.0, -1e30)


def bias_tile(table, head):
    line = jnp.broadcast_to(table[pl.ds(head, 1), :], (TILE, SPAN))
    return pltpu.roll(line, TILE, axis=1, stride=1, stride_axis=0)[:, : 3 * TILE]


def attend_kernel(table, row_ids, col_ids, q, k, v, o, lse, mask, bias):
    tiles = q.shape[0] // TILE
    fill_masks(row_ids, col_ids, mask, tiles)
    lane = lax.broadcasted_iota(jnp.int32, (TILE, TILE), 1)
    lse[...] = jnp.zeros(lse.shape, f32)

    def pair(p, carry):
        cols = pl.ds(pl.multiple_of(p * TILE, TILE), TILE)
        for half in range(2):
            bias[half] = bias_tile(table, 2 * p + half)
        for tile in range(tiles):
            rows = pl.ds(tile * TILE, TILE)
            keys, frame = window(tile, tiles)
            queries = q[rows, cols]
            near_keys, near_values = k[keys, cols], v[keys, cols]
            outs = []
            kept = lse[rows, :]
            for half in range(2):
                mine = (lane >= 64) if half else (lane < 64)
                s = dot_nt(jnp.where(mine, queries, jnp.zeros_like(queries)), near_keys)
                s = s + bias[half][:, frame] + mask[rows, frame]
                top = jnp.max(s, axis=-1, keepdims=True)
                e = jnp.exp(s - top)
                total = jnp.sum(e, axis=-1, keepdims=True)
                weights = (e * (1.0 / total)).astype(bf16)
                outs.append(dot(weights, near_values))
                kept = jnp.where(lane == 2 * p + half, top + jnp.log(total), kept)
            lse[rows, :] = kept
            o[rows, cols] = jnp.where(lane < 64, outs[0], outs[1]).astype(bf16)
        return carry

    lax.fori_loop(0, q.shape[1] // TILE, pair, 0)


def attend(table, row_ids, col_ids, q, k, v):
    length, width = q.shape
    return pl.pallas_call(
        attend_kernel,
        out_shape=(
            jax.ShapeDtypeStruct((length, width), bf16),
            jax.ShapeDtypeStruct((length, TILE), f32),
        ),
        scratch_shapes=[pltpu.VMEM((length, 3 * TILE), f32), pltpu.VMEM((2, TILE, 3 * TILE), f32)],
        compiler_params=pltpu.CompilerParams(vmem_limit_bytes=32 * 1024 * 1024),
        cost_estimate=pl.CostEstimate(flops=10**9, bytes_accessed=3 * 10**6, transcendentals=10**6),
        name="attend",
    )(table, row_ids, col_ids, q, k, v)


def attend_back_pair(p, table, lse, q, k, v, do, dq, dk, dv, mask, bias, grid, dk_sum, dv_sum):
    tiles = q.shape[0] // TILE
    lane = lax.broadcasted_iota(jnp.int32, (TILE, TILE), 1)
    cols = pl.ds(pl.multiple_of(p * TILE, TILE), TILE)
    for half in range(2):
        bias[half] = bias_tile(table, 2 * p + half)
    grid[...] = jnp.zeros(grid.shape, f32)
    dk_sum[...] = jnp.zeros(dk_sum.shape, f32)
    dv_sum[...] = jnp.zeros(dv_sum.shape, f32)
    for tile in range(tiles):
        rows = pl.ds(tile * TILE, TILE)
        keys, frame = window(tile, tiles)
        queries, grads = q[rows, cols], do[rows, cols]
        near_keys, near_values = k[keys, cols], v[keys, cols]
        kept = lse[rows, :]
        outs = []
        for half in range(2):
            mine = (lane >= 64) if half else (lane < 64)
            own_queries = jnp.where(mine, queries, jnp.zeros_like(queries))
            own_grads = jnp.where(mine, grads, jnp.zeros_like(grads))
            log_total = jnp.sum(jnp.where(lane == 2 * p + half, kept, 0.0), axis=-1, keepdims=True)
            s = dot_nt(own_queries, near_keys)
            s = s + bias[half][:, frame] + mask[rows, frame]
            weights = jnp.exp(s - log_total)
            grad_weights = dot_nt(own_grads, near_values)
            mean = jnp.sum(weights * grad_weights, axis=-1, keepdims=True)
            ds = (weights * (grad_weights - mean)).astype(bf16)
            outs.append(dot(ds, near_keys))
            dk_sum[keys, :] += dot_tn(ds, own_queries)
            dv_sum[keys, :] += dot_tn(weights.astype(bf16), own_grads)
            grid[half, :, frame] += ds.astype(f32)
        dq[rows, cols] = jnp.where(lane < 64, outs[0], outs[1]).astype(bf16)
    dk[:, cols] = dk_sum[...].astype(bf16)
    dv[:, cols] = dv_sum[...].astype(bf16)


def diagonals(grid, half):
    row_index = lax.broadcasted_iota(jnp.int32, (TILE, SPAN), 0)
    turned = pltpu.roll(grid[half], SPAN - TILE, axis=1)
    for bit in range(7):
        moved = pltpu.roll(turned, SPAN - (1 << bit), axis=1)
        turned = jnp.where((row_index >> bit) & 1 == 1, moved, turned)
    return jnp.sum(turned, axis=0, keepdims=True)


def attend_back_kernel(
    table, row_ids, col_ids, lse, q, k, v, do, dq, dk, dv, sums, mask, bias, grid, dk_sum, dv_sum
):
    fill_masks(row_ids, col_ids, mask, q.shape[0] // TILE)
    sums[...] = jnp.zeros(sums.shape, f32)

    def pair(p, carry):
        attend_back_pair(p, table, lse, q, k, v, do, dq, dk, dv, mask, bias, grid, dk_sum, dv_sum)
        for half in range(2):
            sums[pl.ds(2 * p + half, 1), :] = diagonals(grid, half)
        return carry

    lax.fori_loop(0, q.shape[1] // TILE, pair, 0)


def attend_back(table, row_ids, col_ids, lse, q, k, v, do):
    length, width = q.shape
    grad = jax.ShapeDtypeStruct((length, width), bf16)
    return pl.pallas_call(
        attend_back_kernel,
        out_shape=(grad, grad, grad, jax.ShapeDtypeStruct(table.shape, f32)),
        scratch_shapes=[
            pltpu.VMEM((length, 3 * TILE), f32),
            pltpu.VMEM((2, TILE, 3 * TILE), f32),
            pltpu.VMEM((2, TILE, SPAN), f32),
            pltpu.VMEM((length, TILE), f32),
            pltpu.VMEM((length, TILE), f32),
        ],
        compiler_params=pltpu.CompilerParams(vmem_limit_bytes=32 * 1024 * 1024),
        cost_estimate=pl.CostEstimate(flops=25 * 10**8, bytes_accessed=4 * 10**6, transcendentals=10**6),
        name="attend_back",
    )(table, row_ids, col_ids, lse, q, k, v, do)


def rms_scale(values, gain_row):
    return (
        values * lax.rsqrt(jnp.mean(values * values, axis=-1, keepdims=True) + norm_eps) * gain_row
    )


def gated_gelu(gate, up):
    return jax.nn.gelu(gate, approximate=True) * up


def normalize(values):
    return values * lax.rsqrt(jnp.sum(values * values, axis=-1, keepdims=True) + vector_eps)


def swap(value, axis):
    return lax.ppermute(value, axis, [(0, 1), (1, 0)])


def sum_of_two(part, axis):
    mine = lax.optimization_barrier(part.astype(bf16))
    return mine.astype(f32) + swap(mine, axis).astype(f32)


def layer_forward(inputs, table, row_ids, col_ids, weights_layer):
    query_weight, kv_weight, out_weight, in_weight, down_weight, gain_attn, gain_ffn = weights_layer
    normed = rms_scale(inputs, gain_attn).astype(bf16)
    q = dot(normed, query_weight).astype(bf16)
    k = dot(normed, kv_weight[0]).astype(bf16)
    v = dot(normed, kv_weight[1]).astype(bf16)
    attended, lse = attend(table, row_ids, col_ids, q, k, v)
    middle = inputs + sum_of_two(dot_nt(attended, out_weight), "mp")
    ffn_input = rms_scale(middle, gain_ffn).astype(bf16)
    gate, up = dot(ffn_input, in_weight[0]), dot(ffn_input, in_weight[1])
    hidden = gated_gelu(gate, up).astype(bf16)
    gate, up = gate.astype(bf16), up.astype(bf16)
    output = middle + sum_of_two(dot_nt(hidden, down_weight), "mp")
    return output, (inputs, normed, q, k, v, lse, attended, middle, ffn_input, gate, up, hidden)


def ffn_backward(grad_output, kept, weights_layer):
    middle, ffn_input, gate, up, hidden = kept[7:]
    in_weight, down_weight, gain_ffn = weights_layer[3], weights_layer[4], weights_layer[6]
    grad_branch = grad_output.astype(bf16)
    grad_hidden = dot(grad_branch, down_weight)
    grad_gate, grad_up = jax.vjp(gated_gelu, gate.astype(f32), up.astype(f32))[1](grad_hidden)
    grad_gate, grad_up = grad_gate.astype(bf16), grad_up.astype(bf16)
    grad_input = sum_of_two(dot_nt(grad_gate, in_weight[0]) + dot_nt(grad_up, in_weight[1]), "mp")
    grad_mid_norm, grad_gain = jax.vjp(rms_scale, middle, gain_ffn)[1](grad_input)
    return grad_output + grad_mid_norm, (grad_branch, ffn_input), (hidden, grad_gate, grad_up), grad_gain


def attention_backward(grad_middle, table, row_ids, col_ids, kept, weights_layer):
    inputs, normed, q, k, v, lse, attended = kept[:7]
    query_weight, kv_weight, out_weight, gain_attn = (
        weights_layer[0],
        weights_layer[1],
        weights_layer[2],
        weights_layer[5],
    )
    grad_attn = grad_middle.astype(bf16)
    do = dot(grad_attn, out_weight).astype(bf16)
    dq, dk, dv, sums = attend_back(table, row_ids, col_ids, lse, q, k, v, do)
    grad_normed = sum_of_two(
        dot_nt(dq, query_weight) + dot_nt(dk, kv_weight[0]) + dot_nt(dv, kv_weight[1]), "mp"
    )
    grad_in_norm, grad_gain = jax.vjp(rms_scale, inputs, gain_attn)[1](grad_normed)
    return grad_middle + grad_in_norm, (grad_attn, normed), (attended, dq, dk, dv), grad_gain, sums


def mesh_id(stream, batch):
    return {"stream": stream, "batch": batch}


def send(source, target, send_sem, recv_sem, device):
    copy = pltpu.make_async_remote_copy(
        src_ref=source,
        dst_ref=target,
        send_sem=send_sem,
        recv_sem=recv_sem,
        device_id=device,
        device_id_type=pl.DeviceIdType.MESH,
    )
    copy.start()


def await_send(source, send_sem):
    pltpu.make_async_copy(source, source, send_sem).wait()


def split_dot(contract, left, right):
    high = left.astype(bf16)
    low = (left - high.astype(f32)).astype(bf16)
    return contract(high, right) + contract(low, right)


def score_kernel(
    count,
    vectors,
    doc_row,
    top_mask,
    positive,
    grad,
    loss,
    queries,
    docs,
    raised,
    totals,
    logits,
    stats,
    own_loss,
    other_loss,
    sent_grads,
    got_grads,
    doc_sum,
    sent_docs,
    got_docs,
    core_sent,
    core_got,
    query_send,
    query_recv,
    doc_send,
    doc_recv,
    stat_send,
    stat_recv,
    loss_sems,
    grad_send,
    grad_recv,
    back_sems,
    core_sems,
):
    side, batch, half = lax.axis_index("stream"), lax.axis_index("batch"), lax.axis_index("mp")
    length, width = vectors.shape
    quarter = length // 4
    slots = quarter // QLEN
    core = {"mp": 1 - half}
    other = {"stream": 1 - side}
    mine = side * count + batch

    barrier = pltpu.get_barrier_semaphore()

    def greet(step, carry):
        peer = lax.rem(mine + step, 2 * count)
        pl.semaphore_signal(
            barrier,
            inc=1,
            device_id=mesh_id(peer // count, lax.rem(peer, count)),
            device_id_type=pl.DeviceIdType.MESH,
        )
        return carry

    lax.fori_loop(1, 2 * count, greet, 0)
    pl.semaphore_signal(barrier, inc=1, device_id=core, device_id_type=pl.DeviceIdType.MESH)
    pl.semaphore_wait(barrier, 2 * count)

    def query_part(plane):
        return vectors.at[pl.ds(pl.multiple_of(half * (length // 2), QLEN) + plane * quarter, quarter), :]

    @pl.when(side == 0)
    def _():
        def push(step, carry):
            peer = lax.rem(batch + step, count)
            send(query_part(1), queries.at[batch], query_send.at[1, peer], query_recv.at[batch], mesh_id(1, peer))

            @pl.when(step > 0)
            def _():
                send(query_part(0), queries.at[batch], query_send.at[0, peer], query_recv.at[batch], mesh_id(0, peer))

            return carry

        lax.fori_loop(0, count, push, 0)
        queries[batch] = vectors[pl.ds(pl.multiple_of(half * (length // 2), QLEN), quarter), :]

    @pl.when(side == 1)
    def _():
        send(vectors, docs, doc_send, doc_recv, mesh_id(0, batch))
        docs[...] = vectors[...]

    lane = lax.broadcasted_iota(jnp.int32, (width, length), 0)
    onehot = jnp.where(lane == jnp.broadcast_to(doc_row[0:1, :], (width, length)), 1.0, 0.0).astype(bf16)

    @pl.when(side == 0)
    def _():
        pltpu.make_async_copy(docs, docs, doc_recv).wait()

    def await_queries(source):
        @pl.when(jnp.logical_or(side == 1, source != batch))
        def _():
            pltpu.make_async_copy(queries.at[source], queries.at[source], query_recv.at[source]).wait()

    def forward(step, carry):
        source = lax.rem(batch + step, count)
        await_queries(source)
        sims = dot_nt(queries[source], docs[...]) * (1.0 / temper)
        for slot in range(slots):
            chosen = top_mask[pl.ds(source * 2 * slots + side * slots + slot, 1), :].astype(f32)
            part = jnp.exp(sims[slot * QLEN : (slot + 1) * QLEN]) * chosen
            raised[source, slot * QLEN : (slot + 1) * QLEN, :] = part
        summed = split_dot(dot_nt, raised[source], onehot)
        totals[source] = summed
        pooled = jnp.log1p(summed) * (logit_scale * temper / QLEN)
        for slot in range(slots):
            logits[pl.ds(source * slots + slot, 1), :] = jnp.sum(
                pooled[slot * QLEN : (slot + 1) * QLEN], axis=0, keepdims=True
            )
        return carry

    lax.fori_loop(0, count, forward, 0)

    doc = lax.broadcasted_iota(jnp.int32, logits.shape, 1)
    local = doc < DOCS_ROW
    scores = logits[...]
    is_positive = jnp.where(
        jnp.logical_and(local, positive[...] == doc + batch * DOCS_ROW), 1.0, 0.0
    )
    exps = jnp.sum(jnp.where(local, jnp.exp(scores), 0.0), axis=1, keepdims=True)
    hits = jnp.sum(is_positive * scores, axis=1, keepdims=True)
    stats[batch] = jnp.where(doc == 0, exps, jnp.where(doc == 1, hits, 0.0))

    def push_stats(step, carry):
        peer = lax.rem(batch + step, count)
        send(stats.at[batch], stats.at[batch], stat_send.at[peer], stat_recv.at[batch], mesh_id(side, peer))
        return carry

    lax.fori_loop(1, count, push_stats, 0)

    def take_stats(step, carry):
        peer = lax.rem(batch + step, count)
        pltpu.make_async_copy(stats.at[peer], stats.at[peer], stat_recv.at[peer]).wait()
        return carry

    lax.fori_loop(1, count, take_stats, 0)
    summed = lax.fori_loop(1, count, lambda source, total: total + stats[source], stats[0])
    log_total = jnp.log(jnp.sum(jnp.where(doc == 0, summed, 0.0), axis=1, keepdims=True))
    hit_total = jnp.sum(jnp.where(doc == 1, summed, 0.0), axis=1, keepdims=True)
    losses = jnp.broadcast_to(log_total - hit_total, logits.shape)
    sent_grad = jnp.where(local, jnp.exp(scores - log_total), 0.0) - is_positive
    logits[...] = losses
    for slot in range(slots):
        own_loss[pl.ds(slot, 1), :] = logits[pl.ds(batch * slots + slot, 1), :]
    send(own_loss, other_loss, loss_sems.at[0], loss_sems.at[1], other)
    logits[...] = sent_grad
    doc_sum[...] = jnp.zeros(doc_sum.shape, f32)

    def backward(step, carry):
        source = lax.rem(batch + step + 1, count)
        parts = []
        for slot in range(slots):
            line = logits[pl.ds(source * slots + slot, 1), :] * (logit_scale / QLEN)
            parts.append(line / (1.0 + totals[source, slot * QLEN : (slot + 1) * QLEN, :]))
        spread = split_dot(dot, jnp.concatenate(parts, axis=0), onehot)
        ds = (raised[source] * spread).astype(bf16)
        back = dot(ds, docs[...]).astype(bf16)
        doc_sum[...] += dot_tn(ds, queries[source])

        @pl.when(jnp.logical_or(side == 1, source != batch))
        def _():
            sent_grads[source] = back
            send(
                sent_grads.at[source],
                got_grads.at[side, batch],
                grad_send.at[source],
                grad_recv.at[side, batch],
                mesh_id(0, source),
            )

        @pl.when(jnp.logical_and(side == 0, source == batch))
        def _():
            got_grads[0, batch] = back

        return carry

    lax.fori_loop(0, count, backward, 0)

    @pl.when(side == 0)
    def _():
        sent_docs[...] = doc_sum[...].astype(bf16)
        send(sent_docs, got_docs, back_sems.at[0], back_sems.at[1], mesh_id(1, batch))

        def take(step, carry):
            peer = lax.rem(batch + step, count)

            @pl.when(step > 0)
            def _():
                pltpu.make_async_copy(got_grads.at[0, peer], got_grads.at[0, peer], grad_recv.at[0, peer]).wait()

            pltpu.make_async_copy(got_grads.at[1, peer], got_grads.at[1, peer], grad_recv.at[1, peer]).wait()
            return carry

        lax.fori_loop(0, count, take, 0)
        for plane in range(2):
            total = lax.fori_loop(
                1,
                count,
                lambda source, total, plane=plane: total + got_grads[plane, source].astype(f32),
                got_grads[plane, 0].astype(f32),
            )
            core_sent[plane * quarter : (plane + 1) * quarter, :] = total.astype(bf16)
        part = core_sent.at[pl.ds(0, length // 2), :]
        there = core_got.at[pl.ds(0, length // 2), :]
        send(part, there, core_sems.at[0], core_sems.at[1], core)
        pltpu.make_async_copy(there, there, core_sems.at[1]).wait()
        first = pl.multiple_of(half * (length // 2), QLEN)
        grad[pl.ds(first, length // 2), :] = core_sent[pl.ds(0, length // 2), :].astype(f32)
        grad[pl.ds(length // 2 - first, length // 2), :] = core_got[pl.ds(0, length // 2), :].astype(f32)
        await_send(part, core_sems.at[0])
        await_send(sent_docs, back_sems.at[0])

    @pl.when(side == 1)
    def _():
        pltpu.make_async_copy(got_docs, got_docs, back_sems.at[1]).wait()
        core_sent[...] = (doc_sum[...] + got_docs[...].astype(f32)).astype(bf16)
        send(core_sent, core_got, core_sems.at[0], core_sems.at[1], core)
        pltpu.make_async_copy(core_got, core_got, core_sems.at[1]).wait()
        grad[...] = (core_sent[...].astype(f32) + core_got[...].astype(f32)).astype(bf16).astype(f32)
        await_send(core_sent, core_sems.at[0])
        await_send(vectors, doc_send)

    pltpu.make_async_copy(other_loss, other_loss, loss_sems.at[1]).wait()
    lower = jnp.where(side == 0, own_loss[0:slots, :], other_loss[0:slots, :])
    upper = jnp.where(side == 0, other_loss[0:slots, :], own_loss[0:slots, :])
    loss[...] = jnp.concatenate([lower, upper], axis=0)
    await_send(own_loss, loss_sems.at[0])

    def settle(step, carry):
        peer = lax.rem(batch + step, count)

        @pl.when(step > 0)
        def _():
            await_send(stats.at[batch], stat_send.at[peer])

        @pl.when(jnp.logical_or(side == 1, step > 0))
        def _():
            await_send(sent_grads.at[peer], grad_send.at[peer])

        @pl.when(side == 0)
        def _():
            await_send(query_part(1), query_send.at[1, peer])

            @pl.when(step > 0)
            def _():
                await_send(query_part(0), query_send.at[0, peer])

        return carry

    lax.fori_loop(0, count, settle, 0)


def score(vectors, doc_row, top_mask, positive):
    count = lax.axis_size("batch")
    length, width = vectors.shape
    quarter = length // 4
    slots = quarter // QLEN
    dma = pltpu.SemaphoreType.DMA
    return pl.pallas_call(
        functools.partial(score_kernel, count),
        out_shape=(
            jax.ShapeDtypeStruct((length, width), f32),
            jax.ShapeDtypeStruct((2 * slots, width), f32),
        ),
        in_specs=[pl.BlockSpec(memory_space=pltpu.VMEM)] * 4,
        out_specs=(pl.BlockSpec(memory_space=pltpu.VMEM),) * 2,
        scratch_shapes=[
            pltpu.VMEM((count, quarter, width), bf16),
            pltpu.VMEM((length, width), bf16),
            pltpu.VMEM((count, quarter, length), f32),
            pltpu.VMEM((count, quarter, width), f32),
            pltpu.VMEM((count * slots, width), f32),
            pltpu.VMEM((count, count * slots, width), f32),
            pltpu.VMEM((8, width), f32),
            pltpu.VMEM((8, width), f32),
            pltpu.VMEM((count, quarter, width), bf16),
            pltpu.VMEM((2, count, quarter, width), bf16),
            pltpu.VMEM((length, width), f32),
            pltpu.VMEM((length, width), bf16),
            pltpu.VMEM((length, width), bf16),
            pltpu.VMEM((length, width), bf16),
            pltpu.VMEM((length, width), bf16),
            dma((2, count)),
            dma((count,)),
            dma,
            dma,
            dma((count,)),
            dma((count,)),
            dma((2,)),
            dma((count,)),
            dma((2, count)),
            dma((2,)),
            dma((2,)),
        ],
        compiler_params=pltpu.CompilerParams(
            collective_id=0, has_side_effects=True, vmem_limit_bytes=56 * 1024 * 1024
        ),
        cost_estimate=pl.CostEstimate(flops=10**9, bytes_accessed=2 * 10**6, transcendentals=10**6),
        name="score",
    )(vectors, doc_row, top_mask, positive)


CHUNK = 384


def block_copy(ref, sem):
    pltpu.make_async_copy(ref, ref, sem).wait()


class Sums:
    def __init__(self, refs):
        self.refs = refs
        self.side, batch = lax.axis_index("stream"), lax.axis_index("batch")
        self.inner, self.outer = lax.rem(batch, 2), batch // 2
        self.batch = batch
        self.count = lax.axis_size("batch") // 2

    def stream_peer(self):
        return {"stream": 1 - self.side}

    def inner_peer(self):
        return {"batch": self.batch + 1 - 2 * self.inner}

    def outer_peer(self, step):
        return {"batch": lax.rem(self.outer + step, self.count) * 2 + self.inner}

    def slot(self, n):
        return n % RING

    def send(self, source, target, stage, n, device):
        n = self.slot(n)
        send(source, target, self.refs["send"].at[stage, n], self.refs["recv"].at[stage, n], device)

    def sent(self, like, stage, n):
        block_copy(like, self.refs["send"].at[stage, self.slot(n)])

    def received(self, like, stage, n):
        block_copy(like, self.refs["recv"].at[stage, self.slot(n)])

    def store(self, n):
        pltpu.make_async_copy(self.refs["done"].at[self.slot(n)], self.refs["out"](n), self.refs["store"].at[self.slot(n)]).start()

    def stored(self, n):
        block_copy(self.refs["done"].at[self.slot(n)], self.refs["store"].at[self.slot(n)])


class StreamFirst(Sums):
    stages = 4

    def half(self, side):
        rows = self.refs["work"].shape[3] // 2
        return pl.ds(pl.multiple_of(side * rows, 16), rows)

    def start(self, n):
        r, m = self.refs, self.slot(n)
        self.send(r["work"].at[m, :, :, self.half(1 - self.side), :], r["got0"].at[m], 0, n, self.stream_peer())

    def step(self, n, stage):
        r, m = self.refs, self.slot(n)
        work, own = r["work"].at[m], self.half(self.side)
        if stage == 1:
            self.received(r["got0"].at[m], 0, n)

            def add(index, carry):
                o, i = index // 2, lax.rem(index, 2)
                total = work[o, i, own, :].astype(f32) + r["got0"][m, o, i].astype(f32)
                work[o, i, own, :] = total.astype(bf16)
                return carry

            lax.fori_loop(0, 2 * self.count, add, 0)
            self.send(work.at[:, 1 - self.inner, own, :], r["got1"].at[m], 1, n, self.inner_peer())
        if stage == 2:
            self.received(r["got1"].at[m], 1, n)

            def add(o, carry):
                total = work[o, self.inner, own, :].astype(f32) + r["got1"][m, o].astype(f32)
                work[o, self.inner, own, :] = total.astype(bf16)
                return carry

            lax.fori_loop(0, self.count, add, 0)
            for step in range(1, self.count):
                o = lax.rem(self.outer + step, self.count)
                self.send(work.at[o, self.inner, own, :], r["got2"].at[m, step - 1], 2, n, self.outer_peer(step))
        if stage == 3:
            self.received(r["got2"].at[m], 2, n)
            total = work[self.outer, self.inner, own, :].astype(f32)
            for step in range(1, self.count):
                total = total + r["got2"][m, step - 1].astype(f32)
            r["last"][m] = total.astype(bf16)
            self.send(r["last"].at[m], r["got3"].at[m], 3, n, self.stream_peer())
            if n >= RING:
                self.stored(n)
            r["done"][m, own, :] = r["last"][m].astype(f32)
            self.sent(r["got0"].at[m], 0, n)
            self.sent(r["got1"].at[m], 1, n)
            self.sent(r["got2"].at[m], 2, n)
        if stage == 4:
            self.received(r["got3"].at[m], 3, n)
            r["done"][m, self.half(1 - self.side), :] = r["got3"][m].astype(f32)
            self.store(n)
            self.sent(r["last"].at[m], 3, n)


class BatchFirst(Sums):
    stages = 3

    def start(self, n):
        r, m = self.refs, self.slot(n)
        self.send(r["work"].at[m, :, 1 - self.inner], r["got0"].at[m], 0, n, self.inner_peer())

    def step(self, n, stage):
        r, m = self.refs, self.slot(n)
        work = r["work"].at[m]
        if stage == 1:
            self.received(r["got0"].at[m], 0, n)

            def add(o, carry):
                total = work[o, self.inner].astype(f32) + r["got0"][m, o].astype(f32)
                work[o, self.inner] = total.astype(bf16)
                return carry

            lax.fori_loop(0, self.count, add, 0)
            for step in range(1, self.count):
                o = lax.rem(self.outer + step, self.count)
                self.send(work.at[o, self.inner], r["got1"].at[m, step - 1], 1, n, self.outer_peer(step))
        if stage == 2:
            self.received(r["got1"].at[m], 1, n)
            total = work[self.outer, self.inner].astype(f32)
            for step in range(1, self.count):
                total = total + r["got1"][m, step - 1].astype(f32)
            r["last"][m] = total.astype(bf16)
            self.send(r["last"].at[m], r["got2"].at[m], 2, n, self.stream_peer())
            self.sent(r["got0"].at[m], 0, n)
            self.sent(r["got1"].at[m], 1, n)
        if stage == 3:
            self.received(r["got2"].at[m], 2, n)
            if n >= RING:
                self.stored(n)
            r["done"][m] = r["last"][m].astype(f32) + r["got2"][m].astype(f32)
            self.store(n)
            self.sent(r["last"].at[m], 2, n)


RING = 4
FIRST_REFS = ("work", "got0", "got1", "got2", "got3", "last", "done", "send", "recv", "store")
LAST_REFS = ("work", "got0", "got1", "got2", "last", "done", "send", "recv", "store")


def first_scratch(outer, rows, width, ring):
    vmem, dma = pltpu.VMEM, pltpu.SemaphoreType.DMA
    half = rows // 2
    return [
        vmem((ring, outer, 2, rows, width), bf16),
        vmem((ring, outer, 2, half, width), bf16),
        vmem((ring, outer, half, width), bf16),
        vmem((ring, outer - 1, half, width), bf16),
        vmem((ring, half, width), bf16),
        vmem((ring, half, width), bf16),
        vmem((ring, rows, width), f32),
        dma((4, ring)),
        dma((4, ring)),
        dma((ring,)),
    ]


def last_scratch(outer, rows, width, ring):
    vmem, dma = pltpu.VMEM, pltpu.SemaphoreType.DMA
    return [
        vmem((ring, outer, 2, rows, width), bf16),
        vmem((ring, outer, rows, width), bf16),
        vmem((ring, outer - 1, rows, width), bf16),
        vmem((ring, rows, width), bf16),
        vmem((ring, rows, width), bf16),
        vmem((ring, rows, width), f32),
        dma((3, ring)),
        dma((3, ring)),
        dma((ring,)),
    ]


def blocks_of(wide):
    found = []
    for layer in (1, 0):
        for left, right, output, index in (("e", "hidden", 0, ()), ("n2", "gate", 1, (0,)), ("n2", "up", 1, (1,))):
            found += [(left + str(layer), right + str(layer), c * CHUNK, output, (layer,) + index) for c in range(wide // CHUNK)]
        for left, right, output, index in (("c", "o", 2, ()), ("n1", "dq", 3, ()), ("n1", "dk", 4, (0,)), ("n1", "dv", 4, (1,))):
            found.append((left + str(layer), right + str(layer), 0, output, (layer,) + index))
    return found


def back_kernel(names, made, blocks, *refs):
    given, refs = dict(zip(names, refs)), refs[len(names) :]
    (table, row_ids, col_ids, gains, little), refs = refs[:5], refs[5:]
    outs, refs = refs[:8], refs[8:]
    held, refs = dict(zip(made, refs)), refs[len(made) :]
    (acc, core_sent, core_got, mask, bias, grid, dk_sum, dv_sum, do, little_got), refs = refs[:10], refs[10:]
    (load_sems, core_sems, little_sems), refs = refs[:3], refs[3:]
    firsts, lasts = blocks[0::2], blocks[1::2]
    half = len(blocks) // 2

    def out_of(blocks):
        def place(n):
            _, _, column, output, index = blocks[n]
            return outs[output].at[index + (slice(None), pl.ds(column, CHUNK))]

        return place

    first_refs, refs = dict(zip(FIRST_REFS, refs), out=out_of(firsts)), refs[len(FIRST_REFS) :]
    last_refs, refs = dict(zip(LAST_REFS, refs), out=out_of(lasts)), refs[len(LAST_REFS) :]
    stream_first, batch_first = StreamFirst(first_refs), BatchFirst(last_refs)
    projection = BatchFirst(dict(zip(LAST_REFS, refs), out=lambda n: outs[5]))
    half_index = lax.axis_index("mp")
    core = {"mp": 1 - half_index}
    length, model = held["grad"].shape
    tiles = length // TILE

    loads = {}

    def fetch(name, source=None, target=None):
        copy = pltpu.make_async_copy(
            given[name] if source is None else source, held[name] if target is None else target, load_sems.at[len(loads)]
        )
        copy.start()
        loads[name] = [copy, False]

    def need(name):
        if name in loads and not loads[name][1]:
            loads[name][0].wait()
            loads[name][1] = True
        return held.get(name)

    def fetch_attention(layer):
        for name in ("wo", "q", "k", "v", "lse", "wq", "wk", "wv", "x"):
            source = given[name + str(layer)] if name + str(layer) in given else None
            if name == "wo":
                source = given["w_out"].at[layer]
            if name == "wq":
                source = given["w_query"].at[layer]
            if name in ("wk", "wv"):
                source = given["w_kv"].at[layer, 0 if name == "wk" else 1]
            fetch(name + str(layer), source, held[name])

    for name in ("e1", "hidden1"):
        fetch(name)
    fetch("grad")
    fetch_attention(1)
    for name in ("n21", "gate1", "up1", "o1", "n11"):
        fetch(name)
    fetch("w_down", given["w_down"].at[0])
    fetch("w_in", given["w_in"].at[0])
    for name in ("gate0", "up0", "xm0", "hidden0", "n20", "o0", "n10", "final", "dproj"):
        fetch(name)

    barrier = pltpu.get_barrier_semaphore()
    peers = [stream_first.stream_peer(), stream_first.inner_peer(), core]
    peers += [stream_first.outer_peer(step) for step in range(1, stream_first.count)]
    for peer in peers:
        pl.semaphore_signal(barrier, inc=1, device_id=peer, device_id_type=pl.DeviceIdType.MESH)
    pl.semaphore_wait(barrier, len(peers))


    def product(left, right, work):
        width = left.shape[1] // 2
        for part in range(2):
            block = dot_tn(left[:, part * width : (part + 1) * width], right).astype(bf16)
            outer = work.shape[0] // 2
            work[part * outer : (part + 1) * outer] = block.reshape((outer,) + work.shape[1:])

    def make(sums, blocks, n):
        left, right, column, _, _ = blocks[n]
        product(need(left), need(right)[:, column : column + CHUNK], sums.refs["work"].at[n % RING])
        sums.start(n)

    def little_start():
        send(little_got.at[0], little_got.at[1], little_sems.at[0], little_sems.at[1], stream_first.stream_peer())

    def little_step(stage):
        if stage == 1:
            block_copy(little_got.at[1], little_sems.at[1])
            little_got[2] = little_got[0] + little_got[1]
            send(little_got.at[2], little_got.at[3], little_sems.at[2], little_sems.at[3], stream_first.inner_peer())
        if stage == 2:
            block_copy(little_got.at[3], little_sems.at[3])
            little_got[4] = little_got[2] + little_got[3]
            for step in range(1, stream_first.count):
                send(little_got.at[4], little_got.at[4 + step], little_sems.at[4], little_sems.at[5], stream_first.outer_peer(step))
        if stage == 3:
            parts = little_got.at[pl.ds(5, stream_first.count - 1)]
            block_copy(parts, little_sems.at[5])
            total = None
            for o in range(stream_first.count):
                step = lax.rem(stream_first.outer - o + stream_first.count, stream_first.count)
                term = little_got[4 + step]
                total = term if total is None else total + term
            outs[6][...] = total
            block_copy(little_got.at[0], little_sems.at[0])
            block_copy(little_got.at[2], little_sems.at[2])
            block_copy(parts, little_sems.at[4])


    grad = held["grad"]

    def rows_of(index):
        return pl.ds(pl.multiple_of(index * TILE, TILE), TILE)

    def share(turn):
        def pack(index, carry):
            core_sent[rows_of(index), :] = acc[rows_of(index), :].astype(bf16)
            return carry

        lax.fori_loop(0, tiles, pack, 0)
        send(core_sent, core_got.at[turn % 2], core_sems.at[0, turn], core_sems.at[1, turn], core)

    def through_norm(turn, values, gain):
        block_copy(core_got.at[turn % 2], core_sems.at[1, turn])
        weight = gains[gain : gain + 1, :]

        def tile(index, total):
            rows = rows_of(index)
            given_grad = core_sent[rows, :].astype(f32) + core_got[turn % 2, rows, :].astype(f32)
            value = values[rows, :]
            scale = lax.rsqrt(jnp.mean(value * value, axis=-1, keepdims=True) + norm_eps)
            weighted = given_grad * weight
            along = jnp.mean(value * weighted, axis=-1, keepdims=True)
            grad[rows, :] = grad[rows, :] + scale * weighted - value * (scale * scale * scale * along)
            return total + jnp.sum(given_grad * (value * scale), axis=0, keepdims=True)

        total = lax.fori_loop(0, tiles, tile, jnp.zeros((1, model), f32))
        little_got[0, gain : gain + 1, 0:model] = total
        block_copy(core_sent, core_sems.at[0, turn])

    def round_grad(target):
        def pack(index, carry):
            target[rows_of(index), :] = grad[rows_of(index), :].astype(bf16)
            return carry

        lax.fori_loop(0, tiles, pack, 0)

    def ffn_tile(column):
        cols = pl.ds(column, CHUNK)

        def tile(index, carry):
            rows = pl.ds(pl.multiple_of(index * 2 * TILE, 2 * TILE), 2 * TILE)
            grad_hidden = dot(held["e0"][rows, :], held["w_down"][:, cols])
            g, u = held["gate0"][rows, cols].astype(f32), held["up0"][rows, cols].astype(f32)
            root = math.sqrt(2.0 / math.pi)
            t = jnp.tanh(root * (g + 0.044715 * (g * g * g)))
            slope = 0.5 * (1.0 + t) + (0.5 * root) * g * (1.0 - t * t) * (1.0 + (3 * 0.044715) * (g * g))
            dg = (grad_hidden * u * slope).astype(bf16)
            du = (grad_hidden * (0.5 * g * (1.0 + t))).astype(bf16)
            held["gate0"][rows, cols] = dg
            held["up0"][rows, cols] = du
            part = dot_nt(dg, held["w_in"][0, :, cols]) + dot_nt(du, held["w_in"][1, :, cols])
            acc[rows, :] = part if column == 0 else acc[rows, :] + part
            return carry

        lax.fori_loop(0, tiles // 2, tile, 0)

    def attention_start(layer):
        c = held["c" + str(layer)]
        round_grad(c)

        def tile(index, carry):
            rows = pl.ds(pl.multiple_of(index * 2 * TILE, 2 * TILE), 2 * TILE)
            do[rows, :] = dot(c[rows, :], held["wo"][...]).astype(bf16)
            return carry

        need("wo" + str(layer))
        lax.fori_loop(0, tiles // 2, tile, 0)
        for name in ("q", "k", "v", "lse"):
            need(name + str(layer))

    def attention_pair(layer, p):
        attend_back_pair(
            p, table, held["lse"], held["q"], held["k"], held["v"], do,
            held["dq" + str(layer)], held["dk" + str(layer)], held["dv" + str(layer)],
            mask, bias, grid, dk_sum, dv_sum,
        )
        for half in range(2):
            line = diagonals(grid, half)
            place = (0, pl.ds(2 * p + half, 1), pl.ds(model, SPAN))
            little_got[place] = little_got[place] + line

    def attention_end(layer, turn):
        for name in ("wq", "wk", "wv"):
            need(name + str(layer))

        def tile(index, carry):
            rows = pl.ds(pl.multiple_of(index * 2 * TILE, 2 * TILE), 2 * TILE)
            acc[rows, :] = (
                dot_nt(held["dq" + str(layer)][rows, :], held["wq"][...])
                + dot_nt(held["dk" + str(layer)][rows, :], held["wk"][...])
                + dot_nt(held["dv" + str(layer)][rows, :], held["wv"][...])
            )
            return carry

        lax.fori_loop(0, tiles // 2, tile, 0)
        share(turn)

    def piece0():
        little_got[0] = little[...]
        fill_masks(row_ids, col_ids, mask, tiles)
        need("grad")
        attention_start(1)
        attention_pair(1, 0)

    def piece4():
        need("x1")
        through_norm(0, held["x"], 2)
        fetch_attention(0)
        round_grad(held["e0"])
        for name in ("w_down", "w_in", "gate0", "up0"):
            need(name)
        ffn_tile(0)
        ffn_tile(CHUNK)

    def piece5():
        ffn_tile(2 * CHUNK)
        ffn_tile(3 * CHUNK)
        share(1)

    def piece6():
        need("xm0")
        through_norm(1, held["xm0"], 1)

    def piece7():
        attention_start(0)
        attention_pair(0, 0)

    def piece11():
        need("x0")
        through_norm(2, held["x"], 0)
        share_rows = length // 2
        outs[7][...] = grad[pl.ds(pl.multiple_of(half_index * share_rows, TILE), share_rows), :]
        little_start()

    pieces = [
        piece0,
        lambda: attention_pair(1, 1),
        lambda: attention_pair(1, 2),
        lambda: attention_end(1, 0),
        piece4,
        piece5,
        piece6,
        piece7,
        lambda: attention_pair(0, 1),
        lambda: attention_pair(0, 2),
        lambda: attention_end(0, 2),
        piece11,
    ]
    for t in range(half + 4):
        if t < half:
            make(stream_first, firsts, t)
            make(batch_first, lasts, t)
        if t == half - 4:
            product(need("final"), need("dproj")[...], projection.refs["work"].at[0])
            projection.start(0)
        if t < len(pieces):
            pieces[t]()
        for stage in (1, 2, 3, 4):
            if 0 <= t - stage < half:
                stream_first.step(t - stage, stage)
                if stage < 4:
                    batch_first.step(t - stage, stage)
            if t - stage == half - 4 and stage < 4:
                projection.step(0, stage)
                little_step(stage)
    for n in range(half - RING, half):
        stream_first.stored(n)
        batch_first.stored(n)
    projection.stored(0)


def back(chain, weights, final_pair, tables, little):
    batch = lax.axis_size("batch")
    outer = batch // 2
    length, model = chain["grad"].shape
    rows = model // batch
    narrow, wide = chain["q1"].shape[1], chain["hidden1"].shape[1]
    width = final_pair[1].shape[1]
    blocks = blocks_of(wide)
    given = dict(chain, final=final_pair[0], dproj=final_pair[1], **weights)
    vmem, dma, shape = pltpu.VMEM, pltpu.SemaphoreType.DMA, jax.ShapeDtypeStruct
    made = {"grad": (length, model), "x": (length, model), "xm0": (length, model), "lse": (length, TILE)}
    made = {name: vmem(dims, f32) for name, dims in made.items()}
    for name in ("e", "n2", "c", "n1"):
        made.update({name + layer: vmem((length, model), bf16) for layer in "01"})
    for name in ("hidden", "gate", "up"):
        made.update({name + layer: vmem((length, wide), bf16) for layer in "01"})
    for name in ("o", "dq", "dk", "dv"):
        made.update({name + layer: vmem((length, narrow), bf16) for layer in "01"})
    made.update({name: vmem((length, narrow), bf16) for name in "qkv"})
    made.update({name: vmem((model, narrow), bf16) for name in ("wo", "wq", "wk", "wv")})
    made.update(w_down=vmem((model, wide), bf16), w_in=vmem((2, model, wide), bf16))
    made.update(final=vmem((length, model), bf16), dproj=vmem((length, width), bf16))
    ins = [pl.BlockSpec(memory_space=pl.ANY)] * len(given) + [pl.BlockSpec(memory_space=vmem)] * 5
    hbm, local = pl.BlockSpec(memory_space=pl.ANY), pl.BlockSpec(memory_space=vmem)
    return pl.pallas_call(
        functools.partial(back_kernel, tuple(given), tuple(made), blocks),
        out_shape=(
            shape((2, rows, wide), f32),
            shape((2, 2, rows, wide), f32),
            shape((2, rows, narrow), f32),
            shape((2, rows, narrow), f32),
            shape((2, 2, rows, narrow), f32),
            shape((rows, width), f32),
            shape(little.shape, f32),
            shape((length // 2, model), f32),
        ),
        in_specs=ins,
        out_specs=(hbm,) * 6 + (local,) * 2,
        scratch_shapes=list(made.values())
        + [
            vmem((length, model), f32),
            vmem((length, model), bf16),
            vmem((2, length, model), bf16),
            vmem((length, 3 * TILE), f32),
            vmem((2, TILE, 3 * TILE), f32),
            vmem((2, TILE, SPAN), f32),
            vmem((length, TILE), f32),
            vmem((length, TILE), f32),
            vmem((length, narrow), bf16),
            vmem((4 + outer,) + little.shape, f32),
            dma((64,)),
            dma((2, 3)),
            dma((6,)),
        ]
        + first_scratch(outer, rows, CHUNK, RING)
        + last_scratch(outer, rows, CHUNK, RING)
        + last_scratch(outer, rows, width, 1),
        compiler_params=pltpu.CompilerParams(
            collective_id=1, has_side_effects=True, vmem_limit_bytes=62 * 1024 * 1024
        ),
        cost_estimate=pl.CostEstimate(flops=2 * 10**10, bytes_accessed=5 * 10**7, transcendentals=10**6),
        name="back",
    )(*given.values(), *tables, little)


def sum_gradients_plainly(kept, final_pair, little):
    def summed(left, right):
        part = lax.psum_scatter(dot_tn(left, right).astype(bf16), "batch", scatter_dimension=0, tiled=True)
        return sum_of_two(part, "stream")

    found = []
    for e, n2, c, n1, hidden, dg, du, o, dq, dk, dv in kept:
        found.append((
            summed(e, hidden),
            jnp.stack([summed(n2, dg), summed(n2, du)]),
            summed(c, o),
            summed(n1, dq),
            jnp.stack([summed(n1, dk), summed(n1, dv)]),
        ))
    return [jnp.stack(parts) for parts in zip(*found)] + [
        summed(*final_pair),
        lax.psum(little, ("stream", "batch")),
    ]


def on_device(
    tokens,
    segments,
    top_mask,
    positive,
    w_query,
    w_kv,
    w_out,
    w_in,
    w_down,
    gains,
    rel_bias,
    w_proj,
):
    stream_side = lax.axis_index("stream")
    batch_index = lax.axis_index("batch")
    mp_index = lax.axis_index("mp")
    row = lax.all_gather(tokens[0], "mp", axis=1, tiled=True)
    row_count, length, model_width = row.shape
    share_len = tokens.shape[2]
    hidden_state = row[0].astype(f32)
    head_count = rel_bias.shape[1]
    layers = w_query.shape[0]
    query_segments = jnp.arange(length, dtype=jnp.int32) // QLEN
    row_segments = jnp.where(stream_side == 0, query_segments, segments[0])
    row_ids = jnp.broadcast_to(row_segments[None, :], (8, length))
    col_ids = jnp.broadcast_to(row_segments[:, None], (length, TILE))
    offset_onehot = (
        offset_buckets()[None, :] == jnp.arange(rel_bias.shape[0], dtype=jnp.int32)[:, None]
    ).astype(f32)
    table = jnp.einsum(
        "bh,bk->hk", jnp.pad(rel_bias, ((0, 0), (0, 8 - head_count))), offset_onehot, precision=highest
    )
    layer_weights = []
    kept_layers = []
    for layer_index in range(layers):
        weights_layer = (
            w_query[layer_index],
            w_kv[layer_index],
            w_out[layer_index],
            w_in[layer_index],
            w_down[layer_index],
            gains[2 * layer_index],
            gains[2 * layer_index + 1],
        )
        layer_weights.append(weights_layer)
        hidden_state, kept_state = layer_forward(
            hidden_state, table, row_ids, col_ids, weights_layer
        )
        kept_layers.append(kept_state)
    final_in = rms_scale(hidden_state, gains[2 * layers]).astype(bf16)
    projected = dot(final_in, w_proj)
    unit_vectors, normalize_back = jax.vjp(normalize, projected)
    vectors = unit_vectors.astype(bf16)
    own_vectors = lax.dynamic_slice_in_dim(vectors, mp_index * share_len, share_len, 0)
    query_rows, slot_count = positive.shape
    plane_slots = slot_count // 2
    own_slots = lax.dynamic_slice_in_dim(positive, stream_side * plane_slots, plane_slots, 1)
    grad_vectors, losses = score(
        vectors,
        jnp.broadcast_to(segments, (8, length)),
        top_mask.reshape(query_rows * slot_count, length),
        jnp.broadcast_to(own_slots.reshape(-1, 1), (query_rows * plane_slots, vectors.shape[1])),
    )
    query_loss = losses[:, 0][None]
    grad_projected = normalize_back(grad_vectors)[0].astype(bf16)
    grad_final = dot_nt(grad_projected, w_proj)
    grad_state, grad_gain_final = jax.vjp(rms_scale, hidden_state, gains[2 * layers])[1](grad_final)
    gain_grads = [None] * (2 * layers)
    batch = lax.axis_size("batch")
    last = layers - 1
    grad_state, ffn_lefts, ffn_rights, gain_grads[2 * last + 1] = ffn_backward(
        grad_state, kept_layers[last], layer_weights[last]
    )
    if layers == 2 and batch % 2 == 0 and batch <= 8 and (model_width // batch) % 32 == 0:
        chain = dict(grad=grad_state)
        for name, value in zip(("e1", "n21", "hidden1", "gate1", "up1"), ffn_lefts + ffn_rights):
            chain[name] = value
        for layer, kept in enumerate(kept_layers):
            for name, value in zip(("x", "n1", "q", "k", "v", "lse", "o"), kept[:7]):
                chain[name + str(layer)] = value
        for name, value in zip(("xm0", "n20", "gate0", "up0", "hidden0"), kept_layers[0][7:]):
            chain[name] = value
        weights = dict(w_query=w_query, w_kv=w_kv, w_out=w_out, w_in=w_in, w_down=w_down)
        zero = jnp.zeros((model_width,), f32)
        little = jnp.stack([zero, zero, zero, gain_grads[3], grad_gain_final, zero, zero, zero])
        little = jnp.concatenate([little, jnp.zeros(table.shape, f32)], axis=1)
        padded_gains = jnp.pad(gains, ((0, 8 - gains.shape[0]), (0, 0)))
        summed = back(
            chain, weights, (final_in, grad_projected), (table, row_ids, col_ids, padded_gains), little
        )
        own_grad = summed[7]
    else:
        operands = [None] * layers
        sums = jnp.zeros(table.shape, f32)
        for layer_index in reversed(range(layers)):
            kept, weights_layer = kept_layers[layer_index], layer_weights[layer_index]
            if layer_index < last:
                grad_state, ffn_lefts, ffn_rights, gain_grads[2 * layer_index + 1] = ffn_backward(
                    grad_state, kept, weights_layer
                )
            grad_state, lefts, rights, gain_grads[2 * layer_index], part = attention_backward(
                grad_state, table, row_ids, col_ids, kept, weights_layer
            )
            operands[layer_index] = ffn_lefts + lefts + ffn_rights + rights
            sums = sums + part
        little = jnp.concatenate(
            [jnp.pad(jnp.stack(gain_grads + [grad_gain_final]), ((0, 7 - 2 * layers), (0, 0))), sums], axis=1
        )
        summed = sum_gradients_plainly(operands, (final_in, grad_projected), little)
        own_grad = lax.dynamic_slice_in_dim(grad_state, mp_index * share_len, share_len, 0)
    grad_down, grad_in, grad_out, grad_query, grad_kv, grad_proj, little = summed[:7]
    grad_bias = jnp.einsum("hk,bk->bh", little[:, model_width:], offset_onehot, precision=highest)
    rows = model_width // batch
    grad_gains = lax.dynamic_slice(little, (0, batch_index * rows), (2 * layers + 1, rows))
    return (
        own_vectors[None, None],
        query_loss,
        own_grad[None, None],
        grad_query,
        grad_kv,
        grad_out,
        grad_in,
        grad_down,
        grad_gains,
        grad_bias[:, :head_count],
        grad_proj,
    )


def solution(mesh):
    placed = (
        P("stream", "batch", "mp", None),
        P("batch", None),
        P(None, "mp", "batch", None),
        P(None, "mp"),
        P(None, None, "mp"),
        P(None, None, None, "mp"),
        P(None, None, "mp"),
        P(None, None, None, "mp"),
        P(None, None, "mp"),
        P(),
        P(None, "mp"),
        P(),
    )
    return jax.shard_map(
        on_device,
        mesh=mesh,
        in_specs=placed,
        out_specs=(
            P("stream", "batch", "mp", None),
            P("batch", "mp"),
            P("stream", "batch", "mp", None),
            P(None, "batch", "mp"),
            P(None, None, "batch", "mp"),
            P(None, "batch", "mp"),
            P(None, None, "batch", "mp"),
            P(None, "batch", "mp"),
            P(None, "batch"),
            P(None, "mp"),
            P("batch", None),
        ),
        check_vma=False,
    )
```

```python
import functools
import math

import jax
import jax.numpy as jnp
from jax import lax
from jax.experimental import pallas as pl
from jax.experimental.pallas import tpu as pltpu
from jax.sharding import PartitionSpec as P

QLEN = 32
DOCS_ROW = 8
TILE = 128
SPAN = 512


norm_eps = 1e-06
vector_eps = 1e-06
temper = 0.05
logit_scale = 32.0
bucket_edges = (12, 16, 23, 32, 46, 64, 91)
highest = lax.Precision.HIGHEST
bf16 = jnp.bfloat16
f32 = jnp.float32


def dot(a, b):
    return lax.dot_general(a, b, (((1,), (0,)), ((), ())), preferred_element_type=f32)


def dot_nt(a, b):
    return lax.dot_general(a, b, (((1,), (1,)), ((), ())), preferred_element_type=f32)


def dot_tn(a, b):
    return lax.dot_general(a, b, (((0,), (0,)), ((), ())), preferred_element_type=f32)


def offset_buckets():
    index = jnp.arange(SPAN, dtype=jnp.int32)
    offsets = jnp.where(index < SPAN // 2, index, index - SPAN)
    magnitude = jnp.abs(offsets)
    far_bucket = jnp.full(offsets.shape, 8, jnp.int32)
    for threshold in bucket_edges:
        far_bucket = far_bucket + (magnitude >= threshold).astype(jnp.int32)
    bucket = jnp.where(magnitude < 8, magnitude, jnp.minimum(far_bucket, 15))
    return bucket + jnp.where(offsets > 0, 16, 0).astype(jnp.int32)


def window(tile, tiles):
    first, last = max(0, tile - 1), min(tiles, tile + 2)
    shift = first - (tile - 1)
    return pl.ds(first * TILE, (last - first) * TILE), slice(shift * TILE, (shift + last - first) * TILE)


def fill_masks(row_ids, col_ids, mask, tiles):
    for tile in range(tiles):
        rows = pl.ds(tile * TILE, TILE)
        own = col_ids[rows, :]
        for near in range(max(0, tile - 1), min(tiles, tile + 2)):
            other = jnp.broadcast_to(row_ids[0:1, near * TILE : (near + 1) * TILE], (TILE, TILE))
            place = (near - tile + 1) * TILE
            mask[rows, place : place + TILE] = jnp.where(own == other, 0.0, -1e30)


def bias_tile(table, head):
    line = jnp.broadcast_to(table[pl.ds(head, 1), :], (TILE, SPAN))
    return pltpu.roll(line, TILE, axis=1, stride=1, stride_axis=0)[:, : 3 * TILE]


def attend_kernel(table, row_ids, col_ids, q, k, v, o, lse, mask, bias):
    tiles = q.shape[0] // TILE
    fill_masks(row_ids, col_ids, mask, tiles)
    lane = lax.broadcasted_iota(jnp.int32, (TILE, TILE), 1)
    lse[...] = jnp.zeros(lse.shape, f32)

    def pair(p, carry):
        cols = pl.ds(pl.multiple_of(p * TILE, TILE), TILE)
        for half in range(2):
            bias[half] = bias_tile(table, 2 * p + half)
        for tile in range(tiles):
            rows = pl.ds(tile * TILE, TILE)
            keys, frame = window(tile, tiles)
            queries = q[rows, cols]
            near_keys, near_values = k[keys, cols], v[keys, cols]
            outs = []
            kept = lse[rows, :]
            for half in range(2):
                mine = (lane >= 64) if half else (lane < 64)
                s = dot_nt(jnp.where(mine, queries, jnp.zeros_like(queries)), near_keys)
                s = s + bias[half][:, frame] + mask[rows, frame]
                top = jnp.max(s, axis=-1, keepdims=True)
                e = jnp.exp(s - top)
                total = jnp.sum(e, axis=-1, keepdims=True)
                weights = (e * (1.0 / total)).astype(bf16)
                outs.append(dot(weights, near_values))
                kept = jnp.where(lane == 2 * p + half, top + jnp.log(total), kept)
            lse[rows, :] = kept
            o[rows, cols] = jnp.where(lane < 64, outs[0], outs[1]).astype(bf16)
        return carry

    lax.fori_loop(0, q.shape[1] // TILE, pair, 0)


def attend(table, row_ids, col_ids, q, k, v):
    length, width = q.shape
    return pl.pallas_call(
        attend_kernel,
        out_shape=(
            jax.ShapeDtypeStruct((length, width), bf16),
            jax.ShapeDtypeStruct((length, TILE), f32),
        ),
        scratch_shapes=[pltpu.VMEM((length, 3 * TILE), f32), pltpu.VMEM((2, TILE, 3 * TILE), f32)],
        compiler_params=pltpu.CompilerParams(vmem_limit_bytes=32 * 1024 * 1024),
        cost_estimate=pl.CostEstimate(flops=10**9, bytes_accessed=3 * 10**6, transcendentals=10**6),
        name="attend",
    )(table, row_ids, col_ids, q, k, v)


def attend_back_pair(p, table, lse, q, k, v, do, dq, dk, dv, mask, bias, grid, dk_sum, dv_sum):
    tiles = q.shape[0] // TILE
    lane = lax.broadcasted_iota(jnp.int32, (TILE, TILE), 1)
    cols = pl.ds(pl.multiple_of(p * TILE, TILE), TILE)
    for half in range(2):
        bias[half] = bias_tile(table, 2 * p + half)
    grid[...] = jnp.zeros(grid.shape, f32)
    dk_sum[...] = jnp.zeros(dk_sum.shape, f32)
    dv_sum[...] = jnp.zeros(dv_sum.shape, f32)
    for tile in range(tiles):
        rows = pl.ds(tile * TILE, TILE)
        keys, frame = window(tile, tiles)
        queries, grads = q[rows, cols], do[rows, cols]
        near_keys, near_values = k[keys, cols], v[keys, cols]
        kept = lse[rows, :]
        outs = []
        for half in range(2):
            mine = (lane >= 64) if half else (lane < 64)
            own_queries = jnp.where(mine, queries, jnp.zeros_like(queries))
            own_grads = jnp.where(mine, grads, jnp.zeros_like(grads))
            log_total = jnp.sum(jnp.where(lane == 2 * p + half, kept, 0.0), axis=-1, keepdims=True)
            s = dot_nt(own_queries, near_keys)
            s = s + bias[half][:, frame] + mask[rows, frame]
            weights = jnp.exp(s - log_total)
            grad_weights = dot_nt(own_grads, near_values)
            mean = jnp.sum(weights * grad_weights, axis=-1, keepdims=True)
            ds = (weights * (grad_weights - mean)).astype(bf16)
            outs.append(dot(ds, near_keys))
            dk_sum[keys, :] += dot_tn(ds, own_queries)
            dv_sum[keys, :] += dot_tn(weights.astype(bf16), own_grads)
            grid[half, :, frame] += ds.astype(f32)
        dq[rows, cols] = jnp.where(lane < 64, outs[0], outs[1]).astype(bf16)
    dk[:, cols] = dk_sum[...].astype(bf16)
    dv[:, cols] = dv_sum[...].astype(bf16)


def diagonals(grid, half):
    row_index = lax.broadcasted_iota(jnp.int32, (TILE, SPAN), 0)
    turned = pltpu.roll(grid[half], SPAN - TILE, axis=1)
    for bit in range(7):
        moved = pltpu.roll(turned, SPAN - (1 << bit), axis=1)
        turned = jnp.where((row_index >> bit) & 1 == 1, moved, turned)
    return jnp.sum(turned, axis=0, keepdims=True)


def attend_back_kernel(
    table, row_ids, col_ids, lse, q, k, v, do, dq, dk, dv, sums, mask, bias, grid, dk_sum, dv_sum
):
    fill_masks(row_ids, col_ids, mask, q.shape[0] // TILE)
    sums[...] = jnp.zeros(sums.shape, f32)

    def pair(p, carry):
        attend_back_pair(p, table, lse, q, k, v, do, dq, dk, dv, mask, bias, grid, dk_sum, dv_sum)
        for half in range(2):
            sums[pl.ds(2 * p + half, 1), :] = diagonals(grid, half)
        return carry

    lax.fori_loop(0, q.shape[1] // TILE, pair, 0)


def attend_back(table, row_ids, col_ids, lse, q, k, v, do):
    length, width = q.shape
    grad = jax.ShapeDtypeStruct((length, width), bf16)
    return pl.pallas_call(
        attend_back_kernel,
        out_shape=(grad, grad, grad, jax.ShapeDtypeStruct(table.shape, f32)),
        scratch_shapes=[
            pltpu.VMEM((length, 3 * TILE), f32),
            pltpu.VMEM((2, TILE, 3 * TILE), f32),
            pltpu.VMEM((2, TILE, SPAN), f32),
            pltpu.VMEM((length, TILE), f32),
            pltpu.VMEM((length, TILE), f32),
        ],
        compiler_params=pltpu.CompilerParams(vmem_limit_bytes=32 * 1024 * 1024),
        cost_estimate=pl.CostEstimate(flops=25 * 10**8, bytes_accessed=4 * 10**6, transcendentals=10**6),
        name="attend_back",
    )(table, row_ids, col_ids, lse, q, k, v, do)


def rms_scale(values, gain_row):
    return (
        values * lax.rsqrt(jnp.mean(values * values, axis=-1, keepdims=True) + norm_eps) * gain_row
    )


def gated_gelu(gate, up):
    return jax.nn.gelu(gate, approximate=True) * up


def normalize(values):
    return values * lax.rsqrt(jnp.sum(values * values, axis=-1, keepdims=True) + vector_eps)


def swap(value, axis):
    return lax.ppermute(value, axis, [(0, 1), (1, 0)])


def sum_of_two(part, axis):
    mine = lax.optimization_barrier(part.astype(bf16))
    return mine.astype(f32) + swap(mine, axis).astype(f32)


def layer_forward(inputs, table, row_ids, col_ids, weights_layer):
    query_weight, kv_weight, out_weight, in_weight, down_weight, gain_attn, gain_ffn = weights_layer
    normed = rms_scale(inputs, gain_attn).astype(bf16)
    q = dot(normed, query_weight).astype(bf16)
    k = dot(normed, kv_weight[0]).astype(bf16)
    v = dot(normed, kv_weight[1]).astype(bf16)
    attended, lse = attend(table, row_ids, col_ids, q, k, v)
    middle = inputs + sum_of_two(dot_nt(attended, out_weight), "mp")
    ffn_input = rms_scale(middle, gain_ffn).astype(bf16)
    gate, up = dot(ffn_input, in_weight[0]), dot(ffn_input, in_weight[1])
    hidden = gated_gelu(gate, up).astype(bf16)
    gate, up = gate.astype(bf16), up.astype(bf16)
    output = middle + sum_of_two(dot_nt(hidden, down_weight), "mp")
    return output, (inputs, normed, q, k, v, lse, attended, middle, ffn_input, gate, up, hidden)


def ffn_backward(grad_output, kept, weights_layer):
    middle, ffn_input, gate, up, hidden = kept[7:]
    in_weight, down_weight, gain_ffn = weights_layer[3], weights_layer[4], weights_layer[6]
    grad_branch = grad_output.astype(bf16)
    grad_hidden = dot(grad_branch, down_weight)
    grad_gate, grad_up = jax.vjp(gated_gelu, gate.astype(f32), up.astype(f32))[1](grad_hidden)
    grad_gate, grad_up = grad_gate.astype(bf16), grad_up.astype(bf16)
    grad_input = sum_of_two(dot_nt(grad_gate, in_weight[0]) + dot_nt(grad_up, in_weight[1]), "mp")
    grad_mid_norm, grad_gain = jax.vjp(rms_scale, middle, gain_ffn)[1](grad_input)
    return grad_output + grad_mid_norm, (grad_branch, ffn_input), (hidden, grad_gate, grad_up), grad_gain


def attention_backward(grad_middle, table, row_ids, col_ids, kept, weights_layer):
    inputs, normed, q, k, v, lse, attended = kept[:7]
    query_weight, kv_weight, out_weight, gain_attn = (
        weights_layer[0],
        weights_layer[1],
        weights_layer[2],
        weights_layer[5],
    )
    grad_attn = grad_middle.astype(bf16)
    do = dot(grad_attn, out_weight).astype(bf16)
    dq, dk, dv, sums = attend_back(table, row_ids, col_ids, lse, q, k, v, do)
    grad_normed = sum_of_two(
        dot_nt(dq, query_weight) + dot_nt(dk, kv_weight[0]) + dot_nt(dv, kv_weight[1]), "mp"
    )
    grad_in_norm, grad_gain = jax.vjp(rms_scale, inputs, gain_attn)[1](grad_normed)
    return grad_middle + grad_in_norm, (grad_attn, normed), (attended, dq, dk, dv), grad_gain, sums


def mesh_id(stream, batch):
    return {"stream": stream, "batch": batch}


def send(source, target, send_sem, recv_sem, device):
    copy = pltpu.make_async_remote_copy(
        src_ref=source,
        dst_ref=target,
        send_sem=send_sem,
        recv_sem=recv_sem,
        device_id=device,
        device_id_type=pl.DeviceIdType.MESH,
    )
    copy.start()


def await_send(source, send_sem):
    pltpu.make_async_copy(source, source, send_sem).wait()


def split_dot(contract, left, right):
    high = left.astype(bf16)
    low = (left - high.astype(f32)).astype(bf16)
    return contract(high, right) + contract(low, right)


def score_kernel(
    count,
    vectors,
    doc_row,
    top_mask,
    positive,
    grad,
    loss,
    queries,
    docs,
    raised,
    totals,
    logits,
    stats,
    own_loss,
    other_loss,
    sent_grads,
    got_grads,
    doc_sum,
    sent_docs,
    got_docs,
    core_sent,
    core_got,
    query_send,
    query_recv,
    doc_send,
    doc_recv,
    stat_send,
    stat_recv,
    loss_sems,
    grad_send,
    grad_recv,
    back_sems,
    core_sems,
):
    side, batch, half = lax.axis_index("stream"), lax.axis_index("batch"), lax.axis_index("mp")
    length, width = vectors.shape
    quarter = length // 4
    slots = quarter // QLEN
    core = {"mp": 1 - half}
    other = {"stream": 1 - side}
    mine = side * count + batch

    barrier = pltpu.get_barrier_semaphore()

    def greet(step, carry):
        peer = lax.rem(mine + step, 2 * count)
        pl.semaphore_signal(
            barrier,
            inc=1,
            device_id=mesh_id(peer // count, lax.rem(peer, count)),
            device_id_type=pl.DeviceIdType.MESH,
        )
        return carry

    lax.fori_loop(1, 2 * count, greet, 0)
    pl.semaphore_signal(barrier, inc=1, device_id=core, device_id_type=pl.DeviceIdType.MESH)
    pl.semaphore_wait(barrier, 2 * count)

    def query_part(plane):
        return vectors.at[pl.ds(pl.multiple_of(half * (length // 2), QLEN) + plane * quarter, quarter), :]

    @pl.when(side == 0)
    def _():
        def push(step, carry):
            peer = lax.rem(batch + step, count)
            send(query_part(1), queries.at[batch], query_send.at[1, peer], query_recv.at[batch], mesh_id(1, peer))

            @pl.when(step > 0)
            def _():
                send(query_part(0), queries.at[batch], query_send.at[0, peer], query_recv.at[batch], mesh_id(0, peer))

            return carry

        lax.fori_loop(0, count, push, 0)
        queries[batch] = vectors[pl.ds(pl.multiple_of(half * (length // 2), QLEN), quarter), :]

    @pl.when(side == 1)
    def _():
        send(vectors, docs, doc_send, doc_recv, mesh_id(0, batch))
        docs[...] = vectors[...]

    lane = lax.broadcasted_iota(jnp.int32, (width, length), 0)
    onehot = jnp.where(lane == jnp.broadcast_to(doc_row[0:1, :], (width, length)), 1.0, 0.0).astype(bf16)

    @pl.when(side == 0)
    def _():
        pltpu.make_async_copy(docs, docs, doc_recv).wait()

    def await_queries(source):
        @pl.when(jnp.logical_or(side == 1, source != batch))
        def _():
            pltpu.make_async_copy(queries.at[source], queries.at[source], query_recv.at[source]).wait()

    def forward(step, carry):
        source = lax.rem(batch + step, count)
        await_queries(source)
        sims = dot_nt(queries[source], docs[...]) * (1.0 / temper)
        for slot in range(slots):
            chosen = top_mask[pl.ds(source * 2 * slots + side * slots + slot, 1), :].astype(f32)
            part = jnp.exp(sims[slot * QLEN : (slot + 1) * QLEN]) * chosen
            raised[source, slot * QLEN : (slot + 1) * QLEN, :] = part
        summed = split_dot(dot_nt, raised[source], onehot)
        totals[source] = summed
        pooled = jnp.log1p(summed) * (logit_scale * temper / QLEN)
        for slot in range(slots):
            logits[pl.ds(source * slots + slot, 1), :] = jnp.sum(
                pooled[slot * QLEN : (slot + 1) * QLEN], axis=0, keepdims=True
            )
        return carry

    lax.fori_loop(0, count, forward, 0)

    doc = lax.broadcasted_iota(jnp.int32, logits.shape, 1)
    local = doc < DOCS_ROW
    scores = logits[...]
    is_positive = jnp.where(
        jnp.logical_and(local, positive[...] == doc + batch * DOCS_ROW), 1.0, 0.0
    )
    exps = jnp.sum(jnp.where(local, jnp.exp(scores), 0.0), axis=1, keepdims=True)
    hits = jnp.sum(is_positive * scores, axis=1, keepdims=True)
    stats[batch] = jnp.where(doc == 0, exps, jnp.where(doc == 1, hits, 0.0))

    def push_stats(step, carry):
        peer = lax.rem(batch + step, count)
        send(stats.at[batch], stats.at[batch], stat_send.at[peer], stat_recv.at[batch], mesh_id(side, peer))
        return carry

    lax.fori_loop(1, count, push_stats, 0)

    def take_stats(step, carry):
        peer = lax.rem(batch + step, count)
        pltpu.make_async_copy(stats.at[peer], stats.at[peer], stat_recv.at[peer]).wait()
        return carry

    lax.fori_loop(1, count, take_stats, 0)
    summed = lax.fori_loop(1, count, lambda source, total: total + stats[source], stats[0])
    log_total = jnp.log(jnp.sum(jnp.where(doc == 0, summed, 0.0), axis=1, keepdims=True))
    hit_total = jnp.sum(jnp.where(doc == 1, summed, 0.0), axis=1, keepdims=True)
    losses = jnp.broadcast_to(log_total - hit_total, logits.shape)
    sent_grad = jnp.where(local, jnp.exp(scores - log_total), 0.0) - is_positive
    logits[...] = losses
    for slot in range(slots):
        own_loss[pl.ds(slot, 1), :] = logits[pl.ds(batch * slots + slot, 1), :]
    send(own_loss, other_loss, loss_sems.at[0], loss_sems.at[1], other)
    logits[...] = sent_grad
    doc_sum[...] = jnp.zeros(doc_sum.shape, f32)

    def backward(step, carry):
        source = lax.rem(batch + step + 1, count)
        parts = []
        for slot in range(slots):
            line = logits[pl.ds(source * slots + slot, 1), :] * (logit_scale / QLEN)
            parts.append(line / (1.0 + totals[source, slot * QLEN : (slot + 1) * QLEN, :]))
        spread = split_dot(dot, jnp.concatenate(parts, axis=0), onehot)
        ds = (raised[source] * spread).astype(bf16)
        back = dot(ds, docs[...]).astype(bf16)
        doc_sum[...] += dot_tn(ds, queries[source])

        @pl.when(jnp.logical_or(side == 1, source != batch))
        def _():
            sent_grads[source] = back
            send(
                sent_grads.at[source],
                got_grads.at[side, batch],
                grad_send.at[source],
                grad_recv.at[side, batch],
                mesh_id(0, source),
            )

        @pl.when(jnp.logical_and(side == 0, source == batch))
        def _():
            got_grads[0, batch] = back

        return carry

    lax.fori_loop(0, count, backward, 0)

    @pl.when(side == 0)
    def _():
        sent_docs[...] = doc_sum[...].astype(bf16)
        send(sent_docs, got_docs, back_sems.at[0], back_sems.at[1], mesh_id(1, batch))

        def take(step, carry):
            peer = lax.rem(batch + step, count)

            @pl.when(step > 0)
            def _():
                pltpu.make_async_copy(got_grads.at[0, peer], got_grads.at[0, peer], grad_recv.at[0, peer]).wait()

            pltpu.make_async_copy(got_grads.at[1, peer], got_grads.at[1, peer], grad_recv.at[1, peer]).wait()
            return carry

        lax.fori_loop(0, count, take, 0)
        for plane in range(2):
            total = lax.fori_loop(
                1,
                count,
                lambda source, total, plane=plane: total + got_grads[plane, source].astype(f32),
                got_grads[plane, 0].astype(f32),
            )
            core_sent[plane * quarter : (plane + 1) * quarter, :] = total.astype(bf16)
        part = core_sent.at[pl.ds(0, length // 2), :]
        there = core_got.at[pl.ds(0, length // 2), :]
        send(part, there, core_sems.at[0], core_sems.at[1], core)
        pltpu.make_async_copy(there, there, core_sems.at[1]).wait()
        first = pl.multiple_of(half * (length // 2), QLEN)
        grad[pl.ds(first, length // 2), :] = core_sent[pl.ds(0, length // 2), :].astype(f32)
        grad[pl.ds(length // 2 - first, length // 2), :] = core_got[pl.ds(0, length // 2), :].astype(f32)
        await_send(part, core_sems.at[0])
        await_send(sent_docs, back_sems.at[0])

    @pl.when(side == 1)
    def _():
        pltpu.make_async_copy(got_docs, got_docs, back_sems.at[1]).wait()
        core_sent[...] = (doc_sum[...] + got_docs[...].astype(f32)).astype(bf16)
        send(core_sent, core_got, core_sems.at[0], core_sems.at[1], core)
        pltpu.make_async_copy(core_got, core_got, core_sems.at[1]).wait()
        grad[...] = (core_sent[...].astype(f32) + core_got[...].astype(f32)).astype(bf16).astype(f32)
        await_send(core_sent, core_sems.at[0])
        await_send(vectors, doc_send)

    pltpu.make_async_copy(other_loss, other_loss, loss_sems.at[1]).wait()
    lower = jnp.where(side == 0, own_loss[0:slots, :], other_loss[0:slots, :])
    upper = jnp.where(side == 0, other_loss[0:slots, :], own_loss[0:slots, :])
    loss[...] = jnp.concatenate([lower, upper], axis=0)
    await_send(own_loss, loss_sems.at[0])

    def settle(step, carry):
        peer = lax.rem(batch + step, count)

        @pl.when(step > 0)
        def _():
            await_send(stats.at[batch], stat_send.at[peer])

        @pl.when(jnp.logical_or(side == 1, step > 0))
        def _():
            await_send(sent_grads.at[peer], grad_send.at[peer])

        @pl.when(side == 0)
        def _():
            await_send(query_part(1), query_send.at[1, peer])

            @pl.when(step > 0)
            def _():
                await_send(query_part(0), query_send.at[0, peer])

        return carry

    lax.fori_loop(0, count, settle, 0)


def score(vectors, doc_row, top_mask, positive):
    count = lax.axis_size("batch")
    length, width = vectors.shape
    quarter = length // 4
    slots = quarter // QLEN
    dma = pltpu.SemaphoreType.DMA
    return pl.pallas_call(
        functools.partial(score_kernel, count),
        out_shape=(
            jax.ShapeDtypeStruct((length, width), f32),
            jax.ShapeDtypeStruct((2 * slots, width), f32),
        ),
        in_specs=[pl.BlockSpec(memory_space=pltpu.VMEM)] * 4,
        out_specs=(pl.BlockSpec(memory_space=pltpu.VMEM),) * 2,
        scratch_shapes=[
            pltpu.VMEM((count, quarter, width), bf16),
            pltpu.VMEM((length, width), bf16),
            pltpu.VMEM((count, quarter, length), f32),
            pltpu.VMEM((count, quarter, width), f32),
            pltpu.VMEM((count * slots, width), f32),
            pltpu.VMEM((count, count * slots, width), f32),
            pltpu.VMEM((8, width), f32),
            pltpu.VMEM((8, width), f32),
            pltpu.VMEM((count, quarter, width), bf16),
            pltpu.VMEM((2, count, quarter, width), bf16),
            pltpu.VMEM((length, width), f32),
            pltpu.VMEM((length, width), bf16),
            pltpu.VMEM((length, width), bf16),
            pltpu.VMEM((length, width), bf16),
            pltpu.VMEM((length, width), bf16),
            dma((2, count)),
            dma((count,)),
            dma,
            dma,
            dma((count,)),
            dma((count,)),
            dma((2,)),
            dma((count,)),
            dma((2, count)),
            dma((2,)),
            dma((2,)),
        ],
        compiler_params=pltpu.CompilerParams(
            collective_id=0, has_side_effects=True, vmem_limit_bytes=56 * 1024 * 1024
        ),
        cost_estimate=pl.CostEstimate(flops=10**9, bytes_accessed=2 * 10**6, transcendentals=10**6),
        name="score",
    )(vectors, doc_row, top_mask, positive)


CHUNK = 384


def block_copy(ref, sem):
    pltpu.make_async_copy(ref, ref, sem).wait()


class Sums:
    def __init__(self, refs):
        self.refs = refs
        self.side, self.batch = lax.axis_index("stream"), lax.axis_index("batch")
        self.near, self.low, self.high = lax.rem(self.batch, 2), lax.rem(self.batch // 2, 2), self.batch // 4

    def stream_peer(self):
        return {"stream": 1 - self.side}

    def near_peer(self):
        return {"batch": self.batch + 1 - 2 * self.near}

    def low_peer(self):
        return {"batch": self.batch + 2 - 4 * self.low}

    def high_peer(self):
        return {"batch": self.batch + 4 - 8 * self.high}

    def slot(self, n):
        return n % RING

    def work(self, n):
        return self.refs["work"].at[n % self.refs["work"].shape[0]]

    def got(self, stage, n):
        return self.refs["got" + str(stage)].at[self.slot(n)]

    def send(self, source, stage, n, device):
        sems = self.refs["send"], self.refs["recv"]
        send(source, self.got(stage, n), sems[0].at[stage, self.slot(n)], sems[1].at[stage, self.slot(n)], device)

    def sent(self, stage, n):
        block_copy(self.got(stage, n), self.refs["send"].at[stage, self.slot(n)])

    def received(self, stage, n):
        block_copy(self.got(stage, n), self.refs["recv"].at[stage, self.slot(n)])

    def store(self, n):
        pltpu.make_async_copy(self.refs["done"].at[self.slot(n)], self.refs["out"](n), self.refs["store"].at[self.slot(n)]).start()

    def stored(self, n):
        block_copy(self.refs["done"].at[self.slot(n)], self.refs["store"].at[self.slot(n)])

    def add(self, count, place, got, at):
        def body(index, carry):
            target = place(index)
            target[...] = (target[...].astype(f32) + got[at(index)].astype(f32)).astype(bf16)
            return carry

        lax.fori_loop(0, count, body, 0)


class StreamFirst(Sums):
    stages = 5

    def half(self, side):
        rows = self.refs["work"].shape[4] // 2
        return pl.ds(pl.multiple_of(side * rows, 16), rows)

    def start(self, n):
        self.send(self.work(n).at[:, :, :, self.half(1 - self.side), :], 0, n, self.stream_peer())

    def step(self, n, stage):
        r, m = self.refs, self.slot(n)
        work, own = self.work(n), self.half(self.side)
        if stage <= 4:
            self.received(stage - 1, n)
        if stage == 1:
            self.add(
                8,
                lambda i: work.at[i // 4, lax.rem(i // 2, 2), lax.rem(i, 2), own, :],
                self.got(0, n),
                lambda i: (i // 4, lax.rem(i // 2, 2), lax.rem(i, 2)),
            )
            self.send(work.at[:, 1 - self.low, :, own, :], 1, n, self.low_peer())
        if stage == 2:
            self.add(
                4,
                lambda i: work.at[i // 2, self.low, lax.rem(i, 2), own, :],
                self.got(1, n),
                lambda i: (i // 2, lax.rem(i, 2)),
            )
            self.send(work.at[:, self.low, 1 - self.near, own, :], 2, n, self.near_peer())
        if stage == 3:
            self.add(2, lambda i: work.at[i, self.low, self.near, own, :], self.got(2, n), lambda i: (i,))
            self.send(work.at[1 - self.high, self.low, self.near, own, :], 3, n, self.high_peer())
            self.sent(0, n)
        if stage == 4:
            total = work[self.high, self.low, self.near, own, :].astype(f32) + r["got3"][m].astype(f32)
            r["last"][m] = total.astype(bf16)
            self.send(r["last"].at[m], 4, n, self.stream_peer())
            if n >= RING:
                self.stored(n)
            r["done"][m, own, :] = r["last"][m]
            for earlier in range(1, 4):
                self.sent(earlier, n)
        if stage == 5:
            self.received(4, n)
            r["done"][m, self.half(1 - self.side), :] = r["got4"][m]
            self.store(n)
            self.sent(4, n)


class BatchFirst(Sums):
    stages = 4

    def start(self, n):
        self.send(self.work(n).at[:, :, 1 - self.near], 0, n, self.near_peer())

    def step(self, n, stage):
        r, m = self.refs, self.slot(n)
        work = self.work(n)
        self.received(stage - 1, n)
        if stage == 1:
            self.add(
                4,
                lambda i: work.at[i // 2, lax.rem(i, 2), self.near],
                self.got(0, n),
                lambda i: (i // 2, lax.rem(i, 2)),
            )
            self.send(work.at[:, 1 - self.low, self.near], 1, n, self.low_peer())
        if stage == 2:
            self.add(2, lambda i: work.at[i, self.low, self.near], self.got(1, n), lambda i: (i,))
            self.send(work.at[1 - self.high, self.low, self.near], 2, n, self.high_peer())
        if stage == 3:
            total = work[self.high, self.low, self.near].astype(f32) + r["got2"][m].astype(f32)
            r["last"][m] = total.astype(bf16)
            self.send(r["last"].at[m], 3, n, self.stream_peer())
            for earlier in range(3):
                self.sent(earlier, n)
        if stage == 4:
            if n >= RING:
                self.stored(n)
            r["done"][m] = (r["last"][m].astype(f32) + r["got3"][m].astype(f32)).astype(bf16)
            self.store(n)
            self.sent(3, n)


RING = 4
WORK_RING = 5
FIRST_REFS = ("work", "got0", "got1", "got2", "got3", "got4", "last", "done", "send", "recv", "store")
LAST_REFS = ("work", "got0", "got1", "got2", "got3", "last", "done", "send", "recv", "store")


def first_scratch(rows, width, ring, work_ring):
    vmem, dma = pltpu.VMEM, pltpu.SemaphoreType.DMA
    half = rows // 2
    return [
        vmem((work_ring, 2, 2, 2, rows, width), bf16),
        vmem((ring, 2, 2, 2, half, width), bf16),
        vmem((ring, 2, 2, half, width), bf16),
        vmem((ring, 2, half, width), bf16),
        vmem((ring, half, width), bf16),
        vmem((ring, half, width), bf16),
        vmem((ring, half, width), bf16),
        vmem((ring, rows, width), bf16),
        dma((5, ring)),
        dma((5, ring)),
        dma((ring,)),
    ]


def last_scratch(rows, width, ring, work_ring):
    vmem, dma = pltpu.VMEM, pltpu.SemaphoreType.DMA
    return [
        vmem((work_ring, 2, 2, 2, rows, width), bf16),
        vmem((ring, 2, 2, rows, width), bf16),
        vmem((ring, 2, rows, width), bf16),
        vmem((ring, rows, width), bf16),
        vmem((ring, rows, width), bf16),
        vmem((ring, rows, width), bf16),
        vmem((ring, rows, width), bf16),
        dma((4, ring)),
        dma((4, ring)),
        dma((ring,)),
    ]


def blocks_of(wide):
    found = []
    for layer in (1, 0):
        for left, right, output, index in (("e", "hidden", 0, ()), ("n2", "gate", 1, (0,)), ("n2", "up", 1, (1,))):
            found += [(left + str(layer), right + str(layer), c * CHUNK, output, (layer,) + index) for c in range(wide // CHUNK)]
        for left, right, output, index in (("c", "o", 2, ()), ("n1", "dq", 3, ()), ("n1", "dk", 4, (0,)), ("n1", "dv", 4, (1,))):
            found.append((left + str(layer), right + str(layer), 0, output, (layer,) + index))
    return found


def back_kernel(names, made, blocks, *refs):
    given, refs = dict(zip(names, refs)), refs[len(names) :]
    (table, row_ids, col_ids, gains, little), refs = refs[:5], refs[5:]
    outs, refs = refs[:8], refs[8:]
    held, refs = dict(zip(made, refs)), refs[len(made) :]
    (acc, core_sent, core_got, mask, bias, grid, dk_sum, dv_sum, do, little_got), refs = refs[:10], refs[10:]
    (load_sems, core_sems, little_sems), refs = refs[:3], refs[3:]
    firsts, lasts = blocks[0::2], blocks[1::2]
    half = len(blocks) // 2

    def out_of(blocks):
        def place(n):
            _, _, column, output, index = blocks[n]
            return outs[output].at[index + (slice(None), pl.ds(column, CHUNK))]

        return place

    first_refs, refs = dict(zip(FIRST_REFS, refs), out=out_of(firsts)), refs[len(FIRST_REFS) :]
    last_refs, refs = dict(zip(LAST_REFS, refs), out=out_of(lasts)), refs[len(LAST_REFS) :]
    stream_first, batch_first = StreamFirst(first_refs), BatchFirst(last_refs)
    projection = BatchFirst(dict(zip(LAST_REFS, refs), out=lambda n: outs[5]))
    half_index = lax.axis_index("mp")
    core = {"mp": 1 - half_index}
    length, model = held["grad"].shape
    tiles = length // TILE

    loads = {}

    def fetch(name, source=None, target=None):
        copy = pltpu.make_async_copy(
            given[name] if source is None else source, held[name] if target is None else target, load_sems.at[len(loads)]
        )
        copy.start()
        loads[name] = [copy, False]

    def need(name):
        if name in loads and not loads[name][1]:
            loads[name][0].wait()
            loads[name][1] = True
        return held.get(name)

    def fetch_attention(layer):
        for name in ("wo", "q", "k", "v", "lse", "wq", "wk", "wv", "x"):
            source = given[name + str(layer)] if name + str(layer) in given else None
            if name == "wo":
                source = given["w_out"].at[layer]
            if name == "wq":
                source = given["w_query"].at[layer]
            if name in ("wk", "wv"):
                source = given["w_kv"].at[layer, 0 if name == "wk" else 1]
            fetch(name + str(layer), source, held[name])

    def fetch_ffn(layer):
        fetch("w_down" + str(layer), given["w_down"].at[layer], held["w_down"])
        fetch("w_in" + str(layer), given["w_in"].at[layer], held["w_in"])
        fetch("xm" + str(layer), None, held["xm"])

    fetch("grad")
    fetch("hidden1")
    fetch("w_down1", given["w_down"].at[1], held["w_down"])
    for name in ("gate1", "up1"):
        fetch(name)
    fetch("w_in1", given["w_in"].at[1], held["w_in"])
    fetch("xm1", None, held["xm"])
    fetch("n21")
    fetch_attention(1)
    for name in ("o1", "n11", "gate0", "up0", "hidden0", "n20", "o0", "n10", "final", "dproj"):
        fetch(name)

    barrier = pltpu.get_barrier_semaphore()
    peers = [stream_first.stream_peer(), stream_first.near_peer(), stream_first.low_peer(), stream_first.high_peer(), core]
    for peer in peers:
        pl.semaphore_signal(barrier, inc=1, device_id=peer, device_id_type=pl.DeviceIdType.MESH)


    def product(left, right, work):
        width = left.shape[1] // 2
        for part in range(2):
            block = dot_tn(left[:, part * width : (part + 1) * width], right).astype(bf16)
            work[part] = block.reshape(work.shape[1:])

    def make(sums, blocks, n):
        left, right, column, _, _ = blocks[n]
        product(need(left), need(right)[:, column : column + CHUNK], sums.work(n))
        if n == 0 and sums is stream_first:
            pl.semaphore_wait(barrier, len(peers))
        sums.start(n)

    def little_step(stage):
        peer = (stream_first.stream_peer, stream_first.near_peer, stream_first.low_peer, stream_first.high_peer)
        if stage > 0:
            block_copy(little_got.at[2 * stage - 1], little_sems.at[2 * stage - 1])
            total = little_got[2 * stage - 2] + little_got[2 * stage - 1]
            block_copy(little_got.at[2 * stage - 2], little_sems.at[2 * stage - 2])
            if stage == 4:
                outs[6][...] = total
            else:
                little_got[2 * stage] = total
        if stage < 4:
            send(
                little_got.at[2 * stage], little_got.at[2 * stage + 1],
                little_sems.at[2 * stage], little_sems.at[2 * stage + 1], peer[stage](),
            )


    grad = held["grad"]

    def rows_of(index):
        return pl.ds(pl.multiple_of(index * TILE, TILE), TILE)

    def share(turn):
        def pack(index, carry):
            core_sent[rows_of(index), :] = acc[rows_of(index), :].astype(bf16)
            return carry

        lax.fori_loop(0, tiles, pack, 0)
        send(core_sent, core_got.at[turn % 2], core_sems.at[0, turn], core_sems.at[1, turn], core)

    def through_norm(turn, values, gain):
        block_copy(core_got.at[turn % 2], core_sems.at[1, turn])
        weight = gains[gain : gain + 1, :]

        def tile(index, total):
            rows = rows_of(index)
            given_grad = core_sent[rows, :].astype(f32) + core_got[turn % 2, rows, :].astype(f32)
            value = values[rows, :]
            scale = lax.rsqrt(jnp.mean(value * value, axis=-1, keepdims=True) + norm_eps)
            weighted = given_grad * weight
            along = jnp.mean(value * weighted, axis=-1, keepdims=True)
            grad[rows, :] = grad[rows, :] + scale * weighted - value * (scale * scale * scale * along)
            return total + jnp.sum(given_grad * (value * scale), axis=0, keepdims=True)

        total = lax.fori_loop(0, tiles, tile, jnp.zeros((1, model), f32))
        little_got[0, gain : gain + 1, 0:model] = total
        block_copy(core_sent, core_sems.at[0, turn])

    def round_grad(target):
        def pack(index, carry):
            target[rows_of(index), :] = grad[rows_of(index), :].astype(bf16)
            return carry

        lax.fori_loop(0, tiles, pack, 0)

    def ffn_tile(layer, column):
        cols = pl.ds(column, CHUNK)
        e, gate, up = (held[name + str(layer)] for name in ("e", "gate", "up"))

        def tile(index, carry):
            rows = pl.ds(pl.multiple_of(index * 2 * TILE, 2 * TILE), 2 * TILE)
            grad_hidden = dot(e[rows, :], held["w_down"][:, cols])
            g, u = gate[rows, cols].astype(f32), up[rows, cols].astype(f32)
            root = math.sqrt(2.0 / math.pi)
            t = jnp.tanh(root * (g + 0.044715 * (g * g * g)))
            slope = 0.5 * (1.0 + t) + (0.5 * root) * g * (1.0 - t * t) * (1.0 + (3 * 0.044715) * (g * g))
            dg = (grad_hidden * u * slope).astype(bf16)
            du = (grad_hidden * (0.5 * g * (1.0 + t))).astype(bf16)
            gate[rows, cols] = dg
            up[rows, cols] = du
            part = dot_nt(dg, held["w_in"][0, :, cols]) + dot_nt(du, held["w_in"][1, :, cols])
            acc[rows, :] = part if column == 0 else acc[rows, :] + part
            return carry

        lax.fori_loop(0, tiles // 2, tile, 0)

    def attention_start(layer):
        c = held["c" + str(layer)]
        round_grad(c)

        def tile(index, carry):
            rows = pl.ds(pl.multiple_of(index * 2 * TILE, 2 * TILE), 2 * TILE)
            do[rows, :] = dot(c[rows, :], held["wo"][...]).astype(bf16)
            return carry

        need("wo" + str(layer))
        lax.fori_loop(0, tiles // 2, tile, 0)
        for name in ("q", "k", "v", "lse"):
            need(name + str(layer))

    def attention_pair(layer, p):
        attend_back_pair(
            p, table, held["lse"], held["q"], held["k"], held["v"], do,
            held["dq" + str(layer)], held["dk" + str(layer)], held["dv" + str(layer)],
            mask, bias, grid, dk_sum, dv_sum,
        )
        for half in range(2):
            line = diagonals(grid, half)
            place = (0, pl.ds(2 * p + half, 1), pl.ds(model, SPAN))
            little_got[place] = little_got[place] + line

    def attention_end(layer, turn):
        for name in ("wq", "wk", "wv"):
            need(name + str(layer))

        def tile(index, carry):
            rows = pl.ds(pl.multiple_of(index * 2 * TILE, 2 * TILE), 2 * TILE)
            acc[rows, :] = (
                dot_nt(held["dq" + str(layer)][rows, :], held["wq"][...])
                + dot_nt(held["dk" + str(layer)][rows, :], held["wk"][...])
                + dot_nt(held["dv" + str(layer)][rows, :], held["wv"][...])
            )
            return carry

        lax.fori_loop(0, tiles // 2, tile, 0)
        share(turn)

    def ffn_half(layer, part):
        if part == 0:
            for name in ("w_down", "w_in", "gate", "up"):
                need(name + str(layer))
        ffn_tile(layer, 2 * part * CHUNK)
        ffn_tile(layer, (2 * part + 1) * CHUNK)

    def piece0():
        little_got[0] = little[...]
        ffn_half(1, 0)

    def piece1():
        ffn_half(1, 1)
        share(0)
        fill_masks(row_ids, col_ids, mask, tiles)

    def piece2():
        need("xm1")
        through_norm(0, held["xm"], 3)
        fetch_ffn(0)
        attention_start(1)
        attention_pair(1, 0)

    def piece6():
        need("x1")
        through_norm(1, held["x"], 2)
        fetch_attention(0)
        round_grad(held["e0"])
        ffn_half(0, 0)

    def piece7():
        ffn_half(0, 1)
        share(2)

    def piece8():
        need("xm0")
        through_norm(2, held["xm"], 1)
        attention_start(0)
        attention_pair(0, 0)

    def piece12():
        need("x0")
        through_norm(3, held["x"], 0)
        share_rows = length // 2
        outs[7][...] = grad[pl.ds(pl.multiple_of(half_index * share_rows, TILE), share_rows), :]

    pieces = [
        piece0,
        piece1,
        piece2,
        lambda: attention_pair(1, 1),
        lambda: attention_pair(1, 2),
        lambda: attention_end(1, 1),
        piece6,
        piece7,
        piece8,
        lambda: attention_pair(0, 1),
        lambda: attention_pair(0, 2),
        lambda: attention_end(0, 3),
        piece12,
    ]
    need("grad")
    round_grad(held["e1"])
    for t in range(half + 5):
        if t < half:
            make(stream_first, firsts, t)
            make(batch_first, lasts, t)
        if t == half - 3:
            product(need("final"), need("dproj")[...], projection.work(0))
            projection.start(0)
        if t < len(pieces):
            pieces[t]()
        for stage in (1, 2, 3, 4, 5):
            if 0 <= t - stage < half:
                stream_first.step(t - stage, stage)
                if stage <= 4:
                    batch_first.step(t - stage, stage)
            if t - stage == half - 3 and stage <= 4:
                projection.step(0, stage)
        if 0 <= t - (half - 3) <= 4:
            little_step(t - (half - 3))
    for n in range(half - RING, half):
        stream_first.stored(n)
        batch_first.stored(n)
    projection.stored(0)


def back(chain, weights, final_pair, tables, little):
    batch = lax.axis_size("batch")
    length, model = chain["grad"].shape
    rows = model // batch
    narrow, wide = chain["q1"].shape[1], chain["hidden1"].shape[1]
    width = final_pair[1].shape[1]
    blocks = blocks_of(wide)
    given = dict(chain, final=final_pair[0], dproj=final_pair[1], **weights)
    vmem, dma, shape = pltpu.VMEM, pltpu.SemaphoreType.DMA, jax.ShapeDtypeStruct
    made = {"grad": (length, model), "x": (length, model), "xm": (length, model), "lse": (length, TILE)}
    made = {name: vmem(dims, f32) for name, dims in made.items()}
    for name in ("e", "n2", "c", "n1"):
        made.update({name + layer: vmem((length, model), bf16) for layer in "01"})
    for name in ("hidden", "gate", "up"):
        made.update({name + layer: vmem((length, wide), bf16) for layer in "01"})
    for name in ("o", "dq", "dk", "dv"):
        made.update({name + layer: vmem((length, narrow), bf16) for layer in "01"})
    made.update({name: vmem((length, narrow), bf16) for name in "qkv"})
    made.update({name: vmem((model, narrow), bf16) for name in ("wo", "wq", "wk", "wv")})
    made.update(w_down=vmem((model, wide), bf16), w_in=vmem((2, model, wide), bf16))
    made.update(final=vmem((length, model), bf16), dproj=vmem((length, width), bf16))
    ins = [pl.BlockSpec(memory_space=pl.ANY)] * len(given) + [pl.BlockSpec(memory_space=vmem)] * 5
    hbm, local = pl.BlockSpec(memory_space=pl.ANY), pl.BlockSpec(memory_space=vmem)
    return pl.pallas_call(
        functools.partial(back_kernel, tuple(given), tuple(made), blocks),
        out_shape=(
            shape((2, rows, wide), bf16),
            shape((2, 2, rows, wide), bf16),
            shape((2, rows, narrow), bf16),
            shape((2, rows, narrow), bf16),
            shape((2, 2, rows, narrow), bf16),
            shape((rows, width), bf16),
            shape(little.shape, f32),
            shape((length // 2, model), f32),
        ),
        in_specs=ins,
        out_specs=(hbm,) * 6 + (local,) * 2,
        scratch_shapes=list(made.values())
        + [
            vmem((length, model), f32),
            vmem((length, model), bf16),
            vmem((2, length, model), bf16),
            vmem((length, 3 * TILE), f32),
            vmem((2, TILE, 3 * TILE), f32),
            vmem((2, TILE, SPAN), f32),
            vmem((length, TILE), f32),
            vmem((length, TILE), f32),
            vmem((length, narrow), bf16),
            vmem((8,) + little.shape, f32),
            dma((64,)),
            dma((2, 4)),
            dma((8,)),
        ]
        + first_scratch(rows, CHUNK, RING, WORK_RING)
        + last_scratch(rows, CHUNK, RING, WORK_RING)
        + last_scratch(rows, width, 1, 1),
        compiler_params=pltpu.CompilerParams(
            collective_id=1, has_side_effects=True, vmem_limit_bytes=62 * 1024 * 1024
        ),
        cost_estimate=pl.CostEstimate(flops=2 * 10**10, bytes_accessed=5 * 10**7, transcendentals=10**6),
        name="back",
    )(*given.values(), *tables, little)


def place_kernel(down, into, out, query, key_value, projection, little, grad, buckets, *outs):
    for source, target in zip((grad, query, key_value, out, into, down, projection), outs[:6] + outs[8:]):
        target[...] = source[...].astype(f32)
    gains, bias = outs[6], outs[7]
    model = grad.shape[1]
    count, rows = gains.shape
    moved = pltpu.roll(little[:, 0:model], lax.rem(model - lax.axis_index("batch") * rows, model), axis=1)
    gains[...] = moved[0:count, 0:rows]
    bias[...] = lax.dot_general(
        buckets[...], little[:, model:], (((1,), (1,)), ((), ())), precision=highest, preferred_element_type=f32
    )


def place(summed, buckets, gain_count):
    down, into, out, query, key_value, projection, little, grad = summed
    shape = jax.ShapeDtypeStruct
    local = pl.BlockSpec(memory_space=pltpu.VMEM)
    return pl.pallas_call(
        place_kernel,
        out_shape=tuple(shape(value.shape, f32) for value in (grad, query, key_value, out, into, down))
        + (
            shape((gain_count, query.shape[1]), f32),
            shape((buckets.shape[0], little.shape[0]), f32),
            shape(projection.shape, f32),
        ),
        in_specs=[local] * 9,
        out_specs=(local,) * 9,
        compiler_params=pltpu.CompilerParams(vmem_limit_bytes=60 * 1024 * 1024),
        name="place",
    )(*summed, buckets)


def sum_gradients_plainly(kept, final_pair, little):
    def summed(left, right):
        part = lax.psum_scatter(dot_tn(left, right).astype(bf16), "batch", scatter_dimension=0, tiled=True)
        return sum_of_two(part, "stream")

    found = []
    for e, n2, c, n1, hidden, dg, du, o, dq, dk, dv in kept:
        found.append((
            summed(e, hidden),
            jnp.stack([summed(n2, dg), summed(n2, du)]),
            summed(c, o),
            summed(n1, dq),
            jnp.stack([summed(n1, dk), summed(n1, dv)]),
        ))
    return [jnp.stack(parts) for parts in zip(*found)] + [
        summed(*final_pair),
        lax.psum(little, ("stream", "batch")),
    ]


def on_device(
    tokens,
    segments,
    top_mask,
    positive,
    w_query,
    w_kv,
    w_out,
    w_in,
    w_down,
    gains,
    rel_bias,
    w_proj,
):
    stream_side = lax.axis_index("stream")
    batch_index = lax.axis_index("batch")
    mp_index = lax.axis_index("mp")
    row = lax.all_gather(tokens[0], "mp", axis=1, tiled=True)
    row_count, length, model_width = row.shape
    share_len = tokens.shape[2]
    hidden_state = row[0].astype(f32)
    head_count = rel_bias.shape[1]
    layers = w_query.shape[0]
    query_segments = jnp.arange(length, dtype=jnp.int32) // QLEN
    row_segments = jnp.where(stream_side == 0, query_segments, segments[0])
    row_ids = jnp.broadcast_to(row_segments[None, :], (8, length))
    col_ids = jnp.broadcast_to(row_segments[:, None], (length, TILE))
    offset_onehot = (
        offset_buckets()[None, :] == jnp.arange(rel_bias.shape[0], dtype=jnp.int32)[:, None]
    ).astype(f32)
    table = jnp.einsum(
        "bh,bk->hk", jnp.pad(rel_bias, ((0, 0), (0, 8 - head_count))), offset_onehot, precision=highest
    )
    layer_weights = []
    kept_layers = []
    for layer_index in range(layers):
        weights_layer = (
            w_query[layer_index],
            w_kv[layer_index],
            w_out[layer_index],
            w_in[layer_index],
            w_down[layer_index],
            gains[2 * layer_index],
            gains[2 * layer_index + 1],
        )
        layer_weights.append(weights_layer)
        hidden_state, kept_state = layer_forward(
            hidden_state, table, row_ids, col_ids, weights_layer
        )
        kept_layers.append(kept_state)
    final_in = rms_scale(hidden_state, gains[2 * layers]).astype(bf16)
    projected = dot(final_in, w_proj)
    unit_vectors, normalize_back = jax.vjp(normalize, projected)
    vectors = unit_vectors.astype(bf16)
    own_vectors = lax.dynamic_slice_in_dim(vectors, mp_index * share_len, share_len, 0)
    query_rows, slot_count = positive.shape
    plane_slots = slot_count // 2
    own_slots = lax.dynamic_slice_in_dim(positive, stream_side * plane_slots, plane_slots, 1)
    grad_vectors, losses = score(
        vectors,
        jnp.broadcast_to(segments, (8, length)),
        top_mask.reshape(query_rows * slot_count, length),
        jnp.broadcast_to(own_slots.reshape(-1, 1), (query_rows * plane_slots, vectors.shape[1])),
    )
    query_loss = losses[:, 0][None]
    grad_projected = normalize_back(grad_vectors)[0].astype(bf16)
    grad_final = dot_nt(grad_projected, w_proj)
    grad_state, grad_gain_final = jax.vjp(rms_scale, hidden_state, gains[2 * layers])[1](grad_final)
    gain_grads = [None] * (2 * layers)
    batch = lax.axis_size("batch")
    if layers == 2 and batch == 8:
        chain = dict(grad=grad_state)
        for layer, kept in enumerate(kept_layers):
            for name, value in zip(("x", "n1", "q", "k", "v", "lse", "o"), kept[:7]):
                chain[name + str(layer)] = value
            for name, value in zip(("xm", "n2", "gate", "up", "hidden"), kept[7:]):
                chain[name + str(layer)] = value
        weights = dict(w_query=w_query, w_kv=w_kv, w_out=w_out, w_in=w_in, w_down=w_down)
        zero = jnp.zeros((model_width,), f32)
        little = jnp.stack([zero, zero, zero, zero, grad_gain_final, zero, zero, zero])
        little = jnp.concatenate([little, jnp.zeros(table.shape, f32)], axis=1)
        padded_gains = jnp.pad(gains, ((0, 8 - gains.shape[0]), (0, 0)))
        summed = back(
            chain, weights, (final_in, grad_projected), (table, row_ids, col_ids, padded_gains), little
        )
        placed = place(summed, offset_onehot, gains.shape[0])
        own_grad, grad_query, grad_kv, grad_out, grad_in, grad_down, grad_gains, grad_bias, grad_proj = placed
    else:
        operands = [None] * layers
        sums = jnp.zeros(table.shape, f32)
        for layer_index in reversed(range(layers)):
            kept, weights_layer = kept_layers[layer_index], layer_weights[layer_index]
            grad_state, ffn_lefts, ffn_rights, gain_grads[2 * layer_index + 1] = ffn_backward(
                grad_state, kept, weights_layer
            )
            grad_state, lefts, rights, gain_grads[2 * layer_index], part = attention_backward(
                grad_state, table, row_ids, col_ids, kept, weights_layer
            )
            operands[layer_index] = ffn_lefts + lefts + ffn_rights + rights
            sums = sums + part
        little = jnp.concatenate(
            [jnp.pad(jnp.stack(gain_grads + [grad_gain_final]), ((0, 7 - 2 * layers), (0, 0))), sums], axis=1
        )
        summed = sum_gradients_plainly(operands, (final_in, grad_projected), little)
        own_grad = lax.dynamic_slice_in_dim(grad_state, mp_index * share_len, share_len, 0)
        grad_down, grad_in, grad_out, grad_query, grad_kv, grad_proj, little = summed
        grad_bias = jnp.einsum("hk,bk->bh", little[:, model_width:], offset_onehot, precision=highest)
        rows = model_width // batch
        grad_gains = lax.dynamic_slice(little, (0, batch_index * rows), (2 * layers + 1, rows))
    return (
        own_vectors[None, None],
        query_loss,
        own_grad[None, None],
        grad_query,
        grad_kv,
        grad_out,
        grad_in,
        grad_down,
        grad_gains,
        grad_bias[:, :head_count],
        grad_proj,
    )


def solution(mesh):
    placed = (
        P("stream", "batch", "mp", None),
        P("batch", None),
        P(None, "mp", "batch", None),
        P(None, "mp"),
        P(None, None, "mp"),
        P(None, None, None, "mp"),
        P(None, None, "mp"),
        P(None, None, None, "mp"),
        P(None, None, "mp"),
        P(),
        P(None, "mp"),
        P(),
    )
    return jax.shard_map(
        on_device,
        mesh=mesh,
        in_specs=placed,
        out_specs=(
            P("stream", "batch", "mp", None),
            P("batch", "mp"),
            P("stream", "batch", "mp", None),
            P(None, "batch", "mp"),
            P(None, None, "batch", "mp"),
            P(None, "batch", "mp"),
            P(None, None, "batch", "mp"),
            P(None, "batch", "mp"),
            P(None, "batch"),
            P(None, "mp"),
            P("batch", None),
        ),
        check_vma=False,
    )
```

```python
import functools
import math

import jax
import jax.numpy as jnp
from jax import lax
from jax.experimental import pallas as pl
from jax.experimental.pallas import tpu as pltpu
from jax.sharding import PartitionSpec as P

QLEN = 32
DOCS_ROW = 8
TILE = 128
STREAM, BATCH, MP = "stream", "batch", "mp"
SPAN = 512


norm_eps = 1e-06
vector_eps = 1e-06
temper = 0.05
logit_scale = 32.0
bucket_edges = (12, 16, 23, 32, 46, 64, 91)
highest = lax.Precision.HIGHEST
bf16 = jnp.bfloat16
f32 = jnp.float32


def dot(a, b):
    return lax.dot_general(a, b, (((1,), (0,)), ((), ())), preferred_element_type=f32)


def dot_nt(a, b):
    return lax.dot_general(a, b, (((1,), (1,)), ((), ())), preferred_element_type=f32)


def dot_tn(a, b):
    return lax.dot_general(a, b, (((0,), (0,)), ((), ())), preferred_element_type=f32)


def offset_buckets():
    index = jnp.arange(SPAN, dtype=jnp.int32)
    offsets = jnp.where(index < SPAN // 2, index, index - SPAN)
    magnitude = jnp.abs(offsets)
    far_bucket = jnp.full(offsets.shape, 8, jnp.int32)
    for threshold in bucket_edges:
        far_bucket = far_bucket + (magnitude >= threshold).astype(jnp.int32)
    bucket = jnp.where(magnitude < 8, magnitude, jnp.minimum(far_bucket, 15))
    return bucket + jnp.where(offsets > 0, 16, 0).astype(jnp.int32)


def bucket_places(count):
    index = lax.broadcasted_iota(jnp.int32, (count, SPAN), 1)
    offsets = jnp.where(index < SPAN // 2, index, index - SPAN)
    magnitude = jnp.abs(offsets)
    far_bucket = jnp.full(offsets.shape, 8, jnp.int32)
    for threshold in bucket_edges:
        far_bucket = far_bucket + jnp.where(magnitude >= threshold, 1, 0)
    bucket = jnp.where(magnitude < 8, magnitude, jnp.minimum(far_bucket, 15))
    bucket = bucket + jnp.where(offsets > 0, 16, 0)
    return jnp.where(bucket == lax.broadcasted_iota(jnp.int32, (count, SPAN), 0), 1.0, 0.0)


def fill_table(rel_bias, table):
    table[...] = jnp.zeros(table.shape, f32)
    table[0 : rel_bias.shape[1], :] = lax.dot_general(
        rel_bias[...],
        bucket_places(rel_bias.shape[0]),
        (((0,), (0,)), ((), ())),
        precision=highest,
        preferred_element_type=f32,
    )


def row_ids_of(segments):
    position = lax.broadcasted_iota(jnp.int32, segments.shape, 1)
    return jnp.where(lax.axis_index(STREAM) == 0, position // QLEN, segments[...])


def window(tile, tiles):
    first, last = max(0, tile - 1), min(tiles, tile + 2)
    shift = first - (tile - 1)
    return pl.ds(first * TILE, (last - first) * TILE), slice(shift * TILE, (shift + last - first) * TILE)


def fill_masks(row_ids, mask, tiles):
    ids = row_ids.astype(f32)
    lines = [jnp.broadcast_to(ids[:, tile * TILE : (tile + 1) * TILE], (TILE, TILE)) for tile in range(tiles)]
    for tile in range(tiles):
        own = jnp.transpose(lines[tile])
        for near in range(max(0, tile - 1), min(tiles, tile + 2)):
            place = (near - tile + 1) * TILE
            mask[tile * TILE : (tile + 1) * TILE, place : place + TILE] = jnp.where(own == lines[near], 0.0, -1e30)


def bias_tile(table, head):
    line = jnp.broadcast_to(table[pl.ds(head, 1), :], (TILE, SPAN))
    return pltpu.roll(line, TILE, axis=1, stride=1, stride_axis=0)[:, : 3 * TILE]


def attend_pair(p, table, q, k, v, o, lse, mask, bias):
    tiles = q.shape[0] // TILE
    lane = lax.broadcasted_iota(jnp.int32, (TILE, TILE), 1)
    cols = pl.ds(pl.multiple_of(p * TILE, TILE), TILE)
    for half in range(2):
        bias[half] = bias_tile(table, 2 * p + half)
    scores = []
    for tile in range(tiles):
        rows = pl.ds(tile * TILE, TILE)
        keys, frame = window(tile, tiles)
        queries, near_keys = q[rows, cols], k[keys, cols]
        for half in range(2):
            mine = (lane >= 64) if half else (lane < 64)
            s = dot_nt(jnp.where(mine, queries, jnp.zeros_like(queries)), near_keys)
            scores.append(s + (bias[half][:, frame] + mask[rows, frame]))
    tops = [jnp.max(s, axis=-1, keepdims=True) for s in scores]
    exps = [jnp.exp(s - top) for s, top in zip(scores, tops)]
    totals = [jnp.sum(e, axis=-1, keepdims=True) for e in exps]
    weights = [(e * (1.0 / total)).astype(bf16) for e, total in zip(exps, totals)]
    for tile in range(tiles):
        rows = pl.ds(tile * TILE, TILE)
        near_values = v[window(tile, tiles)[0], cols]
        outs = [dot(weights[2 * tile + half], near_values) for half in range(2)]
        o[rows, cols] = jnp.where(lane < 64, outs[0], outs[1]).astype(bf16)
        kept = lse[rows, :]
        for half in range(2):
            index = 2 * tile + half
            kept = jnp.where(lane == 2 * p + half, tops[index] + jnp.log(totals[index]), kept)
        lse[rows, :] = kept


def attend_back_pair(p, table, lse, q, k, v, do, dq, dk, dv, mask, bias, grid, dk_sum, dv_sum):
    tiles = q.shape[0] // TILE
    lane = lax.broadcasted_iota(jnp.int32, (TILE, TILE), 1)
    cols = pl.ds(pl.multiple_of(p * TILE, TILE), TILE)
    for half in range(2):
        bias[half] = bias_tile(table, 2 * p + half)
    grid[...] = jnp.zeros(grid.shape, f32)
    dk_sum[...] = jnp.zeros(dk_sum.shape, f32)
    dv_sum[...] = jnp.zeros(dv_sum.shape, f32)
    for first in range(0, tiles, 2):
        some = [(tile, half) for tile in range(first, min(first + 2, tiles)) for half in range(2)]
        own_queries, own_grads, weights, grad_weights = [], [], [], []
        for tile, half in some:
            rows = pl.ds(tile * TILE, TILE)
            keys, frame = window(tile, tiles)
            mine = (lane >= 64) if half else (lane < 64)
            queries, grads = q[rows, cols], do[rows, cols]
            own_queries.append(jnp.where(mine, queries, jnp.zeros_like(queries)))
            own_grads.append(jnp.where(mine, grads, jnp.zeros_like(grads)))
            log_total = jnp.sum(jnp.where(lane == 2 * p + half, lse[rows, :], 0.0), axis=-1, keepdims=True)
            s = dot_nt(own_queries[-1], k[keys, cols])
            s = s + (bias[half][:, frame] + mask[rows, frame])
            weights.append(jnp.exp(s - log_total))
            grad_weights.append(dot_nt(own_grads[-1], v[keys, cols]))
        means = [jnp.sum(w * g, axis=-1, keepdims=True) for w, g in zip(weights, grad_weights)]
        ds = [(w * (g - mean)).astype(bf16) for w, g, mean in zip(weights, grad_weights, means)]
        outs = []
        for index, (tile, half) in enumerate(some):
            keys, frame = window(tile, tiles)
            outs.append(dot(ds[index], k[keys, cols]))
            dk_sum[keys, :] += dot_tn(ds[index], own_queries[index])
            dv_sum[keys, :] += dot_tn(weights[index].astype(bf16), own_grads[index])
            grid[half, :, frame] += ds[index].astype(f32)
        for index in range(0, len(some), 2):
            rows = pl.ds(some[index][0] * TILE, TILE)
            dq[rows, cols] = jnp.where(lane < 64, outs[index], outs[index + 1]).astype(bf16)
    dk[:, cols] = dk_sum[...].astype(bf16)
    dv[:, cols] = dv_sum[...].astype(bf16)


def diagonals(grid, half):
    row_index = lax.broadcasted_iota(jnp.int32, (TILE, SPAN), 0)
    turned = pltpu.roll(grid[half], SPAN - TILE, axis=1)
    for bit in range(7):
        moved = pltpu.roll(turned, SPAN - (1 << bit), axis=1)
        turned = jnp.where((row_index >> bit) & 1 == 1, moved, turned)
    return jnp.sum(turned, axis=0, keepdims=True)


def attend_back_kernel(
    table, row_ids, lse, q, k, v, do, dq, dk, dv, sums, mask, bias, grid, dk_sum, dv_sum
):
    fill_masks(row_ids[...], mask, q.shape[0] // TILE)
    sums[...] = jnp.zeros(sums.shape, f32)

    def pair(p, carry):
        attend_back_pair(p, table, lse, q, k, v, do, dq, dk, dv, mask, bias, grid, dk_sum, dv_sum)
        for half in range(2):
            sums[pl.ds(2 * p + half, 1), :] = diagonals(grid, half)
        return carry

    lax.fori_loop(0, q.shape[1] // TILE, pair, 0)


def attend_back(table, row_ids, lse, q, k, v, do):
    length, width = q.shape
    grad = jax.ShapeDtypeStruct((length, width), bf16)
    return pl.pallas_call(
        attend_back_kernel,
        out_shape=(grad, grad, grad, jax.ShapeDtypeStruct(table.shape, f32)),
        scratch_shapes=[
            pltpu.VMEM((length, 3 * TILE), f32),
            pltpu.VMEM((2, TILE, 3 * TILE), f32),
            pltpu.VMEM((2, TILE, SPAN), f32),
            pltpu.VMEM((length, TILE), f32),
            pltpu.VMEM((length, TILE), f32),
        ],
        compiler_params=pltpu.CompilerParams(vmem_limit_bytes=32 * 1024 * 1024),
        cost_estimate=pl.CostEstimate(flops=25 * 10**8, bytes_accessed=4 * 10**6, transcendentals=10**6),
        name="attend_back",
    )(table, row_ids, lse, q, k, v, do)


def rms_scale(values, gain_row):
    return (
        values * lax.rsqrt(jnp.mean(values * values, axis=-1, keepdims=True) + norm_eps) * gain_row
    )


def gated_gelu(gate, up):
    return jax.nn.gelu(gate, approximate=True) * up


def normalize(values):
    return values * lax.rsqrt(jnp.sum(values * values, axis=-1, keepdims=True) + vector_eps)


def swap(value, axis):
    return lax.ppermute(value, axis, [(0, 1), (1, 0)])


def sum_of_two(part, axis):
    mine = lax.optimization_barrier(part.astype(bf16))
    return mine.astype(f32) + swap(mine, axis).astype(f32)


def ffn_backward(grad_output, kept, weights_layer):
    middle, ffn_input, gate, up, hidden = kept[7:]
    in_weight, down_weight, gain_ffn = weights_layer[3], weights_layer[4], weights_layer[6]
    grad_branch = grad_output.astype(bf16)
    grad_hidden = dot(grad_branch, down_weight)
    grad_gate, grad_up = jax.vjp(gated_gelu, gate.astype(f32), up.astype(f32))[1](grad_hidden)
    grad_gate, grad_up = grad_gate.astype(bf16), grad_up.astype(bf16)
    grad_input = sum_of_two(dot_nt(grad_gate, in_weight[0]) + dot_nt(grad_up, in_weight[1]), MP)
    grad_mid_norm, grad_gain = jax.vjp(rms_scale, middle, gain_ffn)[1](grad_input)
    return grad_output + grad_mid_norm, (grad_branch, ffn_input), (hidden, grad_gate, grad_up), grad_gain


def attention_backward(grad_middle, table, row_ids, kept, weights_layer):
    inputs, normed, q, k, v, lse, attended = kept[:7]
    query_weight, kv_weight, out_weight, gain_attn = (
        weights_layer[0],
        weights_layer[1],
        weights_layer[2],
        weights_layer[5],
    )
    grad_attn = grad_middle.astype(bf16)
    do = dot(grad_attn, out_weight).astype(bf16)
    dq, dk, dv, sums = attend_back(table, row_ids, lse, q, k, v, do)
    grad_normed = sum_of_two(
        dot_nt(dq, query_weight) + dot_nt(dk, kv_weight[0]) + dot_nt(dv, kv_weight[1]), MP
    )
    grad_in_norm, grad_gain = jax.vjp(rms_scale, inputs, gain_attn)[1](grad_normed)
    return grad_middle + grad_in_norm, (grad_attn, normed), (attended, dq, dk, dv), grad_gain, sums


def mesh_id(stream, batch):
    return {STREAM: stream, BATCH: batch}


def send(source, target, send_sem, recv_sem, device):
    copy = pltpu.make_async_remote_copy(
        src_ref=source,
        dst_ref=target,
        send_sem=send_sem,
        recv_sem=recv_sem,
        device_id=device,
        device_id_type=pl.DeviceIdType.MESH,
    )
    copy.start()


def await_send(source, send_sem):
    pltpu.make_async_copy(source, source, send_sem).wait()


def score_kernel(
    count,
    vectors,
    doc_row,
    top_mask,
    positive,
    grad,
    loss,
    queries,
    docs,
    raised,
    totals,
    logits,
    places,
    stats,
    own_loss,
    other_loss,
    sent_grads,
    got_grads,
    doc_sum,
    sent_docs,
    got_docs,
    core_sent,
    core_got,
    query_send,
    query_recv,
    doc_send,
    doc_recv,
    stat_send,
    stat_recv,
    loss_sems,
    grad_send,
    grad_recv,
    back_sems,
    core_sems,
):
    side, batch, half = lax.axis_index(STREAM), lax.axis_index(BATCH), lax.axis_index(MP)
    length, width = vectors.shape
    quarter = length // 4
    slots = quarter // QLEN
    core = {MP: 1 - half}
    other = {STREAM: 1 - side}
    mine = side * count + batch

    barrier = pltpu.get_barrier_semaphore()

    def greet(step, carry):
        peer = lax.rem(mine + step, 2 * count)
        pl.semaphore_signal(
            barrier,
            inc=1,
            device_id=mesh_id(peer // count, lax.rem(peer, count)),
            device_id_type=pl.DeviceIdType.MESH,
        )
        return carry

    lax.fori_loop(1, 2 * count, greet, 0)
    pl.semaphore_signal(barrier, inc=1, device_id=core, device_id_type=pl.DeviceIdType.MESH)
    pl.semaphore_wait(barrier, 2 * count)

    def query_part(plane):
        return vectors.at[pl.ds(pl.multiple_of(half * (length // 2), QLEN) + plane * quarter, quarter), :]

    @pl.when(side == 0)
    def _():
        def push(step, carry):
            peer = lax.rem(batch + step, count)
            send(query_part(1), queries.at[batch], query_send.at[1, peer], query_recv.at[batch], mesh_id(1, peer))

            @pl.when(step > 0)
            def _():
                send(query_part(0), queries.at[batch], query_send.at[0, peer], query_recv.at[batch], mesh_id(0, peer))

            return carry

        lax.fori_loop(0, count, push, 0)
        queries[batch] = vectors[pl.ds(pl.multiple_of(half * (length // 2), QLEN), quarter), :]

    @pl.when(side == 1)
    def _():
        send(vectors, docs, doc_send, doc_recv, mesh_id(0, batch))
        docs[...] = vectors[...]

    lane = lax.broadcasted_iota(jnp.int32, (width, length), 0)
    onehot = jnp.where(lane == jnp.broadcast_to(doc_row[0:1, :], (width, length)), 1.0, 0.0).astype(bf16)

    @pl.when(side == 0)
    def _():
        pltpu.make_async_copy(docs, docs, doc_recv).wait()

    def await_queries(source):
        @pl.when(jnp.logical_or(side == 1, source != batch))
        def _():
            pltpu.make_async_copy(queries.at[source], queries.at[source], query_recv.at[source]).wait()

    group = math.gcd(count, 4)

    def forward(first, carry):
        sources = [lax.rem(batch + first * group + step, count) for step in range(group)]
        sims = []
        for source in sources:
            await_queries(source)
            sims.append(dot_nt(queries[source], docs[...]))
        for source, sim in zip(sources, sims):
            for slot in range(slots):
                chosen = top_mask[pl.ds(source * 2 * slots + side * slots + slot, 1), :].astype(f32)
                part = jnp.exp(sim[slot * QLEN : (slot + 1) * QLEN] * (1.0 / temper)) * chosen
                raised[source, slot * QLEN : (slot + 1) * QLEN, :] = part.astype(bf16)
        summed = [dot_nt(raised[source], onehot) for source in sources]
        for source, total in zip(sources, summed):
            totals[source] = total
            pooled = jnp.log1p(total) * (logit_scale * temper / QLEN)
            for slot in range(slots):
                line = pl.ds(source * slots + slot, 1)
                logits[line, :] = jnp.sum(pooled[slot * QLEN : (slot + 1) * QLEN], axis=0, keepdims=True)
                places[line, :] = jnp.full((1, width), positive[source, side * slots + slot], jnp.int32)
        return carry

    lax.fori_loop(0, count // group, forward, 0)

    doc = lax.broadcasted_iota(jnp.int32, logits.shape, 1)
    local = doc < DOCS_ROW
    scores = logits[...]
    is_positive = jnp.where(
        jnp.logical_and(local, places[...] == doc + batch * DOCS_ROW), 1.0, 0.0
    )
    exps = jnp.sum(jnp.where(local, jnp.exp(scores), 0.0), axis=1, keepdims=True)
    hits = jnp.sum(is_positive * scores, axis=1, keepdims=True)
    stats[batch] = jnp.where(doc == 0, exps, jnp.where(doc == 1, hits, 0.0))

    def push_stats(step, carry):
        peer = lax.rem(batch + step, count)
        send(stats.at[batch], stats.at[batch], stat_send.at[peer], stat_recv.at[batch], mesh_id(side, peer))
        return carry

    lax.fori_loop(1, count, push_stats, 0)

    def take_stats(step, carry):
        peer = lax.rem(batch + step, count)
        pltpu.make_async_copy(stats.at[peer], stats.at[peer], stat_recv.at[peer]).wait()
        return carry

    lax.fori_loop(1, count, take_stats, 0)
    summed = lax.fori_loop(1, count, lambda source, total: total + stats[source], stats[0])
    log_total = jnp.log(jnp.sum(jnp.where(doc == 0, summed, 0.0), axis=1, keepdims=True))
    hit_total = jnp.sum(jnp.where(doc == 1, summed, 0.0), axis=1, keepdims=True)
    losses = jnp.broadcast_to(log_total - hit_total, logits.shape)
    sent_grad = jnp.where(local, jnp.exp(scores - log_total), 0.0) - is_positive
    logits[...] = losses
    for slot in range(slots):
        own_loss[pl.ds(slot, 1), :] = logits[pl.ds(batch * slots + slot, 1), :]
    send(own_loss, other_loss, loss_sems.at[0], loss_sems.at[1], other)
    logits[...] = sent_grad
    doc_sum[...] = jnp.zeros(doc_sum.shape, f32)

    def backward(first, carry):
        sources = [lax.rem(batch + first * group + step + 1, count) for step in range(group)]
        factors = []
        for source in sources:
            parts = []
            for slot in range(slots):
                line = logits[pl.ds(source * slots + slot, 1), :] * (logit_scale / QLEN)
                parts.append(line / (1.0 + totals[source, slot * QLEN : (slot + 1) * QLEN, :]))
            factors.append(jnp.concatenate(parts, axis=0).astype(bf16))
        spreads = [dot(factor, onehot) for factor in factors]
        ds = [(raised[source].astype(f32) * spread).astype(bf16) for source, spread in zip(sources, spreads)]
        backs = [dot(d, docs[...]).astype(bf16) for d in ds]
        for source, back in zip(sources, backs):
            sent_grads[source] = back

            @pl.when(jnp.logical_or(side == 1, source != batch))
            def _():
                send(
                    sent_grads.at[source],
                    got_grads.at[side, batch],
                    grad_send.at[source],
                    grad_recv.at[side, batch],
                    mesh_id(0, source),
                )

            @pl.when(jnp.logical_and(side == 0, source == batch))
            def _():
                got_grads[0, batch] = sent_grads[source]

        change = dot_tn(ds[0], queries[sources[0]])
        for d, source in zip(ds[1:], sources[1:]):
            change = change + dot_tn(d, queries[source])
        doc_sum[...] += change
        return carry

    lax.fori_loop(0, count // group, backward, 0)

    @pl.when(side == 0)
    def _():
        sent_docs[...] = doc_sum[...].astype(bf16)
        send(sent_docs, got_docs, back_sems.at[0], back_sems.at[1], mesh_id(1, batch))

        def take(step, carry):
            peer = lax.rem(batch + step, count)

            @pl.when(step > 0)
            def _():
                pltpu.make_async_copy(got_grads.at[0, peer], got_grads.at[0, peer], grad_recv.at[0, peer]).wait()

            pltpu.make_async_copy(got_grads.at[1, peer], got_grads.at[1, peer], grad_recv.at[1, peer]).wait()
            return carry

        lax.fori_loop(0, count, take, 0)
        for plane in range(2):
            total = lax.fori_loop(
                1,
                count,
                lambda source, total, plane=plane: total + got_grads[plane, source].astype(f32),
                got_grads[plane, 0].astype(f32),
            )
            core_sent[plane * quarter : (plane + 1) * quarter, :] = total.astype(bf16)
        part = core_sent.at[pl.ds(0, length // 2), :]
        there = core_got.at[pl.ds(0, length // 2), :]
        send(part, there, core_sems.at[0], core_sems.at[1], core)
        pltpu.make_async_copy(there, there, core_sems.at[1]).wait()
        first = pl.multiple_of(half * (length // 2), QLEN)
        grad[pl.ds(first, length // 2), :] = core_sent[pl.ds(0, length // 2), :].astype(f32)
        grad[pl.ds(length // 2 - first, length // 2), :] = core_got[pl.ds(0, length // 2), :].astype(f32)
        await_send(part, core_sems.at[0])
        await_send(sent_docs, back_sems.at[0])

    @pl.when(side == 1)
    def _():
        pltpu.make_async_copy(got_docs, got_docs, back_sems.at[1]).wait()
        core_sent[...] = (doc_sum[...] + got_docs[...].astype(f32)).astype(bf16)
        send(core_sent, core_got, core_sems.at[0], core_sems.at[1], core)
        pltpu.make_async_copy(core_got, core_got, core_sems.at[1]).wait()
        grad[...] = (core_sent[...].astype(f32) + core_got[...].astype(f32)).astype(bf16).astype(f32)
        await_send(core_sent, core_sems.at[0])
        await_send(vectors, doc_send)

    pltpu.make_async_copy(other_loss, other_loss, loss_sems.at[1]).wait()
    lower = jnp.where(side == 0, own_loss[0:slots, :], other_loss[0:slots, :])
    upper = jnp.where(side == 0, other_loss[0:slots, :], own_loss[0:slots, :])
    both = jnp.concatenate([lower, upper], axis=0)
    across = lax.broadcasted_iota(jnp.int32, both.shape, 1) == lax.broadcasted_iota(jnp.int32, both.shape, 0)
    loss[...] = jnp.sum(jnp.where(across, both, 0.0), axis=0, keepdims=True)[:, 0 : 2 * slots]
    await_send(own_loss, loss_sems.at[0])

    def settle(step, carry):
        peer = lax.rem(batch + step, count)

        @pl.when(step > 0)
        def _():
            await_send(stats.at[batch], stat_send.at[peer])

        @pl.when(jnp.logical_or(side == 1, step > 0))
        def _():
            await_send(sent_grads.at[peer], grad_send.at[peer])

        @pl.when(side == 0)
        def _():
            await_send(query_part(1), query_send.at[1, peer])

            @pl.when(step > 0)
            def _():
                await_send(query_part(0), query_send.at[0, peer])

        return carry

    lax.fori_loop(0, count, settle, 0)


def score(vectors, doc_row, top_mask, positive):
    count = lax.axis_size(BATCH)
    length, width = vectors.shape
    quarter = length // 4
    slots = quarter // QLEN
    dma = pltpu.SemaphoreType.DMA
    return pl.pallas_call(
        functools.partial(score_kernel, count),
        out_shape=(
            jax.ShapeDtypeStruct((length, width), f32),
            jax.ShapeDtypeStruct((1, 2 * slots), f32),
        ),
        in_specs=[pl.BlockSpec(memory_space=pltpu.VMEM)] * 3 + [pl.BlockSpec(memory_space=pltpu.SMEM)],
        out_specs=(pl.BlockSpec(memory_space=pltpu.VMEM),) * 2,
        scratch_shapes=[
            pltpu.VMEM((count, quarter, width), bf16),
            pltpu.VMEM((length, width), bf16),
            pltpu.VMEM((count, quarter, length), bf16),
            pltpu.VMEM((count, quarter, width), f32),
            pltpu.VMEM((count * slots, width), f32),
            pltpu.VMEM((count * slots, width), jnp.int32),
            pltpu.VMEM((count, count * slots, width), f32),
            pltpu.VMEM((8, width), f32),
            pltpu.VMEM((8, width), f32),
            pltpu.VMEM((count, quarter, width), bf16),
            pltpu.VMEM((2, count, quarter, width), bf16),
            pltpu.VMEM((length, width), f32),
            pltpu.VMEM((length, width), bf16),
            pltpu.VMEM((length, width), bf16),
            pltpu.VMEM((length, width), bf16),
            pltpu.VMEM((length, width), bf16),
            dma((2, count)),
            dma((count,)),
            dma,
            dma,
            dma((count,)),
            dma((count,)),
            dma((2,)),
            dma((count,)),
            dma((2, count)),
            dma((2,)),
            dma((2,)),
        ],
        compiler_params=pltpu.CompilerParams(
            collective_id=0, has_side_effects=True, vmem_limit_bytes=56 * 1024 * 1024
        ),
        cost_estimate=pl.CostEstimate(flops=10**9, bytes_accessed=2 * 10**6, transcendentals=10**6),
        name="score",
    )(vectors, doc_row, top_mask, positive)


def rms_rows(value, weight):
    scale = lax.rsqrt(jnp.mean(value * value, axis=-1, keepdims=True) + norm_eps)
    return (value * scale * weight).astype(bf16)


KEPT = ("x", "n1", "q", "k", "v", "lse", "o", "xm", "n2", "gate", "up", "act")


def forward_kernel(made, results, *refs):
    (tokens, w_query, w_kv, w_out, w_in, w_down, w_proj, rel_bias, segments, gains), refs = refs[:10], refs[10:]
    outs, refs = dict(zip(results, refs)), refs[len(results) :]
    held, refs = dict(zip(made, refs)), refs[len(made) :]
    row_sent, row_got, sent, got, table, mask, bias, load_sems, store_sems, row_sems, send_sems, recv_sems = refs
    half = lax.axis_index(MP)
    core = {MP: 1 - half}
    length, model = held["x0"].shape
    share = length // 2
    narrow, wide = held["q0"].shape[1], held["act0"].shape[1]
    layers = w_query.shape[0]
    loads, stores = [], []

    def fetch(source, target):
        copy = pltpu.make_async_copy(source, target, load_sems.at[len(loads)])
        copy.start()
        loads.append(copy)
        return copy

    def keep(name):
        copy = pltpu.make_async_copy(held[name], outs[name], store_sems.at[len(stores)])
        copy.start()
        stores.append(copy)

    ready = {"tokens": fetch(tokens, row_sent)}
    for layer in range(layers):
        for name, source in (
            ("wq", w_query.at[layer]),
            ("wk", w_kv.at[layer, 0]),
            ("wv", w_kv.at[layer, 1]),
            ("wo", w_out.at[layer]),
            ("wi", w_in.at[layer]),
            ("wd", w_down.at[layer]),
        ):
            ready[name + str(layer)] = fetch(source, held[name + str(layer)])
    ready["w_proj"] = fetch(w_proj, held["w_proj"])
    barrier = pltpu.get_barrier_semaphore()
    pl.semaphore_signal(barrier, inc=1, device_id=core, device_id_type=pl.DeviceIdType.MESH)
    pl.semaphore_wait(barrier, 1)
    ready["tokens"].wait()
    send(row_sent, row_got, row_sems.at[0], row_sems.at[1], core)
    fill_table(rel_bias, table)
    fill_masks(row_ids_of(segments), mask, length // TILE)

    def rows_of(index):
        return pl.ds(pl.multiple_of(index * share, TILE), share)

    def share_part(turn, index, part):
        rows = rows_of(index)
        sent[turn, rows, :] = part.astype(bf16)
        send(
            sent.at[turn, rows, :], got.at[turn, rows, :],
            send_sems.at[turn, index], recv_sems.at[turn, index], core,
        )

    def total(turn, index, base):
        rows = rows_of(index)
        block_copy(got.at[turn, rows, :], recv_sems.at[turn, index])
        return base[rows, :] + (sent[turn, rows, :].astype(f32) + got[turn, rows, :].astype(f32))

    def project(layer, index, value):
        rows, name = rows_of(index), str(layer)
        held["x" + name][rows, :] = value
        n1 = rms_rows(value, gains[2 * layer : 2 * layer + 1, :])
        held["n1" + name][rows, :] = n1
        for part in "qkv":
            held[part + name][rows, :] = dot(n1, held["w" + part + name][...]).astype(bf16)

    for part in "qkv":
        ready["w" + part + "0"].wait()
    project(0, half, row_sent[...].astype(f32))
    block_copy(row_got, row_sems.at[1])
    project(0, 1 - half, row_got[...].astype(f32))

    for layer in range(layers):
        name = str(layer)
        for kept in ("x", "n1", "q", "k", "v"):
            keep(kept + name)
        held["lse" + name][...] = jnp.zeros((length, TILE), f32)

        def pair(p, carry, name=name):
            attend_pair(
                p, table, *(held[part + name] for part in ("q", "k", "v", "o", "lse")), mask, bias
            )
            return carry

        lax.fori_loop(0, narrow // TILE, pair, 0)
        ready["wo" + name].wait()
        for index in range(2):
            share_part(2 * layer, index, dot_nt(held["o" + name][rows_of(index), :], held["wo" + name][...]))
        keep("lse" + name)
        keep("o" + name)
        ready["wi" + name].wait()
        ready["wd" + name].wait()

        def feed(index, carry, layer=layer, name=name):
            rows = rows_of(index)
            value = total(2 * layer, index, held["x" + name])
            held["xm" + name][rows, :] = value
            n2 = rms_rows(value, gains[2 * layer + 1 : 2 * layer + 2, :])
            held["n2" + name][rows, :] = n2
            for column in range(0, wide, CHUNK):
                cols = pl.ds(column, CHUNK)
                g = dot(n2, held["wi" + name][0, :, cols])
                u = dot(n2, held["wi" + name][1, :, cols])
                held["gate" + name][rows, cols] = g.astype(bf16)
                held["up" + name][rows, cols] = u.astype(bf16)
                t = jnp.tanh(math.sqrt(2.0 / math.pi) * (g + 0.044715 * (g * g * g)))
                held["act" + name][rows, cols] = (0.5 * g * (1.0 + t) * u).astype(bf16)
            share_part(2 * layer + 1, index, dot_nt(held["act" + name][rows, :], held["wd" + name][...]))
            return carry

        lax.fori_loop(0, 2, feed, 0)
        for kept in ("xm", "n2", "gate", "up", "act"):
            keep(kept + name)
        if layer + 1 < layers:
            for part in "qkv":
                ready["w" + part + str(layer + 1)].wait()

            def following(index, carry, layer=layer, name=name):
                project(layer + 1, index, total(2 * layer + 1, index, held["xm" + name]))
                return carry

            lax.fori_loop(0, 2, following, 0)

    ready["w_proj"].wait()

    def finish(index, carry):
        rows = rows_of(index)
        value = total(2 * layers - 1, index, held["xm" + str(layers - 1)])
        held["state"][rows, :] = value
        final = rms_rows(value, gains[2 * layers : 2 * layers + 1, :])
        held["final"][rows, :] = final
        projected = dot(final, held["w_proj"][...])
        held["y"][rows, :] = projected
        scale = lax.rsqrt(jnp.sum(projected * projected, axis=-1, keepdims=True) + vector_eps)
        held["vectors"][rows, :] = (projected * scale).astype(bf16)
        return carry

    lax.fori_loop(0, 2, finish, 0)
    for name in ("state", "final", "y", "vectors"):
        keep(name)
    for copy in stores:
        copy.wait()
    block_copy(row_sent, row_sems.at[0])
    for turn in range(2 * layers):
        for index in range(2):
            block_copy(sent.at[turn, rows_of(index), :], send_sems.at[turn, index])


def forward(tokens, weights, tables):
    w_query, w_kv, w_out, w_in, w_down, w_proj = weights
    layers, model, narrow = w_query.shape
    wide, width = w_down.shape[2], w_proj.shape[1]
    length = 2 * tokens.shape[0]
    vmem, dma = pltpu.VMEM, pltpu.SemaphoreType.DMA
    sizes = dict(x=(model, f32), n1=(model, bf16), q=(narrow, bf16), k=(narrow, bf16), v=(narrow, bf16), lse=(TILE, f32),
                 o=(narrow, bf16), xm=(model, f32), n2=(model, bf16), gate=(wide, bf16), up=(wide, bf16), act=(wide, bf16))
    results = {name + str(layer): sizes[name] for layer in range(layers) for name in KEPT}
    results.update(state=(model, f32), final=(model, bf16), y=(width, f32), vectors=(width, bf16))
    made = {name: vmem((length, columns), kind) for name, (columns, kind) in results.items()}
    for layer in range(layers):
        for name in ("wq", "wk", "wv", "wo"):
            made[name + str(layer)] = vmem((model, narrow), bf16)
        made["wi" + str(layer)] = vmem((2, model, wide), bf16)
        made["wd" + str(layer)] = vmem((model, wide), bf16)
    made["w_proj"] = vmem((model, width), bf16)
    hbm, local = pl.BlockSpec(memory_space=pl.ANY), pl.BlockSpec(memory_space=vmem)
    found = pl.pallas_call(
        functools.partial(forward_kernel, tuple(made), tuple(results)),
        out_shape=tuple(jax.ShapeDtypeStruct((length, columns), kind) for columns, kind in results.values()),
        in_specs=[hbm] * 7 + [local] * 3,
        out_specs=(hbm,) * len(results),
        scratch_shapes=list(made.values())
        + [
            vmem(tokens.shape, bf16),
            vmem(tokens.shape, bf16),
            vmem((2 * layers, length, model), bf16),
            vmem((2 * layers, length, model), bf16),
            vmem((8, SPAN), f32),
            vmem((length, 3 * TILE), f32),
            vmem((2, TILE, 3 * TILE), f32),
            dma((6 * layers + 2,)),
            dma((len(results),)),
            dma((2,)),
            dma((2 * layers, 2)),
            dma((2 * layers, 2)),
        ],
        compiler_params=pltpu.CompilerParams(
            collective_id=2, has_side_effects=True, vmem_limit_bytes=62 * 1024 * 1024
        ),
        cost_estimate=pl.CostEstimate(flops=10**10, bytes_accessed=5 * 10**7, transcendentals=10**6),
        name="forward",
    )(tokens, *weights, *tables)
    return dict(zip(results, found))


CHUNK = 384


def block_copy(ref, sem):
    pltpu.make_async_copy(ref, ref, sem).wait()


class Sums:
    def __init__(self, refs):
        self.refs = refs
        self.side, self.batch = lax.axis_index(STREAM), lax.axis_index(BATCH)
        self.near, self.low, self.high = lax.rem(self.batch, 2), lax.rem(self.batch // 2, 2), self.batch // 4

    def stream_peer(self):
        return {STREAM: 1 - self.side}

    def near_peer(self):
        return {BATCH: self.batch + 1 - 2 * self.near}

    def low_peer(self):
        return {BATCH: self.batch + 2 - 4 * self.low}

    def high_peer(self):
        return {BATCH: self.batch + 4 - 8 * self.high}

    def slot(self, n):
        return n % RING

    def work(self, n):
        return self.refs["work"].at[n % self.refs["work"].shape[0]]

    def got(self, stage, n):
        return self.refs["got" + str(stage)].at[self.slot(n)]

    def send(self, source, stage, n, device):
        sems = self.refs["send"], self.refs["recv"]
        send(source, self.got(stage, n), sems[0].at[stage, self.slot(n)], sems[1].at[stage, self.slot(n)], device)

    def sent(self, stage, n):
        block_copy(self.got(stage, n), self.refs["send"].at[stage, self.slot(n)])

    def received(self, stage, n):
        block_copy(self.got(stage, n), self.refs["recv"].at[stage, self.slot(n)])

    def store(self, n):
        pltpu.make_async_copy(self.refs["done"].at[self.slot(n)], self.refs["out"](n), self.refs["store"].at[self.slot(n)]).start()

    def stored(self, n):
        block_copy(self.refs["done"].at[self.slot(n)], self.refs["store"].at[self.slot(n)])

    def add(self, count, place, got, at):
        def body(index, carry):
            target = place(index)
            target[...] = (target[...].astype(f32) + got[at(index)].astype(f32)).astype(bf16)
            return carry

        lax.fori_loop(0, count, body, 0)


class StreamFirst(Sums):
    stages = 5

    def half(self, side):
        rows = self.refs["work"].shape[4] // 2
        return pl.ds(pl.multiple_of(side * rows, 16), rows)

    def start(self, n):
        self.send(self.work(n).at[:, :, :, self.half(1 - self.side), :], 0, n, self.stream_peer())

    def step(self, n, stage):
        r, m = self.refs, self.slot(n)
        work, own = self.work(n), self.half(self.side)
        if stage <= 4:
            self.received(stage - 1, n)
        if stage == 1:
            self.add(
                8,
                lambda i: work.at[i // 4, lax.rem(i // 2, 2), lax.rem(i, 2), own, :],
                self.got(0, n),
                lambda i: (i // 4, lax.rem(i // 2, 2), lax.rem(i, 2)),
            )
            self.send(work.at[:, 1 - self.low, :, own, :], 1, n, self.low_peer())
        if stage == 2:
            self.add(
                4,
                lambda i: work.at[i // 2, self.low, lax.rem(i, 2), own, :],
                self.got(1, n),
                lambda i: (i // 2, lax.rem(i, 2)),
            )
            self.send(work.at[:, self.low, 1 - self.near, own, :], 2, n, self.near_peer())
        if stage == 3:
            self.add(2, lambda i: work.at[i, self.low, self.near, own, :], self.got(2, n), lambda i: (i,))
            self.send(work.at[1 - self.high, self.low, self.near, own, :], 3, n, self.high_peer())
            self.sent(0, n)
        if stage == 4:
            total = work[self.high, self.low, self.near, own, :].astype(f32) + r["got3"][m].astype(f32)
            r["last"][m] = total.astype(bf16)
            self.send(r["last"].at[m], 4, n, self.stream_peer())
            if n >= RING:
                self.stored(n)
            r["done"][m, own, :] = r["last"][m]
            for earlier in range(1, 4):
                self.sent(earlier, n)
        if stage == 5:
            self.received(4, n)
            r["done"][m, self.half(1 - self.side), :] = r["got4"][m]
            self.store(n)
            self.sent(4, n)


class BatchFirst(Sums):
    stages = 4

    def start(self, n):
        self.send(self.work(n).at[:, :, 1 - self.near], 0, n, self.near_peer())

    def step(self, n, stage):
        r, m = self.refs, self.slot(n)
        work = self.work(n)
        self.received(stage - 1, n)
        if stage == 1:
            self.add(
                4,
                lambda i: work.at[i // 2, lax.rem(i, 2), self.near],
                self.got(0, n),
                lambda i: (i // 2, lax.rem(i, 2)),
            )
            self.send(work.at[:, 1 - self.low, self.near], 1, n, self.low_peer())
        if stage == 2:
            self.add(2, lambda i: work.at[i, self.low, self.near], self.got(1, n), lambda i: (i,))
            self.send(work.at[1 - self.high, self.low, self.near], 2, n, self.high_peer())
        if stage == 3:
            total = work[self.high, self.low, self.near].astype(f32) + r["got2"][m].astype(f32)
            r["last"][m] = total.astype(bf16)
            self.send(r["last"].at[m], 3, n, self.stream_peer())
            for earlier in range(3):
                self.sent(earlier, n)
        if stage == 4:
            if n >= RING:
                self.stored(n)
            r["done"][m] = (r["last"][m].astype(f32) + r["got3"][m].astype(f32)).astype(bf16)
            self.store(n)
            self.sent(3, n)


RING = 4
WORK_RING = 5
FIRST_REFS = ("work", "got0", "got1", "got2", "got3", "got4", "last", "done", "send", "recv", "store")
LAST_REFS = ("work", "got0", "got1", "got2", "got3", "last", "done", "send", "recv", "store")


def first_scratch(rows, width, ring, work_ring):
    vmem, dma = pltpu.VMEM, pltpu.SemaphoreType.DMA
    half = rows // 2
    return [
        vmem((work_ring, 2, 2, 2, rows, width), bf16),
        vmem((ring, 2, 2, 2, half, width), bf16),
        vmem((ring, 2, 2, half, width), bf16),
        vmem((ring, 2, half, width), bf16),
        vmem((ring, half, width), bf16),
        vmem((ring, half, width), bf16),
        vmem((ring, half, width), bf16),
        vmem((ring, rows, width), bf16),
        dma((5, ring)),
        dma((5, ring)),
        dma((ring,)),
    ]


def last_scratch(rows, width, ring, work_ring):
    vmem, dma = pltpu.VMEM, pltpu.SemaphoreType.DMA
    return [
        vmem((work_ring, 2, 2, 2, rows, width), bf16),
        vmem((ring, 2, 2, rows, width), bf16),
        vmem((ring, 2, rows, width), bf16),
        vmem((ring, rows, width), bf16),
        vmem((ring, rows, width), bf16),
        vmem((ring, rows, width), bf16),
        vmem((ring, rows, width), bf16),
        dma((4, ring)),
        dma((4, ring)),
        dma((ring,)),
    ]


def blocks_of(wide):
    found = []
    for layer in (1, 0):
        for left, right, output, index in (("e", "act", 0, ()), ("n2", "gate", 1, (0,)), ("n2", "up", 1, (1,))):
            found += [(left + str(layer), right + str(layer), c * CHUNK, output, (layer,) + index) for c in range(wide // CHUNK)]
        for left, right, output, index in (("c", "o", 2, ()), ("n1", "dq", 3, ()), ("n1", "dk", 4, (0,)), ("n1", "dv", 4, (1,))):
            found.append((left + str(layer), right + str(layer), 0, output, (layer,) + index))
    return found


def back_kernel(names, made, blocks, *refs):
    given, refs = dict(zip(names, refs)), refs[len(names) :]
    (rel_bias, segments, gains, projected, grad_vectors, w_proj), refs = refs[:6], refs[6:]
    outs, refs = refs[:8], refs[8:]
    held, refs = dict(zip(made, refs)), refs[len(made) :]
    (acc, core_sent, core_got, table, mask, bias, grid, dk_sum, dv_sum, do, little_got), refs = refs[:11], refs[11:]
    (load_sems, core_sems, little_sems), refs = refs[:3], refs[3:]
    firsts, lasts = blocks[0::2], blocks[1::2]
    half = len(blocks) // 2

    def out_of(blocks):
        def place(n):
            _, _, column, output, index = blocks[n]
            return outs[output].at[index + (slice(None), pl.ds(column, CHUNK))]

        return place

    first_refs, refs = dict(zip(FIRST_REFS, refs), out=out_of(firsts)), refs[len(FIRST_REFS) :]
    last_refs, refs = dict(zip(LAST_REFS, refs), out=out_of(lasts)), refs[len(LAST_REFS) :]
    stream_first, batch_first = StreamFirst(first_refs), BatchFirst(last_refs)
    projection = BatchFirst(dict(zip(LAST_REFS, refs), out=lambda n: outs[5]))
    half_index = lax.axis_index(MP)
    core = {MP: 1 - half_index}
    length, model = held["grad"].shape
    tiles = length // TILE

    loads = {}

    def fetch(name, source=None, target=None):
        copy = pltpu.make_async_copy(
            given[name] if source is None else source, held[name] if target is None else target, load_sems.at[len(loads)]
        )
        copy.start()
        loads[name] = [copy, False]

    def need(name):
        if name in loads and not loads[name][1]:
            loads[name][0].wait()
            loads[name][1] = True
        return held.get(name)

    def fetch_attention(layer):
        for name in ("wo", "q", "k", "v", "lse", "wq", "wk", "wv", "x"):
            source = given[name + str(layer)] if name + str(layer) in given else None
            if name == "wo":
                source = given["w_out"].at[layer]
            if name == "wq":
                source = given["w_query"].at[layer]
            if name in ("wk", "wv"):
                source = given["w_kv"].at[layer, 0 if name == "wk" else 1]
            fetch(name + str(layer), source, held[name])

    def fetch_ffn(layer):
        fetch("wd" + str(layer), given["wd"].at[layer], held["wd"])
        fetch("wi" + str(layer), given["wi"].at[layer], held["wi"])
        fetch("xm" + str(layer), None, held["xm"])

    fetch("state", None, held["x"])
    fetch("act1")
    fetch("wd1", given["wd"].at[1], held["wd"])
    for name in ("gate1", "up1"):
        fetch(name)
    fetch("wi1", given["wi"].at[1], held["wi"])
    fetch("xm1", None, held["xm"])
    fetch("n21")
    for name in ("o1", "n11", "gate0", "up0", "act0", "n20", "o0", "n10", "final"):
        fetch(name)

    barrier = pltpu.get_barrier_semaphore()
    peers = [stream_first.stream_peer(), stream_first.near_peer(), stream_first.low_peer(), stream_first.high_peer(), core]
    for peer in peers:
        pl.semaphore_signal(barrier, inc=1, device_id=peer, device_id_type=pl.DeviceIdType.MESH)


    def product(left, right, work):
        width = left.shape[1] // 2
        for part in range(2):
            block = dot_tn(left[:, part * width : (part + 1) * width], right).astype(bf16)
            work[part] = block.reshape(work.shape[1:])

    def make(sums, blocks, n):
        left, right, column, _, _ = blocks[n]
        product(need(left), need(right)[:, column : column + CHUNK], sums.work(n))
        if n == 0 and sums is stream_first:
            pl.semaphore_wait(barrier, len(peers))
        sums.start(n)

    def little_step(stage):
        peer = (stream_first.stream_peer, stream_first.near_peer, stream_first.low_peer, stream_first.high_peer)
        if stage > 0:
            block_copy(little_got.at[2 * stage - 1], little_sems.at[2 * stage - 1])
            total = little_got[2 * stage - 2] + little_got[2 * stage - 1]
            block_copy(little_got.at[2 * stage - 2], little_sems.at[2 * stage - 2])
            if stage == 4:
                outs[6][...] = total
            else:
                little_got[2 * stage] = total
        if stage < 4:
            send(
                little_got.at[2 * stage], little_got.at[2 * stage + 1],
                little_sems.at[2 * stage], little_sems.at[2 * stage + 1], peer[stage](),
            )


    grad = held["grad"]

    def rows_of(index):
        return pl.ds(pl.multiple_of(index * TILE, TILE), TILE)

    def share(turn):
        def pack(index, carry):
            core_sent[rows_of(index), :] = acc[rows_of(index), :].astype(bf16)
            return carry

        lax.fori_loop(0, tiles, pack, 0)
        send(core_sent, core_got.at[turn % 2], core_sems.at[0, turn], core_sems.at[1, turn], core)

    def norm_back(values, gain, gradient, first):
        weight = gains[gain : gain + 1, :]

        def tile(index, total):
            rows = rows_of(index)
            given_grad = gradient(rows)
            value = values[rows, :]
            scale = lax.rsqrt(jnp.mean(value * value, axis=-1, keepdims=True) + norm_eps)
            weighted = given_grad * weight
            along = jnp.mean(value * weighted, axis=-1, keepdims=True)
            change = scale * weighted - value * (scale * scale * scale * along)
            grad[rows, :] = change if first else grad[rows, :] + change
            return total + jnp.sum(given_grad * (value * scale), axis=0, keepdims=True)

        total = lax.fori_loop(0, tiles, tile, jnp.zeros((1, model), f32))
        little_got[0, gain : gain + 1, 0:model] = total

    def through_norm(turn, values, gain):
        block_copy(core_got.at[turn % 2], core_sems.at[1, turn])
        norm_back(
            values, gain, lambda rows: core_sent[rows, :].astype(f32) + core_got[turn % 2, rows, :].astype(f32), False
        )
        block_copy(core_sent, core_sems.at[0, turn])

    def projection_back():
        def tile(index, carry):
            rows = rows_of(index)
            y, grad_vector = projected[rows, :], grad_vectors[rows, :]
            scale = lax.rsqrt(jnp.sum(y * y, axis=-1, keepdims=True) + vector_eps)
            along = jnp.sum(y * grad_vector, axis=-1, keepdims=True)
            held["dproj"][rows, :] = (scale * grad_vector - y * (scale * scale * scale * along)).astype(bf16)
            return carry

        lax.fori_loop(0, tiles, tile, 0)
        need("state")
        norm_back(held["x"], 4, lambda rows: dot_nt(held["dproj"][rows, :], w_proj[...]), True)

    def round_grad(target):
        def pack(index, carry):
            target[rows_of(index), :] = grad[rows_of(index), :].astype(bf16)
            return carry

        lax.fori_loop(0, tiles, pack, 0)

    def ffn_tile(layer, column):
        cols = pl.ds(column, CHUNK)
        e, gate, up = (held[name + str(layer)] for name in ("e", "gate", "up"))

        def tile(index, carry):
            rows = pl.ds(pl.multiple_of(index * 2 * TILE, 2 * TILE), 2 * TILE)
            grad_hidden = dot(e[rows, :], held["wd"][:, cols])
            g, u = gate[rows, cols].astype(f32), up[rows, cols].astype(f32)
            root = math.sqrt(2.0 / math.pi)
            t = jnp.tanh(root * (g + 0.044715 * (g * g * g)))
            slope = 0.5 * (1.0 + t) + (0.5 * root) * g * (1.0 - t * t) * (1.0 + (3 * 0.044715) * (g * g))
            dg = (grad_hidden * u * slope).astype(bf16)
            du = (grad_hidden * (0.5 * g * (1.0 + t))).astype(bf16)
            gate[rows, cols] = dg
            up[rows, cols] = du
            part = dot_nt(dg, held["wi"][0, :, cols]) + dot_nt(du, held["wi"][1, :, cols])
            acc[rows, :] = part if column == 0 else acc[rows, :] + part
            return carry

        lax.fori_loop(0, tiles // 2, tile, 0)

    def attention_start(layer):
        c = held["c" + str(layer)]
        round_grad(c)

        def tile(index, carry):
            rows = pl.ds(pl.multiple_of(index * 2 * TILE, 2 * TILE), 2 * TILE)
            do[rows, :] = dot(c[rows, :], held["wo"][...]).astype(bf16)
            return carry

        need("wo" + str(layer))
        lax.fori_loop(0, tiles // 2, tile, 0)
        for name in ("q", "k", "v", "lse"):
            need(name + str(layer))

    def attention_pair(layer, p):
        attend_back_pair(
            p, table, held["lse"], held["q"], held["k"], held["v"], do,
            held["dq" + str(layer)], held["dk" + str(layer)], held["dv" + str(layer)],
            mask, bias, grid, dk_sum, dv_sum,
        )
        for half in range(2):
            line = diagonals(grid, half)
            place = (0, pl.ds(2 * p + half, 1), pl.ds(model, SPAN))
            little_got[place] = little_got[place] + line

    def attention_end(layer, turn):
        for name in ("wq", "wk", "wv"):
            need(name + str(layer))

        def tile(index, carry):
            rows = pl.ds(pl.multiple_of(index * 2 * TILE, 2 * TILE), 2 * TILE)
            acc[rows, :] = (
                dot_nt(held["dq" + str(layer)][rows, :], held["wq"][...])
                + dot_nt(held["dk" + str(layer)][rows, :], held["wk"][...])
                + dot_nt(held["dv" + str(layer)][rows, :], held["wv"][...])
            )
            return carry

        lax.fori_loop(0, tiles // 2, tile, 0)
        share(turn)

    def ffn_half(layer, part):
        if part == 0:
            for name in ("wd", "wi", "gate", "up"):
                need(name + str(layer))
        ffn_tile(layer, 2 * part * CHUNK)
        ffn_tile(layer, (2 * part + 1) * CHUNK)

    def piece0():
        ffn_half(1, 0)

    def piece1():
        ffn_half(1, 1)
        share(0)
        fill_table(rel_bias, table)
        fill_masks(row_ids_of(segments), mask, tiles)

    def piece2():
        need("xm1")
        through_norm(0, held["xm"], 3)
        fetch_ffn(0)
        attention_start(1)
        attention_pair(1, 0)

    def piece6():
        need("x1")
        through_norm(1, held["x"], 2)
        fetch_attention(0)
        round_grad(held["e0"])
        ffn_half(0, 0)

    def piece7():
        ffn_half(0, 1)
        share(2)

    def piece8():
        need("xm0")
        through_norm(2, held["xm"], 1)
        attention_start(0)
        attention_pair(0, 0)

    def piece12():
        need("x0")
        through_norm(3, held["x"], 0)
        share_rows = length // 2
        outs[7][...] = grad[pl.ds(pl.multiple_of(half_index * share_rows, TILE), share_rows), :]

    pieces = [
        piece0,
        piece1,
        piece2,
        lambda: attention_pair(1, 1),
        lambda: attention_pair(1, 2),
        lambda: attention_end(1, 1),
        piece6,
        piece7,
        piece8,
        lambda: attention_pair(0, 1),
        lambda: attention_pair(0, 2),
        lambda: attention_end(0, 3),
        piece12,
    ]
    little_got[0] = jnp.zeros(little_got.shape[1:], f32)
    projection_back()
    fetch_attention(1)
    round_grad(held["e1"])
    for t in range(half + 5):
        if t < half:
            make(stream_first, firsts, t)
            make(batch_first, lasts, t)
        if t == half - 3:
            product(need("final"), held["dproj"][...], projection.work(0))
            projection.start(0)
        if t < len(pieces):
            pieces[t]()
        for stage in (1, 2, 3, 4, 5):
            if 0 <= t - stage < half:
                stream_first.step(t - stage, stage)
                if stage <= 4:
                    batch_first.step(t - stage, stage)
            if t - stage == half - 3 and stage <= 4:
                projection.step(0, stage)
        if 0 <= t - (half - 3) <= 4:
            little_step(t - (half - 3))
    for n in range(half - RING, half):
        stream_first.stored(n)
        batch_first.stored(n)
    projection.stored(0)


def back(chain, weights, tables):
    batch = lax.axis_size(BATCH)
    length, model = chain["x0"].shape
    rows = model // batch
    narrow, wide = chain["q1"].shape[1], chain["act1"].shape[1]
    width = tables[-1].shape[1]
    little = jax.ShapeDtypeStruct((8, model + SPAN), f32)
    blocks = blocks_of(wide)
    given = dict(chain, **weights)
    vmem, dma, shape = pltpu.VMEM, pltpu.SemaphoreType.DMA, jax.ShapeDtypeStruct
    made = {"grad": (length, model), "x": (length, model), "xm": (length, model), "lse": (length, TILE)}
    made = {name: vmem(dims, f32) for name, dims in made.items()}
    for name in ("e", "n2", "c", "n1"):
        made.update({name + layer: vmem((length, model), bf16) for layer in "01"})
    for name in ("act", "gate", "up"):
        made.update({name + layer: vmem((length, wide), bf16) for layer in "01"})
    for name in ("o", "dq", "dk", "dv"):
        made.update({name + layer: vmem((length, narrow), bf16) for layer in "01"})
    made.update({name: vmem((length, narrow), bf16) for name in "qkv"})
    made.update({name: vmem((model, narrow), bf16) for name in ("wo", "wq", "wk", "wv")})
    made.update(wd=vmem((model, wide), bf16), wi=vmem((2, model, wide), bf16))
    made.update(final=vmem((length, model), bf16), dproj=vmem((length, width), bf16))
    ins = [pl.BlockSpec(memory_space=pl.ANY)] * len(given) + [pl.BlockSpec(memory_space=vmem)] * 6
    hbm, local = pl.BlockSpec(memory_space=pl.ANY), pl.BlockSpec(memory_space=vmem)
    return pl.pallas_call(
        functools.partial(back_kernel, tuple(given), tuple(made), blocks),
        out_shape=(
            shape((2, rows, wide), bf16),
            shape((2, 2, rows, wide), bf16),
            shape((2, rows, narrow), bf16),
            shape((2, rows, narrow), bf16),
            shape((2, 2, rows, narrow), bf16),
            shape((rows, width), bf16),
            shape(little.shape, f32),
            shape((length // 2, model), f32),
        ),
        in_specs=ins,
        out_specs=(hbm,) * 6 + (local,) * 2,
        scratch_shapes=list(made.values())
        + [
            vmem((length, model), f32),
            vmem((length, model), bf16),
            vmem((2, length, model), bf16),
            vmem((8, SPAN), f32),
            vmem((length, 3 * TILE), f32),
            vmem((2, TILE, 3 * TILE), f32),
            vmem((2, TILE, SPAN), f32),
            vmem((length, TILE), f32),
            vmem((length, TILE), f32),
            vmem((length, narrow), bf16),
            vmem((8,) + little.shape, f32),
            dma((64,)),
            dma((2, 4)),
            dma((8,)),
        ]
        + first_scratch(rows, CHUNK, RING, WORK_RING)
        + last_scratch(rows, CHUNK, RING, WORK_RING)
        + last_scratch(rows, width, 1, 1),
        compiler_params=pltpu.CompilerParams(
            collective_id=1, has_side_effects=True, vmem_limit_bytes=62 * 1024 * 1024
        ),
        cost_estimate=pl.CostEstimate(flops=2 * 10**10, bytes_accessed=5 * 10**7, transcendentals=10**6),
        name="back",
    )(*given.values(), *tables)


def place_kernel(down, into, out, query, key_value, projection, little, grad, vectors, losses, *outs):
    share = outs[0].shape[0]
    first = pl.multiple_of(lax.axis_index(MP) * share, TILE)
    outs[0][...] = vectors[pl.ds(first, share), :]
    outs[1][...] = losses[...]
    for source, target in zip((grad, query, key_value, out, into, down, projection), outs[2:8] + outs[10:]):
        target[...] = source[...].astype(f32)
    gains, bias = outs[8], outs[9]
    model = grad.shape[1]
    count, rows = gains.shape
    moved = pltpu.roll(little[:, 0:model], lax.rem(model - lax.axis_index(BATCH) * rows, model), axis=1)
    gains[...] = moved[0:count, 0:rows]
    bias[...] = lax.dot_general(
        bucket_places(bias.shape[0]),
        little[0 : bias.shape[1], model:],
        (((1,), (1,)), ((), ())),
        precision=highest,
        preferred_element_type=f32,
    )


def place(summed, vectors, losses, gain_count, bias_shape):
    down, into, out, query, key_value, projection, little, grad = summed
    shape = jax.ShapeDtypeStruct
    local = pl.BlockSpec(memory_space=pltpu.VMEM)
    return pl.pallas_call(
        place_kernel,
        out_shape=(shape((grad.shape[0], vectors.shape[1]), bf16), shape(losses.shape, f32))
        + tuple(shape(value.shape, f32) for value in (grad, query, key_value, out, into, down))
        + (shape((gain_count, query.shape[1]), f32), shape(bias_shape, f32), shape(projection.shape, f32)),
        in_specs=[local] * 10,
        out_specs=(local,) * 11,
        compiler_params=pltpu.CompilerParams(vmem_limit_bytes=60 * 1024 * 1024),
        name="place",
    )(*summed, vectors, losses)


def sum_gradients_plainly(kept, final_pair, little):
    def summed(left, right):
        part = lax.psum_scatter(dot_tn(left, right).astype(bf16), BATCH, scatter_dimension=0, tiled=True)
        return sum_of_two(part, STREAM)

    found = []
    for e, n2, c, n1, hidden, dg, du, o, dq, dk, dv in kept:
        found.append((
            summed(e, hidden),
            jnp.stack([summed(n2, dg), summed(n2, du)]),
            summed(c, o),
            summed(n1, dq),
            jnp.stack([summed(n1, dk), summed(n1, dv)]),
        ))
    return [jnp.stack(parts) for parts in zip(*found)] + [
        summed(*final_pair),
        lax.psum(little, (STREAM, BATCH)),
    ]


def on_device(
    tokens,
    segments,
    top_mask,
    positive,
    w_query,
    w_kv,
    w_out,
    w_in,
    w_down,
    gains,
    rel_bias,
    w_proj,
):
    length = segments.shape[1]
    share_len, model_width = tokens.shape[2:]
    head_count = rel_bias.shape[1]
    layers = w_query.shape[0]
    batch = lax.axis_size(BATCH)
    query_rows, slot_count = positive.shape
    tables = (rel_bias, segments, gains)
    kept = forward(tokens[0, 0], (w_query, w_kv, w_out, w_in, w_down, w_proj), tables)
    vectors = kept["vectors"]
    grad_vectors, query_loss = score(
        vectors, segments, top_mask.reshape(query_rows * slot_count, length), positive
    )
    if layers == 2 and batch == 8:
        chain = {name: value for name, value in kept.items() if name not in ("y", "vectors")}
        weights = dict(w_query=w_query, w_kv=w_kv, w_out=w_out, wi=w_in, wd=w_down)
        summed = back(chain, weights, tables + (kept["y"], grad_vectors, w_proj))
        placed = place(summed, vectors, query_loss, gains.shape[0], rel_bias.shape)
        return (placed[0][None, None], placed[1], placed[2][None, None]) + placed[3:]
    else:
        row_segments = jnp.where(
            lax.axis_index(STREAM) == 0, jnp.arange(length, dtype=jnp.int32) // QLEN, segments[0]
        )
        row_ids = row_segments[None]
        offset_onehot = (
            offset_buckets()[None, :] == jnp.arange(rel_bias.shape[0], dtype=jnp.int32)[:, None]
        ).astype(f32)
        table = jnp.einsum(
            "bh,bk->hk", jnp.pad(rel_bias, ((0, 0), (0, 8 - head_count))), offset_onehot, precision=highest
        )
        kept_layers = [[kept[name + str(layer)] for name in KEPT] for layer in range(layers)]
        grad_projected = jax.vjp(normalize, kept["y"])[1](grad_vectors)[0].astype(bf16)
        grad_final = dot_nt(grad_projected, w_proj)
        grad_state, grad_gain_final = jax.vjp(rms_scale, kept["state"], gains[2 * layers])[1](grad_final)
        gain_grads = [None] * (2 * layers)
        operands = [None] * layers
        sums = jnp.zeros(table.shape, f32)
        for layer in reversed(range(layers)):
            weights_layer = (
                w_query[layer],
                w_kv[layer],
                w_out[layer],
                w_in[layer],
                w_down[layer],
                gains[2 * layer],
                gains[2 * layer + 1],
            )
            grad_state, ffn_lefts, ffn_rights, gain_grads[2 * layer + 1] = ffn_backward(
                grad_state, kept_layers[layer], weights_layer
            )
            grad_state, lefts, rights, gain_grads[2 * layer], part = attention_backward(
                grad_state, table, row_ids, kept_layers[layer], weights_layer
            )
            operands[layer] = ffn_lefts + lefts + ffn_rights + rights
            sums = sums + part
        little = jnp.concatenate(
            [jnp.pad(jnp.stack(gain_grads + [grad_gain_final]), ((0, 7 - 2 * layers), (0, 0))), sums], axis=1
        )
        summed = sum_gradients_plainly(operands, (kept["final"], grad_projected), little)
        grad_down, grad_in, grad_out, grad_query, grad_kv, grad_proj, little = summed
        own_grad = lax.dynamic_slice_in_dim(grad_state, lax.axis_index(MP) * share_len, share_len, 0)
        grad_bias = jnp.einsum("hk,bk->bh", little[:, model_width:], offset_onehot, precision=highest)
        rows = model_width // batch
        grad_gains = lax.dynamic_slice(little, (0, lax.axis_index(BATCH) * rows), (2 * layers + 1, rows))
    own_vectors = lax.dynamic_slice_in_dim(vectors, lax.axis_index(MP) * share_len, share_len, 0)
    return (
        own_vectors[None, None],
        query_loss,
        own_grad[None, None],
        grad_query,
        grad_kv,
        grad_out,
        grad_in,
        grad_down,
        grad_gains,
        grad_bias[:, :head_count],
        grad_proj,
    )


def solution(mesh):
    placed = (
        P(STREAM, BATCH, MP, None),
        P(BATCH, None),
        P(None, MP, BATCH, None),
        P(None, MP),
        P(None, None, MP),
        P(None, None, None, MP),
        P(None, None, MP),
        P(None, None, None, MP),
        P(None, None, MP),
        P(),
        P(None, MP),
        P(),
    )
    return jax.shard_map(
        on_device,
        mesh=mesh,
        in_specs=placed,
        out_specs=(
            P(STREAM, BATCH, MP, None),
            P(BATCH, MP),
            P(STREAM, BATCH, MP, None),
            P(None, BATCH, MP),
            P(None, None, BATCH, MP),
            P(None, BATCH, MP),
            P(None, None, BATCH, MP),
            P(None, BATCH, MP),
            P(None, BATCH),
            P(None, MP),
            P(BATCH, None),
        ),
        check_vma=False,
    )
```

```python
import functools
import math

import jax
import jax.numpy as jnp
from jax import lax
from jax.experimental import pallas as pl
from jax.experimental.pallas import tpu as pltpu
from jax.sharding import PartitionSpec as P

QLEN = 32
DOCS_ROW = 8
TILE = 128
STREAM, BATCH, MP = "stream", "batch", "mp"
SPAN = 512


norm_eps = 1e-06
vector_eps = 1e-06
temper = 0.05
logit_scale = 32.0
bucket_edges = (12, 16, 23, 32, 46, 64, 91)
highest = lax.Precision.HIGHEST
bf16 = jnp.bfloat16
f32 = jnp.float32


def dot(a, b):
    return lax.dot_general(a, b, (((1,), (0,)), ((), ())), preferred_element_type=f32)


def dot_nt(a, b):
    return lax.dot_general(a, b, (((1,), (1,)), ((), ())), preferred_element_type=f32)


def dot_tn(a, b):
    return lax.dot_general(a, b, (((0,), (0,)), ((), ())), preferred_element_type=f32)


def offset_buckets():
    index = jnp.arange(SPAN, dtype=jnp.int32)
    offsets = jnp.where(index < SPAN // 2, index, index - SPAN)
    magnitude = jnp.abs(offsets)
    far_bucket = jnp.full(offsets.shape, 8, jnp.int32)
    for threshold in bucket_edges:
        far_bucket = far_bucket + (magnitude >= threshold).astype(jnp.int32)
    bucket = jnp.where(magnitude < 8, magnitude, jnp.minimum(far_bucket, 15))
    return bucket + jnp.where(offsets > 0, 16, 0).astype(jnp.int32)


def bucket_places(count):
    index = lax.broadcasted_iota(jnp.int32, (count, SPAN), 1)
    offsets = jnp.where(index < SPAN // 2, index, index - SPAN)
    magnitude = jnp.abs(offsets)
    far_bucket = jnp.full(offsets.shape, 8, jnp.int32)
    for threshold in bucket_edges:
        far_bucket = far_bucket + jnp.where(magnitude >= threshold, 1, 0)
    bucket = jnp.where(magnitude < 8, magnitude, jnp.minimum(far_bucket, 15))
    bucket = bucket + jnp.where(offsets > 0, 16, 0)
    return jnp.where(bucket == lax.broadcasted_iota(jnp.int32, (count, SPAN), 0), 1.0, 0.0)


def fill_table(rel_bias, table):
    table[...] = jnp.zeros(table.shape, f32)
    table[0 : rel_bias.shape[0], :] = lax.dot_general(
        rel_bias[...],
        bucket_places(rel_bias.shape[1]),
        (((1,), (0,)), ((), ())),
        precision=highest,
        preferred_element_type=f32,
    )


def row_ids_of(segments):
    position = lax.broadcasted_iota(jnp.int32, segments.shape, 1)
    return jnp.where(lax.axis_index(STREAM) == 0, position // QLEN, segments[...])


def window(tile, tiles):
    first, last = max(0, tile - 1), min(tiles, tile + 2)
    shift = first - (tile - 1)
    return pl.ds(first * TILE, (last - first) * TILE), slice(shift * TILE, (shift + last - first) * TILE)


def fill_masks(row_ids, mask, tiles):
    ids = row_ids.astype(f32)
    lines = [jnp.broadcast_to(ids[:, tile * TILE : (tile + 1) * TILE], (TILE, TILE)) for tile in range(tiles)]
    for tile in range(tiles):
        own = jnp.transpose(lines[tile])
        for near in range(max(0, tile - 1), min(tiles, tile + 2)):
            place = (near - tile + 1) * TILE
            mask[tile * TILE : (tile + 1) * TILE, place : place + TILE] = jnp.where(own == lines[near], 0.0, -1e30)


def bias_tile(table, head):
    line = jnp.broadcast_to(table[pl.ds(head, 1), :], (TILE, SPAN))
    return pltpu.roll(line, TILE, axis=1, stride=1, stride_axis=0)[:, : 3 * TILE]


def attend_pair(p, table, q, k, v, o, lse, mask, bias):
    tiles = q.shape[0] // TILE
    lane = lax.broadcasted_iota(jnp.int32, (TILE, TILE), 1)
    cols = pl.ds(pl.multiple_of(p * TILE, TILE), TILE)
    for half in range(2):
        bias[half] = bias_tile(table, 2 * p + half)
    scores = []
    for tile in range(tiles):
        rows = pl.ds(tile * TILE, TILE)
        keys, frame = window(tile, tiles)
        queries, near_keys = q[rows, cols], k[keys, cols]
        for half in range(2):
            mine = (lane >= 64) if half else (lane < 64)
            s = dot_nt(jnp.where(mine, queries, jnp.zeros_like(queries)), near_keys)
            scores.append(s + (bias[half][:, frame] + mask[rows, frame]))
    tops = [jnp.max(s, axis=-1, keepdims=True) for s in scores]
    exps = [jnp.exp(s - top) for s, top in zip(scores, tops)]
    totals = [jnp.sum(e, axis=-1, keepdims=True) for e in exps]
    weights = [(e * (1.0 / total)).astype(bf16) for e, total in zip(exps, totals)]
    for tile in range(tiles):
        rows = pl.ds(tile * TILE, TILE)
        near_values = v[window(tile, tiles)[0], cols]
        outs = [dot(weights[2 * tile + half], near_values) for half in range(2)]
        o[rows, cols] = jnp.where(lane < 64, outs[0], outs[1]).astype(bf16)
        kept = lse[rows, :]
        for half in range(2):
            index = 2 * tile + half
            kept = jnp.where(lane == 2 * p + half, tops[index] + jnp.log(totals[index]), kept)
        lse[rows, :] = kept


def attend_back_pair(p, table, lse, q, k, v, do, dq, dk, dv, mask, bias, grid, dk_sum, dv_sum):
    tiles = q.shape[0] // TILE
    lane = lax.broadcasted_iota(jnp.int32, (TILE, TILE), 1)
    cols = pl.ds(pl.multiple_of(p * TILE, TILE), TILE)
    for half in range(2):
        bias[half] = bias_tile(table, 2 * p + half)
    grid[...] = jnp.zeros(grid.shape, f32)
    dk_sum[...] = jnp.zeros(dk_sum.shape, f32)
    dv_sum[...] = jnp.zeros(dv_sum.shape, f32)
    for first in range(0, tiles, 2):
        some = [(tile, half) for tile in range(first, min(first + 2, tiles)) for half in range(2)]
        own_queries, own_grads, weights, grad_weights = [], [], [], []
        for tile, half in some:
            rows = pl.ds(tile * TILE, TILE)
            keys, frame = window(tile, tiles)
            mine = (lane >= 64) if half else (lane < 64)
            queries, grads = q[rows, cols], do[rows, cols]
            own_queries.append(jnp.where(mine, queries, jnp.zeros_like(queries)))
            own_grads.append(jnp.where(mine, grads, jnp.zeros_like(grads)))
            log_total = jnp.sum(jnp.where(lane == 2 * p + half, lse[rows, :], 0.0), axis=-1, keepdims=True)
            s = dot_nt(own_queries[-1], k[keys, cols])
            s = s + (bias[half][:, frame] + mask[rows, frame])
            weights.append(jnp.exp(s - log_total))
            grad_weights.append(dot_nt(own_grads[-1], v[keys, cols]))
        means = [jnp.sum(w * g, axis=-1, keepdims=True) for w, g in zip(weights, grad_weights)]
        ds = [(w * (g - mean)).astype(bf16) for w, g, mean in zip(weights, grad_weights, means)]
        outs = []
        for index, (tile, half) in enumerate(some):
            keys, frame = window(tile, tiles)
            outs.append(dot(ds[index], k[keys, cols]))
            dk_sum[keys, :] += dot_tn(ds[index], own_queries[index])
            dv_sum[keys, :] += dot_tn(weights[index].astype(bf16), own_grads[index])
            grid[half, :, frame] += ds[index].astype(f32)
        for index in range(0, len(some), 2):
            rows = pl.ds(some[index][0] * TILE, TILE)
            dq[rows, cols] = jnp.where(lane < 64, outs[index], outs[index + 1]).astype(bf16)
    dk[:, cols] = dk_sum[...].astype(bf16)
    dv[:, cols] = dv_sum[...].astype(bf16)


def diagonals(grid, half):
    row_index = lax.broadcasted_iota(jnp.int32, (TILE, SPAN), 0)
    turned = pltpu.roll(grid[half], SPAN - TILE, axis=1)
    for bit in range(7):
        moved = pltpu.roll(turned, SPAN - (1 << bit), axis=1)
        turned = jnp.where((row_index >> bit) & 1 == 1, moved, turned)
    return jnp.sum(turned, axis=0, keepdims=True)


def attend_back_kernel(
    table, row_ids, lse, q, k, v, do, dq, dk, dv, sums, mask, bias, grid, dk_sum, dv_sum
):
    fill_masks(row_ids[...], mask, q.shape[0] // TILE)
    sums[...] = jnp.zeros(sums.shape, f32)

    def pair(p, carry):
        attend_back_pair(p, table, lse, q, k, v, do, dq, dk, dv, mask, bias, grid, dk_sum, dv_sum)
        for half in range(2):
            sums[pl.ds(2 * p + half, 1), :] = diagonals(grid, half)
        return carry

    lax.fori_loop(0, q.shape[1] // TILE, pair, 0)


def attend_back(table, row_ids, lse, q, k, v, do):
    length, width = q.shape
    grad = jax.ShapeDtypeStruct((length, width), bf16)
    return pl.pallas_call(
        attend_back_kernel,
        out_shape=(grad, grad, grad, jax.ShapeDtypeStruct(table.shape, f32)),
        scratch_shapes=[
            pltpu.VMEM((length, 3 * TILE), f32),
            pltpu.VMEM((2, TILE, 3 * TILE), f32),
            pltpu.VMEM((2, TILE, SPAN), f32),
            pltpu.VMEM((length, TILE), f32),
            pltpu.VMEM((length, TILE), f32),
        ],
        compiler_params=pltpu.CompilerParams(vmem_limit_bytes=32 * 1024 * 1024),
        cost_estimate=pl.CostEstimate(flops=25 * 10**8, bytes_accessed=4 * 10**6, transcendentals=10**6),
        name="attend_back",
    )(table, row_ids, lse, q, k, v, do)


def rms_scale(values, gain_row):
    return (
        values * lax.rsqrt(jnp.mean(values * values, axis=-1, keepdims=True) + norm_eps) * gain_row
    )


def gated_gelu(gate, up):
    return jax.nn.gelu(gate, approximate=True) * up


def normalize(values):
    return values * lax.rsqrt(jnp.sum(values * values, axis=-1, keepdims=True) + vector_eps)


def swap(value, axis):
    return lax.ppermute(value, axis, [(0, 1), (1, 0)])


def sum_of_two(part, axis):
    mine = lax.optimization_barrier(part.astype(bf16))
    return mine.astype(f32) + swap(mine, axis).astype(f32)


def ffn_backward(grad_output, kept, weights_layer):
    middle, ffn_input, gate, up, hidden = kept[7:]
    in_weight, down_weight, gain_ffn = weights_layer[3], weights_layer[4], weights_layer[6]
    grad_branch = grad_output.astype(bf16)
    grad_hidden = dot(grad_branch, down_weight)
    grad_gate, grad_up = jax.vjp(gated_gelu, gate.astype(f32), up.astype(f32))[1](grad_hidden)
    grad_gate, grad_up = grad_gate.astype(bf16), grad_up.astype(bf16)
    grad_input = sum_of_two(dot_nt(grad_gate, in_weight[0]) + dot_nt(grad_up, in_weight[1]), MP)
    grad_mid_norm, grad_gain = jax.vjp(rms_scale, middle, gain_ffn)[1](grad_input)
    return grad_output + grad_mid_norm, (grad_branch, ffn_input), (hidden, grad_gate, grad_up), grad_gain


def attention_backward(grad_middle, table, row_ids, kept, weights_layer):
    inputs, normed, q, k, v, lse, attended = kept[:7]
    query_weight, kv_weight, out_weight, gain_attn = (
        weights_layer[0],
        weights_layer[1],
        weights_layer[2],
        weights_layer[5],
    )
    grad_attn = grad_middle.astype(bf16)
    do = dot(grad_attn, out_weight).astype(bf16)
    dq, dk, dv, sums = attend_back(table, row_ids, lse, q, k, v, do)
    grad_normed = sum_of_two(
        dot_nt(dq, query_weight) + dot_nt(dk, kv_weight[0]) + dot_nt(dv, kv_weight[1]), MP
    )
    grad_in_norm, grad_gain = jax.vjp(rms_scale, inputs, gain_attn)[1](grad_normed)
    return grad_middle + grad_in_norm, (grad_attn, normed), (attended, dq, dk, dv), grad_gain, sums


def send(source, target, send_sem, recv_sem, device):
    copy = pltpu.make_async_remote_copy(
        src_ref=source,
        dst_ref=target,
        send_sem=send_sem,
        recv_sem=recv_sem,
        device_id=device,
        device_id_type=pl.DeviceIdType.MESH,
    )
    copy.start()


def score_kernel(
    count,
    vectors,
    doc_row,
    top_mask,
    positive,
    grad,
    loss,
    queries,
    docs,
    raised,
    totals,
    logits,
    places,
    stats,
    own_loss,
    other_loss,
    sent_grads,
    got_grads,
    cross,
    doc_sum,
    sent_docs,
    got_docs,
    core_sent,
    core_got,
    query_send,
    query_recv,
    stat_send,
    stat_recv,
    grad_send,
    grad_recv,
    part_sems,
    doc_sems,
    loss_sems,
    cross_sems,
    back_sems,
    core_sems,
):
    side, batch, half = lax.axis_index(STREAM), lax.axis_index(BATCH), lax.axis_index(MP)
    length, width = vectors.shape
    quarter = length // 4
    slots = quarter // QLEN
    group = math.gcd(count, 4)
    core, other = {MP: 1 - half}, {STREAM: 1 - side}

    def scorer(step):
        return lax.rem(batch + step, count)

    def each(first, body):
        def run(step, carry):
            body(scorer(step))
            return carry

        lax.fori_loop(first, count, run, 0, unroll=count <= 8)

    barrier = pltpu.get_barrier_semaphore()

    def greet(peer):
        pl.semaphore_signal(barrier, inc=1, device_id={BATCH: peer}, device_id_type=pl.DeviceIdType.MESH)

    each(1, greet)
    for peer in (core, other):
        pl.semaphore_signal(barrier, inc=1, device_id=peer, device_id_type=pl.DeviceIdType.MESH)
    pl.semaphore_wait(barrier, count + 1)

    def query_part(plane):
        return vectors.at[pl.ds(pl.multiple_of(half * (length // 2), QLEN) + plane * quarter, quarter), :]

    own = queries.at[batch]

    @pl.when(side == 0)
    def _():
        send(query_part(1), own, part_sems.at[0], part_sems.at[1], other)
        own[...] = query_part(0)[...]

    @pl.when(side == 1)
    def _():
        send(vectors, docs, doc_sems.at[0], doc_sems.at[1], other)
        docs[...] = vectors[...]
        block_copy(own, part_sems.at[1])

    def push(peer):
        send(own, own, query_send.at[peer], query_recv.at[batch], {BATCH: peer})

    each(1, push)
    row = lax.broadcasted_iota(jnp.int32, (width, length), 0)
    onehot = jnp.where(row == jnp.broadcast_to(doc_row[0:1, :], (width, length)), 1.0, 0.0).astype(bf16)

    @pl.when(side == 0)
    def _():
        block_copy(docs, doc_sems.at[1])

    def forward(first, carry):
        sources = [scorer(first * group + step) for step in range(group)]
        sims = []
        for source in sources:

            @pl.when(source != batch)
            def _():
                block_copy(queries.at[source], query_recv.at[source])

            sims.append(dot_nt(queries[source], docs[...]))
        for source, sim in zip(sources, sims):
            for slot in range(slots):
                chosen = top_mask[source, side * slots + slot].astype(f32)
                part = jnp.exp(sim[slot * QLEN : (slot + 1) * QLEN] * (1.0 / temper)) * chosen
                raised[source, slot * QLEN : (slot + 1) * QLEN, :] = part.astype(bf16)
        summed = [dot_nt(raised[source], onehot) for source in sources]
        for source, total in zip(sources, summed):
            totals[source] = total
            pooled = jnp.log1p(total) * (logit_scale * temper / QLEN)
            for slot in range(slots):
                line = pl.ds(source * slots + slot, 1)
                logits[line, :] = jnp.sum(pooled[slot * QLEN : (slot + 1) * QLEN], axis=0, keepdims=True)
                places[line, :] = jnp.full((1, width), positive[source, side * slots + slot], jnp.int32)
        return carry

    lax.fori_loop(0, count // group, forward, 0)

    doc = lax.broadcasted_iota(jnp.int32, logits.shape, 1)
    local = doc < DOCS_ROW
    scores = logits[...]
    is_positive = jnp.where(
        jnp.logical_and(local, places[...] == doc + batch * DOCS_ROW), 1.0, 0.0
    )
    exps = jnp.sum(jnp.where(local, jnp.exp(scores), 0.0), axis=1, keepdims=True)
    hits = jnp.sum(is_positive * scores, axis=1, keepdims=True)
    columns = jnp.where(doc == 0, exps, jnp.where(doc == 1, hits, 0.0))
    lines = stats.shape[2]
    if lines > columns.shape[0]:
        columns = jnp.concatenate([columns, jnp.zeros((lines - columns.shape[0], width), f32)], axis=0)
    stats[batch] = jnp.transpose(columns)[0:8, :]

    def push_stats(peer):
        send(stats.at[batch], stats.at[batch], stat_send.at[peer], stat_recv.at[batch], {BATCH: peer})

    each(1, push_stats)
    each(1, lambda peer: block_copy(stats.at[peer], stat_recv.at[peer]))
    summed = lax.fori_loop(1, count, lambda source, total: total + stats[source], stats[0])
    log_line = jnp.log(summed[0:1, :])
    row = lax.broadcasted_iota(jnp.int32, (width, lines), 0)
    both = jnp.where(row == 0, log_line, jnp.where(row == 1, log_line - summed[1:2, :], 0.0))
    both = jnp.transpose(both)[0 : logits.shape[0], :]
    log_total = jnp.sum(jnp.where(doc == 0, both, 0.0), axis=1, keepdims=True)
    losses = jnp.sum(jnp.where(doc == 1, both, 0.0), axis=1, keepdims=True)
    logits[...] = jnp.broadcast_to(losses, logits.shape)
    for slot in range(slots):
        own_loss[pl.ds(slot, 1), :] = logits[pl.ds(batch * slots + slot, 1), :]
    send(own_loss, other_loss, loss_sems.at[0], loss_sems.at[1], other)
    logits[...] = jnp.where(local, jnp.exp(scores - log_total), 0.0) - is_positive
    doc_sum[...] = jnp.zeros(doc_sum.shape, f32)

    def backward(first, carry):
        sources = [scorer(first * group + step + 1) for step in range(group)]
        factors = []
        for source in sources:
            parts = []
            for slot in range(slots):
                line = logits[pl.ds(source * slots + slot, 1), :] * (logit_scale / QLEN)
                parts.append(line / (1.0 + totals[source, slot * QLEN : (slot + 1) * QLEN, :]))
            factors.append(jnp.concatenate(parts, axis=0).astype(bf16))
        spreads = [dot(factor, onehot) for factor in factors]
        ds = [(raised[source].astype(f32) * spread).astype(bf16) for source, spread in zip(sources, spreads)]
        backs = [dot(d, docs[...]).astype(bf16) for d in ds]
        for source, back in zip(sources, backs):
            sent_grads[source] = back

            @pl.when(source != batch)
            def _():
                send(
                    sent_grads.at[source], got_grads.at[batch], grad_send.at[source], grad_recv.at[batch], {BATCH: source}
                )

        change = dot_tn(ds[0], queries[sources[0]])
        for d, source in zip(ds[1:], sources[1:]):
            change = change + dot_tn(d, queries[source])
        doc_sum[...] += change
        return carry

    lax.fori_loop(0, count // group, backward, 0)

    @pl.when(side == 0)
    def _():
        sent_docs[...] = doc_sum[...].astype(bf16)
        send(sent_docs, got_docs, back_sems.at[0], back_sems.at[1], other)

    got_grads[batch] = sent_grads[batch]
    each(1, lambda peer: block_copy(got_grads.at[peer], grad_recv.at[peer]))
    total = lax.fori_loop(
        1, count, lambda source, total: total + got_grads[source].astype(f32), got_grads[0].astype(f32)
    )
    share = pl.ds(0, length // 2)

    @pl.when(side == 0)
    def _():
        core_sent[0:quarter, :] = total.astype(bf16)
        block_copy(cross.at[1], cross_sems.at[1])
        core_sent[quarter : 2 * quarter, :] = cross[1]
        part, there = core_sent.at[share, :], core_got.at[share, :]
        send(part, there, core_sems.at[0], core_sems.at[1], core)
        block_copy(there, core_sems.at[1])
        first = pl.multiple_of(half * (length // 2), QLEN)
        grad[pl.ds(first, length // 2), :] = core_sent[share, :].astype(f32)
        grad[pl.ds(length // 2 - first, length // 2), :] = core_got[share, :].astype(f32)
        block_copy(part, core_sems.at[0])
        block_copy(sent_docs, back_sems.at[0])
        block_copy(query_part(1), part_sems.at[0])

    @pl.when(side == 1)
    def _():
        cross[0] = total.astype(bf16)
        send(cross.at[0], cross.at[1], cross_sems.at[0], cross_sems.at[1], other)
        block_copy(got_docs, back_sems.at[1])
        core_sent[...] = (doc_sum[...] + got_docs[...].astype(f32)).astype(bf16)
        send(core_sent, core_got, core_sems.at[0], core_sems.at[1], core)
        block_copy(core_got, core_sems.at[1])
        grad[...] = (core_sent[...].astype(f32) + core_got[...].astype(f32)).astype(bf16).astype(f32)
        block_copy(core_sent, core_sems.at[0])
        block_copy(cross.at[0], cross_sems.at[0])
        block_copy(vectors, doc_sems.at[0])

    block_copy(other_loss, loss_sems.at[1])
    lower = jnp.where(side == 0, own_loss[0:slots, :], other_loss[0:slots, :])
    upper = jnp.where(side == 0, other_loss[0:slots, :], own_loss[0:slots, :])
    pair = jnp.concatenate([lower, upper], axis=0)
    across = lax.broadcasted_iota(jnp.int32, pair.shape, 1) == lax.broadcasted_iota(jnp.int32, pair.shape, 0)
    loss[...] = jnp.sum(jnp.where(across, pair, 0.0), axis=0, keepdims=True)[:, 0 : 2 * slots]
    block_copy(own_loss, loss_sems.at[0])

    def settle(peer):
        block_copy(own, query_send.at[peer])
        block_copy(stats.at[batch], stat_send.at[peer])
        block_copy(sent_grads.at[peer], grad_send.at[peer])

    each(1, settle)


def score(vectors, doc_row, top_mask, positive):
    count = lax.axis_size(BATCH)
    length, width = vectors.shape
    quarter = length // 4
    slots = quarter // QLEN
    dma = pltpu.SemaphoreType.DMA
    return pl.pallas_call(
        functools.partial(score_kernel, count),
        out_shape=(
            jax.ShapeDtypeStruct((length, width), f32),
            jax.ShapeDtypeStruct((1, 2 * slots), f32),
        ),
        in_specs=[pl.BlockSpec(memory_space=pltpu.VMEM)] * 3 + [pl.BlockSpec(memory_space=pltpu.SMEM)],
        out_specs=(pl.BlockSpec(memory_space=pltpu.VMEM),) * 2,
        scratch_shapes=[
            pltpu.VMEM((count, quarter, width), bf16),
            pltpu.VMEM((length, width), bf16),
            pltpu.VMEM((count, quarter, length), bf16),
            pltpu.VMEM((count, quarter, width), f32),
            pltpu.VMEM((count * slots, width), f32),
            pltpu.VMEM((count * slots, width), jnp.int32),
            pltpu.VMEM((count, 8, max(TILE, count * slots)), f32),
            pltpu.VMEM((8, width), f32),
            pltpu.VMEM((8, width), f32),
            pltpu.VMEM((count, quarter, width), bf16),
            pltpu.VMEM((count, quarter, width), bf16),
            pltpu.VMEM((2, quarter, width), bf16),
            pltpu.VMEM((length, width), f32),
            pltpu.VMEM((length, width), bf16),
            pltpu.VMEM((length, width), bf16),
            pltpu.VMEM((length, width), bf16),
            pltpu.VMEM((length, width), bf16),
        ]
        + [dma((count,))] * 6
        + [dma((2,))] * 6,
        compiler_params=pltpu.CompilerParams(
            collective_id=0, has_side_effects=True, vmem_limit_bytes=56 * 1024 * 1024
        ),
        cost_estimate=pl.CostEstimate(flops=10**9, bytes_accessed=2 * 10**6, transcendentals=10**6),
        name="score",
    )(vectors, doc_row, top_mask, positive)


def rms_rows(value, weight):
    scale = lax.rsqrt(jnp.mean(value * value, axis=-1, keepdims=True) + norm_eps)
    return (value * scale * weight).astype(bf16)


KEPT = ("x", "n1", "q", "k", "v", "lse", "o", "xm", "n2", "gate", "up", "act")


def forward_kernel(made, results, *refs):
    (tokens, w_query, w_kv, w_out, w_in, w_down, w_proj, rel_bias, segments, gains), refs = refs[:10], refs[10:]
    outs, refs = dict(zip(results, refs)), refs[len(results) :]
    held, refs = dict(zip(made, refs)), refs[len(made) :]
    row_sent, row_got, sent, got, table, mask, bias, load_sems, store_sems, row_sems, send_sems, recv_sems = refs
    half = lax.axis_index(MP)
    core = {MP: 1 - half}
    length, model = held["x0"].shape
    share = length // 2
    narrow, wide = held["q0"].shape[1], held["act0"].shape[1]
    layers = w_query.shape[0]
    loads, stores = [], []

    def fetch(source, target):
        copy = pltpu.make_async_copy(source, target, load_sems.at[len(loads)])
        copy.start()
        loads.append(copy)
        return copy

    def keep(name):
        copy = pltpu.make_async_copy(held[name], outs[name], store_sems.at[len(stores)])
        copy.start()
        stores.append(copy)

    ready = {"tokens": fetch(tokens, row_sent)}
    for layer in range(layers):
        for name, source in (
            ("wq", w_query.at[layer]),
            ("wk", w_kv.at[layer, 0]),
            ("wv", w_kv.at[layer, 1]),
            ("wo", w_out.at[layer]),
            ("wi", w_in.at[layer]),
            ("wd", w_down.at[layer]),
        ):
            ready[name + str(layer)] = fetch(source, held[name + str(layer)])
    ready["w_proj"] = fetch(w_proj, held["w_proj"])
    barrier = pltpu.get_barrier_semaphore()
    pl.semaphore_signal(barrier, inc=1, device_id=core, device_id_type=pl.DeviceIdType.MESH)
    pl.semaphore_wait(barrier, 1)
    ready["tokens"].wait()
    send(row_sent, row_got, row_sems.at[0], row_sems.at[1], core)
    fill_table(rel_bias, table)
    fill_masks(row_ids_of(segments), mask, length // TILE)

    def rows_of(index):
        return pl.ds(pl.multiple_of(index * share, TILE), share)

    def share_part(turn, index, part):
        rows = rows_of(index)
        sent[turn, rows, :] = part.astype(bf16)
        send(
            sent.at[turn, rows, :], got.at[turn, rows, :],
            send_sems.at[turn, index], recv_sems.at[turn, index], core,
        )

    def total(turn, index, base):
        rows = rows_of(index)
        block_copy(got.at[turn, rows, :], recv_sems.at[turn, index])
        return base[rows, :] + (sent[turn, rows, :].astype(f32) + got[turn, rows, :].astype(f32))

    def project(layer, index, value):
        rows, name = rows_of(index), str(layer)
        held["x" + name][rows, :] = value
        n1 = rms_rows(value, gains[2 * layer : 2 * layer + 1, :])
        held["n1" + name][rows, :] = n1
        for part in "qkv":
            held[part + name][rows, :] = dot(n1, held["w" + part + name][...]).astype(bf16)

    for part in "qkv":
        ready["w" + part + "0"].wait()
    project(0, half, row_sent[...].astype(f32))
    block_copy(row_got, row_sems.at[1])
    project(0, 1 - half, row_got[...].astype(f32))

    for layer in range(layers):
        name = str(layer)
        for kept in ("x", "n1", "q", "k", "v"):
            keep(kept + name)
        held["lse" + name][...] = jnp.zeros((length, TILE), f32)

        def pair(p, carry, name=name):
            attend_pair(
                p, table, *(held[part + name] for part in ("q", "k", "v", "o", "lse")), mask, bias
            )
            return carry

        lax.fori_loop(0, narrow // TILE, pair, 0)
        ready["wo" + name].wait()
        for index in range(2):
            share_part(2 * layer, index, dot_nt(held["o" + name][rows_of(index), :], held["wo" + name][...]))
        keep("lse" + name)
        keep("o" + name)
        ready["wi" + name].wait()
        ready["wd" + name].wait()

        def feed(index, carry, layer=layer, name=name):
            rows = rows_of(index)
            value = total(2 * layer, index, held["x" + name])
            held["xm" + name][rows, :] = value
            n2 = rms_rows(value, gains[2 * layer + 1 : 2 * layer + 2, :])
            held["n2" + name][rows, :] = n2
            for column in range(0, wide, CHUNK):
                cols = pl.ds(column, CHUNK)
                g = dot(n2, held["wi" + name][0, :, cols])
                u = dot(n2, held["wi" + name][1, :, cols])
                held["gate" + name][rows, cols] = g.astype(bf16)
                held["up" + name][rows, cols] = u.astype(bf16)
                t = jnp.tanh(math.sqrt(2.0 / math.pi) * (g + 0.044715 * (g * g * g)))
                held["act" + name][rows, cols] = (0.5 * g * (1.0 + t) * u).astype(bf16)
            share_part(2 * layer + 1, index, dot_nt(held["act" + name][rows, :], held["wd" + name][...]))
            return carry

        lax.fori_loop(0, 2, feed, 0)
        for kept in ("xm", "n2", "gate", "up", "act"):
            keep(kept + name)
        if layer + 1 < layers:
            for part in "qkv":
                ready["w" + part + str(layer + 1)].wait()

            def following(index, carry, layer=layer, name=name):
                project(layer + 1, index, total(2 * layer + 1, index, held["xm" + name]))
                return carry

            lax.fori_loop(0, 2, following, 0)

    ready["w_proj"].wait()

    def finish(index, carry):
        rows = rows_of(index)
        value = total(2 * layers - 1, index, held["xm" + str(layers - 1)])
        held["state"][rows, :] = value
        final = rms_rows(value, gains[2 * layers : 2 * layers + 1, :])
        held["final"][rows, :] = final
        projected = dot(final, held["w_proj"][...])
        held["y"][rows, :] = projected
        scale = lax.rsqrt(jnp.sum(projected * projected, axis=-1, keepdims=True) + vector_eps)
        held["vectors"][rows, :] = (projected * scale).astype(bf16)
        return carry

    lax.fori_loop(0, 2, finish, 0)
    for name in ("state", "final", "y", "vectors"):
        keep(name)
    for copy in stores:
        copy.wait()
    block_copy(row_sent, row_sems.at[0])
    for turn in range(2 * layers):
        for index in range(2):
            block_copy(sent.at[turn, rows_of(index), :], send_sems.at[turn, index])


def forward(tokens, weights, tables):
    w_query, w_kv, w_out, w_in, w_down, w_proj = weights
    layers, model, narrow = w_query.shape
    wide, width = w_down.shape[2], w_proj.shape[1]
    length = 2 * tokens.shape[0]
    vmem, dma = pltpu.VMEM, pltpu.SemaphoreType.DMA
    sizes = dict(x=(model, f32), n1=(model, bf16), q=(narrow, bf16), k=(narrow, bf16), v=(narrow, bf16), lse=(TILE, f32),
                 o=(narrow, bf16), xm=(model, f32), n2=(model, bf16), gate=(wide, bf16), up=(wide, bf16), act=(wide, bf16))
    results = {name + str(layer): sizes[name] for layer in range(layers) for name in KEPT}
    results.update(state=(model, f32), final=(model, bf16), y=(width, f32), vectors=(width, bf16))
    made = {name: vmem((length, columns), kind) for name, (columns, kind) in results.items()}
    for layer in range(layers):
        for name in ("wq", "wk", "wv", "wo"):
            made[name + str(layer)] = vmem((model, narrow), bf16)
        made["wi" + str(layer)] = vmem((2, model, wide), bf16)
        made["wd" + str(layer)] = vmem((model, wide), bf16)
    made["w_proj"] = vmem((model, width), bf16)
    hbm, local = pl.BlockSpec(memory_space=pl.ANY), pl.BlockSpec(memory_space=vmem)
    found = pl.pallas_call(
        functools.partial(forward_kernel, tuple(made), tuple(results)),
        out_shape=tuple(jax.ShapeDtypeStruct((length, columns), kind) for columns, kind in results.values()),
        in_specs=[hbm] * 7 + [local] * 3,
        out_specs=(hbm,) * len(results),
        scratch_shapes=list(made.values())
        + [
            vmem(tokens.shape, bf16),
            vmem(tokens.shape, bf16),
            vmem((2 * layers, length, model), bf16),
            vmem((2 * layers, length, model), bf16),
            vmem((8, SPAN), f32),
            vmem((length, 3 * TILE), f32),
            vmem((2, TILE, 3 * TILE), f32),
            dma((6 * layers + 2,)),
            dma((len(results),)),
            dma((2,)),
            dma((2 * layers, 2)),
            dma((2 * layers, 2)),
        ],
        compiler_params=pltpu.CompilerParams(
            collective_id=2, has_side_effects=True, vmem_limit_bytes=62 * 1024 * 1024
        ),
        cost_estimate=pl.CostEstimate(flops=10**10, bytes_accessed=5 * 10**7, transcendentals=10**6),
        name="forward",
    )(tokens, *weights, *tables)
    return dict(zip(results, found))


CHUNK = 384


def block_copy(ref, sem):
    pltpu.make_async_copy(ref, ref, sem).wait()


class Sums:
    def __init__(self, refs):
        self.refs = refs
        self.side, self.batch = lax.axis_index(STREAM), lax.axis_index(BATCH)
        self.near, self.low, self.high = lax.rem(self.batch, 2), lax.rem(self.batch // 2, 2), self.batch // 4

    def stream_peer(self):
        return {STREAM: 1 - self.side}

    def near_peer(self):
        return {BATCH: self.batch + 1 - 2 * self.near}

    def low_peer(self):
        return {BATCH: self.batch + 2 - 4 * self.low}

    def high_peer(self):
        return {BATCH: self.batch + 4 - 8 * self.high}

    def slot(self, n):
        return n % RING

    def work(self, n):
        return self.refs["work"].at[n % self.refs["work"].shape[0]]

    def got(self, stage, n):
        return self.refs["got" + str(stage)].at[self.slot(n)]

    def send(self, source, stage, n, device):
        sems = self.refs["send"], self.refs["recv"]
        send(source, self.got(stage, n), sems[0].at[stage, self.slot(n)], sems[1].at[stage, self.slot(n)], device)

    def sent(self, stage, n):
        block_copy(self.got(stage, n), self.refs["send"].at[stage, self.slot(n)])

    def received(self, stage, n):
        block_copy(self.got(stage, n), self.refs["recv"].at[stage, self.slot(n)])

    def store(self, n):
        pltpu.make_async_copy(self.refs["done"].at[self.slot(n)], self.refs["out"](n), self.refs["store"].at[self.slot(n)]).start()

    def stored(self, n):
        block_copy(self.refs["done"].at[self.slot(n)], self.refs["store"].at[self.slot(n)])

    def add(self, count, place, got, at):
        def body(index, carry):
            target = place(index)
            target[...] = (target[...].astype(f32) + got[at(index)].astype(f32)).astype(bf16)
            return carry

        lax.fori_loop(0, count, body, 0)


class StreamFirst(Sums):
    stages = 5

    def half(self, side):
        rows = self.refs["work"].shape[4] // 2
        return pl.ds(pl.multiple_of(side * rows, 16), rows)

    def start(self, n):
        self.send(self.work(n).at[:, :, :, self.half(1 - self.side), :], 0, n, self.stream_peer())

    def step(self, n, stage):
        r, m = self.refs, self.slot(n)
        work, own = self.work(n), self.half(self.side)
        if stage <= 4:
            self.received(stage - 1, n)
        if stage == 1:
            self.add(
                8,
                lambda i: work.at[i // 4, lax.rem(i // 2, 2), lax.rem(i, 2), own, :],
                self.got(0, n),
                lambda i: (i // 4, lax.rem(i // 2, 2), lax.rem(i, 2)),
            )
            self.send(work.at[:, 1 - self.low, :, own, :], 1, n, self.low_peer())
        if stage == 2:
            self.add(
                4,
                lambda i: work.at[i // 2, self.low, lax.rem(i, 2), own, :],
                self.got(1, n),
                lambda i: (i // 2, lax.rem(i, 2)),
            )
            self.send(work.at[:, self.low, 1 - self.near, own, :], 2, n, self.near_peer())
        if stage == 3:
            self.add(2, lambda i: work.at[i, self.low, self.near, own, :], self.got(2, n), lambda i: (i,))
            self.send(work.at[1 - self.high, self.low, self.near, own, :], 3, n, self.high_peer())
            self.sent(0, n)
        if stage == 4:
            total = work[self.high, self.low, self.near, own, :].astype(f32) + r["got3"][m].astype(f32)
            r["last"][m] = total.astype(bf16)
            self.send(r["last"].at[m], 4, n, self.stream_peer())
            if n >= RING:
                self.stored(n)
            r["done"][m, own, :] = r["last"][m]
            for earlier in range(1, 4):
                self.sent(earlier, n)
        if stage == 5:
            self.received(4, n)
            r["done"][m, self.half(1 - self.side), :] = r["got4"][m]
            self.store(n)
            self.sent(4, n)


class BatchFirst(Sums):
    stages = 4

    def start(self, n):
        self.send(self.work(n).at[:, :, 1 - self.near], 0, n, self.near_peer())

    def step(self, n, stage):
        r, m = self.refs, self.slot(n)
        work = self.work(n)
        self.received(stage - 1, n)
        if stage == 1:
            self.add(
                4,
                lambda i: work.at[i // 2, lax.rem(i, 2), self.near],
                self.got(0, n),
                lambda i: (i // 2, lax.rem(i, 2)),
            )
            self.send(work.at[:, 1 - self.low, self.near], 1, n, self.low_peer())
        if stage == 2:
            self.add(2, lambda i: work.at[i, self.low, self.near], self.got(1, n), lambda i: (i,))
            self.send(work.at[1 - self.high, self.low, self.near], 2, n, self.high_peer())
        if stage == 3:
            total = work[self.high, self.low, self.near].astype(f32) + r["got2"][m].astype(f32)
            r["last"][m] = total.astype(bf16)
            self.send(r["last"].at[m], 3, n, self.stream_peer())
            for earlier in range(3):
                self.sent(earlier, n)
        if stage == 4:
            if n >= RING:
                self.stored(n)
            r["done"][m] = (r["last"][m].astype(f32) + r["got3"][m].astype(f32)).astype(bf16)
            self.store(n)
            self.sent(3, n)


RING = 4
WORK_RING = 5
FIRST_REFS = ("work", "got0", "got1", "got2", "got3", "got4", "last", "done", "send", "recv", "store")
LAST_REFS = ("work", "got0", "got1", "got2", "got3", "last", "done", "send", "recv", "store")


def first_scratch(rows, width, ring, work_ring):
    vmem, dma = pltpu.VMEM, pltpu.SemaphoreType.DMA
    half = rows // 2
    return [
        vmem((work_ring, 2, 2, 2, rows, width), bf16),
        vmem((ring, 2, 2, 2, half, width), bf16),
        vmem((ring, 2, 2, half, width), bf16),
        vmem((ring, 2, half, width), bf16),
        vmem((ring, half, width), bf16),
        vmem((ring, half, width), bf16),
        vmem((ring, half, width), bf16),
        vmem((ring, rows, width), bf16),
        dma((5, ring)),
        dma((5, ring)),
        dma((ring,)),
    ]


def last_scratch(rows, width, ring, work_ring):
    vmem, dma = pltpu.VMEM, pltpu.SemaphoreType.DMA
    return [
        vmem((work_ring, 2, 2, 2, rows, width), bf16),
        vmem((ring, 2, 2, rows, width), bf16),
        vmem((ring, 2, rows, width), bf16),
        vmem((ring, rows, width), bf16),
        vmem((ring, rows, width), bf16),
        vmem((ring, rows, width), bf16),
        vmem((ring, rows, width), bf16),
        dma((4, ring)),
        dma((4, ring)),
        dma((ring,)),
    ]


def blocks_of(wide):
    found = []
    for layer in (1, 0):
        for left, right, output, index in (("e", "act", 0, ()), ("n2", "gate", 1, (0,)), ("n2", "up", 1, (1,))):
            found += [(left + str(layer), right + str(layer), c * CHUNK, output, (layer,) + index) for c in range(wide // CHUNK)]
        for left, right, output, index in (("c", "o", 2, ()), ("n1", "dq", 3, ()), ("n1", "dk", 4, (0,)), ("n1", "dv", 4, (1,))):
            found.append((left + str(layer), right + str(layer), 0, output, (layer,) + index))
    return found


def back_kernel(names, made, blocks, *refs):
    given, refs = dict(zip(names, refs)), refs[len(names) :]
    (rel_bias, segments, gains, projected, grad_vectors, w_proj), refs = refs[:6], refs[6:]
    outs, refs = refs[:8], refs[8:]
    held, refs = dict(zip(made, refs)), refs[len(made) :]
    (acc, core_sent, core_got, table, mask, bias, grid, dk_sum, dv_sum, do, little_got), refs = refs[:11], refs[11:]
    (load_sems, core_sems, little_sems), refs = refs[:3], refs[3:]
    firsts, lasts = blocks[0::2], blocks[1::2]
    half = len(blocks) // 2

    def out_of(blocks):
        def place(n):
            _, _, column, output, index = blocks[n]
            return outs[output].at[index + (slice(None), pl.ds(column, CHUNK))]

        return place

    first_refs, refs = dict(zip(FIRST_REFS, refs), out=out_of(firsts)), refs[len(FIRST_REFS) :]
    last_refs, refs = dict(zip(LAST_REFS, refs), out=out_of(lasts)), refs[len(LAST_REFS) :]
    stream_first, batch_first = StreamFirst(first_refs), BatchFirst(last_refs)
    projection = BatchFirst(dict(zip(LAST_REFS, refs), out=lambda n: outs[5]))
    half_index = lax.axis_index(MP)
    core = {MP: 1 - half_index}
    length, model = held["grad"].shape
    tiles = length // TILE

    loads = {}

    def fetch(name, source=None, target=None):
        copy = pltpu.make_async_copy(
            given[name] if source is None else source, held[name] if target is None else target, load_sems.at[len(loads)]
        )
        copy.start()
        loads[name] = [copy, False]

    def need(name):
        if name in loads and not loads[name][1]:
            loads[name][0].wait()
            loads[name][1] = True
        return held.get(name)

    def fetch_attention(layer):
        for name in ("wo", "q", "k", "v", "lse", "wq", "wk", "wv", "x"):
            source = given[name + str(layer)] if name + str(layer) in given else None
            if name == "wo":
                source = given["w_out"].at[layer]
            if name == "wq":
                source = given["w_query"].at[layer]
            if name in ("wk", "wv"):
                source = given["w_kv"].at[layer, 0 if name == "wk" else 1]
            fetch(name + str(layer), source, held[name])

    def fetch_ffn(layer):
        fetch("wd" + str(layer), given["wd"].at[layer], held["wd"])
        fetch("wi" + str(layer), given["wi"].at[layer], held["wi"])
        fetch("xm" + str(layer), None, held["xm"])

    fetch("state", None, held["x"])
    fetch("act1")
    fetch("wd1", given["wd"].at[1], held["wd"])
    for name in ("gate1", "up1"):
        fetch(name)
    fetch("wi1", given["wi"].at[1], held["wi"])
    fetch("xm1", None, held["xm"])
    fetch("n21")
    for name in ("o1", "n11", "gate0", "up0", "act0", "n20", "o0", "n10", "final"):
        fetch(name)

    barrier = pltpu.get_barrier_semaphore()
    peers = [stream_first.stream_peer(), stream_first.near_peer(), stream_first.low_peer(), stream_first.high_peer(), core]
    for peer in peers:
        pl.semaphore_signal(barrier, inc=1, device_id=peer, device_id_type=pl.DeviceIdType.MESH)


    def product(left, right, work):
        width = left.shape[1] // 2
        for part in range(2):
            block = dot_tn(left[:, part * width : (part + 1) * width], right).astype(bf16)
            work[part] = block.reshape(work.shape[1:])

    def make(sums, blocks, n):
        left, right, column, _, _ = blocks[n]
        product(need(left), need(right)[:, column : column + CHUNK], sums.work(n))
        if n == 0 and sums is stream_first:
            pl.semaphore_wait(barrier, len(peers))
        sums.start(n)

    def little_step(stage):
        peer = (stream_first.stream_peer, stream_first.near_peer, stream_first.low_peer, stream_first.high_peer)
        if stage > 0:
            block_copy(little_got.at[2 * stage - 1], little_sems.at[2 * stage - 1])
            total = little_got[2 * stage - 2] + little_got[2 * stage - 1]
            block_copy(little_got.at[2 * stage - 2], little_sems.at[2 * stage - 2])
            if stage == 4:
                outs[6][...] = total
            else:
                little_got[2 * stage] = total
        if stage < 4:
            send(
                little_got.at[2 * stage], little_got.at[2 * stage + 1],
                little_sems.at[2 * stage], little_sems.at[2 * stage + 1], peer[stage](),
            )


    grad = held["grad"]

    def rows_of(index):
        return pl.ds(pl.multiple_of(index * TILE, TILE), TILE)

    def share(turn):
        def pack(index, carry):
            core_sent[rows_of(index), :] = acc[rows_of(index), :].astype(bf16)
            return carry

        lax.fori_loop(0, tiles, pack, 0)
        send(core_sent, core_got.at[turn % 2], core_sems.at[0, turn], core_sems.at[1, turn], core)

    def norm_back(values, gain, gradient, first):
        weight = gains[gain : gain + 1, :]

        def tile(index, total):
            rows = rows_of(index)
            given_grad = gradient(rows)
            value = values[rows, :]
            scale = lax.rsqrt(jnp.mean(value * value, axis=-1, keepdims=True) + norm_eps)
            weighted = given_grad * weight
            along = jnp.mean(value * weighted, axis=-1, keepdims=True)
            change = scale * weighted - value * (scale * scale * scale * along)
            grad[rows, :] = change if first else grad[rows, :] + change
            return total + jnp.sum(given_grad * (value * scale), axis=0, keepdims=True)

        total = lax.fori_loop(0, tiles, tile, jnp.zeros((1, model), f32))
        little_got[0, gain : gain + 1, 0:model] = total

    def through_norm(turn, values, gain):
        block_copy(core_got.at[turn % 2], core_sems.at[1, turn])
        norm_back(
            values, gain, lambda rows: core_sent[rows, :].astype(f32) + core_got[turn % 2, rows, :].astype(f32), False
        )
        block_copy(core_sent, core_sems.at[0, turn])

    def projection_back():
        def tile(index, carry):
            rows = rows_of(index)
            y, grad_vector = projected[rows, :], grad_vectors[rows, :]
            scale = lax.rsqrt(jnp.sum(y * y, axis=-1, keepdims=True) + vector_eps)
            along = jnp.sum(y * grad_vector, axis=-1, keepdims=True)
            held["dproj"][rows, :] = (scale * grad_vector - y * (scale * scale * scale * along)).astype(bf16)
            return carry

        lax.fori_loop(0, tiles, tile, 0)
        need("state")
        norm_back(held["x"], 4, lambda rows: dot_nt(held["dproj"][rows, :], w_proj[...]), True)

    def round_grad(target):
        def pack(index, carry):
            target[rows_of(index), :] = grad[rows_of(index), :].astype(bf16)
            return carry

        lax.fori_loop(0, tiles, pack, 0)

    def ffn_tile(layer, column):
        cols = pl.ds(column, CHUNK)
        e, gate, up = (held[name + str(layer)] for name in ("e", "gate", "up"))

        def tile(index, carry):
            rows = pl.ds(pl.multiple_of(index * 2 * TILE, 2 * TILE), 2 * TILE)
            grad_hidden = dot(e[rows, :], held["wd"][:, cols])
            g, u = gate[rows, cols].astype(f32), up[rows, cols].astype(f32)
            root = math.sqrt(2.0 / math.pi)
            t = jnp.tanh(root * (g + 0.044715 * (g * g * g)))
            slope = 0.5 * (1.0 + t) + (0.5 * root) * g * (1.0 - t * t) * (1.0 + (3 * 0.044715) * (g * g))
            dg = (grad_hidden * u * slope).astype(bf16)
            du = (grad_hidden * (0.5 * g * (1.0 + t))).astype(bf16)
            gate[rows, cols] = dg
            up[rows, cols] = du
            part = dot_nt(dg, held["wi"][0, :, cols]) + dot_nt(du, held["wi"][1, :, cols])
            acc[rows, :] = part if column == 0 else acc[rows, :] + part
            return carry

        lax.fori_loop(0, tiles // 2, tile, 0)

    def attention_start(layer):
        c = held["c" + str(layer)]
        round_grad(c)

        def tile(index, carry):
            rows = pl.ds(pl.multiple_of(index * 2 * TILE, 2 * TILE), 2 * TILE)
            do[rows, :] = dot(c[rows, :], held["wo"][...]).astype(bf16)
            return carry

        need("wo" + str(layer))
        lax.fori_loop(0, tiles // 2, tile, 0)
        for name in ("q", "k", "v", "lse"):
            need(name + str(layer))

    def attention_pair(layer, p):
        attend_back_pair(
            p, table, held["lse"], held["q"], held["k"], held["v"], do,
            held["dq" + str(layer)], held["dk" + str(layer)], held["dv" + str(layer)],
            mask, bias, grid, dk_sum, dv_sum,
        )
        for half in range(2):
            line = diagonals(grid, half)
            place = (0, pl.ds(2 * p + half, 1), pl.ds(model, SPAN))
            little_got[place] = little_got[place] + line

    def attention_end(layer, turn):
        for name in ("wq", "wk", "wv"):
            need(name + str(layer))

        def tile(index, carry):
            rows = pl.ds(pl.multiple_of(index * 2 * TILE, 2 * TILE), 2 * TILE)
            acc[rows, :] = (
                dot_nt(held["dq" + str(layer)][rows, :], held["wq"][...])
                + dot_nt(held["dk" + str(layer)][rows, :], held["wk"][...])
                + dot_nt(held["dv" + str(layer)][rows, :], held["wv"][...])
            )
            return carry

        lax.fori_loop(0, tiles // 2, tile, 0)
        share(turn)

    def ffn_half(layer, part):
        if part == 0:
            for name in ("wd", "wi", "gate", "up"):
                need(name + str(layer))
        ffn_tile(layer, 2 * part * CHUNK)
        ffn_tile(layer, (2 * part + 1) * CHUNK)

    def piece0():
        ffn_half(1, 0)

    def piece1():
        ffn_half(1, 1)
        share(0)
        fill_table(rel_bias, table)
        fill_masks(row_ids_of(segments), mask, tiles)

    def piece2():
        need("xm1")
        through_norm(0, held["xm"], 3)
        fetch_ffn(0)
        attention_start(1)
        attention_pair(1, 0)

    def piece6():
        need("x1")
        through_norm(1, held["x"], 2)
        fetch_attention(0)
        round_grad(held["e0"])
        ffn_half(0, 0)

    def piece7():
        ffn_half(0, 1)
        share(2)

    def piece8():
        need("xm0")
        through_norm(2, held["xm"], 1)
        attention_start(0)
        attention_pair(0, 0)

    def piece12():
        need("x0")
        through_norm(3, held["x"], 0)
        share_rows = length // 2
        outs[7][...] = grad[pl.ds(pl.multiple_of(half_index * share_rows, TILE), share_rows), :]

    pieces = [
        piece0,
        piece1,
        piece2,
        lambda: attention_pair(1, 1),
        lambda: attention_pair(1, 2),
        lambda: attention_end(1, 1),
        piece6,
        piece7,
        piece8,
        lambda: attention_pair(0, 1),
        lambda: attention_pair(0, 2),
        lambda: attention_end(0, 3),
        piece12,
    ]
    little_got[0] = jnp.zeros(little_got.shape[1:], f32)
    projection_back()
    fetch_attention(1)
    round_grad(held["e1"])
    for t in range(half + 5):
        if t < half:
            make(stream_first, firsts, t)
            make(batch_first, lasts, t)
        if t == half - 3:
            product(need("final"), held["dproj"][...], projection.work(0))
            projection.start(0)
        if t < len(pieces):
            pieces[t]()
        for stage in (1, 2, 3, 4, 5):
            if 0 <= t - stage < half:
                stream_first.step(t - stage, stage)
                if stage <= 4:
                    batch_first.step(t - stage, stage)
            if t - stage == half - 3 and stage <= 4:
                projection.step(0, stage)
        if 0 <= t - (half - 3) <= 4:
            little_step(t - (half - 3))
    for n in range(half - RING, half):
        stream_first.stored(n)
        batch_first.stored(n)
    projection.stored(0)


def back(chain, weights, tables):
    batch = lax.axis_size(BATCH)
    length, model = chain["x0"].shape
    rows = model // batch
    narrow, wide = chain["q1"].shape[1], chain["act1"].shape[1]
    width = tables[-1].shape[1]
    little = jax.ShapeDtypeStruct((8, model + SPAN), f32)
    blocks = blocks_of(wide)
    given = dict(chain, **weights)
    vmem, dma, shape = pltpu.VMEM, pltpu.SemaphoreType.DMA, jax.ShapeDtypeStruct
    made = {"grad": (length, model), "x": (length, model), "xm": (length, model), "lse": (length, TILE)}
    made = {name: vmem(dims, f32) for name, dims in made.items()}
    for name in ("e", "n2", "c", "n1"):
        made.update({name + layer: vmem((length, model), bf16) for layer in "01"})
    for name in ("act", "gate", "up"):
        made.update({name + layer: vmem((length, wide), bf16) for layer in "01"})
    for name in ("o", "dq", "dk", "dv"):
        made.update({name + layer: vmem((length, narrow), bf16) for layer in "01"})
    made.update({name: vmem((length, narrow), bf16) for name in "qkv"})
    made.update({name: vmem((model, narrow), bf16) for name in ("wo", "wq", "wk", "wv")})
    made.update(wd=vmem((model, wide), bf16), wi=vmem((2, model, wide), bf16))
    made.update(final=vmem((length, model), bf16), dproj=vmem((length, width), bf16))
    ins = [pl.BlockSpec(memory_space=pl.ANY)] * len(given) + [pl.BlockSpec(memory_space=vmem)] * 6
    hbm, local = pl.BlockSpec(memory_space=pl.ANY), pl.BlockSpec(memory_space=vmem)
    return pl.pallas_call(
        functools.partial(back_kernel, tuple(given), tuple(made), blocks),
        out_shape=(
            shape((2, rows, wide), bf16),
            shape((2, 2, rows, wide), bf16),
            shape((2, rows, narrow), bf16),
            shape((2, rows, narrow), bf16),
            shape((2, 2, rows, narrow), bf16),
            shape((rows, width), bf16),
            shape(little.shape, f32),
            shape((length // 2, model), f32),
        ),
        in_specs=ins,
        out_specs=(hbm,) * 6 + (local,) * 2,
        scratch_shapes=list(made.values())
        + [
            vmem((length, model), f32),
            vmem((length, model), bf16),
            vmem((2, length, model), bf16),
            vmem((8, SPAN), f32),
            vmem((length, 3 * TILE), f32),
            vmem((2, TILE, 3 * TILE), f32),
            vmem((2, TILE, SPAN), f32),
            vmem((length, TILE), f32),
            vmem((length, TILE), f32),
            vmem((length, narrow), bf16),
            vmem((8,) + little.shape, f32),
            dma((64,)),
            dma((2, 4)),
            dma((8,)),
        ]
        + first_scratch(rows, CHUNK, RING, WORK_RING)
        + last_scratch(rows, CHUNK, RING, WORK_RING)
        + last_scratch(rows, width, 1, 1),
        compiler_params=pltpu.CompilerParams(
            collective_id=1, has_side_effects=True, vmem_limit_bytes=62 * 1024 * 1024
        ),
        cost_estimate=pl.CostEstimate(flops=2 * 10**10, bytes_accessed=5 * 10**7, transcendentals=10**6),
        name="back",
    )(*given.values(), *tables)


def place_kernel(down, into, out, query, key_value, projection, little, grad, vectors, losses, *outs):
    share = outs[0].shape[0]
    first = pl.multiple_of(lax.axis_index(MP) * share, TILE)
    outs[0][...] = vectors[pl.ds(first, share), :]
    outs[1][...] = losses[...]
    for source, target in zip((grad, query, key_value, out, into, down, projection), outs[2:8] + outs[10:]):
        target[...] = source[...].astype(f32)
    gains, bias = outs[8], outs[9]
    model = grad.shape[1]
    count, rows = gains.shape
    moved = pltpu.roll(little[:, 0:model], lax.rem(model - lax.axis_index(BATCH) * rows, model), axis=1)
    gains[...] = moved[0:count, 0:rows]
    bias[...] = lax.dot_general(
        little[0 : bias.shape[0], model:],
        bucket_places(bias.shape[1]),
        (((1,), (1,)), ((), ())),
        precision=highest,
        preferred_element_type=f32,
    )


def place(summed, vectors, losses, gain_count, bias_shape):
    down, into, out, query, key_value, projection, little, grad = summed
    shape = jax.ShapeDtypeStruct
    local = pl.BlockSpec(memory_space=pltpu.VMEM)
    return pl.pallas_call(
        place_kernel,
        out_shape=(shape((grad.shape[0], vectors.shape[1]), bf16), shape(losses.shape, f32))
        + tuple(shape(value.shape, f32) for value in (grad, query, key_value, out, into, down))
        + (shape((gain_count, query.shape[1]), f32), shape(bias_shape, f32), shape(projection.shape, f32)),
        in_specs=[local] * 10,
        out_specs=(local,) * 11,
        compiler_params=pltpu.CompilerParams(vmem_limit_bytes=60 * 1024 * 1024),
        name="place",
    )(*summed, vectors, losses)


def sum_gradients_plainly(kept, final_pair, little):
    def summed(left, right):
        part = lax.psum_scatter(dot_tn(left, right).astype(bf16), BATCH, scatter_dimension=0, tiled=True)
        return sum_of_two(part, STREAM)

    found = []
    for e, n2, c, n1, hidden, dg, du, o, dq, dk, dv in kept:
        found.append((
            summed(e, hidden),
            jnp.stack([summed(n2, dg), summed(n2, du)]),
            summed(c, o),
            summed(n1, dq),
            jnp.stack([summed(n1, dk), summed(n1, dv)]),
        ))
    return [jnp.stack(parts) for parts in zip(*found)] + [
        summed(*final_pair),
        lax.psum(little, (STREAM, BATCH)),
    ]


def on_device(
    tokens,
    segments,
    top_mask,
    positive,
    w_query,
    w_kv,
    w_out,
    w_in,
    w_down,
    gains,
    rel_bias,
    w_proj,
):
    length = segments.shape[1]
    share_len, model_width = tokens.shape[2:]
    head_count = rel_bias.shape[1]
    layers = w_query.shape[0]
    batch = lax.axis_size(BATCH)
    bias_rows = jnp.transpose(rel_bias)
    tables = (bias_rows, segments, gains)
    kept = forward(tokens[0, 0], (w_query, w_kv, w_out, w_in, w_down, w_proj), tables)
    vectors = kept["vectors"]
    grad_vectors, query_loss = score(
        vectors, segments, top_mask, positive
    )
    if layers == 2 and batch == 8:
        chain = {name: value for name, value in kept.items() if name not in ("y", "vectors")}
        weights = dict(w_query=w_query, w_kv=w_kv, w_out=w_out, wi=w_in, wd=w_down)
        summed = back(chain, weights, tables + (kept["y"], grad_vectors, w_proj))
        placed = place(summed, vectors, query_loss, gains.shape[0], bias_rows.shape)
        return (placed[0][None, None], placed[1], placed[2][None, None]) + placed[3:9] + (placed[9].T, placed[10])
    else:
        row_segments = jnp.where(
            lax.axis_index(STREAM) == 0, jnp.arange(length, dtype=jnp.int32) // QLEN, segments[0]
        )
        row_ids = row_segments[None]
        offset_onehot = (
            offset_buckets()[None, :] == jnp.arange(rel_bias.shape[0], dtype=jnp.int32)[:, None]
        ).astype(f32)
        table = jnp.einsum(
            "bh,bk->hk", jnp.pad(rel_bias, ((0, 0), (0, 8 - head_count))), offset_onehot, precision=highest
        )
        kept_layers = [[kept[name + str(layer)] for name in KEPT] for layer in range(layers)]
        grad_projected = jax.vjp(normalize, kept["y"])[1](grad_vectors)[0].astype(bf16)
        grad_final = dot_nt(grad_projected, w_proj)
        grad_state, grad_gain_final = jax.vjp(rms_scale, kept["state"], gains[2 * layers])[1](grad_final)
        gain_grads = [None] * (2 * layers)
        operands = [None] * layers
        sums = jnp.zeros(table.shape, f32)
        for layer in reversed(range(layers)):
            weights_layer = (
                w_query[layer],
                w_kv[layer],
                w_out[layer],
                w_in[layer],
                w_down[layer],
                gains[2 * layer],
                gains[2 * layer + 1],
            )
            grad_state, ffn_lefts, ffn_rights, gain_grads[2 * layer + 1] = ffn_backward(
                grad_state, kept_layers[layer], weights_layer
            )
            grad_state, lefts, rights, gain_grads[2 * layer], part = attention_backward(
                grad_state, table, row_ids, kept_layers[layer], weights_layer
            )
            operands[layer] = ffn_lefts + lefts + ffn_rights + rights
            sums = sums + part
        little = jnp.concatenate(
            [jnp.pad(jnp.stack(gain_grads + [grad_gain_final]), ((0, 7 - 2 * layers), (0, 0))), sums], axis=1
        )
        summed = sum_gradients_plainly(operands, (kept["final"], grad_projected), little)
        grad_down, grad_in, grad_out, grad_query, grad_kv, grad_proj, little = summed
        own_grad = lax.dynamic_slice_in_dim(grad_state, lax.axis_index(MP) * share_len, share_len, 0)
        grad_bias = jnp.einsum("hk,bk->bh", little[:, model_width:], offset_onehot, precision=highest)
        rows = model_width // batch
        grad_gains = lax.dynamic_slice(little, (0, lax.axis_index(BATCH) * rows), (2 * layers + 1, rows))
    own_vectors = lax.dynamic_slice_in_dim(vectors, lax.axis_index(MP) * share_len, share_len, 0)
    return (
        own_vectors[None, None],
        query_loss,
        own_grad[None, None],
        grad_query,
        grad_kv,
        grad_out,
        grad_in,
        grad_down,
        grad_gains,
        grad_bias[:, :head_count],
        grad_proj,
    )


def solution(mesh):
    placed = (
        P(STREAM, BATCH, MP, None),
        P(BATCH, None),
        P(None, MP, BATCH, None),
        P(None, MP),
        P(None, None, MP),
        P(None, None, None, MP),
        P(None, None, MP),
        P(None, None, None, MP),
        P(None, None, MP),
        P(),
        P(None, MP),
        P(),
    )
    return jax.shard_map(
        on_device,
        mesh=mesh,
        in_specs=placed,
        out_specs=(
            P(STREAM, BATCH, MP, None),
            P(BATCH, MP),
            P(STREAM, BATCH, MP, None),
            P(None, BATCH, MP),
            P(None, None, BATCH, MP),
            P(None, BATCH, MP),
            P(None, None, BATCH, MP),
            P(None, BATCH, MP),
            P(None, BATCH),
            P(None, MP),
            P(BATCH, None),
        ),
        check_vma=False,
    )
```

```python
import functools
import math

import jax
import jax.numpy as jnp
from jax import lax
from jax.experimental import pallas as pl
from jax.experimental.pallas import tpu as pltpu
from jax.sharding import PartitionSpec as P

QLEN = 32
DOCS_ROW = 8
TILE = 128
STREAM, BATCH, MP = "stream", "batch", "mp"
SPAN = 512


norm_eps = 1e-06
vector_eps = 1e-06
temper = 0.05
logit_scale = 32.0
bucket_edges = (12, 16, 23, 32, 46, 64, 91)
highest = lax.Precision.HIGHEST
bf16 = jnp.bfloat16
f32 = jnp.float32


def dot(a, b):
    return lax.dot_general(a, b, (((1,), (0,)), ((), ())), preferred_element_type=f32)


def dot_nt(a, b):
    return lax.dot_general(a, b, (((1,), (1,)), ((), ())), preferred_element_type=f32)


def dot_tn(a, b):
    return lax.dot_general(a, b, (((0,), (0,)), ((), ())), preferred_element_type=f32)


def offset_buckets():
    index = jnp.arange(SPAN, dtype=jnp.int32)
    offsets = jnp.where(index < SPAN // 2, index, index - SPAN)
    magnitude = jnp.abs(offsets)
    far_bucket = jnp.full(offsets.shape, 8, jnp.int32)
    for threshold in bucket_edges:
        far_bucket = far_bucket + (magnitude >= threshold).astype(jnp.int32)
    bucket = jnp.where(magnitude < 8, magnitude, jnp.minimum(far_bucket, 15))
    return bucket + jnp.where(offsets > 0, 16, 0).astype(jnp.int32)


def bucket_places(count):
    index = lax.broadcasted_iota(jnp.int32, (count, SPAN), 1)
    offsets = jnp.where(index < SPAN // 2, index, index - SPAN)
    magnitude = jnp.abs(offsets)
    far_bucket = jnp.full(offsets.shape, 8, jnp.int32)
    for threshold in bucket_edges:
        far_bucket = far_bucket + jnp.where(magnitude >= threshold, 1, 0)
    bucket = jnp.where(magnitude < 8, magnitude, jnp.minimum(far_bucket, 15))
    bucket = bucket + jnp.where(offsets > 0, 16, 0)
    return jnp.where(bucket == lax.broadcasted_iota(jnp.int32, (count, SPAN), 0), 1.0, 0.0)


def fill_table(rel_bias, table):
    table[...] = jnp.zeros(table.shape, f32)
    table[0 : rel_bias.shape[0], :] = lax.dot_general(
        rel_bias[...],
        bucket_places(rel_bias.shape[1]),
        (((1,), (0,)), ((), ())),
        precision=highest,
        preferred_element_type=f32,
    )


def row_ids_of(segments):
    position = lax.broadcasted_iota(jnp.int32, segments.shape, 1)
    return jnp.where(lax.axis_index(STREAM) == 0, position // QLEN, segments[...])


def window(tile, tiles):
    first, last = max(0, tile - 1), min(tiles, tile + 2)
    shift = first - (tile - 1)
    return pl.ds(first * TILE, (last - first) * TILE), slice(shift * TILE, (shift + last - first) * TILE)


def fill_masks(row_ids, mask, tiles):
    ids = row_ids.astype(f32)
    lines = [jnp.broadcast_to(ids[:, tile * TILE : (tile + 1) * TILE], (TILE, TILE)) for tile in range(tiles)]
    for tile in range(tiles):
        own = jnp.transpose(lines[tile])
        for near in range(max(0, tile - 1), min(tiles, tile + 2)):
            place = (near - tile + 1) * TILE
            mask[tile * TILE : (tile + 1) * TILE, place : place + TILE] = jnp.where(own == lines[near], 0.0, -1e30)


def bias_tile(table, head):
    line = jnp.broadcast_to(table[pl.ds(head, 1), :], (TILE, SPAN))
    return pltpu.roll(line, TILE, axis=1, stride=1, stride_axis=0)[:, : 3 * TILE]


def attend_pair(p, table, q, k, v, o, lse, mask, bias):
    tiles = q.shape[0] // TILE
    lane = lax.broadcasted_iota(jnp.int32, (TILE, TILE), 1)
    cols = pl.ds(pl.multiple_of(p * TILE, TILE), TILE)
    for half in range(2):
        bias[half] = bias_tile(table, 2 * p + half)
    scores = []
    for tile in range(tiles):
        rows = pl.ds(tile * TILE, TILE)
        keys, frame = window(tile, tiles)
        queries, near_keys = q[rows, cols], k[keys, cols]
        for half in range(2):
            mine = (lane >= 64) if half else (lane < 64)
            s = dot_nt(jnp.where(mine, queries, jnp.zeros_like(queries)), near_keys)
            scores.append(s + (bias[half][:, frame] + mask[rows, frame]))
    tops = [jnp.max(s, axis=-1, keepdims=True) for s in scores]
    exps = [jnp.exp(s - top) for s, top in zip(scores, tops)]
    totals = [jnp.sum(e, axis=-1, keepdims=True) for e in exps]
    weights = [(e * (1.0 / total)).astype(bf16) for e, total in zip(exps, totals)]
    for tile in range(tiles):
        rows = pl.ds(tile * TILE, TILE)
        near_values = v[window(tile, tiles)[0], cols]
        outs = [dot(weights[2 * tile + half], near_values) for half in range(2)]
        o[rows, cols] = jnp.where(lane < 64, outs[0], outs[1]).astype(bf16)
        kept = lse[rows, :]
        for half in range(2):
            index = 2 * tile + half
            kept = jnp.where(lane == 2 * p + half, tops[index] + jnp.log(totals[index]), kept)
        lse[rows, :] = kept


def attend_back_pair(p, table, lse, q, k, v, do, dq, dk, dv, mask, bias, grid, dk_sum, dv_sum):
    tiles = q.shape[0] // TILE
    lane = lax.broadcasted_iota(jnp.int32, (TILE, TILE), 1)
    cols = pl.ds(pl.multiple_of(p * TILE, TILE), TILE)
    for half in range(2):
        bias[half] = bias_tile(table, 2 * p + half)
    grid[...] = jnp.zeros(grid.shape, f32)
    dk_sum[...] = jnp.zeros(dk_sum.shape, f32)
    dv_sum[...] = jnp.zeros(dv_sum.shape, f32)
    for first in range(0, tiles, 2):
        some = [(tile, half) for tile in range(first, min(first + 2, tiles)) for half in range(2)]
        own_queries, own_grads, weights, grad_weights = [], [], [], []
        for tile, half in some:
            rows = pl.ds(tile * TILE, TILE)
            keys, frame = window(tile, tiles)
            mine = (lane >= 64) if half else (lane < 64)
            queries, grads = q[rows, cols], do[rows, cols]
            own_queries.append(jnp.where(mine, queries, jnp.zeros_like(queries)))
            own_grads.append(jnp.where(mine, grads, jnp.zeros_like(grads)))
            log_total = jnp.sum(jnp.where(lane == 2 * p + half, lse[rows, :], 0.0), axis=-1, keepdims=True)
            s = dot_nt(own_queries[-1], k[keys, cols])
            s = s + (bias[half][:, frame] + mask[rows, frame])
            weights.append(jnp.exp(s - log_total))
            grad_weights.append(dot_nt(own_grads[-1], v[keys, cols]))
        means = [jnp.sum(w * g, axis=-1, keepdims=True) for w, g in zip(weights, grad_weights)]
        ds = [(w * (g - mean)).astype(bf16) for w, g, mean in zip(weights, grad_weights, means)]
        outs = []
        for index, (tile, half) in enumerate(some):
            keys, frame = window(tile, tiles)
            outs.append(dot(ds[index], k[keys, cols]))
            dk_sum[keys, :] += dot_tn(ds[index], own_queries[index])
            dv_sum[keys, :] += dot_tn(weights[index].astype(bf16), own_grads[index])
            grid[half, :, frame] += ds[index].astype(f32)
        for index in range(0, len(some), 2):
            rows = pl.ds(some[index][0] * TILE, TILE)
            dq[rows, cols] = jnp.where(lane < 64, outs[index], outs[index + 1]).astype(bf16)
    dk[:, cols] = dk_sum[...].astype(bf16)
    dv[:, cols] = dv_sum[...].astype(bf16)


def diagonals(grid, half):
    row_index = lax.broadcasted_iota(jnp.int32, (TILE, SPAN), 0)
    turned = pltpu.roll(grid[half], SPAN - TILE, axis=1)
    for bit in range(7):
        moved = pltpu.roll(turned, SPAN - (1 << bit), axis=1)
        turned = jnp.where((row_index >> bit) & 1 == 1, moved, turned)
    return jnp.sum(turned, axis=0, keepdims=True)


def attend_back_kernel(
    table, row_ids, lse, q, k, v, do, dq, dk, dv, sums, mask, bias, grid, dk_sum, dv_sum
):
    fill_masks(row_ids[...], mask, q.shape[0] // TILE)
    sums[...] = jnp.zeros(sums.shape, f32)

    def pair(p, carry):
        attend_back_pair(p, table, lse, q, k, v, do, dq, dk, dv, mask, bias, grid, dk_sum, dv_sum)
        for half in range(2):
            sums[pl.ds(2 * p + half, 1), :] = diagonals(grid, half)
        return carry

    lax.fori_loop(0, q.shape[1] // TILE, pair, 0)


def attend_back(table, row_ids, lse, q, k, v, do):
    length, width = q.shape
    grad = jax.ShapeDtypeStruct((length, width), bf16)
    return pl.pallas_call(
        attend_back_kernel,
        out_shape=(grad, grad, grad, jax.ShapeDtypeStruct(table.shape, f32)),
        scratch_shapes=[
            pltpu.VMEM((length, 3 * TILE), f32),
            pltpu.VMEM((2, TILE, 3 * TILE), f32),
            pltpu.VMEM((2, TILE, SPAN), f32),
            pltpu.VMEM((length, TILE), f32),
            pltpu.VMEM((length, TILE), f32),
        ],
        compiler_params=pltpu.CompilerParams(vmem_limit_bytes=32 * 1024 * 1024),
        cost_estimate=pl.CostEstimate(flops=25 * 10**8, bytes_accessed=4 * 10**6, transcendentals=10**6),
        name="attend_back",
    )(table, row_ids, lse, q, k, v, do)


def rms_scale(values, gain_row):
    return (
        values * lax.rsqrt(jnp.mean(values * values, axis=-1, keepdims=True) + norm_eps) * gain_row
    )


def gated_gelu(gate, up):
    return jax.nn.gelu(gate, approximate=True) * up


def normalize(values):
    return values * lax.rsqrt(jnp.sum(values * values, axis=-1, keepdims=True) + vector_eps)


def swap(value, axis):
    return lax.ppermute(value, axis, [(0, 1), (1, 0)])


def sum_of_two(part, axis):
    mine = lax.optimization_barrier(part.astype(bf16))
    return mine.astype(f32) + swap(mine, axis).astype(f32)


def ffn_backward(grad_output, kept, weights_layer):
    middle, ffn_input, gate, up, hidden = kept[7:]
    in_weight, down_weight, gain_ffn = weights_layer[3], weights_layer[4], weights_layer[6]
    grad_branch = grad_output.astype(bf16)
    grad_hidden = dot(grad_branch, down_weight)
    grad_gate, grad_up = jax.vjp(gated_gelu, gate.astype(f32), up.astype(f32))[1](grad_hidden)
    grad_gate, grad_up = grad_gate.astype(bf16), grad_up.astype(bf16)
    grad_input = sum_of_two(dot_nt(grad_gate, in_weight[0]) + dot_nt(grad_up, in_weight[1]), MP)
    grad_mid_norm, grad_gain = jax.vjp(rms_scale, middle, gain_ffn)[1](grad_input)
    return grad_output + grad_mid_norm, (grad_branch, ffn_input), (hidden, grad_gate, grad_up), grad_gain


def attention_backward(grad_middle, table, row_ids, kept, weights_layer):
    inputs, normed, q, k, v, lse, attended = kept[:7]
    query_weight, kv_weight, out_weight, gain_attn = (
        weights_layer[0],
        weights_layer[1],
        weights_layer[2],
        weights_layer[5],
    )
    grad_attn = grad_middle.astype(bf16)
    do = dot(grad_attn, out_weight).astype(bf16)
    dq, dk, dv, sums = attend_back(table, row_ids, lse, q, k, v, do)
    grad_normed = sum_of_two(
        dot_nt(dq, query_weight) + dot_nt(dk, kv_weight[0]) + dot_nt(dv, kv_weight[1]), MP
    )
    grad_in_norm, grad_gain = jax.vjp(rms_scale, inputs, gain_attn)[1](grad_normed)
    return grad_middle + grad_in_norm, (grad_attn, normed), (attended, dq, dk, dv), grad_gain, sums


def send(source, target, send_sem, recv_sem, device):
    copy = pltpu.make_async_remote_copy(
        src_ref=source,
        dst_ref=target,
        send_sem=send_sem,
        recv_sem=recv_sem,
        device_id=device,
        device_id_type=pl.DeviceIdType.MESH,
    )
    copy.start()


def score_steps(
    count,
    vectors,
    doc_row,
    top_mask,
    positive,
    grad,
    loss,
    queries,
    docs,
    raised,
    totals,
    logits,
    places,
    stats,
    own_loss,
    other_loss,
    sent_grads,
    got_grads,
    cross,
    doc_sum,
    sent_docs,
    got_docs,
    core_sent,
    core_got,
    query_send,
    query_recv,
    stat_send,
    stat_recv,
    grad_send,
    grad_recv,
    part_sems,
    doc_sems,
    loss_sems,
    cross_sems,
    back_sems,
    core_sems,
):
    side, batch, half = lax.axis_index(STREAM), lax.axis_index(BATCH), lax.axis_index(MP)
    length, width = vectors.shape
    quarter = length // 4
    slots = quarter // QLEN
    group = math.gcd(count, 4)
    core, other = {MP: 1 - half}, {STREAM: 1 - side}

    def scorer(step):
        return lax.rem(batch + step, count)

    def each(first, body):
        def run(step, carry):
            body(scorer(step))
            return carry

        lax.fori_loop(first, count, run, 0, unroll=count <= 8)

    barrier = pltpu.get_barrier_semaphore()

    def greet(peer):
        pl.semaphore_signal(barrier, inc=1, device_id={BATCH: peer}, device_id_type=pl.DeviceIdType.MESH)

    def greet_all():
        each(1, greet)
        for peer in (core, other):
            pl.semaphore_signal(barrier, inc=1, device_id=peer, device_id_type=pl.DeviceIdType.MESH)
        pl.semaphore_wait(barrier, count + 1)

    def query_part(plane):
        return vectors.at[pl.ds(pl.multiple_of(half * (length // 2), QLEN) + plane * quarter, quarter), :]

    own = queries.at[batch]

    def push(peer):
        send(own, own, query_send.at[peer], query_recv.at[batch], {BATCH: peer})

    def begin():
        @pl.when(side == 0)
        def _():
            send(query_part(1), own, part_sems.at[0], part_sems.at[1], other)
            own[...] = query_part(0)[...]
            each(1, push)

    def finish():
        @pl.when(side == 1)
        def _():
            send(vectors, docs, doc_sems.at[0], doc_sems.at[1], other)
            docs[...] = vectors[...]
            block_copy(own, part_sems.at[1])
            each(1, push)

        row = lax.broadcasted_iota(jnp.int32, (width, length), 0)
        onehot = jnp.where(row == jnp.broadcast_to(doc_row[0:1, :], (width, length)), 1.0, 0.0).astype(bf16)

        @pl.when(side == 0)
        def _():
            block_copy(docs, doc_sems.at[1])

        def forward(first, carry):
            sources = [scorer(first * group + step) for step in range(group)]
            sims = []
            for source in sources:

                @pl.when(source != batch)
                def _():
                    block_copy(queries.at[source], query_recv.at[source])

                sims.append(dot_nt(queries[source], docs[...]))
            for source, sim in zip(sources, sims):
                for slot in range(slots):
                    chosen = top_mask[source, side * slots + slot].astype(f32)
                    part = jnp.exp(sim[slot * QLEN : (slot + 1) * QLEN] * (1.0 / temper)) * chosen
                    raised[source, slot * QLEN : (slot + 1) * QLEN, :] = part.astype(bf16)
            summed = [dot_nt(raised[source], onehot) for source in sources]
            for source, total in zip(sources, summed):
                totals[source] = total
                pooled = jnp.log1p(total) * (logit_scale * temper / QLEN)
                for slot in range(slots):
                    line = pl.ds(source * slots + slot, 1)
                    logits[line, :] = jnp.sum(pooled[slot * QLEN : (slot + 1) * QLEN], axis=0, keepdims=True)
                    places[line, :] = jnp.full((1, width), positive[source, side * slots + slot], jnp.int32)
            return carry

        lax.fori_loop(0, count // group, forward, 0)

        doc = lax.broadcasted_iota(jnp.int32, logits.shape, 1)
        local = doc < DOCS_ROW
        scores = logits[...]
        is_positive = jnp.where(
            jnp.logical_and(local, places[...] == doc + batch * DOCS_ROW), 1.0, 0.0
        )
        exps = jnp.sum(jnp.where(local, jnp.exp(scores), 0.0), axis=1, keepdims=True)
        hits = jnp.sum(is_positive * scores, axis=1, keepdims=True)
        columns = jnp.where(doc == 0, exps, jnp.where(doc == 1, hits, 0.0))
        lines = stats.shape[2]
        if lines > columns.shape[0]:
            columns = jnp.concatenate([columns, jnp.zeros((lines - columns.shape[0], width), f32)], axis=0)
        stats[batch] = jnp.transpose(columns)[0:8, :]

        def push_stats(peer):
            send(stats.at[batch], stats.at[batch], stat_send.at[peer], stat_recv.at[batch], {BATCH: peer})

        each(1, push_stats)
        each(1, lambda peer: block_copy(stats.at[peer], stat_recv.at[peer]))
        summed = lax.fori_loop(1, count, lambda source, total: total + stats[source], stats[0])
        log_line = jnp.log(summed[0:1, :])
        row = lax.broadcasted_iota(jnp.int32, (width, lines), 0)
        both = jnp.where(row == 0, log_line, jnp.where(row == 1, log_line - summed[1:2, :], 0.0))
        both = jnp.transpose(both)[0 : logits.shape[0], :]
        log_total = jnp.sum(jnp.where(doc == 0, both, 0.0), axis=1, keepdims=True)
        losses = jnp.sum(jnp.where(doc == 1, both, 0.0), axis=1, keepdims=True)
        logits[...] = jnp.broadcast_to(losses, logits.shape)
        for slot in range(slots):
            own_loss[pl.ds(slot, 1), :] = logits[pl.ds(batch * slots + slot, 1), :]
        send(own_loss, other_loss, loss_sems.at[0], loss_sems.at[1], other)
        logits[...] = jnp.where(local, jnp.exp(scores - log_total), 0.0) - is_positive
        doc_sum[...] = jnp.zeros(doc_sum.shape, f32)

        def backward(first, carry):
            sources = [scorer(first * group + step + 1) for step in range(group)]
            factors = []
            for source in sources:
                parts = []
                for slot in range(slots):
                    line = logits[pl.ds(source * slots + slot, 1), :] * (logit_scale / QLEN)
                    parts.append(line / (1.0 + totals[source, slot * QLEN : (slot + 1) * QLEN, :]))
                factors.append(jnp.concatenate(parts, axis=0).astype(bf16))
            spreads = [dot(factor, onehot) for factor in factors]
            ds = [(raised[source].astype(f32) * spread).astype(bf16) for source, spread in zip(sources, spreads)]
            backs = [dot(d, docs[...]).astype(bf16) for d in ds]
            for source, back in zip(sources, backs):
                sent_grads[source] = back

                @pl.when(source != batch)
                def _():
                    send(
                        sent_grads.at[source], got_grads.at[batch], grad_send.at[source], grad_recv.at[batch], {BATCH: source}
                    )

            change = dot_tn(ds[0], queries[sources[0]])
            for d, source in zip(ds[1:], sources[1:]):
                change = change + dot_tn(d, queries[source])
            doc_sum[...] += change
            return carry

        lax.fori_loop(0, count // group, backward, 0)

        @pl.when(side == 0)
        def _():
            sent_docs[...] = doc_sum[...].astype(bf16)
            send(sent_docs, got_docs, back_sems.at[0], back_sems.at[1], other)

        got_grads[batch] = sent_grads[batch]
        each(1, lambda peer: block_copy(got_grads.at[peer], grad_recv.at[peer]))
        total = lax.fori_loop(
            1, count, lambda source, total: total + got_grads[source].astype(f32), got_grads[0].astype(f32)
        )
        share = pl.ds(0, length // 2)

        @pl.when(side == 0)
        def _():
            core_sent[0:quarter, :] = total.astype(bf16)
            block_copy(cross.at[1], cross_sems.at[1])
            core_sent[quarter : 2 * quarter, :] = cross[1]
            part, there = core_sent.at[share, :], core_got.at[share, :]
            send(part, there, core_sems.at[0], core_sems.at[1], core)
            block_copy(there, core_sems.at[1])
            first = pl.multiple_of(half * (length // 2), QLEN)
            grad[pl.ds(first, length // 2), :] = core_sent[share, :].astype(f32)
            grad[pl.ds(length // 2 - first, length // 2), :] = core_got[share, :].astype(f32)
            block_copy(part, core_sems.at[0])
            block_copy(sent_docs, back_sems.at[0])
            block_copy(query_part(1), part_sems.at[0])

        @pl.when(side == 1)
        def _():
            cross[0] = total.astype(bf16)
            send(cross.at[0], cross.at[1], cross_sems.at[0], cross_sems.at[1], other)
            block_copy(got_docs, back_sems.at[1])
            core_sent[...] = (doc_sum[...] + got_docs[...].astype(f32)).astype(bf16)
            send(core_sent, core_got, core_sems.at[0], core_sems.at[1], core)
            block_copy(core_got, core_sems.at[1])
            grad[...] = (core_sent[...].astype(f32) + core_got[...].astype(f32)).astype(bf16).astype(f32)
            block_copy(core_sent, core_sems.at[0])
            block_copy(cross.at[0], cross_sems.at[0])
            block_copy(vectors, doc_sems.at[0])

        block_copy(other_loss, loss_sems.at[1])
        lower = jnp.where(side == 0, own_loss[0:slots, :], other_loss[0:slots, :])
        upper = jnp.where(side == 0, other_loss[0:slots, :], own_loss[0:slots, :])
        pair = jnp.concatenate([lower, upper], axis=0)
        across = lax.broadcasted_iota(jnp.int32, pair.shape, 1) == lax.broadcasted_iota(jnp.int32, pair.shape, 0)
        loss[...] = jnp.sum(jnp.where(across, pair, 0.0), axis=0, keepdims=True)[:, 0 : 2 * slots]
        block_copy(own_loss, loss_sems.at[0])

        def settle(peer):
            block_copy(own, query_send.at[peer])
            block_copy(stats.at[batch], stat_send.at[peer])
            block_copy(sent_grads.at[peer], grad_send.at[peer])

        each(1, settle)

    return greet_all, begin, finish


def score_kernel(count, *refs):
    greet, begin, finish = score_steps(count, *refs)
    greet()
    begin()
    finish()


def score_scratch(count, length, width):
    quarter = length // 4
    slots = quarter // QLEN
    dma = pltpu.SemaphoreType.DMA
    return [
        pltpu.VMEM((count, quarter, width), bf16),
        pltpu.VMEM((length, width), bf16),
        pltpu.VMEM((count, quarter, length), bf16),
        pltpu.VMEM((count, quarter, width), f32),
        pltpu.VMEM((count * slots, width), f32),
        pltpu.VMEM((count * slots, width), jnp.int32),
        pltpu.VMEM((count, 8, max(TILE, count * slots)), f32),
        pltpu.VMEM((8, width), f32),
        pltpu.VMEM((8, width), f32),
        pltpu.VMEM((count, quarter, width), bf16),
        pltpu.VMEM((count, quarter, width), bf16),
        pltpu.VMEM((2, quarter, width), bf16),
        pltpu.VMEM((length, width), f32),
        pltpu.VMEM((length, width), bf16),
        pltpu.VMEM((length, width), bf16),
        pltpu.VMEM((length, width), bf16),
        pltpu.VMEM((length, width), bf16),
    ] + [dma((count,))] * 6 + [dma((2,))] * 6


def score(vectors, doc_row, top_mask, positive):
    count = lax.axis_size(BATCH)
    length, width = vectors.shape
    slots = length // 4 // QLEN
    return pl.pallas_call(
        functools.partial(score_kernel, count),
        out_shape=(
            jax.ShapeDtypeStruct((length, width), f32),
            jax.ShapeDtypeStruct((1, 2 * slots), f32),
        ),
        in_specs=[pl.BlockSpec(memory_space=pltpu.VMEM)] * 3 + [pl.BlockSpec(memory_space=pltpu.SMEM)],
        out_specs=(pl.BlockSpec(memory_space=pltpu.VMEM),) * 2,
        scratch_shapes=score_scratch(count, length, width),
        compiler_params=pltpu.CompilerParams(
            collective_id=0, has_side_effects=True, vmem_limit_bytes=56 * 1024 * 1024
        ),
        cost_estimate=pl.CostEstimate(flops=10**9, bytes_accessed=2 * 10**6, transcendentals=10**6),
        name="score",
    )(vectors, doc_row, top_mask, positive)


def rms_rows(value, weight):
    scale = lax.rsqrt(jnp.mean(value * value, axis=-1, keepdims=True) + norm_eps)
    return (value * scale * weight).astype(bf16)


KEPT = ("x", "n1", "q", "k", "v", "lse", "o", "xm", "n2", "gate", "up", "act")


def forward_kernel(made, results, count, *refs):
    (tokens, w_query, w_kv, w_out, w_in, w_down, w_proj, rel_bias, segments, gains), refs = refs[:10], refs[10:]
    asked, refs = (refs[:2], refs[2:]) if count else ((), refs)
    outs, refs = dict(zip(results, refs)), refs[len(results) :]
    found, refs = (refs[:2], refs[2:]) if count else ((), refs)
    held, refs = dict(zip(made, refs)), refs[len(made) :]
    (row_sent, row_got, sent, got, table, mask, bias, load_sems, store_sems, row_sems, send_sems, recv_sems), refs = (
        refs[:12],
        refs[12:],
    )
    half = lax.axis_index(MP)
    core = {MP: 1 - half}
    length, model = held["x0"].shape
    share = length // 2
    narrow, wide = held["q0"].shape[1], held["act0"].shape[1]
    layers = w_query.shape[0]
    loads, stores = [], []

    def fetch(source, target):
        copy = pltpu.make_async_copy(source, target, load_sems.at[len(loads)])
        copy.start()
        loads.append(copy)
        return copy

    def keep(name):
        copy = pltpu.make_async_copy(held[name], outs[name], store_sems.at[len(stores)])
        copy.start()
        stores.append(copy)

    ready = {"tokens": fetch(tokens, row_sent)}
    for layer in range(layers):
        for name, source in (
            ("wq", w_query.at[layer]),
            ("wk", w_kv.at[layer, 0]),
            ("wv", w_kv.at[layer, 1]),
            ("wo", w_out.at[layer]),
            ("wi", w_in.at[layer]),
            ("wd", w_down.at[layer]),
        ):
            ready[name + str(layer)] = fetch(source, held[name + str(layer)])
    ready["w_proj"] = fetch(w_proj, held["w_proj"])
    if count:
        greet, begin_score, finish_score = score_steps(count, held["vectors"], segments, *asked, *found, *refs)
        greet()
    else:
        barrier = pltpu.get_barrier_semaphore()
        pl.semaphore_signal(barrier, inc=1, device_id=core, device_id_type=pl.DeviceIdType.MESH)
        pl.semaphore_wait(barrier, 1)
    ready["tokens"].wait()
    send(row_sent, row_got, row_sems.at[0], row_sems.at[1], core)
    fill_table(rel_bias, table)
    fill_masks(row_ids_of(segments), mask, length // TILE)

    def rows_of(index):
        return pl.ds(pl.multiple_of(index * share, TILE), share)

    def share_part(turn, index, part):
        rows = rows_of(index)
        sent[turn, rows, :] = part.astype(bf16)
        send(
            sent.at[turn, rows, :], got.at[turn, rows, :],
            send_sems.at[turn, index], recv_sems.at[turn, index], core,
        )

    def total(turn, index, base):
        rows = rows_of(index)
        block_copy(got.at[turn, rows, :], recv_sems.at[turn, index])
        return base[rows, :] + (sent[turn, rows, :].astype(f32) + got[turn, rows, :].astype(f32))

    def project(layer, index, value):
        rows, name = rows_of(index), str(layer)
        held["x" + name][rows, :] = value
        n1 = rms_rows(value, gains[2 * layer : 2 * layer + 1, :])
        held["n1" + name][rows, :] = n1
        for part in "qkv":
            held[part + name][rows, :] = dot(n1, held["w" + part + name][...]).astype(bf16)

    for part in "qkv":
        ready["w" + part + "0"].wait()
    project(0, half, row_sent[...].astype(f32))
    block_copy(row_got, row_sems.at[1])
    project(0, 1 - half, row_got[...].astype(f32))

    for layer in range(layers):
        name = str(layer)
        for kept in ("x", "n1", "q", "k", "v"):
            keep(kept + name)
        held["lse" + name][...] = jnp.zeros((length, TILE), f32)

        def pair(p, carry, name=name):
            attend_pair(
                p, table, *(held[part + name] for part in ("q", "k", "v", "o", "lse")), mask, bias
            )
            return carry

        lax.fori_loop(0, narrow // TILE, pair, 0)
        ready["wo" + name].wait()
        for index in range(2):
            share_part(2 * layer, index, dot_nt(held["o" + name][rows_of(index), :], held["wo" + name][...]))
        keep("lse" + name)
        keep("o" + name)
        ready["wi" + name].wait()
        ready["wd" + name].wait()

        def feed(index, carry, layer=layer, name=name):
            rows = rows_of(index)
            value = total(2 * layer, index, held["x" + name])
            held["xm" + name][rows, :] = value
            n2 = rms_rows(value, gains[2 * layer + 1 : 2 * layer + 2, :])
            held["n2" + name][rows, :] = n2
            for column in range(0, wide, CHUNK):
                cols = pl.ds(column, CHUNK)
                g = dot(n2, held["wi" + name][0, :, cols])
                u = dot(n2, held["wi" + name][1, :, cols])
                held["gate" + name][rows, cols] = g.astype(bf16)
                held["up" + name][rows, cols] = u.astype(bf16)
                t = jnp.tanh(math.sqrt(2.0 / math.pi) * (g + 0.044715 * (g * g * g)))
                held["act" + name][rows, cols] = (0.5 * g * (1.0 + t) * u).astype(bf16)
            share_part(2 * layer + 1, index, dot_nt(held["act" + name][rows, :], held["wd" + name][...]))
            return carry

        lax.fori_loop(0, 2, feed, 0)
        for kept in ("xm", "n2", "gate", "up", "act"):
            keep(kept + name)
        if layer + 1 < layers:
            for part in "qkv":
                ready["w" + part + str(layer + 1)].wait()

            def following(index, carry, layer=layer, name=name):
                project(layer + 1, index, total(2 * layer + 1, index, held["xm" + name]))
                return carry

            lax.fori_loop(0, 2, following, 0)

    ready["w_proj"].wait()

    def finish(index, carry):
        rows = rows_of(index)
        value = total(2 * layers - 1, index, held["xm" + str(layers - 1)])
        held["state"][rows, :] = value
        final = rms_rows(value, gains[2 * layers : 2 * layers + 1, :])
        held["final"][rows, :] = final
        projected = dot(final, held["w_proj"][...])
        held["y"][rows, :] = projected
        scale = lax.rsqrt(jnp.sum(projected * projected, axis=-1, keepdims=True) + vector_eps)
        held["vectors"][rows, :] = (projected * scale).astype(bf16)
        return carry

    finish(half, 0)
    if count:
        begin_score()
    finish(1 - half, 0)
    for name in ("state", "final", "y", "vectors"):
        keep(name)
    if count:
        finish_score()
    for copy in stores:
        copy.wait()
    block_copy(row_sent, row_sems.at[0])
    for turn in range(2 * layers):
        for index in range(2):
            block_copy(sent.at[turn, rows_of(index), :], send_sems.at[turn, index])


def forward(tokens, weights, tables, scored):
    w_query, w_kv, w_out, w_in, w_down, w_proj = weights
    layers, model, narrow = w_query.shape
    wide, width = w_down.shape[2], w_proj.shape[1]
    length = 2 * tokens.shape[0]
    vmem, dma = pltpu.VMEM, pltpu.SemaphoreType.DMA
    sizes = dict(x=(model, f32), n1=(model, bf16), q=(narrow, bf16), k=(narrow, bf16), v=(narrow, bf16), lse=(TILE, f32),
                 o=(narrow, bf16), xm=(model, f32), n2=(model, bf16), gate=(wide, bf16), up=(wide, bf16), act=(wide, bf16))
    results = {name + str(layer): sizes[name] for layer in range(layers) for name in KEPT}
    results.update(state=(model, f32), final=(model, bf16), y=(width, f32), vectors=(width, bf16))
    made = {name: vmem((length, columns), kind) for name, (columns, kind) in results.items()}
    for layer in range(layers):
        for name in ("wq", "wk", "wv", "wo"):
            made[name + str(layer)] = vmem((model, narrow), bf16)
        made["wi" + str(layer)] = vmem((2, model, wide), bf16)
        made["wd" + str(layer)] = vmem((model, wide), bf16)
    made["w_proj"] = vmem((model, width), bf16)
    hbm, local = pl.BlockSpec(memory_space=pl.ANY), pl.BlockSpec(memory_space=vmem)
    count = lax.axis_size(BATCH) if scored else 0
    shapes = [jax.ShapeDtypeStruct((length, columns), kind) for columns, kind in results.values()]
    if scored:
        shapes += [
            jax.ShapeDtypeStruct((length, width), f32),
            jax.ShapeDtypeStruct((1, length // 2 // QLEN), f32),
        ]
    found = pl.pallas_call(
        functools.partial(forward_kernel, tuple(made), tuple(results), count),
        out_shape=tuple(shapes),
        in_specs=[hbm] * 7 + [local] * 3 + [local, pl.BlockSpec(memory_space=pltpu.SMEM)][: len(scored)],
        out_specs=(hbm,) * len(results) + (local,) * len(scored),
        scratch_shapes=list(made.values())
        + [
            vmem(tokens.shape, bf16),
            vmem(tokens.shape, bf16),
            vmem((2 * layers, length, model), bf16),
            vmem((2 * layers, length, model), bf16),
            vmem((8, SPAN), f32),
            vmem((length, 3 * TILE), f32),
            vmem((2, TILE, 3 * TILE), f32),
            dma((6 * layers + 2,)),
            dma((len(results),)),
            dma((2,)),
            dma((2 * layers, 2)),
            dma((2 * layers, 2)),
        ]
        + (score_scratch(count, length, width) if scored else []),
        compiler_params=pltpu.CompilerParams(
            collective_id=2, has_side_effects=True, vmem_limit_bytes=62 * 1024 * 1024
        ),
        cost_estimate=pl.CostEstimate(flops=10**10, bytes_accessed=5 * 10**7, transcendentals=10**6),
        name="forward",
    )(tokens, *weights, *tables, *scored)
    return dict(zip(results, found)), found[len(results) :]


CHUNK = 384


def block_copy(ref, sem):
    pltpu.make_async_copy(ref, ref, sem).wait()


class Sums:
    def __init__(self, refs):
        self.refs = refs
        self.side, self.batch = lax.axis_index(STREAM), lax.axis_index(BATCH)
        self.near, self.low, self.high = lax.rem(self.batch, 2), lax.rem(self.batch // 2, 2), self.batch // 4

    def stream_peer(self):
        return {STREAM: 1 - self.side}

    def near_peer(self):
        return {BATCH: self.batch + 1 - 2 * self.near}

    def low_peer(self):
        return {BATCH: self.batch + 2 - 4 * self.low}

    def high_peer(self):
        return {BATCH: self.batch + 4 - 8 * self.high}

    def slot(self, n):
        return n % RING

    def work(self, n):
        return self.refs["work"].at[n % self.refs["work"].shape[0]]

    def got(self, stage, n):
        return self.refs["got" + str(stage)].at[self.slot(n)]

    def send(self, source, stage, n, device):
        sems = self.refs["send"], self.refs["recv"]
        send(source, self.got(stage, n), sems[0].at[stage, self.slot(n)], sems[1].at[stage, self.slot(n)], device)

    def sent(self, stage, n):
        block_copy(self.got(stage, n), self.refs["send"].at[stage, self.slot(n)])

    def received(self, stage, n):
        block_copy(self.got(stage, n), self.refs["recv"].at[stage, self.slot(n)])

    def store(self, n):
        pltpu.make_async_copy(self.refs["done"].at[self.slot(n)], self.refs["out"](n), self.refs["store"].at[self.slot(n)]).start()

    def stored(self, n):
        block_copy(self.refs["done"].at[self.slot(n)], self.refs["store"].at[self.slot(n)])

    def add(self, count, place, got, at):
        def body(index, carry):
            target = place(index)
            target[...] = (target[...].astype(f32) + got[at(index)].astype(f32)).astype(bf16)
            return carry

        lax.fori_loop(0, count, body, 0)


class StreamFirst(Sums):
    stages = 5

    def half(self, side):
        rows = self.refs["work"].shape[4] // 2
        return pl.ds(pl.multiple_of(side * rows, 16), rows)

    def start(self, n):
        self.send(self.work(n).at[:, :, :, self.half(1 - self.side), :], 0, n, self.stream_peer())

    def step(self, n, stage):
        r, m = self.refs, self.slot(n)
        work, own = self.work(n), self.half(self.side)
        if stage <= 4:
            self.received(stage - 1, n)
        if stage == 1:
            for low in (1 - self.low, self.low):
                self.add(
                    4,
                    lambda i, low=low: work.at[i // 2, low, lax.rem(i, 2), own, :],
                    self.got(0, n),
                    lambda i, low=low: (i // 2, low, lax.rem(i, 2)),
                )
                if low is not self.low:
                    self.send(work.at[:, low, :, own, :], 1, n, self.low_peer())
        if stage == 2:
            for near in (1 - self.near, self.near):
                self.add(
                    2,
                    lambda i, near=near: work.at[i, self.low, near, own, :],
                    self.got(1, n),
                    lambda i, near=near: (i, near),
                )
                if near is not self.near:
                    self.send(work.at[:, self.low, near, own, :], 2, n, self.near_peer())
        if stage == 3:
            self.add(2, lambda i: work.at[i, self.low, self.near, own, :], self.got(2, n), lambda i: (i,))
            self.send(work.at[1 - self.high, self.low, self.near, own, :], 3, n, self.high_peer())
            self.sent(0, n)
        if stage == 4:
            total = work[self.high, self.low, self.near, own, :].astype(f32) + r["got3"][m].astype(f32)
            r["last"][m] = total.astype(bf16)
            self.send(r["last"].at[m], 4, n, self.stream_peer())
            if n >= RING:
                self.stored(n)
            r["done"][m, own, :] = r["last"][m]
            for earlier in range(1, 4):
                self.sent(earlier, n)
        if stage == 5:
            self.received(4, n)
            r["done"][m, self.half(1 - self.side), :] = r["got4"][m]
            self.store(n)
            self.sent(4, n)


class BatchFirst(Sums):
    stages = 4

    def start(self, n):
        self.send(self.work(n).at[:, :, 1 - self.near], 0, n, self.near_peer())

    def step(self, n, stage):
        r, m = self.refs, self.slot(n)
        work = self.work(n)
        self.received(stage - 1, n)
        if stage == 1:
            for low in (1 - self.low, self.low):
                self.add(
                    2,
                    lambda i, low=low: work.at[i, low, self.near],
                    self.got(0, n),
                    lambda i, low=low: (i, low),
                )
                if low is not self.low:
                    self.send(work.at[:, low, self.near], 1, n, self.low_peer())
        if stage == 2:
            self.add(2, lambda i: work.at[i, self.low, self.near], self.got(1, n), lambda i: (i,))
            self.send(work.at[1 - self.high, self.low, self.near], 2, n, self.high_peer())
        if stage == 3:
            total = work[self.high, self.low, self.near].astype(f32) + r["got2"][m].astype(f32)
            r["last"][m] = total.astype(bf16)
            self.send(r["last"].at[m], 3, n, self.stream_peer())
            for earlier in range(3):
                self.sent(earlier, n)
        if stage == 4:
            if n >= RING:
                self.stored(n)
            r["done"][m] = (r["last"][m].astype(f32) + r["got3"][m].astype(f32)).astype(bf16)
            self.store(n)
            self.sent(3, n)


RING = 4
WORK_RING = 5
FIRST_REFS = ("work", "got0", "got1", "got2", "got3", "got4", "last", "done", "send", "recv", "store")
LAST_REFS = ("work", "got0", "got1", "got2", "got3", "last", "done", "send", "recv", "store")


def first_scratch(rows, width, ring, work_ring):
    vmem, dma = pltpu.VMEM, pltpu.SemaphoreType.DMA
    half = rows // 2
    return [
        vmem((work_ring, 2, 2, 2, rows, width), bf16),
        vmem((ring, 2, 2, 2, half, width), bf16),
        vmem((ring, 2, 2, half, width), bf16),
        vmem((ring, 2, half, width), bf16),
        vmem((ring, half, width), bf16),
        vmem((ring, half, width), bf16),
        vmem((ring, half, width), bf16),
        vmem((ring, rows, width), bf16),
        dma((5, ring)),
        dma((5, ring)),
        dma((ring,)),
    ]


def last_scratch(rows, width, ring, work_ring):
    vmem, dma = pltpu.VMEM, pltpu.SemaphoreType.DMA
    return [
        vmem((work_ring, 2, 2, 2, rows, width), bf16),
        vmem((ring, 2, 2, rows, width), bf16),
        vmem((ring, 2, rows, width), bf16),
        vmem((ring, rows, width), bf16),
        vmem((ring, rows, width), bf16),
        vmem((ring, rows, width), bf16),
        vmem((ring, rows, width), bf16),
        dma((4, ring)),
        dma((4, ring)),
        dma((ring,)),
    ]


def blocks_of(wide):
    found = []
    for layer in (1, 0):
        for left, right, output, index in (("e", "act", 0, ()), ("n2", "gate", 1, (0,)), ("n2", "up", 1, (1,))):
            found += [(left + str(layer), right + str(layer), c * CHUNK, output, (layer,) + index) for c in range(wide // CHUNK)]
        for left, right, output, index in (("c", "o", 2, ()), ("n1", "dq", 3, ()), ("n1", "dk", 4, (0,)), ("n1", "dv", 4, (1,))):
            found.append((left + str(layer), right + str(layer), 0, output, (layer,) + index))
    return found


def back_kernel(names, made, blocks, *refs):
    given, refs = dict(zip(names, refs)), refs[len(names) :]
    (rel_bias, segments, gains, projected, grad_vectors, w_proj), refs = refs[:6], refs[6:]
    outs, refs = refs[:8], refs[8:]
    held, refs = dict(zip(made, refs)), refs[len(made) :]
    (acc, core_sent, core_got, table, mask, bias, grid, dk_sum, dv_sum, do, little_got), refs = refs[:11], refs[11:]
    (load_sems, core_sems, little_sems), refs = refs[:3], refs[3:]
    firsts, lasts = blocks[0::2], blocks[1::2]
    half = len(blocks) // 2

    def out_of(blocks):
        def place(n):
            _, _, column, output, index = blocks[n]
            return outs[output].at[index + (slice(None), pl.ds(column, CHUNK))]

        return place

    first_refs, refs = dict(zip(FIRST_REFS, refs), out=out_of(firsts)), refs[len(FIRST_REFS) :]
    last_refs, refs = dict(zip(LAST_REFS, refs), out=out_of(lasts)), refs[len(LAST_REFS) :]
    stream_first, batch_first = StreamFirst(first_refs), BatchFirst(last_refs)
    projection = BatchFirst(dict(zip(LAST_REFS, refs), out=lambda n: outs[5]))
    half_index = lax.axis_index(MP)
    core = {MP: 1 - half_index}
    length, model = held["grad"].shape
    tiles = length // TILE

    loads = {}

    def fetch(name, source=None, target=None):
        copy = pltpu.make_async_copy(
            given[name] if source is None else source, held[name] if target is None else target, load_sems.at[len(loads)]
        )
        copy.start()
        loads[name] = [copy, False]

    def need(name):
        if name in loads and not loads[name][1]:
            loads[name][0].wait()
            loads[name][1] = True
        return held.get(name)

    def fetch_attention(layer):
        for name in ("wo", "q", "k", "v", "lse", "wq", "wk", "wv", "x"):
            source = given[name + str(layer)] if name + str(layer) in given else None
            if name == "wo":
                source = given["w_out"].at[layer]
            if name == "wq":
                source = given["w_query"].at[layer]
            if name in ("wk", "wv"):
                source = given["w_kv"].at[layer, 0 if name == "wk" else 1]
            fetch(name + str(layer), source, held[name])

    def fetch_ffn(layer):
        fetch("wd" + str(layer), given["wd"].at[layer], held["wd"])
        fetch("wi" + str(layer), given["wi"].at[layer], held["wi"])
        fetch("xm" + str(layer), None, held["xm"])

    fetch("state", None, held["x"])
    fetch("act1")
    fetch("wd1", given["wd"].at[1], held["wd"])
    for name in ("gate1", "up1"):
        fetch(name)
    fetch("wi1", given["wi"].at[1], held["wi"])
    fetch("xm1", None, held["xm"])
    fetch("n21")
    for name in ("o1", "n11", "gate0", "up0", "act0", "n20", "o0", "n10", "final"):
        fetch(name)

    barrier = pltpu.get_barrier_semaphore()
    peers = [stream_first.stream_peer(), stream_first.near_peer(), stream_first.low_peer(), stream_first.high_peer(), core]
    for peer in peers:
        pl.semaphore_signal(barrier, inc=1, device_id=peer, device_id_type=pl.DeviceIdType.MESH)


    def product(left, right, work):
        width = left.shape[1] // 2
        for part in range(2):
            block = dot_tn(left[:, part * width : (part + 1) * width], right).astype(bf16)
            work[part] = block.reshape(work.shape[1:])

    def make(sums, blocks, n):
        left, right, column, _, _ = blocks[n]
        product(need(left), need(right)[:, column : column + CHUNK], sums.work(n))
        if n == 0 and sums is stream_first:
            pl.semaphore_wait(barrier, len(peers))
        sums.start(n)

    def little_step(stage):
        peer = (stream_first.stream_peer, stream_first.near_peer, stream_first.low_peer, stream_first.high_peer)
        if stage > 0:
            block_copy(little_got.at[2 * stage - 1], little_sems.at[2 * stage - 1])
            total = little_got[2 * stage - 2] + little_got[2 * stage - 1]
            block_copy(little_got.at[2 * stage - 2], little_sems.at[2 * stage - 2])
            if stage == 4:
                outs[6][...] = total
            else:
                little_got[2 * stage] = total
        if stage < 4:
            send(
                little_got.at[2 * stage], little_got.at[2 * stage + 1],
                little_sems.at[2 * stage], little_sems.at[2 * stage + 1], peer[stage](),
            )


    grad = held["grad"]

    def rows_of(index):
        return pl.ds(pl.multiple_of(index * TILE, TILE), TILE)

    def share(turn):
        def pack(index, carry):
            core_sent[rows_of(index), :] = acc[rows_of(index), :].astype(bf16)
            return carry

        lax.fori_loop(0, tiles, pack, 0)
        send(core_sent, core_got.at[turn % 2], core_sems.at[0, turn], core_sems.at[1, turn], core)

    def norm_back(values, gain, gradient, first):
        weight = gains[gain : gain + 1, :]

        def tile(index, total):
            rows = rows_of(index)
            given_grad = gradient(rows)
            value = values[rows, :]
            scale = lax.rsqrt(jnp.mean(value * value, axis=-1, keepdims=True) + norm_eps)
            weighted = given_grad * weight
            along = jnp.mean(value * weighted, axis=-1, keepdims=True)
            change = scale * weighted - value * (scale * scale * scale * along)
            grad[rows, :] = change if first else grad[rows, :] + change
            return total + jnp.sum(given_grad * (value * scale), axis=0, keepdims=True)

        total = lax.fori_loop(0, tiles, tile, jnp.zeros((1, model), f32))
        little_got[0, gain : gain + 1, 0:model] = total

    def through_norm(turn, values, gain):
        block_copy(core_got.at[turn % 2], core_sems.at[1, turn])
        norm_back(
            values, gain, lambda rows: core_sent[rows, :].astype(f32) + core_got[turn % 2, rows, :].astype(f32), False
        )
        block_copy(core_sent, core_sems.at[0, turn])

    def projection_back():
        def tile(index, carry):
            rows = rows_of(index)
            y, grad_vector = projected[rows, :], grad_vectors[rows, :]
            scale = lax.rsqrt(jnp.sum(y * y, axis=-1, keepdims=True) + vector_eps)
            along = jnp.sum(y * grad_vector, axis=-1, keepdims=True)
            held["dproj"][rows, :] = (scale * grad_vector - y * (scale * scale * scale * along)).astype(bf16)
            return carry

        lax.fori_loop(0, tiles, tile, 0)
        need("state")
        norm_back(held["x"], 4, lambda rows: dot_nt(held["dproj"][rows, :], w_proj[...]), True)

    def round_grad(target):
        def pack(index, carry):
            target[rows_of(index), :] = grad[rows_of(index), :].astype(bf16)
            return carry

        lax.fori_loop(0, tiles, pack, 0)

    def ffn_tile(layer, column):
        cols = pl.ds(column, CHUNK)
        e, gate, up = (held[name + str(layer)] for name in ("e", "gate", "up"))

        def tile(index, carry):
            rows = pl.ds(pl.multiple_of(index * 2 * TILE, 2 * TILE), 2 * TILE)
            grad_hidden = dot(e[rows, :], held["wd"][:, cols])
            g, u = gate[rows, cols].astype(f32), up[rows, cols].astype(f32)
            root = math.sqrt(2.0 / math.pi)
            t = jnp.tanh(root * (g + 0.044715 * (g * g * g)))
            slope = 0.5 * (1.0 + t) + (0.5 * root) * g * (1.0 - t * t) * (1.0 + (3 * 0.044715) * (g * g))
            dg = (grad_hidden * u * slope).astype(bf16)
            du = (grad_hidden * (0.5 * g * (1.0 + t))).astype(bf16)
            gate[rows, cols] = dg
            up[rows, cols] = du
            part = dot_nt(dg, held["wi"][0, :, cols]) + dot_nt(du, held["wi"][1, :, cols])
            acc[rows, :] = part if column == 0 else acc[rows, :] + part
            return carry

        lax.fori_loop(0, tiles // 2, tile, 0)

    def attention_start(layer):
        c = held["c" + str(layer)]
        round_grad(c)

        def tile(index, carry):
            rows = pl.ds(pl.multiple_of(index * 2 * TILE, 2 * TILE), 2 * TILE)
            do[rows, :] = dot(c[rows, :], held["wo"][...]).astype(bf16)
            return carry

        need("wo" + str(layer))
        lax.fori_loop(0, tiles // 2, tile, 0)
        for name in ("q", "k", "v", "lse"):
            need(name + str(layer))

    def attention_pair(layer, p):
        attend_back_pair(
            p, table, held["lse"], held["q"], held["k"], held["v"], do,
            held["dq" + str(layer)], held["dk" + str(layer)], held["dv" + str(layer)],
            mask, bias, grid, dk_sum, dv_sum,
        )
        for half in range(2):
            line = diagonals(grid, half)
            place = (0, pl.ds(2 * p + half, 1), pl.ds(model, SPAN))
            little_got[place] = little_got[place] + line

    def attention_end(layer, turn):
        for name in ("wq", "wk", "wv"):
            need(name + str(layer))

        def tile(index, carry):
            rows = pl.ds(pl.multiple_of(index * 2 * TILE, 2 * TILE), 2 * TILE)
            acc[rows, :] = (
                dot_nt(held["dq" + str(layer)][rows, :], held["wq"][...])
                + dot_nt(held["dk" + str(layer)][rows, :], held["wk"][...])
                + dot_nt(held["dv" + str(layer)][rows, :], held["wv"][...])
            )
            return carry

        lax.fori_loop(0, tiles // 2, tile, 0)
        share(turn)

    def ffn_half(layer, part):
        if part == 0:
            for name in ("wd", "wi", "gate", "up"):
                need(name + str(layer))
        ffn_tile(layer, 2 * part * CHUNK)
        ffn_tile(layer, (2 * part + 1) * CHUNK)

    def piece0():
        ffn_half(1, 0)

    def piece1():
        ffn_half(1, 1)
        share(0)
        fill_table(rel_bias, table)
        fill_masks(row_ids_of(segments), mask, tiles)

    def piece2():
        need("xm1")
        through_norm(0, held["xm"], 3)
        fetch_ffn(0)
        attention_start(1)
        attention_pair(1, 0)

    def piece6():
        need("x1")
        through_norm(1, held["x"], 2)
        fetch_attention(0)
        round_grad(held["e0"])
        ffn_half(0, 0)

    def piece7():
        ffn_half(0, 1)
        share(2)

    def piece8():
        need("xm0")
        through_norm(2, held["xm"], 1)
        attention_start(0)
        attention_pair(0, 0)

    def piece12():
        need("x0")
        through_norm(3, held["x"], 0)
        share_rows = length // 2
        outs[7][...] = grad[pl.ds(pl.multiple_of(half_index * share_rows, TILE), share_rows), :]

    pieces = [
        piece0,
        piece1,
        piece2,
        lambda: attention_pair(1, 1),
        lambda: attention_pair(1, 2),
        lambda: attention_end(1, 1),
        piece6,
        piece7,
        piece8,
        lambda: attention_pair(0, 1),
        lambda: attention_pair(0, 2),
        lambda: attention_end(0, 3),
        piece12,
    ]
    little_got[0] = jnp.zeros(little_got.shape[1:], f32)
    projection_back()
    fetch_attention(1)
    round_grad(held["e1"])
    for t in range(half + 5):
        if t < half:
            make(stream_first, firsts, t)
            make(batch_first, lasts, t)
        if t == half - 3:
            product(need("final"), held["dproj"][...], projection.work(0))
            projection.start(0)
        if t < len(pieces):
            pieces[t]()
        for stage in (1, 2, 3, 4, 5):
            if 0 <= t - stage < half:
                stream_first.step(t - stage, stage)
                if stage <= 4:
                    batch_first.step(t - stage, stage)
            if t - stage == half - 3 and stage <= 4:
                projection.step(0, stage)
        if 0 <= t - (half - 3) <= 4:
            little_step(t - (half - 3))
    for n in range(half - RING, half):
        stream_first.stored(n)
        batch_first.stored(n)
    projection.stored(0)


def back(chain, weights, tables):
    batch = lax.axis_size(BATCH)
    length, model = chain["x0"].shape
    rows = model // batch
    narrow, wide = chain["q1"].shape[1], chain["act1"].shape[1]
    width = tables[-1].shape[1]
    little = jax.ShapeDtypeStruct((8, model + SPAN), f32)
    blocks = blocks_of(wide)
    given = dict(chain, **weights)
    vmem, dma, shape = pltpu.VMEM, pltpu.SemaphoreType.DMA, jax.ShapeDtypeStruct
    made = {"grad": (length, model), "x": (length, model), "xm": (length, model), "lse": (length, TILE)}
    made = {name: vmem(dims, f32) for name, dims in made.items()}
    for name in ("e", "n2", "c", "n1"):
        made.update({name + layer: vmem((length, model), bf16) for layer in "01"})
    for name in ("act", "gate", "up"):
        made.update({name + layer: vmem((length, wide), bf16) for layer in "01"})
    for name in ("o", "dq", "dk", "dv"):
        made.update({name + layer: vmem((length, narrow), bf16) for layer in "01"})
    made.update({name: vmem((length, narrow), bf16) for name in "qkv"})
    made.update({name: vmem((model, narrow), bf16) for name in ("wo", "wq", "wk", "wv")})
    made.update(wd=vmem((model, wide), bf16), wi=vmem((2, model, wide), bf16))
    made.update(final=vmem((length, model), bf16), dproj=vmem((length, width), bf16))
    ins = [pl.BlockSpec(memory_space=pl.ANY)] * len(given) + [pl.BlockSpec(memory_space=vmem)] * 6
    hbm, local = pl.BlockSpec(memory_space=pl.ANY), pl.BlockSpec(memory_space=vmem)
    return pl.pallas_call(
        functools.partial(back_kernel, tuple(given), tuple(made), blocks),
        out_shape=(
            shape((2, rows, wide), bf16),
            shape((2, 2, rows, wide), bf16),
            shape((2, rows, narrow), bf16),
            shape((2, rows, narrow), bf16),
            shape((2, 2, rows, narrow), bf16),
            shape((rows, width), bf16),
            shape(little.shape, f32),
            shape((length // 2, model), f32),
        ),
        in_specs=ins,
        out_specs=(hbm,) * 6 + (local,) * 2,
        scratch_shapes=list(made.values())
        + [
            vmem((length, model), f32),
            vmem((length, model), bf16),
            vmem((2, length, model), bf16),
            vmem((8, SPAN), f32),
            vmem((length, 3 * TILE), f32),
            vmem((2, TILE, 3 * TILE), f32),
            vmem((2, TILE, SPAN), f32),
            vmem((length, TILE), f32),
            vmem((length, TILE), f32),
            vmem((length, narrow), bf16),
            vmem((8,) + little.shape, f32),
            dma((64,)),
            dma((2, 4)),
            dma((8,)),
        ]
        + first_scratch(rows, CHUNK, RING, WORK_RING)
        + last_scratch(rows, CHUNK, RING, WORK_RING)
        + last_scratch(rows, width, 1, 1),
        compiler_params=pltpu.CompilerParams(
            collective_id=1, has_side_effects=True, vmem_limit_bytes=62 * 1024 * 1024
        ),
        cost_estimate=pl.CostEstimate(flops=2 * 10**10, bytes_accessed=5 * 10**7, transcendentals=10**6),
        name="back",
    )(*given.values(), *tables)


def place_kernel(down, into, out, query, key_value, projection, little, grad, vectors, losses, *outs):
    share = outs[0].shape[0]
    first = pl.multiple_of(lax.axis_index(MP) * share, TILE)
    outs[0][...] = vectors[pl.ds(first, share), :]
    outs[1][...] = losses[...]
    for source, target in zip((grad, query, key_value, out, into, down, projection), outs[2:8] + outs[10:]):
        target[...] = source[...].astype(f32)
    gains, bias = outs[8], outs[9]
    model = grad.shape[1]
    count, rows = gains.shape
    moved = pltpu.roll(little[:, 0:model], lax.rem(model - lax.axis_index(BATCH) * rows, model), axis=1)
    gains[...] = moved[0:count, 0:rows]
    bias[...] = lax.dot_general(
        little[0 : bias.shape[0], model:],
        bucket_places(bias.shape[1]),
        (((1,), (1,)), ((), ())),
        precision=highest,
        preferred_element_type=f32,
    )


def place(summed, vectors, losses, gain_count, bias_shape):
    down, into, out, query, key_value, projection, little, grad = summed
    shape = jax.ShapeDtypeStruct
    local = pl.BlockSpec(memory_space=pltpu.VMEM)
    return pl.pallas_call(
        place_kernel,
        out_shape=(shape((grad.shape[0], vectors.shape[1]), bf16), shape(losses.shape, f32))
        + tuple(shape(value.shape, f32) for value in (grad, query, key_value, out, into, down))
        + (shape((gain_count, query.shape[1]), f32), shape(bias_shape, f32), shape(projection.shape, f32)),
        in_specs=[local] * 10,
        out_specs=(local,) * 11,
        compiler_params=pltpu.CompilerParams(vmem_limit_bytes=60 * 1024 * 1024),
        name="place",
    )(*summed, vectors, losses)


def sum_gradients_plainly(kept, final_pair, little):
    def summed(left, right):
        part = lax.psum_scatter(dot_tn(left, right).astype(bf16), BATCH, scatter_dimension=0, tiled=True)
        return sum_of_two(part, STREAM)

    found = []
    for e, n2, c, n1, hidden, dg, du, o, dq, dk, dv in kept:
        found.append((
            summed(e, hidden),
            jnp.stack([summed(n2, dg), summed(n2, du)]),
            summed(c, o),
            summed(n1, dq),
            jnp.stack([summed(n1, dk), summed(n1, dv)]),
        ))
    return [jnp.stack(parts) for parts in zip(*found)] + [
        summed(*final_pair),
        lax.psum(little, (STREAM, BATCH)),
    ]


def on_device(
    tokens,
    segments,
    top_mask,
    positive,
    w_query,
    w_kv,
    w_out,
    w_in,
    w_down,
    gains,
    rel_bias,
    w_proj,
):
    length = segments.shape[1]
    share_len, model_width = tokens.shape[2:]
    head_count = rel_bias.shape[1]
    layers = w_query.shape[0]
    batch = lax.axis_size(BATCH)
    bias_rows = jnp.transpose(rel_bias)
    tables = (bias_rows, segments, gains)
    together = batch <= 8
    kept, scores = forward(
        tokens[0, 0],
        (w_query, w_kv, w_out, w_in, w_down, w_proj),
        tables,
        (top_mask, positive) if together else (),
    )
    vectors = kept["vectors"]
    grad_vectors, query_loss = scores if together else score(vectors, segments, top_mask, positive)
    if layers == 2 and batch == 8:
        chain = {name: value for name, value in kept.items() if name not in ("y", "vectors")}
        weights = dict(w_query=w_query, w_kv=w_kv, w_out=w_out, wi=w_in, wd=w_down)
        summed = back(chain, weights, tables + (kept["y"], grad_vectors, w_proj))
        placed = place(summed, vectors, query_loss, gains.shape[0], bias_rows.shape)
        return (placed[0][None, None], placed[1], placed[2][None, None]) + placed[3:9] + (placed[9].T, placed[10])
    else:
        row_segments = jnp.where(
            lax.axis_index(STREAM) == 0, jnp.arange(length, dtype=jnp.int32) // QLEN, segments[0]
        )
        row_ids = row_segments[None]
        offset_onehot = (
            offset_buckets()[None, :] == jnp.arange(rel_bias.shape[0], dtype=jnp.int32)[:, None]
        ).astype(f32)
        table = jnp.einsum(
            "bh,bk->hk", jnp.pad(rel_bias, ((0, 0), (0, 8 - head_count))), offset_onehot, precision=highest
        )
        kept_layers = [[kept[name + str(layer)] for name in KEPT] for layer in range(layers)]
        grad_projected = jax.vjp(normalize, kept["y"])[1](grad_vectors)[0].astype(bf16)
        grad_final = dot_nt(grad_projected, w_proj)
        grad_state, grad_gain_final = jax.vjp(rms_scale, kept["state"], gains[2 * layers])[1](grad_final)
        gain_grads = [None] * (2 * layers)
        operands = [None] * layers
        sums = jnp.zeros(table.shape, f32)
        for layer in reversed(range(layers)):
            weights_layer = (
                w_query[layer],
                w_kv[layer],
                w_out[layer],
                w_in[layer],
                w_down[layer],
                gains[2 * layer],
                gains[2 * layer + 1],
            )
            grad_state, ffn_lefts, ffn_rights, gain_grads[2 * layer + 1] = ffn_backward(
                grad_state, kept_layers[layer], weights_layer
            )
            grad_state, lefts, rights, gain_grads[2 * layer], part = attention_backward(
                grad_state, table, row_ids, kept_layers[layer], weights_layer
            )
            operands[layer] = ffn_lefts + lefts + ffn_rights + rights
            sums = sums + part
        little = jnp.concatenate(
            [jnp.pad(jnp.stack(gain_grads + [grad_gain_final]), ((0, 7 - 2 * layers), (0, 0))), sums], axis=1
        )
        summed = sum_gradients_plainly(operands, (kept["final"], grad_projected), little)
        grad_down, grad_in, grad_out, grad_query, grad_kv, grad_proj, little = summed
        own_grad = lax.dynamic_slice_in_dim(grad_state, lax.axis_index(MP) * share_len, share_len, 0)
        grad_bias = jnp.einsum("hk,bk->bh", little[:, model_width:], offset_onehot, precision=highest)
        rows = model_width // batch
        grad_gains = lax.dynamic_slice(little, (0, lax.axis_index(BATCH) * rows), (2 * layers + 1, rows))
    own_vectors = lax.dynamic_slice_in_dim(vectors, lax.axis_index(MP) * share_len, share_len, 0)
    return (
        own_vectors[None, None],
        query_loss,
        own_grad[None, None],
        grad_query,
        grad_kv,
        grad_out,
        grad_in,
        grad_down,
        grad_gains,
        grad_bias[:, :head_count],
        grad_proj,
    )


def solution(mesh):
    placed = (
        P(STREAM, BATCH, MP, None),
        P(BATCH, None),
        P(None, MP, BATCH, None),
        P(None, MP),
        P(None, None, MP),
        P(None, None, None, MP),
        P(None, None, MP),
        P(None, None, None, MP),
        P(None, None, MP),
        P(),
        P(None, MP),
        P(),
    )
    return jax.shard_map(
        on_device,
        mesh=mesh,
        in_specs=placed,
        out_specs=(
            P(STREAM, BATCH, MP, None),
            P(BATCH, MP),
            P(STREAM, BATCH, MP, None),
            P(None, BATCH, MP),
            P(None, None, BATCH, MP),
            P(None, BATCH, MP),
            P(None, None, BATCH, MP),
            P(None, BATCH, MP),
            P(None, BATCH),
            P(None, MP),
            P(BATCH, None),
        ),
        check_vma=False,
    )
```

```python
import functools
import math

import jax
import jax.numpy as jnp
from jax import lax
from jax.experimental import pallas as pl
from jax.experimental.pallas import tpu as pltpu
from jax.sharding import PartitionSpec as P

QLEN = 32
DOCS_ROW = 8
TILE = 128
STREAM, BATCH, MP = "stream", "batch", "mp"
SPAN = 512


norm_eps = 1e-06
vector_eps = 1e-06
temper = 0.05
logit_scale = 32.0
bucket_edges = (12, 16, 23, 32, 46, 64, 91)
highest = lax.Precision.HIGHEST
bf16 = jnp.bfloat16
f32 = jnp.float32


def dot(a, b):
    return lax.dot_general(a, b, (((1,), (0,)), ((), ())), preferred_element_type=f32)


def dot_nt(a, b):
    return lax.dot_general(a, b, (((1,), (1,)), ((), ())), preferred_element_type=f32)


def dot_tn(a, b):
    return lax.dot_general(a, b, (((0,), (0,)), ((), ())), preferred_element_type=f32)


def offset_buckets():
    index = jnp.arange(SPAN, dtype=jnp.int32)
    offsets = jnp.where(index < SPAN // 2, index, index - SPAN)
    magnitude = jnp.abs(offsets)
    far_bucket = jnp.full(offsets.shape, 8, jnp.int32)
    for threshold in bucket_edges:
        far_bucket = far_bucket + (magnitude >= threshold).astype(jnp.int32)
    bucket = jnp.where(magnitude < 8, magnitude, jnp.minimum(far_bucket, 15))
    return bucket + jnp.where(offsets > 0, 16, 0).astype(jnp.int32)


def bucket_places(count):
    index = lax.broadcasted_iota(jnp.int32, (count, SPAN), 1)
    offsets = jnp.where(index < SPAN // 2, index, index - SPAN)
    magnitude = jnp.abs(offsets)
    far_bucket = jnp.full(offsets.shape, 8, jnp.int32)
    for threshold in bucket_edges:
        far_bucket = far_bucket + jnp.where(magnitude >= threshold, 1, 0)
    bucket = jnp.where(magnitude < 8, magnitude, jnp.minimum(far_bucket, 15))
    bucket = bucket + jnp.where(offsets > 0, 16, 0)
    return jnp.where(bucket == lax.broadcasted_iota(jnp.int32, (count, SPAN), 0), 1.0, 0.0)


def fill_table(rel_bias, table):
    table[...] = jnp.zeros(table.shape, f32)
    table[0 : rel_bias.shape[0], :] = lax.dot_general(
        rel_bias[...],
        bucket_places(rel_bias.shape[1]),
        (((1,), (0,)), ((), ())),
        precision=highest,
        preferred_element_type=f32,
    )


def row_ids_of(segments):
    position = lax.broadcasted_iota(jnp.int32, segments.shape, 1)
    return jnp.where(lax.axis_index(STREAM) == 0, position // QLEN, segments[...])


def window(tile, tiles):
    first, last = max(0, tile - 1), min(tiles, tile + 2)
    shift = first - (tile - 1)
    return pl.ds(first * TILE, (last - first) * TILE), slice(shift * TILE, (shift + last - first) * TILE)


def fill_masks(row_ids, mask, tiles):
    ids = row_ids.astype(f32)
    lines = [jnp.broadcast_to(ids[:, tile * TILE : (tile + 1) * TILE], (TILE, TILE)) for tile in range(tiles)]
    for tile in range(tiles):
        own = jnp.transpose(lines[tile])
        for near in range(max(0, tile - 1), min(tiles, tile + 2)):
            place = (near - tile + 1) * TILE
            mask[tile * TILE : (tile + 1) * TILE, place : place + TILE] = jnp.where(own == lines[near], 0.0, -1e30)


def bias_tile(table, head):
    line = jnp.broadcast_to(table[pl.ds(head, 1), :], (TILE, SPAN))
    return pltpu.roll(line, TILE, axis=1, stride=1, stride_axis=0)[:, : 3 * TILE]


def attend_pair(p, table, q, k, v, o, lse, mask, bias):
    tiles = q.shape[0] // TILE
    lane = lax.broadcasted_iota(jnp.int32, (TILE, TILE), 1)
    cols = pl.ds(pl.multiple_of(p * TILE, TILE), TILE)
    for half in range(2):
        bias[half] = bias_tile(table, 2 * p + half)
    scores = []
    for tile in range(tiles):
        rows = pl.ds(tile * TILE, TILE)
        keys, frame = window(tile, tiles)
        queries, near_keys = q[rows, cols], k[keys, cols]
        for half in range(2):
            mine = (lane >= 64) if half else (lane < 64)
            s = dot_nt(jnp.where(mine, queries, jnp.zeros_like(queries)), near_keys)
            scores.append(s + (bias[half][:, frame] + mask[rows, frame]))
    tops = [jnp.max(s, axis=-1, keepdims=True) for s in scores]
    exps = [jnp.exp(s - top) for s, top in zip(scores, tops)]
    totals = [jnp.sum(e, axis=-1, keepdims=True) for e in exps]
    weights = [(e * (1.0 / total)).astype(bf16) for e, total in zip(exps, totals)]
    for tile in range(tiles):
        rows = pl.ds(tile * TILE, TILE)
        near_values = v[window(tile, tiles)[0], cols]
        outs = [dot(weights[2 * tile + half], near_values) for half in range(2)]
        o[rows, cols] = jnp.where(lane < 64, outs[0], outs[1]).astype(bf16)
        kept = lse[rows, :]
        for half in range(2):
            index = 2 * tile + half
            kept = jnp.where(lane == 2 * p + half, tops[index] + jnp.log(totals[index]), kept)
        lse[rows, :] = kept


def attend_back_pair(p, table, lse, q, k, v, do, dq, dk, dv, mask, bias, grid, dk_sum, dv_sum):
    tiles = q.shape[0] // TILE
    lane = lax.broadcasted_iota(jnp.int32, (TILE, TILE), 1)
    cols = pl.ds(pl.multiple_of(p * TILE, TILE), TILE)
    for half in range(2):
        bias[half] = bias_tile(table, 2 * p + half)
    grid[...] = jnp.zeros(grid.shape, f32)
    dk_sum[...] = jnp.zeros(dk_sum.shape, f32)
    dv_sum[...] = jnp.zeros(dv_sum.shape, f32)
    for first in range(0, tiles, 2):
        some = [(tile, half) for tile in range(first, min(first + 2, tiles)) for half in range(2)]
        own_queries, own_grads, weights, grad_weights = [], [], [], []
        for tile, half in some:
            rows = pl.ds(tile * TILE, TILE)
            keys, frame = window(tile, tiles)
            mine = (lane >= 64) if half else (lane < 64)
            queries, grads = q[rows, cols], do[rows, cols]
            own_queries.append(jnp.where(mine, queries, jnp.zeros_like(queries)))
            own_grads.append(jnp.where(mine, grads, jnp.zeros_like(grads)))
            log_total = jnp.sum(jnp.where(lane == 2 * p + half, lse[rows, :], 0.0), axis=-1, keepdims=True)
            s = dot_nt(own_queries[-1], k[keys, cols])
            s = s + (bias[half][:, frame] + mask[rows, frame])
            weights.append(jnp.exp(s - log_total))
            grad_weights.append(dot_nt(own_grads[-1], v[keys, cols]))
        means = [jnp.sum(w * g, axis=-1, keepdims=True) for w, g in zip(weights, grad_weights)]
        ds = [(w * (g - mean)).astype(bf16) for w, g, mean in zip(weights, grad_weights, means)]
        outs = []
        for index, (tile, half) in enumerate(some):
            keys, frame = window(tile, tiles)
            outs.append(dot(ds[index], k[keys, cols]))
            dk_sum[keys, :] += dot_tn(ds[index], own_queries[index])
            dv_sum[keys, :] += dot_tn(weights[index].astype(bf16), own_grads[index])
            grid[half, :, frame] += ds[index].astype(f32)
        for index in range(0, len(some), 2):
            rows = pl.ds(some[index][0] * TILE, TILE)
            dq[rows, cols] = jnp.where(lane < 64, outs[index], outs[index + 1]).astype(bf16)
    dk[:, cols] = dk_sum[...].astype(bf16)
    dv[:, cols] = dv_sum[...].astype(bf16)


def diagonals(grid, half):
    row_index = lax.broadcasted_iota(jnp.int32, (TILE, SPAN), 0)
    turned = pltpu.roll(grid[half], SPAN - TILE, axis=1)
    for bit in range(7):
        moved = pltpu.roll(turned, SPAN - (1 << bit), axis=1)
        turned = jnp.where((row_index >> bit) & 1 == 1, moved, turned)
    return jnp.sum(turned, axis=0, keepdims=True)


def attend_back_kernel(
    table, row_ids, lse, q, k, v, do, dq, dk, dv, sums, mask, bias, grid, dk_sum, dv_sum
):
    fill_masks(row_ids[...], mask, q.shape[0] // TILE)
    sums[...] = jnp.zeros(sums.shape, f32)

    def pair(p, carry):
        attend_back_pair(p, table, lse, q, k, v, do, dq, dk, dv, mask, bias, grid, dk_sum, dv_sum)
        for half in range(2):
            sums[pl.ds(2 * p + half, 1), :] = diagonals(grid, half)
        return carry

    lax.fori_loop(0, q.shape[1] // TILE, pair, 0)


def attend_back(table, row_ids, lse, q, k, v, do):
    length, width = q.shape
    grad = jax.ShapeDtypeStruct((length, width), bf16)
    return pl.pallas_call(
        attend_back_kernel,
        out_shape=(grad, grad, grad, jax.ShapeDtypeStruct(table.shape, f32)),
        scratch_shapes=[
            pltpu.VMEM((length, 3 * TILE), f32),
            pltpu.VMEM((2, TILE, 3 * TILE), f32),
            pltpu.VMEM((2, TILE, SPAN), f32),
            pltpu.VMEM((length, TILE), f32),
            pltpu.VMEM((length, TILE), f32),
        ],
        compiler_params=pltpu.CompilerParams(vmem_limit_bytes=32 * 1024 * 1024),
        cost_estimate=pl.CostEstimate(flops=25 * 10**8, bytes_accessed=4 * 10**6, transcendentals=10**6),
        name="attend_back",
    )(table, row_ids, lse, q, k, v, do)


def rms_scale(values, gain_row):
    return (
        values * lax.rsqrt(jnp.mean(values * values, axis=-1, keepdims=True) + norm_eps) * gain_row
    )


def gated_gelu(gate, up):
    return jax.nn.gelu(gate, approximate=True) * up


def normalize(values):
    return values * lax.rsqrt(jnp.sum(values * values, axis=-1, keepdims=True) + vector_eps)


def swap(value, axis):
    return lax.ppermute(value, axis, [(0, 1), (1, 0)])


def sum_of_two(part, axis):
    mine = lax.optimization_barrier(part.astype(bf16))
    return mine.astype(f32) + swap(mine, axis).astype(f32)


def ffn_backward(grad_output, kept, weights_layer):
    middle, ffn_input, gate, up, hidden = kept[7:]
    in_weight, down_weight, gain_ffn = weights_layer[3], weights_layer[4], weights_layer[6]
    grad_branch = grad_output.astype(bf16)
    grad_hidden = dot(grad_branch, down_weight)
    grad_gate, grad_up = jax.vjp(gated_gelu, gate.astype(f32), up.astype(f32))[1](grad_hidden)
    grad_gate, grad_up = grad_gate.astype(bf16), grad_up.astype(bf16)
    grad_input = sum_of_two(dot_nt(grad_gate, in_weight[0]) + dot_nt(grad_up, in_weight[1]), MP)
    grad_mid_norm, grad_gain = jax.vjp(rms_scale, middle, gain_ffn)[1](grad_input)
    return grad_output + grad_mid_norm, (grad_branch, ffn_input), (hidden, grad_gate, grad_up), grad_gain


def attention_backward(grad_middle, table, row_ids, kept, weights_layer):
    inputs, normed, q, k, v, lse, attended = kept[:7]
    query_weight, kv_weight, out_weight, gain_attn = (
        weights_layer[0],
        weights_layer[1],
        weights_layer[2],
        weights_layer[5],
    )
    grad_attn = grad_middle.astype(bf16)
    do = dot(grad_attn, out_weight).astype(bf16)
    dq, dk, dv, sums = attend_back(table, row_ids, lse, q, k, v, do)
    grad_normed = sum_of_two(
        dot_nt(dq, query_weight) + dot_nt(dk, kv_weight[0]) + dot_nt(dv, kv_weight[1]), MP
    )
    grad_in_norm, grad_gain = jax.vjp(rms_scale, inputs, gain_attn)[1](grad_normed)
    return grad_middle + grad_in_norm, (grad_attn, normed), (attended, dq, dk, dv), grad_gain, sums


def send(source, target, send_sem, recv_sem, device):
    copy = pltpu.make_async_remote_copy(
        src_ref=source,
        dst_ref=target,
        send_sem=send_sem,
        recv_sem=recv_sem,
        device_id=device,
        device_id_type=pl.DeviceIdType.MESH,
    )
    copy.start()


def score_steps(
    count,
    vectors,
    doc_row,
    top_mask,
    positive,
    grad,
    loss,
    queries,
    docs,
    raised,
    totals,
    logits,
    places,
    stats,
    own_loss,
    other_loss,
    sent_grads,
    got_grads,
    cross,
    doc_sum,
    sent_docs,
    got_docs,
    core_sent,
    core_got,
    query_send,
    query_recv,
    stat_send,
    stat_recv,
    grad_send,
    grad_recv,
    part_sems,
    doc_sems,
    loss_sems,
    cross_sems,
    back_sems,
    core_sems,
):
    side, batch, half = lax.axis_index(STREAM), lax.axis_index(BATCH), lax.axis_index(MP)
    length, width = vectors.shape
    quarter = length // 4
    slots = quarter // QLEN
    group = math.gcd(count, 4)
    core, other = {MP: 1 - half}, {STREAM: 1 - side}

    def scorer(step):
        return lax.rem(batch + step, count)

    def each(first, body):
        def run(step, carry):
            body(scorer(step))
            return carry

        lax.fori_loop(first, count, run, 0, unroll=count <= 8)

    barrier = pltpu.get_barrier_semaphore()

    def greet(peer):
        pl.semaphore_signal(barrier, inc=1, device_id={BATCH: peer}, device_id_type=pl.DeviceIdType.MESH)

    def greet_all():
        each(1, greet)
        for peer in (core, other):
            pl.semaphore_signal(barrier, inc=1, device_id=peer, device_id_type=pl.DeviceIdType.MESH)
        pl.semaphore_wait(barrier, count + 1)

    def query_part(plane):
        return vectors.at[pl.ds(pl.multiple_of(half * (length // 2), QLEN) + plane * quarter, quarter), :]

    own = queries.at[batch]

    def push(peer):
        send(own, own, query_send.at[peer], query_recv.at[batch], {BATCH: peer})

    def begin():
        @pl.when(side == 0)
        def _():
            send(query_part(1), own, part_sems.at[0], part_sems.at[1], other)
            own[...] = query_part(0)[...]
            each(1, push)

    def finish():
        @pl.when(side == 1)
        def _():
            send(vectors, docs, doc_sems.at[0], doc_sems.at[1], other)
            docs[...] = vectors[...]
            block_copy(own, part_sems.at[1])
            each(1, push)

        row = lax.broadcasted_iota(jnp.int32, (width, length), 0)
        onehot = jnp.where(row == jnp.broadcast_to(doc_row[0:1, :], (width, length)), 1.0, 0.0).astype(bf16)

        @pl.when(side == 0)
        def _():
            block_copy(docs, doc_sems.at[1])

        def forward(first, carry):
            sources = [scorer(first * group + step) for step in range(group)]
            sims = []
            for source in sources:

                @pl.when(source != batch)
                def _():
                    block_copy(queries.at[source], query_recv.at[source])

                sims.append(dot_nt(queries[source], docs[...]))
            for source, sim in zip(sources, sims):
                for slot in range(slots):
                    chosen = top_mask[source, side * slots + slot].astype(f32)
                    part = jnp.exp(sim[slot * QLEN : (slot + 1) * QLEN] * (1.0 / temper)) * chosen
                    raised[source, slot * QLEN : (slot + 1) * QLEN, :] = part.astype(bf16)
            summed = [dot_nt(raised[source], onehot) for source in sources]
            for source, total in zip(sources, summed):
                totals[source] = total
                pooled = jnp.log1p(total) * (logit_scale * temper / QLEN)
                for slot in range(slots):
                    line = pl.ds(source * slots + slot, 1)
                    logits[line, :] = jnp.sum(pooled[slot * QLEN : (slot + 1) * QLEN], axis=0, keepdims=True)
                    places[line, :] = jnp.full((1, width), positive[source, side * slots + slot], jnp.int32)
            return carry

        lax.fori_loop(0, count // group, forward, 0)

        doc = lax.broadcasted_iota(jnp.int32, logits.shape, 1)
        local = doc < DOCS_ROW
        scores = logits[...]
        is_positive = jnp.where(
            jnp.logical_and(local, places[...] == doc + batch * DOCS_ROW), 1.0, 0.0
        )
        exps = jnp.sum(jnp.where(local, jnp.exp(scores), 0.0), axis=1, keepdims=True)
        hits = jnp.sum(is_positive * scores, axis=1, keepdims=True)
        columns = jnp.where(doc == 0, exps, jnp.where(doc == 1, hits, 0.0))
        lines = stats.shape[2]
        if lines > columns.shape[0]:
            columns = jnp.concatenate([columns, jnp.zeros((lines - columns.shape[0], width), f32)], axis=0)
        stats[batch] = jnp.transpose(columns)[0:8, :]

        def push_stats(peer):
            send(stats.at[batch], stats.at[batch], stat_send.at[peer], stat_recv.at[batch], {BATCH: peer})

        each(1, push_stats)
        each(1, lambda peer: block_copy(stats.at[peer], stat_recv.at[peer]))
        summed = lax.fori_loop(1, count, lambda source, total: total + stats[source], stats[0])
        log_line = jnp.log(summed[0:1, :])
        row = lax.broadcasted_iota(jnp.int32, (width, lines), 0)
        both = jnp.where(row == 0, log_line, jnp.where(row == 1, log_line - summed[1:2, :], 0.0))
        both = jnp.transpose(both)[0 : logits.shape[0], :]
        log_total = jnp.sum(jnp.where(doc == 0, both, 0.0), axis=1, keepdims=True)
        losses = jnp.sum(jnp.where(doc == 1, both, 0.0), axis=1, keepdims=True)
        logits[...] = jnp.broadcast_to(losses, logits.shape)
        for slot in range(slots):
            own_loss[pl.ds(slot, 1), :] = logits[pl.ds(batch * slots + slot, 1), :]
        send(own_loss, other_loss, loss_sems.at[0], loss_sems.at[1], other)
        logits[...] = jnp.where(local, jnp.exp(scores - log_total), 0.0) - is_positive
        doc_sum[...] = jnp.zeros(doc_sum.shape, f32)

        def backward(first, carry):
            sources = [scorer(first * group + step + 1) for step in range(group)]
            factors = []
            for source in sources:
                parts = []
                for slot in range(slots):
                    line = logits[pl.ds(source * slots + slot, 1), :] * (logit_scale / QLEN)
                    parts.append(line / (1.0 + totals[source, slot * QLEN : (slot + 1) * QLEN, :]))
                factors.append(jnp.concatenate(parts, axis=0).astype(bf16))
            spreads = [dot(factor, onehot) for factor in factors]
            ds = [(raised[source].astype(f32) * spread).astype(bf16) for source, spread in zip(sources, spreads)]
            backs = [dot(d, docs[...]).astype(bf16) for d in ds]
            for source, back in zip(sources, backs):
                sent_grads[source] = back

                @pl.when(source != batch)
                def _():
                    send(
                        sent_grads.at[source], got_grads.at[batch], grad_send.at[source], grad_recv.at[batch], {BATCH: source}
                    )

            change = dot_tn(ds[0], queries[sources[0]])
            for d, source in zip(ds[1:], sources[1:]):
                change = change + dot_tn(d, queries[source])
            doc_sum[...] += change
            return carry

        lax.fori_loop(0, count // group, backward, 0)

        @pl.when(side == 0)
        def _():
            sent_docs[...] = doc_sum[...].astype(bf16)
            send(sent_docs, got_docs, back_sems.at[0], back_sems.at[1], other)

        got_grads[batch] = sent_grads[batch]
        each(1, lambda peer: block_copy(got_grads.at[peer], grad_recv.at[peer]))
        total = lax.fori_loop(
            1, count, lambda source, total: total + got_grads[source].astype(f32), got_grads[0].astype(f32)
        )
        share = pl.ds(0, length // 2)

        @pl.when(side == 0)
        def _():
            core_sent[0:quarter, :] = total.astype(bf16)
            block_copy(cross.at[1], cross_sems.at[1])
            core_sent[quarter : 2 * quarter, :] = cross[1]
            part, there = core_sent.at[share, :], core_got.at[share, :]
            send(part, there, core_sems.at[0], core_sems.at[1], core)
            block_copy(there, core_sems.at[1])
            first = pl.multiple_of(half * (length // 2), QLEN)
            grad[pl.ds(first, length // 2), :] = core_sent[share, :].astype(f32)
            grad[pl.ds(length // 2 - first, length // 2), :] = core_got[share, :].astype(f32)
            block_copy(part, core_sems.at[0])
            block_copy(sent_docs, back_sems.at[0])
            block_copy(query_part(1), part_sems.at[0])

        @pl.when(side == 1)
        def _():
            cross[0] = total.astype(bf16)
            send(cross.at[0], cross.at[1], cross_sems.at[0], cross_sems.at[1], other)
            block_copy(got_docs, back_sems.at[1])
            core_sent[...] = (doc_sum[...] + got_docs[...].astype(f32)).astype(bf16)
            send(core_sent, core_got, core_sems.at[0], core_sems.at[1], core)
            block_copy(core_got, core_sems.at[1])
            grad[...] = (core_sent[...].astype(f32) + core_got[...].astype(f32)).astype(bf16).astype(f32)
            block_copy(core_sent, core_sems.at[0])
            block_copy(cross.at[0], cross_sems.at[0])
            block_copy(vectors, doc_sems.at[0])

        block_copy(other_loss, loss_sems.at[1])
        lower = jnp.where(side == 0, own_loss[0:slots, :], other_loss[0:slots, :])
        upper = jnp.where(side == 0, other_loss[0:slots, :], own_loss[0:slots, :])
        pair = jnp.concatenate([lower, upper], axis=0)
        across = lax.broadcasted_iota(jnp.int32, pair.shape, 1) == lax.broadcasted_iota(jnp.int32, pair.shape, 0)
        loss[...] = jnp.sum(jnp.where(across, pair, 0.0), axis=0, keepdims=True)[:, 0 : 2 * slots]
        block_copy(own_loss, loss_sems.at[0])

        def settle(peer):
            block_copy(own, query_send.at[peer])
            block_copy(stats.at[batch], stat_send.at[peer])
            block_copy(sent_grads.at[peer], grad_send.at[peer])

        each(1, settle)

    return greet_all, begin, finish


def score_kernel(count, *refs):
    greet, begin, finish = score_steps(count, *refs)
    greet()
    begin()
    finish()


def score_scratch(count, length, width):
    quarter = length // 4
    slots = quarter // QLEN
    dma = pltpu.SemaphoreType.DMA
    return [
        pltpu.VMEM((count, quarter, width), bf16),
        pltpu.VMEM((length, width), bf16),
        pltpu.VMEM((count, quarter, length), bf16),
        pltpu.VMEM((count, quarter, width), f32),
        pltpu.VMEM((count * slots, width), f32),
        pltpu.VMEM((count * slots, width), jnp.int32),
        pltpu.VMEM((count, 8, max(TILE, count * slots)), f32),
        pltpu.VMEM((8, width), f32),
        pltpu.VMEM((8, width), f32),
        pltpu.VMEM((count, quarter, width), bf16),
        pltpu.VMEM((count, quarter, width), bf16),
        pltpu.VMEM((2, quarter, width), bf16),
        pltpu.VMEM((length, width), f32),
        pltpu.VMEM((length, width), bf16),
        pltpu.VMEM((length, width), bf16),
        pltpu.VMEM((length, width), bf16),
        pltpu.VMEM((length, width), bf16),
    ] + [dma((count,))] * 6 + [dma((2,))] * 6


def score(vectors, doc_row, top_mask, positive):
    count = lax.axis_size(BATCH)
    length, width = vectors.shape
    slots = length // 4 // QLEN
    return pl.pallas_call(
        functools.partial(score_kernel, count),
        out_shape=(
            jax.ShapeDtypeStruct((length, width), f32),
            jax.ShapeDtypeStruct((1, 2 * slots), f32),
        ),
        in_specs=[pl.BlockSpec(memory_space=pltpu.VMEM)] * 3 + [pl.BlockSpec(memory_space=pltpu.SMEM)],
        out_specs=(pl.BlockSpec(memory_space=pltpu.VMEM),) * 2,
        scratch_shapes=score_scratch(count, length, width),
        compiler_params=pltpu.CompilerParams(
            collective_id=0, has_side_effects=True, vmem_limit_bytes=56 * 1024 * 1024
        ),
        cost_estimate=pl.CostEstimate(flops=10**9, bytes_accessed=2 * 10**6, transcendentals=10**6),
        name="score",
    )(vectors, doc_row, top_mask, positive)


def rms_rows(value, weight):
    scale = lax.rsqrt(jnp.mean(value * value, axis=-1, keepdims=True) + norm_eps)
    return (value * scale * weight).astype(bf16)


KEPT = ("x", "n1", "q", "k", "v", "lse", "o", "xm", "n2", "gate", "up", "act")


def forward_kernel(made, results, count, *refs):
    (tokens, w_query, w_kv, w_out, w_in, w_down, w_proj, rel_bias, segments, gains), refs = refs[:10], refs[10:]
    asked, refs = (refs[:2], refs[2:]) if count else ((), refs)
    outs, refs = dict(zip(results, refs)), refs[len(results) :]
    found, refs = (refs[:2], refs[2:]) if count else ((), refs)
    held, refs = dict(zip(made, refs)), refs[len(made) :]
    (row_sent, row_got, sent, got, table, mask, bias, load_sems, store_sems, row_sems, send_sems, recv_sems), refs = (
        refs[:12],
        refs[12:],
    )
    half = lax.axis_index(MP)
    core = {MP: 1 - half}
    length, model = held["x0"].shape
    share = length // 2
    narrow, wide = held["q0"].shape[1], held["act0"].shape[1]
    layers = w_query.shape[0]
    loads, stores = [], []

    def fetch(source, target):
        copy = pltpu.make_async_copy(source, target, load_sems.at[len(loads)])
        copy.start()
        loads.append(copy)
        return copy

    def keep(name):
        copy = pltpu.make_async_copy(held[name], outs[name], store_sems.at[len(stores)])
        copy.start()
        stores.append(copy)

    ready = {"tokens": fetch(tokens, row_sent)}
    for layer in range(layers):
        for name, source in (
            ("wq", w_query.at[layer]),
            ("wk", w_kv.at[layer, 0]),
            ("wv", w_kv.at[layer, 1]),
            ("wo", w_out.at[layer]),
            ("wi", w_in.at[layer]),
            ("wd", w_down.at[layer]),
        ):
            ready[name + str(layer)] = fetch(source, held[name + str(layer)])
    ready["w_proj"] = fetch(w_proj, held["w_proj"])
    if count:
        greet, begin_score, finish_score = score_steps(count, held["vectors"], segments, *asked, *found, *refs)
        greet()
    else:
        barrier = pltpu.get_barrier_semaphore()
        pl.semaphore_signal(barrier, inc=1, device_id=core, device_id_type=pl.DeviceIdType.MESH)
        pl.semaphore_wait(barrier, 1)
    ready["tokens"].wait()
    send(row_sent, row_got, row_sems.at[0], row_sems.at[1], core)
    fill_table(rel_bias, table)
    fill_masks(row_ids_of(segments), mask, length // TILE)

    def rows_of(index):
        return pl.ds(pl.multiple_of(index * share, TILE), share)

    def share_part(turn, index, part):
        rows = rows_of(index)
        sent[turn, rows, :] = part.astype(bf16)
        send(
            sent.at[turn, rows, :], got.at[turn, rows, :],
            send_sems.at[turn, index], recv_sems.at[turn, index], core,
        )

    def total(turn, index, base):
        rows = rows_of(index)
        block_copy(got.at[turn, rows, :], recv_sems.at[turn, index])
        return base[rows, :] + (sent[turn, rows, :].astype(f32) + got[turn, rows, :].astype(f32))

    def project(layer, index, value):
        rows, name = rows_of(index), str(layer)
        held["x" + name][rows, :] = value
        n1 = rms_rows(value, gains[2 * layer : 2 * layer + 1, :])
        held["n1" + name][rows, :] = n1
        for part in "qkv":
            held[part + name][rows, :] = dot(n1, held["w" + part + name][...]).astype(bf16)

    for part in "qkv":
        ready["w" + part + "0"].wait()
    project(0, half, row_sent[...].astype(f32))
    block_copy(row_got, row_sems.at[1])
    project(0, 1 - half, row_got[...].astype(f32))

    for layer in range(layers):
        name = str(layer)
        for kept in ("x", "n1", "q", "k", "v"):
            keep(kept + name)
        held["lse" + name][...] = jnp.zeros((length, TILE), f32)

        def pair(p, carry, name=name):
            attend_pair(
                p, table, *(held[part + name] for part in ("q", "k", "v", "o", "lse")), mask, bias
            )
            return carry

        lax.fori_loop(0, narrow // TILE, pair, 0)
        ready["wo" + name].wait()
        for index in range(2):
            share_part(2 * layer, index, dot_nt(held["o" + name][rows_of(index), :], held["wo" + name][...]))
        keep("lse" + name)
        keep("o" + name)
        ready["wi" + name].wait()
        ready["wd" + name].wait()

        def feed(index, carry, layer=layer, name=name):
            rows = rows_of(index)
            value = total(2 * layer, index, held["x" + name])
            held["xm" + name][rows, :] = value
            n2 = rms_rows(value, gains[2 * layer + 1 : 2 * layer + 2, :])
            held["n2" + name][rows, :] = n2
            for column in range(0, wide, CHUNK):
                cols = pl.ds(column, CHUNK)
                g = dot(n2, held["wi" + name][0, :, cols])
                u = dot(n2, held["wi" + name][1, :, cols])
                held["gate" + name][rows, cols] = g.astype(bf16)
                held["up" + name][rows, cols] = u.astype(bf16)
                t = jnp.tanh(math.sqrt(2.0 / math.pi) * (g + 0.044715 * (g * g * g)))
                held["act" + name][rows, cols] = (0.5 * g * (1.0 + t) * u).astype(bf16)
            share_part(2 * layer + 1, index, dot_nt(held["act" + name][rows, :], held["wd" + name][...]))
            return carry

        lax.fori_loop(0, 2, feed, 0)
        for kept in ("xm", "n2", "gate", "up", "act"):
            keep(kept + name)
        if layer + 1 < layers:
            for part in "qkv":
                ready["w" + part + str(layer + 1)].wait()

            def following(index, carry, layer=layer, name=name):
                project(layer + 1, index, total(2 * layer + 1, index, held["xm" + name]))
                return carry

            lax.fori_loop(0, 2, following, 0)

    ready["w_proj"].wait()

    def finish(index, carry):
        rows = rows_of(index)
        value = total(2 * layers - 1, index, held["xm" + str(layers - 1)])
        held["state"][rows, :] = value
        final = rms_rows(value, gains[2 * layers : 2 * layers + 1, :])
        held["final"][rows, :] = final
        projected = dot(final, held["w_proj"][...])
        held["y"][rows, :] = projected
        scale = lax.rsqrt(jnp.sum(projected * projected, axis=-1, keepdims=True) + vector_eps)
        held["vectors"][rows, :] = (projected * scale).astype(bf16)
        return carry

    finish(half, 0)
    if count:
        begin_score()
    finish(1 - half, 0)
    for name in ("state", "final", "y", "vectors"):
        keep(name)
    if count:
        finish_score()
    for copy in stores:
        copy.wait()
    block_copy(row_sent, row_sems.at[0])
    for turn in range(2 * layers):
        for index in range(2):
            block_copy(sent.at[turn, rows_of(index), :], send_sems.at[turn, index])


def forward(tokens, weights, tables, scored):
    w_query, w_kv, w_out, w_in, w_down, w_proj = weights
    layers, model, narrow = w_query.shape
    wide, width = w_down.shape[2], w_proj.shape[1]
    length = 2 * tokens.shape[0]
    vmem, dma = pltpu.VMEM, pltpu.SemaphoreType.DMA
    sizes = dict(x=(model, f32), n1=(model, bf16), q=(narrow, bf16), k=(narrow, bf16), v=(narrow, bf16), lse=(TILE, f32),
                 o=(narrow, bf16), xm=(model, f32), n2=(model, bf16), gate=(wide, bf16), up=(wide, bf16), act=(wide, bf16))
    results = {name + str(layer): sizes[name] for layer in range(layers) for name in KEPT}
    results.update(state=(model, f32), final=(model, bf16), y=(width, f32), vectors=(width, bf16))
    made = {name: vmem((length, columns), kind) for name, (columns, kind) in results.items()}
    for layer in range(layers):
        for name in ("wq", "wk", "wv", "wo"):
            made[name + str(layer)] = vmem((model, narrow), bf16)
        made["wi" + str(layer)] = vmem((2, model, wide), bf16)
        made["wd" + str(layer)] = vmem((model, wide), bf16)
    made["w_proj"] = vmem((model, width), bf16)
    hbm, local = pl.BlockSpec(memory_space=pl.ANY), pl.BlockSpec(memory_space=vmem)
    count = lax.axis_size(BATCH) if scored else 0
    shapes = [jax.ShapeDtypeStruct((length, columns), kind) for columns, kind in results.values()]
    if scored:
        shapes += [
            jax.ShapeDtypeStruct((length, width), f32),
            jax.ShapeDtypeStruct((1, length // 2 // QLEN), f32),
        ]
    found = pl.pallas_call(
        functools.partial(forward_kernel, tuple(made), tuple(results), count),
        out_shape=tuple(shapes),
        in_specs=[hbm] * 7 + [local] * 3 + [local, pl.BlockSpec(memory_space=pltpu.SMEM)][: len(scored)],
        out_specs=(hbm,) * len(results) + (local,) * len(scored),
        scratch_shapes=list(made.values())
        + [
            vmem(tokens.shape, bf16),
            vmem(tokens.shape, bf16),
            vmem((2 * layers, length, model), bf16),
            vmem((2 * layers, length, model), bf16),
            vmem((8, SPAN), f32),
            vmem((length, 3 * TILE), f32),
            vmem((2, TILE, 3 * TILE), f32),
            dma((6 * layers + 2,)),
            dma((len(results),)),
            dma((2,)),
            dma((2 * layers, 2)),
            dma((2 * layers, 2)),
        ]
        + (score_scratch(count, length, width) if scored else []),
        compiler_params=pltpu.CompilerParams(
            collective_id=2, has_side_effects=True, vmem_limit_bytes=62 * 1024 * 1024
        ),
        cost_estimate=pl.CostEstimate(flops=10**10, bytes_accessed=5 * 10**7, transcendentals=10**6),
        name="forward",
    )(tokens, *weights, *tables, *scored)
    return dict(zip(results, found)), found[len(results) :]


CHUNK = 384


def block_copy(ref, sem):
    pltpu.make_async_copy(ref, ref, sem).wait()


class Sums:
    def __init__(self, refs):
        self.refs = refs
        self.side, self.batch = lax.axis_index(STREAM), lax.axis_index(BATCH)
        self.near, self.low, self.high = lax.rem(self.batch, 2), lax.rem(self.batch // 2, 2), self.batch // 4

    def stream_peer(self):
        return {STREAM: 1 - self.side}

    def near_peer(self):
        return {BATCH: self.batch + 1 - 2 * self.near}

    def low_peer(self):
        return {BATCH: self.batch + 2 - 4 * self.low}

    def high_peer(self):
        return {BATCH: self.batch + 4 - 8 * self.high}

    def slot(self, n):
        return n % RING

    def work(self, n):
        return self.refs["work"].at[n % self.refs["work"].shape[0]]

    def got(self, stage, n):
        return self.refs["got" + str(stage)].at[self.slot(n)]

    def send(self, source, stage, n, device):
        sems = self.refs["send"], self.refs["recv"]
        send(source, self.got(stage, n), sems[0].at[stage, self.slot(n)], sems[1].at[stage, self.slot(n)], device)

    def sent(self, stage, n):
        block_copy(self.got(stage, n), self.refs["send"].at[stage, self.slot(n)])

    def received(self, stage, n):
        block_copy(self.got(stage, n), self.refs["recv"].at[stage, self.slot(n)])

    def store(self, n):
        pltpu.make_async_copy(self.refs["done"].at[self.slot(n)], self.refs["out"](n), self.refs["store"].at[self.slot(n)]).start()

    def stored(self, n):
        block_copy(self.refs["done"].at[self.slot(n)], self.refs["store"].at[self.slot(n)])

    def add(self, count, place, got, at):
        def body(index, carry):
            target = place(index)
            target[...] = (target[...].astype(f32) + got[at(index)].astype(f32)).astype(bf16)
            return carry

        lax.fori_loop(0, count, body, 0)


class StreamFirst(Sums):
    stages = 5

    def half(self, side):
        rows = self.refs["work"].shape[4] // 2
        return pl.ds(pl.multiple_of(side * rows, 16), rows)

    def start(self, n):
        self.send(self.work(n).at[:, :, :, self.half(1 - self.side), :], 0, n, self.stream_peer())

    def step(self, n, stage):
        r, m = self.refs, self.slot(n)
        work, own = self.work(n), self.half(self.side)
        if stage <= 4:
            self.received(stage - 1, n)
        if stage == 1:
            for low in (1 - self.low, self.low):
                self.add(
                    4,
                    lambda i, low=low: work.at[i // 2, low, lax.rem(i, 2), own, :],
                    self.got(0, n),
                    lambda i, low=low: (i // 2, low, lax.rem(i, 2)),
                )
                if low is not self.low:
                    self.send(work.at[:, low, :, own, :], 1, n, self.low_peer())
        if stage == 2:
            for near in (1 - self.near, self.near):
                self.add(
                    2,
                    lambda i, near=near: work.at[i, self.low, near, own, :],
                    self.got(1, n),
                    lambda i, near=near: (i, near),
                )
                if near is not self.near:
                    self.send(work.at[:, self.low, near, own, :], 2, n, self.near_peer())
        if stage == 3:
            self.add(2, lambda i: work.at[i, self.low, self.near, own, :], self.got(2, n), lambda i: (i,))
            self.send(work.at[1 - self.high, self.low, self.near, own, :], 3, n, self.high_peer())
            self.sent(0, n)
        if stage == 4:
            total = work[self.high, self.low, self.near, own, :].astype(f32) + r["got3"][m].astype(f32)
            r["last"][m] = total.astype(bf16)
            self.send(r["last"].at[m], 4, n, self.stream_peer())
            if n >= RING:
                self.stored(n)
            r["done"][m, own, :] = r["last"][m]
            for earlier in range(1, 4):
                self.sent(earlier, n)
        if stage == 5:
            self.received(4, n)
            r["done"][m, self.half(1 - self.side), :] = r["got4"][m]
            self.store(n)
            self.sent(4, n)


class BatchFirst(Sums):
    stages = 4

    def start(self, n):
        self.send(self.work(n).at[:, :, 1 - self.near], 0, n, self.near_peer())

    def step(self, n, stage):
        r, m = self.refs, self.slot(n)
        work = self.work(n)
        self.received(stage - 1, n)
        if stage == 1:
            for low in (1 - self.low, self.low):
                self.add(
                    2,
                    lambda i, low=low: work.at[i, low, self.near],
                    self.got(0, n),
                    lambda i, low=low: (i, low),
                )
                if low is not self.low:
                    self.send(work.at[:, low, self.near], 1, n, self.low_peer())
        if stage == 2:
            self.add(2, lambda i: work.at[i, self.low, self.near], self.got(1, n), lambda i: (i,))
            self.send(work.at[1 - self.high, self.low, self.near], 2, n, self.high_peer())
        if stage == 3:
            total = work[self.high, self.low, self.near].astype(f32) + r["got2"][m].astype(f32)
            r["last"][m] = total.astype(bf16)
            self.send(r["last"].at[m], 3, n, self.stream_peer())
            for earlier in range(3):
                self.sent(earlier, n)
        if stage == 4:
            if n >= RING:
                self.stored(n)
            r["done"][m] = (r["last"][m].astype(f32) + r["got3"][m].astype(f32)).astype(bf16)
            self.store(n)
            self.sent(3, n)


RING = 4
WORK_RING = 5
FIRST_REFS = ("work", "got0", "got1", "got2", "got3", "got4", "last", "done", "send", "recv", "store")
LAST_REFS = ("work", "got0", "got1", "got2", "got3", "last", "done", "send", "recv", "store")


def first_scratch(rows, width, ring, work_ring):
    vmem, dma = pltpu.VMEM, pltpu.SemaphoreType.DMA
    half = rows // 2
    return [
        vmem((work_ring, 2, 2, 2, rows, width), bf16),
        vmem((ring, 2, 2, 2, half, width), bf16),
        vmem((ring, 2, 2, half, width), bf16),
        vmem((ring, 2, half, width), bf16),
        vmem((ring, half, width), bf16),
        vmem((ring, half, width), bf16),
        vmem((ring, half, width), bf16),
        vmem((ring, rows, width), bf16),
        dma((5, ring)),
        dma((5, ring)),
        dma((ring,)),
    ]


def last_scratch(rows, width, ring, work_ring):
    vmem, dma = pltpu.VMEM, pltpu.SemaphoreType.DMA
    return [
        vmem((work_ring, 2, 2, 2, rows, width), bf16),
        vmem((ring, 2, 2, rows, width), bf16),
        vmem((ring, 2, rows, width), bf16),
        vmem((ring, rows, width), bf16),
        vmem((ring, rows, width), bf16),
        vmem((ring, rows, width), bf16),
        vmem((ring, rows, width), bf16),
        dma((4, ring)),
        dma((4, ring)),
        dma((ring,)),
    ]


def blocks_of(wide):
    found = []
    for layer in (1, 0):
        columns = range(0, wide, CHUNK)
        found += [("e" + str(layer), "act" + str(layer), column, 0, (layer,)) for column in columns]
        for column in columns:
            for index, right in enumerate(("gate", "up")):
                found.append(("n2" + str(layer), right + str(layer), column, 1, (layer, index)))
        for left, right, output, index in (("c", "o", 2, ()), ("n1", "dq", 3, ()), ("n1", "dk", 4, (0,)), ("n1", "dv", 4, (1,))):
            found.append((left + str(layer), right + str(layer), 0, output, (layer,) + index))
    return found


def back_kernel(names, made, blocks, *refs):
    given, refs = dict(zip(names, refs)), refs[len(names) :]
    (rel_bias, segments, gains, projected, grad_vectors, w_proj), refs = refs[:6], refs[6:]
    outs, refs = refs[:8], refs[8:]
    held, refs = dict(zip(made, refs)), refs[len(made) :]
    (acc, core_sent, core_got, table, mask, bias, grid, dk_sum, dv_sum, do, little_got), refs = refs[:11], refs[11:]
    (load_sems, core_sems, little_sems), refs = refs[:3], refs[3:]
    firsts, lasts = blocks[0::2], blocks[1::2]
    half = len(blocks) // 2

    def out_of(blocks):
        def place(n):
            _, _, column, output, index = blocks[n]
            return outs[output].at[index + (slice(None), pl.ds(column, CHUNK))]

        return place

    first_refs, refs = dict(zip(FIRST_REFS, refs), out=out_of(firsts)), refs[len(FIRST_REFS) :]
    last_refs, refs = dict(zip(LAST_REFS, refs), out=out_of(lasts)), refs[len(LAST_REFS) :]
    stream_first, batch_first = StreamFirst(first_refs), BatchFirst(last_refs)
    projection = BatchFirst(dict(zip(LAST_REFS, refs), out=lambda n: outs[5]))
    half_index = lax.axis_index(MP)
    core = {MP: 1 - half_index}
    length, model = held["grad"].shape
    tiles = length // TILE

    loads = {}

    def fetch(name, source=None, target=None):
        copy = pltpu.make_async_copy(
            given[name] if source is None else source, held[name] if target is None else target, load_sems.at[len(loads)]
        )
        copy.start()
        loads[name] = [copy, False]

    def need(name):
        if name in loads and not loads[name][1]:
            loads[name][0].wait()
            loads[name][1] = True
        return held.get(name)

    def fetch_attention(layer):
        for name in ("wo", "q", "k", "v", "lse", "wq", "wk", "wv", "x"):
            source = given[name + str(layer)] if name + str(layer) in given else None
            if name == "wo":
                source = given["w_out"].at[layer]
            if name == "wq":
                source = given["w_query"].at[layer]
            if name in ("wk", "wv"):
                source = given["w_kv"].at[layer, 0 if name == "wk" else 1]
            fetch(name + str(layer), source, held[name])

    def fetch_ffn(layer):
        fetch("wd" + str(layer), given["wd"].at[layer], held["wd"])
        fetch("wi" + str(layer), given["wi"].at[layer], held["wi"])
        fetch("xm" + str(layer), None, held["xm"])

    fetch("state", None, held["x"])
    fetch("act1")
    fetch("wd1", given["wd"].at[1], held["wd"])
    for name in ("gate1", "up1"):
        fetch(name)
    fetch("wi1", given["wi"].at[1], held["wi"])
    fetch("xm1", None, held["xm"])
    fetch("n21")
    for name in ("o1", "n11", "gate0", "up0", "act0", "n20", "o0", "n10", "final"):
        fetch(name)

    barrier = pltpu.get_barrier_semaphore()
    peers = [stream_first.stream_peer(), stream_first.near_peer(), stream_first.low_peer(), stream_first.high_peer(), core]
    for peer in peers:
        pl.semaphore_signal(barrier, inc=1, device_id=peer, device_id_type=pl.DeviceIdType.MESH)


    def product(left, right, work):
        width = left.shape[1] // 2
        for part in range(2):
            block = dot_tn(left[:, part * width : (part + 1) * width], right).astype(bf16)
            work[part] = block.reshape(work.shape[1:])

    def make(sums, blocks, n):
        left, right, column, _, _ = blocks[n]
        product(need(left), need(right)[:, column : column + CHUNK], sums.work(n))
        if n == 0 and sums is stream_first:
            pl.semaphore_wait(barrier, len(peers))
        sums.start(n)

    def little_step(stage):
        peer = (stream_first.stream_peer, stream_first.near_peer, stream_first.low_peer, stream_first.high_peer)
        if stage > 0:
            block_copy(little_got.at[2 * stage - 1], little_sems.at[2 * stage - 1])
            total = little_got[2 * stage - 2] + little_got[2 * stage - 1]
            block_copy(little_got.at[2 * stage - 2], little_sems.at[2 * stage - 2])
            if stage == 4:
                outs[6][...] = total
            else:
                little_got[2 * stage] = total
        if stage < 4:
            send(
                little_got.at[2 * stage], little_got.at[2 * stage + 1],
                little_sems.at[2 * stage], little_sems.at[2 * stage + 1], peer[stage](),
            )


    grad = held["grad"]

    def rows_of(index):
        return pl.ds(pl.multiple_of(index * TILE, TILE), TILE)

    def share(turn):
        def pack(index, carry):
            core_sent[rows_of(index), :] = acc[rows_of(index), :].astype(bf16)
            return carry

        lax.fori_loop(0, tiles, pack, 0)
        send(core_sent, core_got.at[turn % 2], core_sems.at[0, turn], core_sems.at[1, turn], core)

    def norm_back(values, gain, gradient, first):
        weight = gains[gain : gain + 1, :]

        def tile(index, total):
            rows = rows_of(index)
            given_grad = gradient(rows)
            value = values[rows, :]
            scale = lax.rsqrt(jnp.mean(value * value, axis=-1, keepdims=True) + norm_eps)
            weighted = given_grad * weight
            along = jnp.mean(value * weighted, axis=-1, keepdims=True)
            change = scale * weighted - value * (scale * scale * scale * along)
            grad[rows, :] = change if first else grad[rows, :] + change
            return total + jnp.sum(given_grad * (value * scale), axis=0, keepdims=True)

        total = lax.fori_loop(0, tiles, tile, jnp.zeros((1, model), f32))
        little_got[0, gain : gain + 1, 0:model] = total

    def through_norm(turn, values, gain):
        block_copy(core_got.at[turn % 2], core_sems.at[1, turn])
        norm_back(
            values, gain, lambda rows: core_sent[rows, :].astype(f32) + core_got[turn % 2, rows, :].astype(f32), False
        )
        block_copy(core_sent, core_sems.at[0, turn])

    def projection_back():
        def tile(index, carry):
            rows = rows_of(index)
            y, grad_vector = projected[rows, :], grad_vectors[rows, :]
            scale = lax.rsqrt(jnp.sum(y * y, axis=-1, keepdims=True) + vector_eps)
            along = jnp.sum(y * grad_vector, axis=-1, keepdims=True)
            held["dproj"][rows, :] = (scale * grad_vector - y * (scale * scale * scale * along)).astype(bf16)
            return carry

        lax.fori_loop(0, tiles, tile, 0)
        need("state")
        norm_back(held["x"], 4, lambda rows: dot_nt(held["dproj"][rows, :], w_proj[...]), True)

    def round_grad(target):
        def pack(index, carry):
            target[rows_of(index), :] = grad[rows_of(index), :].astype(bf16)
            return carry

        lax.fori_loop(0, tiles, pack, 0)

    def ffn_tile(layer, column):
        cols = pl.ds(column, CHUNK)
        e, gate, up = (held[name + str(layer)] for name in ("e", "gate", "up"))

        def tile(index, carry):
            rows = pl.ds(pl.multiple_of(index * 2 * TILE, 2 * TILE), 2 * TILE)
            grad_hidden = dot(e[rows, :], held["wd"][:, cols])
            g, u = gate[rows, cols].astype(f32), up[rows, cols].astype(f32)
            root = math.sqrt(2.0 / math.pi)
            t = jnp.tanh(root * (g + 0.044715 * (g * g * g)))
            slope = 0.5 * (1.0 + t) + (0.5 * root) * g * (1.0 - t * t) * (1.0 + (3 * 0.044715) * (g * g))
            dg = (grad_hidden * u * slope).astype(bf16)
            du = (grad_hidden * (0.5 * g * (1.0 + t))).astype(bf16)
            gate[rows, cols] = dg
            up[rows, cols] = du
            part = dot_nt(dg, held["wi"][0, :, cols]) + dot_nt(du, held["wi"][1, :, cols])
            acc[rows, :] = part if column == 0 else acc[rows, :] + part
            return carry

        lax.fori_loop(0, tiles // 2, tile, 0)

    def attention_start(layer):
        c = held["c" + str(layer)]
        round_grad(c)

        def tile(index, carry):
            rows = pl.ds(pl.multiple_of(index * 2 * TILE, 2 * TILE), 2 * TILE)
            do[rows, :] = dot(c[rows, :], held["wo"][...]).astype(bf16)
            return carry

        need("wo" + str(layer))
        lax.fori_loop(0, tiles // 2, tile, 0)
        for name in ("q", "k", "v", "lse"):
            need(name + str(layer))

    def attention_pair(layer, p):
        attend_back_pair(
            p, table, held["lse"], held["q"], held["k"], held["v"], do,
            held["dq" + str(layer)], held["dk" + str(layer)], held["dv" + str(layer)],
            mask, bias, grid, dk_sum, dv_sum,
        )
        for half in range(2):
            line = diagonals(grid, half)
            place = (0, pl.ds(2 * p + half, 1), pl.ds(model, SPAN))
            little_got[place] = little_got[place] + line

    def attention_end(layer, turn):
        for name in ("wq", "wk", "wv"):
            need(name + str(layer))

        def tile(index, carry):
            rows = pl.ds(pl.multiple_of(index * 2 * TILE, 2 * TILE), 2 * TILE)
            acc[rows, :] = (
                dot_nt(held["dq" + str(layer)][rows, :], held["wq"][...])
                + dot_nt(held["dk" + str(layer)][rows, :], held["wk"][...])
                + dot_nt(held["dv" + str(layer)][rows, :], held["wv"][...])
            )
            return carry

        lax.fori_loop(0, tiles // 2, tile, 0)
        share(turn)

    def ffn_step(layer, number, turn):
        if number == 0:
            for name in ("wd", "wi", "gate", "up"):
                need(name + str(layer))
        ffn_tile(layer, number * CHUNK)
        if number == 3:
            share(turn)

    def setup():
        fill_table(rel_bias, table)
        fill_masks(row_ids_of(segments), mask, tiles)

    def attention_first(layer, turn):
        need("xm" + str(layer))
        through_norm(turn, held["xm"], 2 * layer + 1)
        if layer:
            fetch_ffn(0)
        attention_start(layer)
        attention_pair(layer, 0)

    def layer_end(layer, turn):
        need("x" + str(layer))
        through_norm(turn, held["x"], 2 * layer)
        if layer:
            fetch_attention(0)
            round_grad(held["e0"])
            ffn_step(0, 0, 2)
        else:
            share_rows = length // 2
            outs[7][...] = grad[pl.ds(pl.multiple_of(half_index * share_rows, TILE), share_rows), :]

    pieces = [
        [lambda: ffn_step(1, 0, 0)],
        [lambda: ffn_step(1, 1, 0)],
        [lambda: ffn_step(1, 2, 0)],
        [lambda: ffn_step(1, 3, 0), setup],
        [lambda: attention_first(1, 0)],
        [lambda: attention_pair(1, 1), lambda: attention_pair(1, 2)],
        [lambda: attention_end(1, 1)],
        [lambda: layer_end(1, 1)],
        [lambda: ffn_step(0, 1, 2)],
        [lambda: ffn_step(0, 2, 2)],
        [lambda: ffn_step(0, 3, 2)],
        [lambda: attention_first(0, 2)],
        [lambda: attention_pair(0, 1)],
        [lambda: attention_pair(0, 2)],
        [lambda: attention_end(0, 3)],
        [lambda: layer_end(0, 3)],
    ]
    little_got[0] = jnp.zeros(little_got.shape[1:], f32)
    projection_back()
    fetch_attention(1)
    round_grad(held["e1"])
    for t in range(half + 5):
        if t < half:
            make(stream_first, firsts, t)
            make(batch_first, lasts, t)
        if t == half - 3:
            product(need("final"), held["dproj"][...], projection.work(0))
            projection.start(0)
        if t < len(pieces):
            for piece in pieces[t]:
                piece()
        for stage in (1, 2, 3, 4, 5):
            if 0 <= t - stage < half:
                stream_first.step(t - stage, stage)
                if stage <= 4:
                    batch_first.step(t - stage, stage)
            if t - stage == half - 3 and stage <= 4:
                projection.step(0, stage)
        if 0 <= t - half <= 4:
            little_step(t - half)
    for n in range(half - RING, half):
        stream_first.stored(n)
        batch_first.stored(n)
    projection.stored(0)


def back(chain, weights, tables):
    batch = lax.axis_size(BATCH)
    length, model = chain["x0"].shape
    rows = model // batch
    narrow, wide = chain["q1"].shape[1], chain["act1"].shape[1]
    width = tables[-1].shape[1]
    little = jax.ShapeDtypeStruct((8, model + SPAN), f32)
    blocks = blocks_of(wide)
    given = dict(chain, **weights)
    vmem, dma, shape = pltpu.VMEM, pltpu.SemaphoreType.DMA, jax.ShapeDtypeStruct
    made = {"grad": (length, model), "x": (length, model), "xm": (length, model), "lse": (length, TILE)}
    made = {name: vmem(dims, f32) for name, dims in made.items()}
    for name in ("e", "n2", "c", "n1"):
        made.update({name + layer: vmem((length, model), bf16) for layer in "01"})
    for name in ("act", "gate", "up"):
        made.update({name + layer: vmem((length, wide), bf16) for layer in "01"})
    for name in ("o", "dq", "dk", "dv"):
        made.update({name + layer: vmem((length, narrow), bf16) for layer in "01"})
    made.update({name: vmem((length, narrow), bf16) for name in "qkv"})
    made.update({name: vmem((model, narrow), bf16) for name in ("wo", "wq", "wk", "wv")})
    made.update(wd=vmem((model, wide), bf16), wi=vmem((2, model, wide), bf16))
    made.update(final=vmem((length, model), bf16), dproj=vmem((length, width), bf16))
    ins = [pl.BlockSpec(memory_space=pl.ANY)] * len(given) + [pl.BlockSpec(memory_space=vmem)] * 6
    hbm, local = pl.BlockSpec(memory_space=pl.ANY), pl.BlockSpec(memory_space=vmem)
    return pl.pallas_call(
        functools.partial(back_kernel, tuple(given), tuple(made), blocks),
        out_shape=(
            shape((2, rows, wide), bf16),
            shape((2, 2, rows, wide), bf16),
            shape((2, rows, narrow), bf16),
            shape((2, rows, narrow), bf16),
            shape((2, 2, rows, narrow), bf16),
            shape((rows, width), bf16),
            shape(little.shape, f32),
            shape((length // 2, model), f32),
        ),
        in_specs=ins,
        out_specs=(hbm,) * 6 + (local,) * 2,
        scratch_shapes=list(made.values())
        + [
            vmem((length, model), f32),
            vmem((length, model), bf16),
            vmem((2, length, model), bf16),
            vmem((8, SPAN), f32),
            vmem((length, 3 * TILE), f32),
            vmem((2, TILE, 3 * TILE), f32),
            vmem((2, TILE, SPAN), f32),
            vmem((length, TILE), f32),
            vmem((length, TILE), f32),
            vmem((length, narrow), bf16),
            vmem((8,) + little.shape, f32),
            dma((64,)),
            dma((2, 4)),
            dma((8,)),
        ]
        + first_scratch(rows, CHUNK, RING, WORK_RING)
        + last_scratch(rows, CHUNK, RING, WORK_RING)
        + last_scratch(rows, width, 1, 1),
        compiler_params=pltpu.CompilerParams(
            collective_id=1, has_side_effects=True, vmem_limit_bytes=62 * 1024 * 1024
        ),
        cost_estimate=pl.CostEstimate(flops=2 * 10**10, bytes_accessed=5 * 10**7, transcendentals=10**6),
        name="back",
    )(*given.values(), *tables)


def place_kernel(down, into, out, query, key_value, projection, little, grad, vectors, losses, *outs):
    share = outs[0].shape[0]
    first = pl.multiple_of(lax.axis_index(MP) * share, TILE)
    outs[0][...] = vectors[pl.ds(first, share), :]
    outs[1][...] = losses[...]
    for source, target in zip((grad, query, key_value, out, into, down, projection), outs[2:8] + outs[10:]):
        target[...] = source[...].astype(f32)
    gains, bias = outs[8], outs[9]
    model = grad.shape[1]
    count, rows = gains.shape
    moved = pltpu.roll(little[:, 0:model], lax.rem(model - lax.axis_index(BATCH) * rows, model), axis=1)
    gains[...] = moved[0:count, 0:rows]
    bias[...] = lax.dot_general(
        little[0 : bias.shape[0], model:],
        bucket_places(bias.shape[1]),
        (((1,), (1,)), ((), ())),
        precision=highest,
        preferred_element_type=f32,
    )


def place(summed, vectors, losses, gain_count, bias_shape):
    down, into, out, query, key_value, projection, little, grad = summed
    shape = jax.ShapeDtypeStruct
    local = pl.BlockSpec(memory_space=pltpu.VMEM)
    return pl.pallas_call(
        place_kernel,
        out_shape=(shape((grad.shape[0], vectors.shape[1]), bf16), shape(losses.shape, f32))
        + tuple(shape(value.shape, f32) for value in (grad, query, key_value, out, into, down))
        + (shape((gain_count, query.shape[1]), f32), shape(bias_shape, f32), shape(projection.shape, f32)),
        in_specs=[local] * 10,
        out_specs=(local,) * 11,
        compiler_params=pltpu.CompilerParams(vmem_limit_bytes=60 * 1024 * 1024),
        name="place",
    )(*summed, vectors, losses)


def sum_gradients_plainly(kept, final_pair, little):
    def summed(left, right):
        part = lax.psum_scatter(dot_tn(left, right).astype(bf16), BATCH, scatter_dimension=0, tiled=True)
        return sum_of_two(part, STREAM)

    found = []
    for e, n2, c, n1, hidden, dg, du, o, dq, dk, dv in kept:
        found.append((
            summed(e, hidden),
            jnp.stack([summed(n2, dg), summed(n2, du)]),
            summed(c, o),
            summed(n1, dq),
            jnp.stack([summed(n1, dk), summed(n1, dv)]),
        ))
    return [jnp.stack(parts) for parts in zip(*found)] + [
        summed(*final_pair),
        lax.psum(little, (STREAM, BATCH)),
    ]


def on_device(
    tokens,
    segments,
    top_mask,
    positive,
    w_query,
    w_kv,
    w_out,
    w_in,
    w_down,
    gains,
    rel_bias,
    w_proj,
):
    length = segments.shape[1]
    share_len, model_width = tokens.shape[2:]
    head_count = rel_bias.shape[1]
    layers = w_query.shape[0]
    batch = lax.axis_size(BATCH)
    bias_rows = jnp.transpose(rel_bias)
    tables = (bias_rows, segments, gains)
    together = batch <= 8
    kept, scores = forward(
        tokens[0, 0],
        (w_query, w_kv, w_out, w_in, w_down, w_proj),
        tables,
        (top_mask, positive) if together else (),
    )
    vectors = kept["vectors"]
    grad_vectors, query_loss = scores if together else score(vectors, segments, top_mask, positive)
    if layers == 2 and batch == 8:
        chain = {name: value for name, value in kept.items() if name not in ("y", "vectors")}
        weights = dict(w_query=w_query, w_kv=w_kv, w_out=w_out, wi=w_in, wd=w_down)
        summed = back(chain, weights, tables + (kept["y"], grad_vectors, w_proj))
        placed = place(summed, vectors, query_loss, gains.shape[0], bias_rows.shape)
        return (placed[0][None, None], placed[1], placed[2][None, None]) + placed[3:9] + (placed[9].T, placed[10])
    else:
        row_segments = jnp.where(
            lax.axis_index(STREAM) == 0, jnp.arange(length, dtype=jnp.int32) // QLEN, segments[0]
        )
        row_ids = row_segments[None]
        offset_onehot = (
            offset_buckets()[None, :] == jnp.arange(rel_bias.shape[0], dtype=jnp.int32)[:, None]
        ).astype(f32)
        table = jnp.einsum(
            "bh,bk->hk", jnp.pad(rel_bias, ((0, 0), (0, 8 - head_count))), offset_onehot, precision=highest
        )
        kept_layers = [[kept[name + str(layer)] for name in KEPT] for layer in range(layers)]
        grad_projected = jax.vjp(normalize, kept["y"])[1](grad_vectors)[0].astype(bf16)
        grad_final = dot_nt(grad_projected, w_proj)
        grad_state, grad_gain_final = jax.vjp(rms_scale, kept["state"], gains[2 * layers])[1](grad_final)
        gain_grads = [None] * (2 * layers)
        operands = [None] * layers
        sums = jnp.zeros(table.shape, f32)
        for layer in reversed(range(layers)):
            weights_layer = (
                w_query[layer],
                w_kv[layer],
                w_out[layer],
                w_in[layer],
                w_down[layer],
                gains[2 * layer],
                gains[2 * layer + 1],
            )
            grad_state, ffn_lefts, ffn_rights, gain_grads[2 * layer + 1] = ffn_backward(
                grad_state, kept_layers[layer], weights_layer
            )
            grad_state, lefts, rights, gain_grads[2 * layer], part = attention_backward(
                grad_state, table, row_ids, kept_layers[layer], weights_layer
            )
            operands[layer] = ffn_lefts + lefts + ffn_rights + rights
            sums = sums + part
        little = jnp.concatenate(
            [jnp.pad(jnp.stack(gain_grads + [grad_gain_final]), ((0, 7 - 2 * layers), (0, 0))), sums], axis=1
        )
        summed = sum_gradients_plainly(operands, (kept["final"], grad_projected), little)
        grad_down, grad_in, grad_out, grad_query, grad_kv, grad_proj, little = summed
        own_grad = lax.dynamic_slice_in_dim(grad_state, lax.axis_index(MP) * share_len, share_len, 0)
        grad_bias = jnp.einsum("hk,bk->bh", little[:, model_width:], offset_onehot, precision=highest)
        rows = model_width // batch
        grad_gains = lax.dynamic_slice(little, (0, lax.axis_index(BATCH) * rows), (2 * layers + 1, rows))
    own_vectors = lax.dynamic_slice_in_dim(vectors, lax.axis_index(MP) * share_len, share_len, 0)
    return (
        own_vectors[None, None],
        query_loss,
        own_grad[None, None],
        grad_query,
        grad_kv,
        grad_out,
        grad_in,
        grad_down,
        grad_gains,
        grad_bias[:, :head_count],
        grad_proj,
    )


def solution(mesh):
    placed = (
        P(STREAM, BATCH, MP, None),
        P(BATCH, None),
        P(None, MP, BATCH, None),
        P(None, MP),
        P(None, None, MP),
        P(None, None, None, MP),
        P(None, None, MP),
        P(None, None, None, MP),
        P(None, None, MP),
        P(),
        P(None, MP),
        P(),
    )
    return jax.shard_map(
        on_device,
        mesh=mesh,
        in_specs=placed,
        out_specs=(
            P(STREAM, BATCH, MP, None),
            P(BATCH, MP),
            P(STREAM, BATCH, MP, None),
            P(None, BATCH, MP),
            P(None, None, BATCH, MP),
            P(None, BATCH, MP),
            P(None, None, BATCH, MP),
            P(None, BATCH, MP),
            P(None, BATCH),
            P(None, MP),
            P(BATCH, None),
        ),
        check_vma=False,
    )
```

```python
import functools
import math

import jax
import jax.numpy as jnp
from jax import lax
from jax.experimental import pallas as pl
from jax.experimental.pallas import tpu as pltpu
from jax.sharding import PartitionSpec as P

QLEN = 32
DOCS_ROW = 8
TILE = 128
STREAM, BATCH, MP = "stream", "batch", "mp"
SPAN = 512


norm_eps = 1e-06
vector_eps = 1e-06
temper = 0.05
logit_scale = 32.0
bucket_edges = (12, 16, 23, 32, 46, 64, 91)
highest = lax.Precision.HIGHEST
bf16 = jnp.bfloat16
f32 = jnp.float32


def dot(a, b):
    return lax.dot_general(a, b, (((1,), (0,)), ((), ())), preferred_element_type=f32)


def dot_nt(a, b):
    return lax.dot_general(a, b, (((1,), (1,)), ((), ())), preferred_element_type=f32)


def dot_tn(a, b):
    return lax.dot_general(a, b, (((0,), (0,)), ((), ())), preferred_element_type=f32)


def offset_buckets():
    index = jnp.arange(SPAN, dtype=jnp.int32)
    offsets = jnp.where(index < SPAN // 2, index, index - SPAN)
    magnitude = jnp.abs(offsets)
    far_bucket = jnp.full(offsets.shape, 8, jnp.int32)
    for threshold in bucket_edges:
        far_bucket = far_bucket + (magnitude >= threshold).astype(jnp.int32)
    bucket = jnp.where(magnitude < 8, magnitude, jnp.minimum(far_bucket, 15))
    return bucket + jnp.where(offsets > 0, 16, 0).astype(jnp.int32)


def bucket_places(count):
    index = lax.broadcasted_iota(jnp.int32, (count, SPAN), 1)
    offsets = jnp.where(index < SPAN // 2, index, index - SPAN)
    magnitude = jnp.abs(offsets)
    far_bucket = jnp.full(offsets.shape, 8, jnp.int32)
    for threshold in bucket_edges:
        far_bucket = far_bucket + jnp.where(magnitude >= threshold, 1, 0)
    bucket = jnp.where(magnitude < 8, magnitude, jnp.minimum(far_bucket, 15))
    bucket = bucket + jnp.where(offsets > 0, 16, 0)
    return jnp.where(bucket == lax.broadcasted_iota(jnp.int32, (count, SPAN), 0), 1.0, 0.0)


def fill_table(rel_bias, table):
    table[...] = jnp.zeros(table.shape, f32)
    table[0 : rel_bias.shape[0], :] = lax.dot_general(
        rel_bias[...],
        bucket_places(rel_bias.shape[1]),
        (((1,), (0,)), ((), ())),
        precision=highest,
        preferred_element_type=f32,
    )


def row_ids_of(segments):
    position = lax.broadcasted_iota(jnp.int32, segments.shape, 1)
    return jnp.where(lax.axis_index(STREAM) == 0, position // QLEN, segments[...])


def window(tile, tiles):
    first, last = max(0, tile - 1), min(tiles, tile + 2)
    shift = first - (tile - 1)
    return pl.ds(first * TILE, (last - first) * TILE), slice(shift * TILE, (shift + last - first) * TILE)


def fill_masks(row_ids, mask, tiles):
    ids = row_ids.astype(f32)
    lines = [jnp.broadcast_to(ids[:, tile * TILE : (tile + 1) * TILE], (TILE, TILE)) for tile in range(tiles)]
    for tile in range(tiles):
        own = jnp.transpose(lines[tile])
        for near in range(max(0, tile - 1), min(tiles, tile + 2)):
            place = (near - tile + 1) * TILE
            mask[tile * TILE : (tile + 1) * TILE, place : place + TILE] = jnp.where(own == lines[near], 0.0, -1e30)


def bias_tile(table, head):
    line = jnp.broadcast_to(table[pl.ds(head, 1), :], (TILE, SPAN))
    return pltpu.roll(line, TILE, axis=1, stride=1, stride_axis=0)[:, : 3 * TILE]


def attend_pair(p, table, q, k, v, o, lse, mask, bias):
    tiles = q.shape[0] // TILE
    lane = lax.broadcasted_iota(jnp.int32, (TILE, TILE), 1)
    cols = pl.ds(pl.multiple_of(p * TILE, TILE), TILE)
    for half in range(2):
        bias[half] = bias_tile(table, 2 * p + half)
    scores = []
    for tile in range(tiles):
        rows = pl.ds(tile * TILE, TILE)
        keys, frame = window(tile, tiles)
        queries, near_keys = q[rows, cols], k[keys, cols]
        for half in range(2):
            mine = (lane >= 64) if half else (lane < 64)
            s = dot_nt(jnp.where(mine, queries, jnp.zeros_like(queries)), near_keys)
            scores.append(s + (bias[half][:, frame] + mask[rows, frame]))
    tops = [jnp.max(s, axis=-1, keepdims=True) for s in scores]
    exps = [jnp.exp(s - top) for s, top in zip(scores, tops)]
    totals = [jnp.sum(e, axis=-1, keepdims=True) for e in exps]
    weights = [(e * (1.0 / total)).astype(bf16) for e, total in zip(exps, totals)]
    for tile in range(tiles):
        rows = pl.ds(tile * TILE, TILE)
        near_values = v[window(tile, tiles)[0], cols]
        outs = [dot(weights[2 * tile + half], near_values) for half in range(2)]
        o[rows, cols] = jnp.where(lane < 64, outs[0], outs[1]).astype(bf16)
        kept = lse[rows, :]
        for half in range(2):
            index = 2 * tile + half
            kept = jnp.where(lane == 2 * p + half, tops[index] + jnp.log(totals[index]), kept)
        lse[rows, :] = kept


def attend_back_pair(p, table, lse, q, k, v, do, dq, dk, dv, mask, bias, grid, dk_sum, dv_sum):
    tiles = q.shape[0] // TILE
    lane = lax.broadcasted_iota(jnp.int32, (TILE, TILE), 1)
    cols = pl.ds(pl.multiple_of(p * TILE, TILE), TILE)
    for half in range(2):
        bias[half] = bias_tile(table, 2 * p + half)
    grid[...] = jnp.zeros(grid.shape, f32)
    dk_sum[...] = jnp.zeros(dk_sum.shape, f32)
    dv_sum[...] = jnp.zeros(dv_sum.shape, f32)
    for first in range(0, tiles, 2):
        some = [(tile, half) for tile in range(first, min(first + 2, tiles)) for half in range(2)]
        own_queries, own_grads, weights, grad_weights = [], [], [], []
        for tile, half in some:
            rows = pl.ds(tile * TILE, TILE)
            keys, frame = window(tile, tiles)
            mine = (lane >= 64) if half else (lane < 64)
            queries, grads = q[rows, cols], do[rows, cols]
            own_queries.append(jnp.where(mine, queries, jnp.zeros_like(queries)))
            own_grads.append(jnp.where(mine, grads, jnp.zeros_like(grads)))
            log_total = jnp.sum(jnp.where(lane == 2 * p + half, lse[rows, :], 0.0), axis=-1, keepdims=True)
            s = dot_nt(own_queries[-1], k[keys, cols])
            s = s + (bias[half][:, frame] + mask[rows, frame])
            weights.append(jnp.exp(s - log_total))
            grad_weights.append(dot_nt(own_grads[-1], v[keys, cols]))
        means = [jnp.sum(w * g, axis=-1, keepdims=True) for w, g in zip(weights, grad_weights)]
        ds = [(w * (g - mean)).astype(bf16) for w, g, mean in zip(weights, grad_weights, means)]
        outs = []
        for index, (tile, half) in enumerate(some):
            keys, frame = window(tile, tiles)
            outs.append(dot(ds[index], k[keys, cols]))
            dk_sum[keys, :] += dot_tn(ds[index], own_queries[index])
            dv_sum[keys, :] += dot_tn(weights[index].astype(bf16), own_grads[index])
            grid[half, :, frame] += ds[index].astype(f32)
        for index in range(0, len(some), 2):
            rows = pl.ds(some[index][0] * TILE, TILE)
            dq[rows, cols] = jnp.where(lane < 64, outs[index], outs[index + 1]).astype(bf16)
    dk[:, cols] = dk_sum[...].astype(bf16)
    dv[:, cols] = dv_sum[...].astype(bf16)


def diagonals(grid, half):
    row_index = lax.broadcasted_iota(jnp.int32, (TILE, SPAN), 0)
    turned = pltpu.roll(grid[half], SPAN - TILE, axis=1)
    for bit in range(7):
        moved = pltpu.roll(turned, SPAN - (1 << bit), axis=1)
        turned = jnp.where((row_index >> bit) & 1 == 1, moved, turned)
    return jnp.sum(turned, axis=0, keepdims=True)


def attend_back_kernel(
    table, row_ids, lse, q, k, v, do, dq, dk, dv, sums, mask, bias, grid, dk_sum, dv_sum
):
    fill_masks(row_ids[...], mask, q.shape[0] // TILE)
    sums[...] = jnp.zeros(sums.shape, f32)

    def pair(p, carry):
        attend_back_pair(p, table, lse, q, k, v, do, dq, dk, dv, mask, bias, grid, dk_sum, dv_sum)
        for half in range(2):
            sums[pl.ds(2 * p + half, 1), :] = diagonals(grid, half)
        return carry

    lax.fori_loop(0, q.shape[1] // TILE, pair, 0)


def attend_back(table, row_ids, lse, q, k, v, do):
    length, width = q.shape
    grad = jax.ShapeDtypeStruct((length, width), bf16)
    return pl.pallas_call(
        attend_back_kernel,
        out_shape=(grad, grad, grad, jax.ShapeDtypeStruct(table.shape, f32)),
        scratch_shapes=[
            pltpu.VMEM((length, 3 * TILE), f32),
            pltpu.VMEM((2, TILE, 3 * TILE), f32),
            pltpu.VMEM((2, TILE, SPAN), f32),
            pltpu.VMEM((length, TILE), f32),
            pltpu.VMEM((length, TILE), f32),
        ],
        compiler_params=pltpu.CompilerParams(vmem_limit_bytes=32 * 1024 * 1024),
        cost_estimate=pl.CostEstimate(flops=25 * 10**8, bytes_accessed=4 * 10**6, transcendentals=10**6),
        name="attend_back",
    )(table, row_ids, lse, q, k, v, do)


def rms_scale(values, gain_row):
    return (
        values * lax.rsqrt(jnp.mean(values * values, axis=-1, keepdims=True) + norm_eps) * gain_row
    )


def gated_gelu(gate, up):
    return jax.nn.gelu(gate, approximate=True) * up


def normalize(values):
    return values * lax.rsqrt(jnp.sum(values * values, axis=-1, keepdims=True) + vector_eps)


def swap(value, axis):
    return lax.ppermute(value, axis, [(0, 1), (1, 0)])


def sum_of_two(part, axis):
    mine = lax.optimization_barrier(part.astype(bf16))
    return mine.astype(f32) + swap(mine, axis).astype(f32)


def ffn_backward(grad_output, kept, weights_layer):
    middle, ffn_input, gate, up, hidden = kept[7:]
    in_weight, down_weight, gain_ffn = weights_layer[3], weights_layer[4], weights_layer[6]
    grad_branch = grad_output.astype(bf16)
    grad_hidden = dot(grad_branch, down_weight)
    grad_gate, grad_up = jax.vjp(gated_gelu, gate.astype(f32), up.astype(f32))[1](grad_hidden)
    grad_gate, grad_up = grad_gate.astype(bf16), grad_up.astype(bf16)
    grad_input = sum_of_two(dot_nt(grad_gate, in_weight[0]) + dot_nt(grad_up, in_weight[1]), MP)
    grad_mid_norm, grad_gain = jax.vjp(rms_scale, middle, gain_ffn)[1](grad_input)
    return grad_output + grad_mid_norm, (grad_branch, ffn_input), (hidden, grad_gate, grad_up), grad_gain


def attention_backward(grad_middle, table, row_ids, kept, weights_layer):
    inputs, normed, q, k, v, lse, attended = kept[:7]
    query_weight, kv_weight, out_weight, gain_attn = (
        weights_layer[0],
        weights_layer[1],
        weights_layer[2],
        weights_layer[5],
    )
    grad_attn = grad_middle.astype(bf16)
    do = dot(grad_attn, out_weight).astype(bf16)
    dq, dk, dv, sums = attend_back(table, row_ids, lse, q, k, v, do)
    grad_normed = sum_of_two(
        dot_nt(dq, query_weight) + dot_nt(dk, kv_weight[0]) + dot_nt(dv, kv_weight[1]), MP
    )
    grad_in_norm, grad_gain = jax.vjp(rms_scale, inputs, gain_attn)[1](grad_normed)
    return grad_middle + grad_in_norm, (grad_attn, normed), (attended, dq, dk, dv), grad_gain, sums


def send(source, target, send_sem, recv_sem, device):
    copy = pltpu.make_async_remote_copy(
        src_ref=source,
        dst_ref=target,
        send_sem=send_sem,
        recv_sem=recv_sem,
        device_id=device,
        device_id_type=pl.DeviceIdType.MESH,
    )
    copy.start()


def score_steps(
    count,
    vectors,
    doc_row,
    top_mask,
    positive,
    grad,
    loss,
    queries,
    docs,
    raised,
    totals,
    logits,
    places,
    stats,
    own_loss,
    other_loss,
    sent_grads,
    got_grads,
    cross,
    doc_sum,
    sent_docs,
    got_docs,
    core_sent,
    core_got,
    query_send,
    query_recv,
    stat_send,
    stat_recv,
    grad_send,
    grad_recv,
    part_sems,
    doc_sems,
    loss_sems,
    cross_sems,
    back_sems,
    core_sems,
    early_sems,
):
    side, batch, half = lax.axis_index(STREAM), lax.axis_index(BATCH), lax.axis_index(MP)
    length, width = vectors.shape
    quarter = length // 4
    slots = quarter // QLEN
    group = math.gcd(count, 4)
    core, other = {MP: 1 - half}, {STREAM: 1 - side}

    def scorer(step):
        return lax.rem(batch + step, count)

    def each(first, body):
        def run(step, carry):
            body(scorer(step))
            return carry

        lax.fori_loop(first, count, run, 0, unroll=count <= 8)

    barrier = pltpu.get_barrier_semaphore()

    def greet(peer):
        pl.semaphore_signal(barrier, inc=1, device_id={BATCH: peer}, device_id_type=pl.DeviceIdType.MESH)

    def greet_all():
        each(1, greet)
        for peer in (core, other):
            pl.semaphore_signal(barrier, inc=1, device_id=peer, device_id_type=pl.DeviceIdType.MESH)
        pl.semaphore_wait(barrier, count + 1)

    def query_part(plane):
        return vectors.at[pl.ds(pl.multiple_of(half * (length // 2), QLEN) + plane * quarter, quarter), :]

    own = queries.at[batch]

    def push(peer):
        send(own, own, query_send.at[peer], query_recv.at[batch], {BATCH: peer})

    def begin():
        @pl.when(side == 0)
        def _():
            send(query_part(1), own, part_sems.at[0], part_sems.at[1], other)
            own[...] = query_part(0)[...]
            each(1, push)

    def finish():
        @pl.when(side == 1)
        def _():
            send(vectors, docs, doc_sems.at[0], doc_sems.at[1], other)
            docs[...] = vectors[...]
            block_copy(own, part_sems.at[1])
            each(1, push)

        row = lax.broadcasted_iota(jnp.int32, (width, length), 0)
        onehot = jnp.where(row == jnp.broadcast_to(doc_row[0:1, :], (width, length)), 1.0, 0.0).astype(bf16)

        @pl.when(side == 0)
        def _():
            block_copy(docs, doc_sems.at[1])

        def forward(first, carry):
            sources = [scorer(first * group + step) for step in range(group)]
            sims = []
            for source in sources:

                @pl.when(source != batch)
                def _():
                    block_copy(queries.at[source], query_recv.at[source])

                sims.append(dot_nt(queries[source], docs[...]))
            for source, sim in zip(sources, sims):
                for slot in range(slots):
                    chosen = top_mask[source, side * slots + slot].astype(f32)
                    part = jnp.exp(sim[slot * QLEN : (slot + 1) * QLEN] * (1.0 / temper)) * chosen
                    raised[source, slot * QLEN : (slot + 1) * QLEN, :] = part.astype(bf16)
            summed = [dot_nt(raised[source], onehot) for source in sources]
            for source, total in zip(sources, summed):
                totals[source] = total
                pooled = jnp.log1p(total) * (logit_scale * temper / QLEN)
                for slot in range(slots):
                    line = pl.ds(source * slots + slot, 1)
                    logits[line, :] = jnp.sum(pooled[slot * QLEN : (slot + 1) * QLEN], axis=0, keepdims=True)
                    places[line, :] = jnp.full((1, width), positive[source, side * slots + slot], jnp.int32)
            return carry

        lax.fori_loop(0, count // group, forward, 0)

        doc = lax.broadcasted_iota(jnp.int32, logits.shape, 1)
        local = doc < DOCS_ROW
        scores = logits[...]
        is_positive = jnp.where(
            jnp.logical_and(local, places[...] == doc + batch * DOCS_ROW), 1.0, 0.0
        )
        exps = jnp.sum(jnp.where(local, jnp.exp(scores), 0.0), axis=1, keepdims=True)
        hits = jnp.sum(is_positive * scores, axis=1, keepdims=True)
        columns = jnp.where(doc == 0, exps, jnp.where(doc == 1, hits, 0.0))
        lines = stats.shape[2]
        if lines > columns.shape[0]:
            columns = jnp.concatenate([columns, jnp.zeros((lines - columns.shape[0], width), f32)], axis=0)
        stats[batch] = jnp.transpose(columns)[0:8, :]

        def push_stats(peer):
            send(stats.at[batch], stats.at[batch], stat_send.at[peer], stat_recv.at[batch], {BATCH: peer})

        each(1, push_stats)
        each(1, lambda peer: block_copy(stats.at[peer], stat_recv.at[peer]))
        summed = lax.fori_loop(1, count, lambda source, total: total + stats[source], stats[0])
        log_line = jnp.log(summed[0:1, :])
        row = lax.broadcasted_iota(jnp.int32, (width, lines), 0)
        both = jnp.where(row == 0, log_line, jnp.where(row == 1, log_line - summed[1:2, :], 0.0))
        both = jnp.transpose(both)[0 : logits.shape[0], :]
        log_total = jnp.sum(jnp.where(doc == 0, both, 0.0), axis=1, keepdims=True)
        losses = jnp.sum(jnp.where(doc == 1, both, 0.0), axis=1, keepdims=True)
        logits[...] = jnp.broadcast_to(losses, logits.shape)
        for slot in range(slots):
            own_loss[pl.ds(slot, 1), :] = logits[pl.ds(batch * slots + slot, 1), :]
        send(own_loss, other_loss, loss_sems.at[0], loss_sems.at[1], other)
        logits[...] = jnp.where(local, jnp.exp(scores - log_total), 0.0) - is_positive
        doc_sum[...] = jnp.zeros(doc_sum.shape, f32)

        def backward(first, carry):
            sources = [scorer(first * group + step + 1) for step in range(group)]
            factors = []
            for source in sources:
                parts = []
                for slot in range(slots):
                    line = logits[pl.ds(source * slots + slot, 1), :] * (logit_scale / QLEN)
                    parts.append(line / (1.0 + totals[source, slot * QLEN : (slot + 1) * QLEN, :]))
                factors.append(jnp.concatenate(parts, axis=0).astype(bf16))
            spreads = [dot(factor, onehot) for factor in factors]
            ds = [(raised[source].astype(f32) * spread).astype(bf16) for source, spread in zip(sources, spreads)]
            backs = [dot(d, docs[...]).astype(bf16) for d in ds]
            for source, back in zip(sources, backs):
                sent_grads[source] = back

                @pl.when(source != batch)
                def _():
                    send(
                        sent_grads.at[source], got_grads.at[batch], grad_send.at[source], grad_recv.at[batch], {BATCH: source}
                    )

            change = dot_tn(ds[0], queries[sources[0]])
            for d, source in zip(ds[1:], sources[1:]):
                change = change + dot_tn(d, queries[source])
            doc_sum[...] += change
            return carry

        lax.fori_loop(0, count // group, backward, 0)

        @pl.when(side == 0)
        def _():
            sent_docs[...] = doc_sum[...].astype(bf16)
            send(sent_docs, got_docs, back_sems.at[0], back_sems.at[1], other)

        got_grads[batch] = sent_grads[batch]
        each(1, lambda peer: block_copy(got_grads.at[peer], grad_recv.at[peer]))
        total = lax.fori_loop(
            1, count, lambda source, total: total + got_grads[source].astype(f32), got_grads[0].astype(f32)
        )
        share = pl.ds(0, length // 2)

        @pl.when(side == 0)
        def _():
            core_sent[0:quarter, :] = total.astype(bf16)
            parts = [core_sent.at[pl.ds(plane * quarter, quarter), :] for plane in range(2)]
            theirs = [core_got.at[pl.ds(plane * quarter, quarter), :] for plane in range(2)]
            send(parts[0], theirs[0], early_sems.at[0], early_sems.at[1], core)
            block_copy(cross.at[1], cross_sems.at[1])
            core_sent[quarter : 2 * quarter, :] = cross[1]
            send(parts[1], theirs[1], core_sems.at[0], core_sems.at[1], core)
            first = pl.multiple_of(half * (length // 2), QLEN)
            grad[pl.ds(first, length // 2), :] = core_sent[share, :].astype(f32)
            block_copy(theirs[0], early_sems.at[1])
            block_copy(theirs[1], core_sems.at[1])
            grad[pl.ds(length // 2 - first, length // 2), :] = core_got[share, :].astype(f32)
            block_copy(parts[0], early_sems.at[0])
            block_copy(parts[1], core_sems.at[0])
            block_copy(sent_docs, back_sems.at[0])
            block_copy(query_part(1), part_sems.at[0])

        @pl.when(side == 1)
        def _():
            cross[0] = total.astype(bf16)
            send(cross.at[0], cross.at[1], cross_sems.at[0], cross_sems.at[1], other)
            block_copy(got_docs, back_sems.at[1])
            core_sent[...] = (doc_sum[...] + got_docs[...].astype(f32)).astype(bf16)
            send(core_sent, core_got, core_sems.at[0], core_sems.at[1], core)
            block_copy(core_got, core_sems.at[1])
            grad[...] = (core_sent[...].astype(f32) + core_got[...].astype(f32)).astype(bf16).astype(f32)
            block_copy(core_sent, core_sems.at[0])
            block_copy(cross.at[0], cross_sems.at[0])
            block_copy(vectors, doc_sems.at[0])

        block_copy(other_loss, loss_sems.at[1])
        lower = jnp.where(side == 0, own_loss[0:slots, :], other_loss[0:slots, :])
        upper = jnp.where(side == 0, other_loss[0:slots, :], own_loss[0:slots, :])
        pair = jnp.concatenate([lower, upper], axis=0)
        across = lax.broadcasted_iota(jnp.int32, pair.shape, 1) == lax.broadcasted_iota(jnp.int32, pair.shape, 0)
        loss[...] = jnp.sum(jnp.where(across, pair, 0.0), axis=0, keepdims=True)[:, 0 : 2 * slots]
        block_copy(own_loss, loss_sems.at[0])

        def settle(peer):
            block_copy(own, query_send.at[peer])
            block_copy(stats.at[batch], stat_send.at[peer])
            block_copy(sent_grads.at[peer], grad_send.at[peer])

        each(1, settle)

    return greet_all, begin, finish


def score_kernel(count, *refs):
    greet, begin, finish = score_steps(count, *refs)
    greet()
    begin()
    finish()


def score_scratch(count, length, width):
    quarter = length // 4
    slots = quarter // QLEN
    dma = pltpu.SemaphoreType.DMA
    return [
        pltpu.VMEM((count, quarter, width), bf16),
        pltpu.VMEM((length, width), bf16),
        pltpu.VMEM((count, quarter, length), bf16),
        pltpu.VMEM((count, quarter, width), f32),
        pltpu.VMEM((count * slots, width), f32),
        pltpu.VMEM((count * slots, width), jnp.int32),
        pltpu.VMEM((count, 8, max(TILE, count * slots)), f32),
        pltpu.VMEM((8, width), f32),
        pltpu.VMEM((8, width), f32),
        pltpu.VMEM((count, quarter, width), bf16),
        pltpu.VMEM((count, quarter, width), bf16),
        pltpu.VMEM((2, quarter, width), bf16),
        pltpu.VMEM((length, width), f32),
        pltpu.VMEM((length, width), bf16),
        pltpu.VMEM((length, width), bf16),
        pltpu.VMEM((length, width), bf16),
        pltpu.VMEM((length, width), bf16),
    ] + [dma((count,))] * 6 + [dma((2,))] * 7


def score(vectors, doc_row, top_mask, positive):
    count = lax.axis_size(BATCH)
    length, width = vectors.shape
    slots = length // 4 // QLEN
    return pl.pallas_call(
        functools.partial(score_kernel, count),
        out_shape=(
            jax.ShapeDtypeStruct((length, width), f32),
            jax.ShapeDtypeStruct((1, 2 * slots), f32),
        ),
        in_specs=[pl.BlockSpec(memory_space=pltpu.VMEM)] * 3 + [pl.BlockSpec(memory_space=pltpu.SMEM)],
        out_specs=(pl.BlockSpec(memory_space=pltpu.VMEM),) * 2,
        scratch_shapes=score_scratch(count, length, width),
        compiler_params=pltpu.CompilerParams(
            collective_id=0, has_side_effects=True, vmem_limit_bytes=56 * 1024 * 1024
        ),
        cost_estimate=pl.CostEstimate(flops=10**9, bytes_accessed=2 * 10**6, transcendentals=10**6),
        name="score",
    )(vectors, doc_row, top_mask, positive)


def rms_rows(value, weight):
    scale = lax.rsqrt(jnp.mean(value * value, axis=-1, keepdims=True) + norm_eps)
    return (value * scale * weight).astype(bf16)


KEPT = ("x", "n1", "q", "k", "v", "lse", "o", "xm", "n2", "gate", "up", "act")


def forward_kernel(made, results, count, *refs):
    (tokens, w_query, w_kv, w_out, w_in, w_down, w_proj, rel_bias, segments, gains), refs = refs[:10], refs[10:]
    asked, refs = (refs[:2], refs[2:]) if count else ((), refs)
    outs, refs = dict(zip(results, refs)), refs[len(results) :]
    found, refs = (refs[:2], refs[2:]) if count else ((), refs)
    held, refs = dict(zip(made, refs)), refs[len(made) :]
    (row_sent, row_got, sent, got, table, mask, bias, load_sems, store_sems, row_sems, send_sems, recv_sems), refs = (
        refs[:12],
        refs[12:],
    )
    half = lax.axis_index(MP)
    core = {MP: 1 - half}
    length, model = held["x0"].shape
    share = length // 2
    narrow, wide = held["q0"].shape[1], held["act0"].shape[1]
    layers = w_query.shape[0]
    loads, stores = [], []

    def fetch(source, target):
        copy = pltpu.make_async_copy(source, target, load_sems.at[len(loads)])
        copy.start()
        loads.append(copy)
        return copy

    def keep(name):
        copy = pltpu.make_async_copy(held[name], outs[name], store_sems.at[len(stores)])
        copy.start()
        stores.append(copy)

    ready = {"tokens": fetch(tokens, row_sent)}
    for layer in range(layers):
        for name, source in (
            ("wq", w_query.at[layer]),
            ("wk", w_kv.at[layer, 0]),
            ("wv", w_kv.at[layer, 1]),
            ("wo", w_out.at[layer]),
            ("wi", w_in.at[layer]),
            ("wd", w_down.at[layer]),
        ):
            ready[name + str(layer)] = fetch(source, held[name + str(layer)])
    ready["w_proj"] = fetch(w_proj, held["w_proj"])
    if count:
        greet, begin_score, finish_score = score_steps(count, held["vectors"], segments, *asked, *found, *refs)
        greet()
    else:
        barrier = pltpu.get_barrier_semaphore()
        pl.semaphore_signal(barrier, inc=1, device_id=core, device_id_type=pl.DeviceIdType.MESH)
        pl.semaphore_wait(barrier, 1)
    ready["tokens"].wait()
    send(row_sent, row_got, row_sems.at[0], row_sems.at[1], core)
    fill_table(rel_bias, table)
    fill_masks(row_ids_of(segments), mask, length // TILE)

    def rows_of(index):
        return pl.ds(pl.multiple_of(index * share, TILE), share)

    def share_part(turn, index, part):
        rows = rows_of(index)
        sent[turn, rows, :] = part.astype(bf16)
        send(
            sent.at[turn, rows, :], got.at[turn, rows, :],
            send_sems.at[turn, index], recv_sems.at[turn, index], core,
        )

    def total(turn, index, base):
        rows = rows_of(index)
        block_copy(got.at[turn, rows, :], recv_sems.at[turn, index])
        return base[rows, :] + (sent[turn, rows, :].astype(f32) + got[turn, rows, :].astype(f32))

    def project(layer, index, value):
        rows, name = rows_of(index), str(layer)
        held["x" + name][rows, :] = value
        n1 = rms_rows(value, gains[2 * layer : 2 * layer + 1, :])
        held["n1" + name][rows, :] = n1
        for part in "qkv":
            held[part + name][rows, :] = dot(n1, held["w" + part + name][...]).astype(bf16)

    for part in "qkv":
        ready["w" + part + "0"].wait()
    project(0, half, row_sent[...].astype(f32))
    block_copy(row_got, row_sems.at[1])
    project(0, 1 - half, row_got[...].astype(f32))

    for layer in range(layers):
        name = str(layer)
        for kept in ("x", "n1", "q", "k", "v"):
            keep(kept + name)
        held["lse" + name][...] = jnp.zeros((length, TILE), f32)

        def pair(p, carry, name=name):
            attend_pair(
                p, table, *(held[part + name] for part in ("q", "k", "v", "o", "lse")), mask, bias
            )
            return carry

        lax.fori_loop(0, narrow // TILE, pair, 0)
        ready["wo" + name].wait()
        for index in range(2):
            share_part(2 * layer, index, dot_nt(held["o" + name][rows_of(index), :], held["wo" + name][...]))
        keep("lse" + name)
        keep("o" + name)
        ready["wi" + name].wait()
        ready["wd" + name].wait()

        def feed(index, carry, layer=layer, name=name):
            rows = rows_of(index)
            value = total(2 * layer, index, held["x" + name])
            held["xm" + name][rows, :] = value
            n2 = rms_rows(value, gains[2 * layer + 1 : 2 * layer + 2, :])
            held["n2" + name][rows, :] = n2
            for column in range(0, wide, CHUNK):
                cols = pl.ds(column, CHUNK)
                g = dot(n2, held["wi" + name][0, :, cols])
                u = dot(n2, held["wi" + name][1, :, cols])
                held["gate" + name][rows, cols] = g.astype(bf16)
                held["up" + name][rows, cols] = u.astype(bf16)
                t = jnp.tanh(math.sqrt(2.0 / math.pi) * (g + 0.044715 * (g * g * g)))
                held["act" + name][rows, cols] = (0.5 * g * (1.0 + t) * u).astype(bf16)
            share_part(2 * layer + 1, index, dot_nt(held["act" + name][rows, :], held["wd" + name][...]))
            return carry

        lax.fori_loop(0, 2, feed, 0)
        for kept in ("xm", "n2", "gate", "up", "act"):
            keep(kept + name)
        if layer + 1 < layers:
            for part in "qkv":
                ready["w" + part + str(layer + 1)].wait()

            def following(index, carry, layer=layer, name=name):
                project(layer + 1, index, total(2 * layer + 1, index, held["xm" + name]))
                return carry

            lax.fori_loop(0, 2, following, 0)

    ready["w_proj"].wait()

    def finish(index, carry):
        rows = rows_of(index)
        value = total(2 * layers - 1, index, held["xm" + str(layers - 1)])
        held["state"][rows, :] = value
        final = rms_rows(value, gains[2 * layers : 2 * layers + 1, :])
        held["final"][rows, :] = final
        projected = dot(final, held["w_proj"][...])
        held["y"][rows, :] = projected
        scale = lax.rsqrt(jnp.sum(projected * projected, axis=-1, keepdims=True) + vector_eps)
        held["vectors"][rows, :] = (projected * scale).astype(bf16)
        return carry

    finish(half, 0)
    if count:
        begin_score()
    finish(1 - half, 0)
    for name in ("state", "final", "y", "vectors"):
        keep(name)
    if count:
        finish_score()
    for copy in stores:
        copy.wait()
    block_copy(row_sent, row_sems.at[0])
    for turn in range(2 * layers):
        for index in range(2):
            block_copy(sent.at[turn, rows_of(index), :], send_sems.at[turn, index])


def forward(tokens, weights, tables, scored):
    w_query, w_kv, w_out, w_in, w_down, w_proj = weights
    layers, model, narrow = w_query.shape
    wide, width = w_down.shape[2], w_proj.shape[1]
    length = 2 * tokens.shape[0]
    vmem, dma = pltpu.VMEM, pltpu.SemaphoreType.DMA
    sizes = dict(x=(model, f32), n1=(model, bf16), q=(narrow, bf16), k=(narrow, bf16), v=(narrow, bf16), lse=(TILE, f32),
                 o=(narrow, bf16), xm=(model, f32), n2=(model, bf16), gate=(wide, bf16), up=(wide, bf16), act=(wide, bf16))
    results = {name + str(layer): sizes[name] for layer in range(layers) for name in KEPT}
    results.update(state=(model, f32), final=(model, bf16), y=(width, f32), vectors=(width, bf16))
    made = {name: vmem((length, columns), kind) for name, (columns, kind) in results.items()}
    for layer in range(layers):
        for name in ("wq", "wk", "wv", "wo"):
            made[name + str(layer)] = vmem((model, narrow), bf16)
        made["wi" + str(layer)] = vmem((2, model, wide), bf16)
        made["wd" + str(layer)] = vmem((model, wide), bf16)
    made["w_proj"] = vmem((model, width), bf16)
    hbm, local = pl.BlockSpec(memory_space=pl.ANY), pl.BlockSpec(memory_space=vmem)
    count = lax.axis_size(BATCH) if scored else 0
    shapes = [jax.ShapeDtypeStruct((length, columns), kind) for columns, kind in results.values()]
    if scored:
        shapes += [
            jax.ShapeDtypeStruct((length, width), f32),
            jax.ShapeDtypeStruct((1, length // 2 // QLEN), f32),
        ]
    found = pl.pallas_call(
        functools.partial(forward_kernel, tuple(made), tuple(results), count),
        out_shape=tuple(shapes),
        in_specs=[hbm] * 7 + [local] * 3 + [local, pl.BlockSpec(memory_space=pltpu.SMEM)][: len(scored)],
        out_specs=(hbm,) * len(results) + (local,) * len(scored),
        scratch_shapes=list(made.values())
        + [
            vmem(tokens.shape, bf16),
            vmem(tokens.shape, bf16),
            vmem((2 * layers, length, model), bf16),
            vmem((2 * layers, length, model), bf16),
            vmem((8, SPAN), f32),
            vmem((length, 3 * TILE), f32),
            vmem((2, TILE, 3 * TILE), f32),
            dma((6 * layers + 2,)),
            dma((len(results),)),
            dma((2,)),
            dma((2 * layers, 2)),
            dma((2 * layers, 2)),
        ]
        + (score_scratch(count, length, width) if scored else []),
        compiler_params=pltpu.CompilerParams(
            collective_id=2, has_side_effects=True, vmem_limit_bytes=62 * 1024 * 1024
        ),
        cost_estimate=pl.CostEstimate(flops=10**10, bytes_accessed=5 * 10**7, transcendentals=10**6),
        name="forward",
    )(tokens, *weights, *tables, *scored)
    return dict(zip(results, found)), found[len(results) :]


CHUNK = 384


def block_copy(ref, sem):
    pltpu.make_async_copy(ref, ref, sem).wait()


class Sums:
    def __init__(self, refs):
        self.refs = refs
        self.side, self.batch = lax.axis_index(STREAM), lax.axis_index(BATCH)
        self.near, self.low, self.high = lax.rem(self.batch, 2), lax.rem(self.batch // 2, 2), self.batch // 4

    def stream_peer(self):
        return {STREAM: 1 - self.side}

    def near_peer(self):
        return {BATCH: self.batch + 1 - 2 * self.near}

    def low_peer(self):
        return {BATCH: self.batch + 2 - 4 * self.low}

    def high_peer(self):
        return {BATCH: self.batch + 4 - 8 * self.high}

    def slot(self, n):
        return n % RING

    def work(self, n):
        return self.refs["work"].at[n % self.refs["work"].shape[0]]

    def got(self, stage, n):
        return self.refs["got" + str(stage)].at[self.slot(n)]

    def send(self, source, stage, n, device):
        sems = self.refs["send"], self.refs["recv"]
        send(source, self.got(stage, n), sems[0].at[stage, self.slot(n)], sems[1].at[stage, self.slot(n)], device)

    def sent(self, stage, n):
        block_copy(self.got(stage, n), self.refs["send"].at[stage, self.slot(n)])

    def received(self, stage, n):
        block_copy(self.got(stage, n), self.refs["recv"].at[stage, self.slot(n)])

    def store(self, n):
        pltpu.make_async_copy(self.refs["done"].at[self.slot(n)], self.refs["out"](n), self.refs["store"].at[self.slot(n)]).start()

    def stored(self, n):
        block_copy(self.refs["done"].at[self.slot(n)], self.refs["store"].at[self.slot(n)])

    def add(self, count, place, got, at):
        def body(index, carry):
            target = place(index)
            target[...] = (target[...].astype(f32) + got[at(index)].astype(f32)).astype(bf16)
            return carry

        lax.fori_loop(0, count, body, 0)


class StreamFirst(Sums):
    stages = 5

    def half(self, side):
        rows = self.refs["work"].shape[4] // 2
        return pl.ds(pl.multiple_of(side * rows, 16), rows)

    def start(self, n):
        self.send(self.work(n).at[:, :, :, self.half(1 - self.side), :], 0, n, self.stream_peer())

    def step(self, n, stage):
        r, m = self.refs, self.slot(n)
        work, own = self.work(n), self.half(self.side)
        if stage <= 4:
            self.received(stage - 1, n)
        if stage == 1:
            for low in (1 - self.low, self.low):
                self.add(
                    4,
                    lambda i, low=low: work.at[i // 2, low, lax.rem(i, 2), own, :],
                    self.got(0, n),
                    lambda i, low=low: (i // 2, low, lax.rem(i, 2)),
                )
                if low is not self.low:
                    self.send(work.at[:, low, :, own, :], 1, n, self.low_peer())
        if stage == 2:
            for near in (1 - self.near, self.near):
                self.add(
                    2,
                    lambda i, near=near: work.at[i, self.low, near, own, :],
                    self.got(1, n),
                    lambda i, near=near: (i, near),
                )
                if near is not self.near:
                    self.send(work.at[:, self.low, near, own, :], 2, n, self.near_peer())
        if stage == 3:
            self.add(2, lambda i: work.at[i, self.low, self.near, own, :], self.got(2, n), lambda i: (i,))
            self.send(work.at[1 - self.high, self.low, self.near, own, :], 3, n, self.high_peer())
            self.sent(0, n)
        if stage == 4:
            total = work[self.high, self.low, self.near, own, :].astype(f32) + r["got3"][m].astype(f32)
            r["last"][m] = total.astype(bf16)
            self.send(r["last"].at[m], 4, n, self.stream_peer())
            if n >= RING:
                self.stored(n)
            r["done"][m, own, :] = r["last"][m]
            for earlier in range(1, 4):
                self.sent(earlier, n)
        if stage == 5:
            self.received(4, n)
            r["done"][m, self.half(1 - self.side), :] = r["got4"][m]
            self.store(n)
            self.sent(4, n)


class BatchFirst(Sums):
    stages = 4

    def start(self, n):
        self.send(self.work(n).at[:, :, 1 - self.near], 0, n, self.near_peer())

    def step(self, n, stage):
        r, m = self.refs, self.slot(n)
        work = self.work(n)
        self.received(stage - 1, n)
        if stage == 1:
            for low in (1 - self.low, self.low):
                self.add(
                    2,
                    lambda i, low=low: work.at[i, low, self.near],
                    self.got(0, n),
                    lambda i, low=low: (i, low),
                )
                if low is not self.low:
                    self.send(work.at[:, low, self.near], 1, n, self.low_peer())
        if stage == 2:
            self.add(2, lambda i: work.at[i, self.low, self.near], self.got(1, n), lambda i: (i,))
            self.send(work.at[1 - self.high, self.low, self.near], 2, n, self.high_peer())
        if stage == 3:
            total = work[self.high, self.low, self.near].astype(f32) + r["got2"][m].astype(f32)
            r["last"][m] = total.astype(bf16)
            self.send(r["last"].at[m], 3, n, self.stream_peer())
            for earlier in range(3):
                self.sent(earlier, n)
        if stage == 4:
            if n >= RING:
                self.stored(n)
            r["done"][m] = (r["last"][m].astype(f32) + r["got3"][m].astype(f32)).astype(bf16)
            self.store(n)
            self.sent(3, n)


RING = 4
WORK_RING = 5
FIRST_REFS = ("work", "got0", "got1", "got2", "got3", "got4", "last", "done", "send", "recv", "store")
LAST_REFS = ("work", "got0", "got1", "got2", "got3", "last", "done", "send", "recv", "store")


def first_scratch(rows, width, ring, work_ring):
    vmem, dma = pltpu.VMEM, pltpu.SemaphoreType.DMA
    half = rows // 2
    return [
        vmem((work_ring, 2, 2, 2, rows, width), bf16),
        vmem((ring, 2, 2, 2, half, width), bf16),
        vmem((ring, 2, 2, half, width), bf16),
        vmem((ring, 2, half, width), bf16),
        vmem((ring, half, width), bf16),
        vmem((ring, half, width), bf16),
        vmem((ring, half, width), bf16),
        vmem((ring, rows, width), bf16),
        dma((5, ring)),
        dma((5, ring)),
        dma((ring,)),
    ]


def last_scratch(rows, width, ring, work_ring):
    vmem, dma = pltpu.VMEM, pltpu.SemaphoreType.DMA
    return [
        vmem((work_ring, 2, 2, 2, rows, width), bf16),
        vmem((ring, 2, 2, rows, width), bf16),
        vmem((ring, 2, rows, width), bf16),
        vmem((ring, rows, width), bf16),
        vmem((ring, rows, width), bf16),
        vmem((ring, rows, width), bf16),
        vmem((ring, rows, width), bf16),
        dma((4, ring)),
        dma((4, ring)),
        dma((ring,)),
    ]


def blocks_of(wide):
    found = []
    for layer in (1, 0):
        columns = range(0, wide, CHUNK)
        found += [("e" + str(layer), "act" + str(layer), column, 0, (layer,)) for column in columns]
        for column in columns:
            for index, right in enumerate(("gate", "up")):
                found.append(("n2" + str(layer), right + str(layer), column, 1, (layer, index)))
        for left, right, output, index in (("c", "o", 2, ()), ("n1", "dq", 3, ()), ("n1", "dk", 4, (0,)), ("n1", "dv", 4, (1,))):
            found.append((left + str(layer), right + str(layer), 0, output, (layer,) + index))
    return found


def back_kernel(names, made, blocks, *refs):
    given, refs = dict(zip(names, refs)), refs[len(names) :]
    (rel_bias, segments, gains, projected, grad_vectors, w_proj), refs = refs[:6], refs[6:]
    outs, refs = refs[:8], refs[8:]
    held, refs = dict(zip(made, refs)), refs[len(made) :]
    (acc, core_sent, core_got, table, mask, bias, grid, dk_sum, dv_sum, do, little_got), refs = refs[:11], refs[11:]
    (load_sems, core_sems, little_sems), refs = refs[:3], refs[3:]
    firsts, lasts = blocks[0::2], blocks[1::2]
    half = len(blocks) // 2

    def out_of(blocks):
        def place(n):
            _, _, column, output, index = blocks[n]
            return outs[output].at[index + (slice(None), pl.ds(column, CHUNK))]

        return place

    first_refs, refs = dict(zip(FIRST_REFS, refs), out=out_of(firsts)), refs[len(FIRST_REFS) :]
    last_refs, refs = dict(zip(LAST_REFS, refs), out=out_of(lasts)), refs[len(LAST_REFS) :]
    stream_first, batch_first = StreamFirst(first_refs), BatchFirst(last_refs)
    projection = BatchFirst(dict(zip(LAST_REFS, refs), out=lambda n: outs[5]))
    half_index = lax.axis_index(MP)
    core = {MP: 1 - half_index}
    length, model = held["grad"].shape
    tiles = length // TILE

    loads = {}

    def fetch(name, source=None, target=None):
        copy = pltpu.make_async_copy(
            given[name] if source is None else source, held[name] if target is None else target, load_sems.at[len(loads)]
        )
        copy.start()
        loads[name] = [copy, False]

    def need(name):
        if name in loads and not loads[name][1]:
            loads[name][0].wait()
            loads[name][1] = True
        return held.get(name)

    def fetch_attention(layer):
        for name in ("wo", "q", "k", "v", "lse", "wq", "wk", "wv", "x"):
            source = given[name + str(layer)] if name + str(layer) in given else None
            if name == "wo":
                source = given["w_out"].at[layer]
            if name == "wq":
                source = given["w_query"].at[layer]
            if name in ("wk", "wv"):
                source = given["w_kv"].at[layer, 0 if name == "wk" else 1]
            fetch(name + str(layer), source, held[name])

    def fetch_ffn(layer):
        fetch("wd" + str(layer), given["wd"].at[layer], held["wd"])
        fetch("wi" + str(layer), given["wi"].at[layer], held["wi"])
        fetch("xm" + str(layer), None, held["xm"])

    fetch("state", None, held["x"])
    fetch("act1")
    fetch("wd1", given["wd"].at[1], held["wd"])
    for name in ("gate1", "up1"):
        fetch(name)
    fetch("wi1", given["wi"].at[1], held["wi"])
    fetch("xm1", None, held["xm"])
    fetch("n21")
    for name in ("o1", "n11", "gate0", "up0", "act0", "n20", "o0", "n10", "final"):
        fetch(name)

    barrier = pltpu.get_barrier_semaphore()
    peers = [stream_first.stream_peer(), stream_first.near_peer(), stream_first.low_peer(), stream_first.high_peer(), core]
    for peer in peers:
        pl.semaphore_signal(barrier, inc=1, device_id=peer, device_id_type=pl.DeviceIdType.MESH)


    def product(left, right, work):
        width = left.shape[1] // 2
        for part in range(2):
            block = dot_tn(left[:, part * width : (part + 1) * width], right).astype(bf16)
            work[part] = block.reshape(work.shape[1:])

    def make(sums, blocks, n):
        left, right, column, _, _ = blocks[n]
        product(need(left), need(right)[:, column : column + CHUNK], sums.work(n))
        if n == 0 and sums is stream_first:
            pl.semaphore_wait(barrier, len(peers))
        sums.start(n)

    def little_step(stage):
        peer = (stream_first.stream_peer, stream_first.near_peer, stream_first.low_peer, stream_first.high_peer)
        if stage > 0:
            block_copy(little_got.at[2 * stage - 1], little_sems.at[2 * stage - 1])
            total = little_got[2 * stage - 2] + little_got[2 * stage - 1]
            block_copy(little_got.at[2 * stage - 2], little_sems.at[2 * stage - 2])
            if stage == 4:
                outs[6][...] = total
            else:
                little_got[2 * stage] = total
        if stage < 4:
            send(
                little_got.at[2 * stage], little_got.at[2 * stage + 1],
                little_sems.at[2 * stage], little_sems.at[2 * stage + 1], peer[stage](),
            )


    grad = held["grad"]

    def rows_of(index):
        return pl.ds(pl.multiple_of(index * TILE, TILE), TILE)

    def share(turn):
        def pack(index, carry):
            core_sent[rows_of(index), :] = acc[rows_of(index), :].astype(bf16)
            return carry

        lax.fori_loop(0, tiles, pack, 0)
        send(core_sent, core_got.at[turn % 2], core_sems.at[0, turn], core_sems.at[1, turn], core)

    def norm_back(values, gain, gradient, first):
        weight = gains[gain : gain + 1, :]

        def tile(index, total):
            rows = rows_of(index)
            given_grad = gradient(rows)
            value = values[rows, :]
            scale = lax.rsqrt(jnp.mean(value * value, axis=-1, keepdims=True) + norm_eps)
            weighted = given_grad * weight
            along = jnp.mean(value * weighted, axis=-1, keepdims=True)
            change = scale * weighted - value * (scale * scale * scale * along)
            grad[rows, :] = change if first else grad[rows, :] + change
            return total + jnp.sum(given_grad * (value * scale), axis=0, keepdims=True)

        total = lax.fori_loop(0, tiles, tile, jnp.zeros((1, model), f32))
        little_got[0, gain : gain + 1, 0:model] = total

    def through_norm(turn, values, gain):
        block_copy(core_got.at[turn % 2], core_sems.at[1, turn])
        norm_back(
            values, gain, lambda rows: core_sent[rows, :].astype(f32) + core_got[turn % 2, rows, :].astype(f32), False
        )
        block_copy(core_sent, core_sems.at[0, turn])

    def projection_back():
        def tile(index, carry):
            rows = rows_of(index)
            y, grad_vector = projected[rows, :], grad_vectors[rows, :]
            scale = lax.rsqrt(jnp.sum(y * y, axis=-1, keepdims=True) + vector_eps)
            along = jnp.sum(y * grad_vector, axis=-1, keepdims=True)
            held["dproj"][rows, :] = (scale * grad_vector - y * (scale * scale * scale * along)).astype(bf16)
            return carry

        lax.fori_loop(0, tiles, tile, 0)
        need("state")
        norm_back(held["x"], 4, lambda rows: dot_nt(held["dproj"][rows, :], w_proj[...]), True)

    def round_grad(target):
        def pack(index, carry):
            target[rows_of(index), :] = grad[rows_of(index), :].astype(bf16)
            return carry

        lax.fori_loop(0, tiles, pack, 0)

    def ffn_tile(layer, column):
        cols = pl.ds(column, CHUNK)
        e, gate, up = (held[name + str(layer)] for name in ("e", "gate", "up"))

        def tile(index, carry):
            rows = pl.ds(pl.multiple_of(index * 2 * TILE, 2 * TILE), 2 * TILE)
            grad_hidden = dot(e[rows, :], held["wd"][:, cols])
            g, u = gate[rows, cols].astype(f32), up[rows, cols].astype(f32)
            root = math.sqrt(2.0 / math.pi)
            t = jnp.tanh(root * (g + 0.044715 * (g * g * g)))
            slope = 0.5 * (1.0 + t) + (0.5 * root) * g * (1.0 - t * t) * (1.0 + (3 * 0.044715) * (g * g))
            dg = (grad_hidden * u * slope).astype(bf16)
            du = (grad_hidden * (0.5 * g * (1.0 + t))).astype(bf16)
            gate[rows, cols] = dg
            up[rows, cols] = du
            part = dot_nt(dg, held["wi"][0, :, cols]) + dot_nt(du, held["wi"][1, :, cols])
            acc[rows, :] = part if column == 0 else acc[rows, :] + part
            return carry

        lax.fori_loop(0, tiles // 2, tile, 0)

    def attention_start(layer):
        c = held["c" + str(layer)]
        round_grad(c)

        def tile(index, carry):
            rows = pl.ds(pl.multiple_of(index * 2 * TILE, 2 * TILE), 2 * TILE)
            do[rows, :] = dot(c[rows, :], held["wo"][...]).astype(bf16)
            return carry

        need("wo" + str(layer))
        lax.fori_loop(0, tiles // 2, tile, 0)
        for name in ("q", "k", "v", "lse"):
            need(name + str(layer))

    def attention_pair(layer, p):
        attend_back_pair(
            p, table, held["lse"], held["q"], held["k"], held["v"], do,
            held["dq" + str(layer)], held["dk" + str(layer)], held["dv" + str(layer)],
            mask, bias, grid, dk_sum, dv_sum,
        )
        for half in range(2):
            line = diagonals(grid, half)
            place = (0, pl.ds(2 * p + half, 1), pl.ds(model, SPAN))
            little_got[place] = little_got[place] + line

    def attention_end(layer, turn):
        for name in ("wq", "wk", "wv"):
            need(name + str(layer))

        def tile(index, carry):
            rows = pl.ds(pl.multiple_of(index * 2 * TILE, 2 * TILE), 2 * TILE)
            acc[rows, :] = (
                dot_nt(held["dq" + str(layer)][rows, :], held["wq"][...])
                + dot_nt(held["dk" + str(layer)][rows, :], held["wk"][...])
                + dot_nt(held["dv" + str(layer)][rows, :], held["wv"][...])
            )
            return carry

        lax.fori_loop(0, tiles // 2, tile, 0)
        share(turn)

    def ffn_step(layer, number, turn):
        if number == 0:
            for name in ("wd", "wi", "gate", "up"):
                need(name + str(layer))
        ffn_tile(layer, number * CHUNK)
        if number == 3:
            share(turn)

    def setup():
        fill_table(rel_bias, table)
        fill_masks(row_ids_of(segments), mask, tiles)

    def attention_first(layer, turn):
        need("xm" + str(layer))
        through_norm(turn, held["xm"], 2 * layer + 1)
        if layer:
            fetch_ffn(0)
        attention_start(layer)
        attention_pair(layer, 0)

    def layer_end(layer, turn):
        need("x" + str(layer))
        through_norm(turn, held["x"], 2 * layer)
        if layer:
            fetch_attention(0)
            round_grad(held["e0"])
            ffn_step(0, 0, 2)
        else:
            share_rows = length // 2
            outs[7][...] = grad[pl.ds(pl.multiple_of(half_index * share_rows, TILE), share_rows), :]

    pieces = [
        [lambda: ffn_step(1, 0, 0)],
        [lambda: ffn_step(1, 1, 0)],
        [lambda: ffn_step(1, 2, 0)],
        [lambda: ffn_step(1, 3, 0), setup],
        [lambda: attention_first(1, 0)],
        [lambda: attention_pair(1, 1), lambda: attention_pair(1, 2)],
        [lambda: attention_end(1, 1)],
        [lambda: layer_end(1, 1)],
        [lambda: ffn_step(0, 1, 2)],
        [lambda: ffn_step(0, 2, 2)],
        [lambda: ffn_step(0, 3, 2)],
        [lambda: attention_first(0, 2)],
        [lambda: attention_pair(0, 1)],
        [lambda: attention_pair(0, 2)],
        [lambda: attention_end(0, 3)],
        [lambda: layer_end(0, 3)],
    ]
    little_got[0] = jnp.zeros(little_got.shape[1:], f32)
    projection_back()
    fetch_attention(1)
    round_grad(held["e1"])
    for t in range(half + 5):
        if t < half:
            make(stream_first, firsts, t)
            make(batch_first, lasts, t)
        if t == half - 3:
            product(need("final"), held["dproj"][...], projection.work(0))
            projection.start(0)
        if t < len(pieces):
            for piece in pieces[t]:
                piece()
        for stage in (1, 2, 3, 4, 5):
            if 0 <= t - stage < half:
                stream_first.step(t - stage, stage)
                if stage <= 4:
                    batch_first.step(t - stage, stage)
            if t - stage == half - 3 and stage <= 4:
                projection.step(0, stage)
        if 0 <= t - half + 1 <= 4:
            little_step(t - half + 1)
    for n in range(half - RING, half):
        stream_first.stored(n)
        batch_first.stored(n)
    projection.stored(0)


def back(chain, weights, tables):
    batch = lax.axis_size(BATCH)
    length, model = chain["x0"].shape
    rows = model // batch
    narrow, wide = chain["q1"].shape[1], chain["act1"].shape[1]
    width = tables[-1].shape[1]
    little = jax.ShapeDtypeStruct((8, model + SPAN), f32)
    blocks = blocks_of(wide)
    given = dict(chain, **weights)
    vmem, dma, shape = pltpu.VMEM, pltpu.SemaphoreType.DMA, jax.ShapeDtypeStruct
    made = {"grad": (length, model), "x": (length, model), "xm": (length, model), "lse": (length, TILE)}
    made = {name: vmem(dims, f32) for name, dims in made.items()}
    for name in ("e", "n2", "c", "n1"):
        made.update({name + layer: vmem((length, model), bf16) for layer in "01"})
    for name in ("act", "gate", "up"):
        made.update({name + layer: vmem((length, wide), bf16) for layer in "01"})
    for name in ("o", "dq", "dk", "dv"):
        made.update({name + layer: vmem((length, narrow), bf16) for layer in "01"})
    made.update({name: vmem((length, narrow), bf16) for name in "qkv"})
    made.update({name: vmem((model, narrow), bf16) for name in ("wo", "wq", "wk", "wv")})
    made.update(wd=vmem((model, wide), bf16), wi=vmem((2, model, wide), bf16))
    made.update(final=vmem((length, model), bf16), dproj=vmem((length, width), bf16))
    ins = [pl.BlockSpec(memory_space=pl.ANY)] * len(given) + [pl.BlockSpec(memory_space=vmem)] * 6
    hbm, local = pl.BlockSpec(memory_space=pl.ANY), pl.BlockSpec(memory_space=vmem)
    return pl.pallas_call(
        functools.partial(back_kernel, tuple(given), tuple(made), blocks),
        out_shape=(
            shape((2, rows, wide), bf16),
            shape((2, 2, rows, wide), bf16),
            shape((2, rows, narrow), bf16),
            shape((2, rows, narrow), bf16),
            shape((2, 2, rows, narrow), bf16),
            shape((rows, width), bf16),
            shape(little.shape, f32),
            shape((length // 2, model), f32),
        ),
        in_specs=ins,
        out_specs=(hbm,) * 6 + (local,) * 2,
        scratch_shapes=list(made.values())
        + [
            vmem((length, model), f32),
            vmem((length, model), bf16),
            vmem((2, length, model), bf16),
            vmem((8, SPAN), f32),
            vmem((length, 3 * TILE), f32),
            vmem((2, TILE, 3 * TILE), f32),
            vmem((2, TILE, SPAN), f32),
            vmem((length, TILE), f32),
            vmem((length, TILE), f32),
            vmem((length, narrow), bf16),
            vmem((8,) + little.shape, f32),
            dma((64,)),
            dma((2, 4)),
            dma((8,)),
        ]
        + first_scratch(rows, CHUNK, RING, WORK_RING)
        + last_scratch(rows, CHUNK, RING, WORK_RING)
        + last_scratch(rows, width, 1, 1),
        compiler_params=pltpu.CompilerParams(
            collective_id=1, has_side_effects=True, vmem_limit_bytes=62 * 1024 * 1024
        ),
        cost_estimate=pl.CostEstimate(flops=2 * 10**10, bytes_accessed=5 * 10**7, transcendentals=10**6),
        name="back",
    )(*given.values(), *tables)


def place_kernel(down, into, out, query, key_value, projection, little, grad, vectors, losses, *outs):
    share = outs[0].shape[0]
    first = pl.multiple_of(lax.axis_index(MP) * share, TILE)
    outs[0][...] = vectors[pl.ds(first, share), :]
    outs[1][...] = losses[...]
    for source, target in zip((grad, query, key_value, out, into, down, projection), outs[2:8] + outs[10:]):
        target[...] = source[...].astype(f32)
    gains, bias = outs[8], outs[9]
    model = grad.shape[1]
    count, rows = gains.shape
    moved = pltpu.roll(little[:, 0:model], lax.rem(model - lax.axis_index(BATCH) * rows, model), axis=1)
    gains[...] = moved[0:count, 0:rows]
    bias[...] = lax.dot_general(
        little[0 : bias.shape[0], model:],
        bucket_places(bias.shape[1]),
        (((1,), (1,)), ((), ())),
        precision=highest,
        preferred_element_type=f32,
    )


def place(summed, vectors, losses, gain_count, bias_shape):
    down, into, out, query, key_value, projection, little, grad = summed
    shape = jax.ShapeDtypeStruct
    local = pl.BlockSpec(memory_space=pltpu.VMEM)
    return pl.pallas_call(
        place_kernel,
        out_shape=(shape((grad.shape[0], vectors.shape[1]), bf16), shape(losses.shape, f32))
        + tuple(shape(value.shape, f32) for value in (grad, query, key_value, out, into, down))
        + (shape((gain_count, query.shape[1]), f32), shape(bias_shape, f32), shape(projection.shape, f32)),
        in_specs=[local] * 10,
        out_specs=(local,) * 11,
        compiler_params=pltpu.CompilerParams(vmem_limit_bytes=60 * 1024 * 1024),
        name="place",
    )(*summed, vectors, losses)


def sum_gradients_plainly(kept, final_pair, little):
    def summed(left, right):
        part = lax.psum_scatter(dot_tn(left, right).astype(bf16), BATCH, scatter_dimension=0, tiled=True)
        return sum_of_two(part, STREAM)

    found = []
    for e, n2, c, n1, hidden, dg, du, o, dq, dk, dv in kept:
        found.append((
            summed(e, hidden),
            jnp.stack([summed(n2, dg), summed(n2, du)]),
            summed(c, o),
            summed(n1, dq),
            jnp.stack([summed(n1, dk), summed(n1, dv)]),
        ))
    return [jnp.stack(parts) for parts in zip(*found)] + [
        summed(*final_pair),
        lax.psum(little, (STREAM, BATCH)),
    ]


def on_device(
    tokens,
    segments,
    top_mask,
    positive,
    w_query,
    w_kv,
    w_out,
    w_in,
    w_down,
    gains,
    rel_bias,
    w_proj,
):
    length = segments.shape[1]
    share_len, model_width = tokens.shape[2:]
    head_count = rel_bias.shape[1]
    layers = w_query.shape[0]
    batch = lax.axis_size(BATCH)
    bias_rows = jnp.transpose(rel_bias)
    tables = (bias_rows, segments, gains)
    together = batch <= 8
    kept, scores = forward(
        tokens[0, 0],
        (w_query, w_kv, w_out, w_in, w_down, w_proj),
        tables,
        (top_mask, positive) if together else (),
    )
    vectors = kept["vectors"]
    grad_vectors, query_loss = scores if together else score(vectors, segments, top_mask, positive)
    if layers == 2 and batch == 8:
        chain = {name: value for name, value in kept.items() if name not in ("y", "vectors")}
        weights = dict(w_query=w_query, w_kv=w_kv, w_out=w_out, wi=w_in, wd=w_down)
        summed = back(chain, weights, tables + (kept["y"], grad_vectors, w_proj))
        placed = place(summed, vectors, query_loss, gains.shape[0], bias_rows.shape)
        return (placed[0][None, None], placed[1], placed[2][None, None]) + placed[3:9] + (placed[9].T, placed[10])
    else:
        row_segments = jnp.where(
            lax.axis_index(STREAM) == 0, jnp.arange(length, dtype=jnp.int32) // QLEN, segments[0]
        )
        row_ids = row_segments[None]
        offset_onehot = (
            offset_buckets()[None, :] == jnp.arange(rel_bias.shape[0], dtype=jnp.int32)[:, None]
        ).astype(f32)
        table = jnp.einsum(
            "bh,bk->hk", jnp.pad(rel_bias, ((0, 0), (0, 8 - head_count))), offset_onehot, precision=highest
        )
        kept_layers = [[kept[name + str(layer)] for name in KEPT] for layer in range(layers)]
        grad_projected = jax.vjp(normalize, kept["y"])[1](grad_vectors)[0].astype(bf16)
        grad_final = dot_nt(grad_projected, w_proj)
        grad_state, grad_gain_final = jax.vjp(rms_scale, kept["state"], gains[2 * layers])[1](grad_final)
        gain_grads = [None] * (2 * layers)
        operands = [None] * layers
        sums = jnp.zeros(table.shape, f32)
        for layer in reversed(range(layers)):
            weights_layer = (
                w_query[layer],
                w_kv[layer],
                w_out[layer],
                w_in[layer],
                w_down[layer],
                gains[2 * layer],
                gains[2 * layer + 1],
            )
            grad_state, ffn_lefts, ffn_rights, gain_grads[2 * layer + 1] = ffn_backward(
                grad_state, kept_layers[layer], weights_layer
            )
            grad_state, lefts, rights, gain_grads[2 * layer], part = attention_backward(
                grad_state, table, row_ids, kept_layers[layer], weights_layer
            )
            operands[layer] = ffn_lefts + lefts + ffn_rights + rights
            sums = sums + part
        little = jnp.concatenate(
            [jnp.pad(jnp.stack(gain_grads + [grad_gain_final]), ((0, 7 - 2 * layers), (0, 0))), sums], axis=1
        )
        summed = sum_gradients_plainly(operands, (kept["final"], grad_projected), little)
        grad_down, grad_in, grad_out, grad_query, grad_kv, grad_proj, little = summed
        own_grad = lax.dynamic_slice_in_dim(grad_state, lax.axis_index(MP) * share_len, share_len, 0)
        grad_bias = jnp.einsum("hk,bk->bh", little[:, model_width:], offset_onehot, precision=highest)
        rows = model_width // batch
        grad_gains = lax.dynamic_slice(little, (0, lax.axis_index(BATCH) * rows), (2 * layers + 1, rows))
    own_vectors = lax.dynamic_slice_in_dim(vectors, lax.axis_index(MP) * share_len, share_len, 0)
    return (
        own_vectors[None, None],
        query_loss,
        own_grad[None, None],
        grad_query,
        grad_kv,
        grad_out,
        grad_in,
        grad_down,
        grad_gains,
        grad_bias[:, :head_count],
        grad_proj,
    )


def solution(mesh):
    placed = (
        P(STREAM, BATCH, MP, None),
        P(BATCH, None),
        P(None, MP, BATCH, None),
        P(None, MP),
        P(None, None, MP),
        P(None, None, None, MP),
        P(None, None, MP),
        P(None, None, None, MP),
        P(None, None, MP),
        P(),
        P(None, MP),
        P(),
    )
    return jax.shard_map(
        on_device,
        mesh=mesh,
        in_specs=placed,
        out_specs=(
            P(STREAM, BATCH, MP, None),
            P(BATCH, MP),
            P(STREAM, BATCH, MP, None),
            P(None, BATCH, MP),
            P(None, None, BATCH, MP),
            P(None, BATCH, MP),
            P(None, None, BATCH, MP),
            P(None, BATCH, MP),
            P(None, BATCH),
            P(None, MP),
            P(BATCH, None),
        ),
        check_vma=False,
    )
```
